128 devices in a mesh: seq: 32 (over y, x, core), mp: 4 (over z).
Axes of the slice: x: 4, y: 4, z: 4, core: 2. Of those that a mesh axis runs over, the one named last changes fastest.
Arguments:
- tokens: bfloat16 [32768, 1024], P('seq', 'mp'), may hold values from -400 to 400
- w_query: bfloat16 [1024, 1024], P(None, 'mp'), may hold values from -0.125 to 0.125
- w_key: bfloat16 [1024, 1024], P(None, 'mp'), may hold values from -3.875 to 3.875
- w_value: bfloat16 [1024, 1024], P(None, 'mp'), may hold values from -0.1875 to 0.1875
- w_out: bfloat16 [1024, 1024], P('mp'), may hold values from -1.5 to 1.5
- grad_out: bfloat16 [32768, 1024], P('seq', 'mp'), may hold values from -6 to 6
Outputs:
- attn_out: bfloat16 [32768, 1024], P('seq', 'mp')
- grad_tokens: float32 [32768, 1024], P('seq', 'mp')
- grad_w_query: float32 [1024, 1024], P('seq', 'mp')
- grad_w_key: float32 [1024, 1024], P('seq', 'mp')
- grad_w_value: float32 [1024, 1024], P('seq', 'mp')
- grad_w_out: float32 [1024, 1024], P('mp', 'seq')
The draws below stay inside these ranges and needn't reach their ends.
All inputs are finite; a program needn't handle non-finite values.
Results may differ from the reference program's by a relative error of at most 0.02.
The reference program's roundings to bfloat16 on the way count: a program that leaves them out, or rounds other values in their place, can miss the bound.
Values may be sent and summed in bfloat16 or wider, within the bound.
No kernel may reach another device: no remote copies, remote signals or barrier semaphores. Data moves between devices by JAX's collectives and lax.ppermute only.
A program may use at most 192 MiB of HBM per device.

```python
import math
import jax
import jax.numpy as jnp
from jax import lax

D = 1024
HD = 64
BLOCK = 256
LEVELS = 3
TOK_DEV = 1024
TOKENS = 32768
N_SEQ = 32
N_MP = 4


def shared_base(key):
    return jnp.clip(jax.random.normal(key, (D, D), jnp.float32), -4.0, 4.0) * D ** (-0.5)


def draw_tokens(key, part):
    key = jax.random.fold_in(key, 11)
    key_base, key_cols, key_rows = jax.random.split(key, 3)
    column_scale = jnp.exp(jax.random.uniform(key_cols, (1, D), jnp.float32) * math.log(10.0))
    row_scale = jnp.exp(jax.random.uniform(key_rows, (TOKENS, 1), jnp.float32) * math.log(10.0))
    rough = jnp.clip(jax.random.normal(key_base, (TOKENS, D), jnp.float32), -4.0, 4.0)
    return (rough * column_scale * row_scale).astype(jnp.bfloat16)


def draw_w_query(key, part):
    base = shared_base(key)
    return base.astype(jnp.bfloat16)


def draw_w_key(key, part):
    key = jax.random.fold_in(key, 13)
    key_fresh = jax.random.fold_in(key, 0)
    fresh = jnp.clip(jax.random.normal(key_fresh, (D, D), jnp.float32), -4.0, 4.0) * D ** (-0.5)
    return fresh.astype(jnp.bfloat16)


def levels(rng, shape, shards, smallest, high):
    def one(dim, parts):
        draws = jax.random.uniform(jax.random.fold_in(jax.random.fold_in(rng, 6), dim), (parts,), jnp.float32, smallest / len(shards), high / len(shards))
        return jnp.repeat(jnp.exp(draws), shape[dim] // parts).reshape((-1,) + (1,) * (len(shape) - dim - 1))

    level = one(*shards[0])
    for cut in shards[1:]:
        level = level * one(*cut)
    return level


def bell_draw(stream_key, extent, width, limit, cuts=(), held_as=jnp.bfloat16):
    loudness = levels(stream_key, extent, cuts, -0.22, 0.18) if cuts else 1.0
    result = jax.random.normal(stream_key, extent, jnp.float32) * width * loudness
    return jnp.minimum(jnp.maximum(result, -limit), limit).astype(held_as)


def setup_inputs(seed: int = 0) -> dict:
    seeds = jax.random.split(jax.random.key(seed), 7)
    tokens = draw_tokens(jax.random.fold_in(seeds[6], 71), 0)
    w_query = draw_w_query(jax.random.fold_in(seeds[6], 71), 0)
    w_key = draw_w_key(jax.random.fold_in(seeds[6], 71), 0)
    w_value = bell_draw(seeds[3], (D, D), D ** -0.5, 0.1875, ((1, 4),))
    w_out = bell_draw(seeds[4], (D, D), (D // 64) ** -0.5, 1.5, ((0, 4),))
    grad_out = bell_draw(seeds[5], (TOKENS, D), 1.0, 6.0, ((0, 32), (1, 4)))
    return dict(tokens=tokens, w_query=w_query, w_key=w_key, w_value=w_value, w_out=w_out, grad_out=grad_out)


EPSILON = 1e-06
NEGATIVE = -1e+30

def product(form, left_side, right_side):
    return jnp.einsum(form, left_side.astype(jnp.float32), right_side.astype(jnp.float32))

def pool_rows(source, factor):
    if factor == 1:
        return source
    row_count, channels = source.shape
    grouped = source.reshape(row_count // factor, factor, channels)
    return lax.optimization_barrier(jnp.mean(grouped, axis=1, dtype=jnp.float32)).astype(jnp.bfloat16)

def pool_sums(source, factor):
    if factor == 1:
        return source
    row_count, channels = source.shape
    grouped = source.reshape(row_count // factor, factor, channels)
    return lax.optimization_barrier(jnp.sum(grouped, axis=1, dtype=jnp.float32)).astype(jnp.bfloat16)

def usable_keys(first_block, block_total, block_count, offsets):
    neighbour = first_block + jnp.arange(block_count, dtype=jnp.int32)[:, None] + jnp.array(offsets, dtype=jnp.int32)[None, :] - 1
    return jnp.repeat((neighbour >= 0) & (neighbour < block_total), BLOCK, axis=1)

def level_scores(queries, extended, first_block, block_total, with_own):
    row_count, channels = queries.shape
    head_count = channels // HD
    block_count = row_count // BLOCK
    offsets = (0, 1, 2) if with_own else (0, 2)
    blocks_ext = extended.reshape(block_count + 2, BLOCK, 2, head_count, HD)
    picked = jnp.concatenate([blocks_ext[offset:offset + block_count] for offset in offsets], axis=1)
    key_rows = picked[:, :, 0]
    value_rows = picked[:, :, 1]
    query_blocks = queries.reshape(block_count, BLOCK, head_count, HD)
    scores = product('jqhd,jkhd->jhqk', query_blocks, key_rows) * HD ** (-0.5)
    usable = usable_keys(first_block, block_total, block_count, offsets)
    scores = jnp.where(usable[:, None, None, :], scores, NEGATIVE)
    row_max = lax.optimization_barrier(jnp.max(scores, axis=-1, keepdims=True))
    exponent = jnp.exp(scores - row_max)
    probabilities = exponent / lax.optimization_barrier(jnp.sum(exponent, axis=-1, keepdims=True))
    return (query_blocks, key_rows, value_rows, probabilities, offsets)

def level_forward(queries, extended, first_block, block_total, with_own):
    query_blocks, key_rows, value_rows, probabilities, offsets = level_scores(queries, extended, first_block, block_total, with_own)
    weights = probabilities.astype(jnp.bfloat16)
    level_out = product('jhqk,jkhd->jqhd', weights, value_rows)
    return level_out.reshape(queries.shape)

def level_backward(queries, extended, first_block, block_total, with_own, d_level):
    query_blocks, key_rows, value_rows, probabilities, offsets = level_scores(queries, extended, first_block, block_total, with_own)
    row_count, channels = queries.shape
    head_count = channels // HD
    block_count = row_count // BLOCK
    weights = probabilities.astype(jnp.bfloat16)
    grad_blocks = d_level.reshape(block_count, BLOCK, head_count, HD)
    d_weights = product('jqhd,jkhd->jhqk', grad_blocks, value_rows)
    d_value_rows = product('jhqk,jqhd->jkhd', weights, grad_blocks)
    row_dot = lax.optimization_barrier(jnp.sum(probabilities * d_weights, axis=-1, keepdims=True))
    d_scores = (probabilities * (d_weights - row_dot) * HD ** (-0.5)).astype(jnp.bfloat16)
    d_query_blocks = product('jhqk,jkhd->jqhd', d_scores, key_rows)
    d_key_rows = product('jhqk,jqhd->jkhd', d_scores, query_blocks)
    d_picked = jnp.stack([d_key_rows, d_value_rows], axis=2).reshape(block_count, len(offsets), BLOCK, 2 * channels)
    d_ext = jnp.zeros((block_count + 2, BLOCK, 2 * channels), jnp.float32)
    for position, offset in enumerate(offsets):
        d_ext = d_ext.at[offset:offset + block_count].add(d_picked[:, position])
    return (d_query_blocks.reshape(row_count, channels), d_ext.reshape((block_count + 2) * BLOCK, 2 * channels))

def rounded(source):
    return lax.optimization_barrier(source.astype(jnp.bfloat16)).astype(jnp.float32)

def reference(tokens, w_query, w_key, w_value, w_out, grad_out):
    as_float = tokens.astype(jnp.float32)
    inverse = lax.rsqrt(lax.optimization_barrier(jnp.mean(as_float * as_float, axis=1, keepdims=True)) + EPSILON)
    normed_f = as_float * inverse
    normed = normed_f.astype(jnp.bfloat16)
    stacked_w = jnp.concatenate([w_query, w_key, w_value], axis=1)
    projected = jnp.dot(normed, stacked_w, preferred_element_type=jnp.float32).astype(jnp.bfloat16)
    queries = projected[:, :D]
    key_value = projected[:, D:]
    shard_ids = jnp.arange(N_SEQ, dtype=jnp.int32)
    attended_f = jnp.zeros((TOKENS, D), jnp.float32)
    saved = []
    for level_index in range(LEVELS):
        factor = 2 ** level_index
        pooled_q = pool_rows(queries, factor)
        padded = jnp.pad(pool_rows(key_value, factor), ((BLOCK, BLOCK), (0, 0)))
        span_rows = TOK_DEV // factor
        block_total = TOKENS // (BLOCK * factor)
        saved.append((pooled_q, padded, span_rows, block_total))

        def one_shard(shard_index, pooled_q=pooled_q, padded=padded, span_rows=span_rows, block_total=block_total, with_own=level_index == 0):
            query_part = lax.dynamic_slice_in_dim(pooled_q, shard_index * span_rows, span_rows, 0)
            ext_part = lax.dynamic_slice_in_dim(padded, shard_index * span_rows, span_rows + 2 * BLOCK, 0)
            return level_forward(query_part, ext_part, shard_index * (span_rows // BLOCK), block_total, with_own)
        level_out = lax.map(one_shard, shard_ids).reshape(TOKENS // factor, D)
        attended_f = attended_f + jnp.repeat(level_out, factor, axis=0)
    attended = attended_f.astype(jnp.bfloat16)
    group_width = D // N_MP
    out_f = jnp.zeros((TOKENS, D), jnp.float32)
    for group_index in range(N_MP):
        lo_col = group_index * group_width
        term = jnp.dot(attended[:, lo_col:lo_col + group_width], w_out[lo_col:lo_col + group_width, :], preferred_element_type=jnp.float32)
        out_f = out_f + rounded(term)
    attn_out = out_f.astype(jnp.bfloat16)
    d_attended = jnp.dot(grad_out, w_out.T, preferred_element_type=jnp.float32).astype(jnp.bfloat16)
    d_queries_f = jnp.zeros((TOKENS, D), jnp.float32)
    d_kv_f = jnp.zeros((TOKENS, 2 * D), jnp.float32)
    for level_index in range(LEVELS):
        factor = 2 ** level_index
        pooled_q, padded, span_rows, block_total = saved[level_index]
        d_level = pool_sums(d_attended, factor)

        def back_shard(shard_index, pooled_q=pooled_q, padded=padded, span_rows=span_rows, block_total=block_total, with_own=level_index == 0, d_level=d_level):
            query_part = lax.dynamic_slice_in_dim(pooled_q, shard_index * span_rows, span_rows, 0)
            ext_part = lax.dynamic_slice_in_dim(padded, shard_index * span_rows, span_rows + 2 * BLOCK, 0)
            grad_part = lax.dynamic_slice_in_dim(d_level, shard_index * span_rows, span_rows, 0)
            return level_backward(query_part, ext_part, shard_index * (span_rows // BLOCK), block_total, with_own, grad_part)
        d_query_parts, d_ext_parts = lax.map(back_shard, shard_ids)
        middle = d_ext_parts[:, BLOCK:BLOCK + span_rows]
        middle = middle.at[:-1, span_rows - BLOCK:].add(d_ext_parts[1:, :BLOCK])
        middle = middle.at[1:, :BLOCK].add(d_ext_parts[:-1, span_rows + BLOCK:])
        d_queries_f = d_queries_f + jnp.repeat(d_query_parts.reshape(TOKENS // factor, D), factor, axis=0) / factor
        d_kv_f = d_kv_f + jnp.repeat(middle.reshape(TOKENS // factor, 2 * D), factor, axis=0) / factor
    d_queries = d_queries_f.astype(jnp.bfloat16)
    d_kv = d_kv_f.astype(jnp.bfloat16)
    d_keys = d_kv[:, :D]
    d_values = d_kv[:, D:]
    grad_w_query = jnp.dot(normed.T, d_queries, preferred_element_type=jnp.float32)
    grad_w_key = jnp.dot(normed.T, d_keys, preferred_element_type=jnp.float32)
    grad_w_value = jnp.dot(normed.T, d_values, preferred_element_type=jnp.float32)
    grad_w_out = jnp.dot(attended.T, grad_out, preferred_element_type=jnp.float32)
    d_normed = jnp.zeros((TOKENS, D), jnp.float32)
    for group_index in range(N_MP):
        lo_col = group_index * group_width
        hi_col = lo_col + group_width
        term = jnp.dot(d_queries[:, lo_col:hi_col], w_query[:, lo_col:hi_col].T, preferred_element_type=jnp.float32)
        term = term + jnp.dot(d_keys[:, lo_col:hi_col], w_key[:, lo_col:hi_col].T, preferred_element_type=jnp.float32)
        term = term + jnp.dot(d_values[:, lo_col:hi_col], w_value[:, lo_col:hi_col].T, preferred_element_type=jnp.float32)
        d_normed = d_normed + rounded(term)
    row_dot = lax.optimization_barrier(jnp.mean(d_normed * normed_f, axis=1, keepdims=True))
    grad_tokens = inverse * (d_normed - normed_f * row_dot)
    return (attn_out, grad_tokens, grad_w_query, grad_w_key, grad_w_value, grad_w_out)
```

```python
import jax
import jax.numpy as jnp
from jax import lax
from jax.experimental import pallas as pl
from jax.experimental.pallas import tpu as pltpu
from jax.sharding import PartitionSpec as P

HD = 64
BLOCK = 256
LEVELS = 3
PAIR = 2 * HD
MP = 4
LANES = 128
DOT_ROWS = 16

EPSILON = 1e-06
NEGATIVE = -1e30

F32 = jnp.float32
BF16 = jnp.bfloat16

FIRST_EXT = (0, 6, 10)
EXT_BLOCKS = (6, 4, 3)
EXT_TOTAL = 13


def nn(left, right):
    return lax.dot_general(left, right, (((1,), (0,)), ((), ())), preferred_element_type=F32)


def nt(left, right):
    return lax.dot_general(left, right, (((1,), (1,)), ((), ())), preferred_element_type=F32)


def tn(left, right):
    return lax.dot_general(left, right, (((0,), (0,)), ((), ())), preferred_element_type=F32)


def pool_matrix(coarse, factor, value):
    shape = (coarse, coarse * factor)
    row = lax.broadcasted_iota(jnp.int32, shape, 0)
    low = row * factor
    col = lax.broadcasted_iota(jnp.int32, shape, 1)
    return jnp.where((col >= low) & (col < low + factor), value, 0.0).astype(BF16)


def spread_matrix(coarse, factor, value):
    shape = (coarse * factor, coarse)
    low = lax.broadcasted_iota(jnp.int32, shape, 1) * factor
    row = lax.broadcasted_iota(jnp.int32, shape, 0)
    return jnp.where((row >= low) & (row < low + factor), value, 0.0).astype(BF16)


def share_rows(me, step, width):
    return pl.ds(pl.multiple_of(((me + step) & (MP - 1)) * width, width), width)


def params(limit_mib):
    return pltpu.CompilerParams(vmem_limit_bytes=limit_mib * 2**20)


SMALL = pl.CostEstimate(flops=10**6, bytes_accessed=10**4, transcendentals=0)


def in_hbm(*values):
    return [pltpu.with_memory_space_constraint(value, pltpu.HBM) for value in values]


def hbm_shape(shape, dtype):
    return pltpu.HBM(shape, dtype)


def whole(shape):
    return pl.BlockSpec(shape, lambda i: (0,) * len(shape))


def rows_spec(rows, width):
    return pl.BlockSpec((rows, width), lambda i: (i, 0))


SCALAR = pl.BlockSpec(memory_space=pltpu.SMEM)


def low_spec(width):
    return pl.BlockSpec((BLOCK, width), lambda i: (jnp.minimum(i, 1), 0))


def high_spec(width):
    return pl.BlockSpec((BLOCK, width), lambda i: (jnp.maximum(i - 2, 0), 0))


def share_specs(width):
    return [rows_spec(BLOCK, width)] + [low_spec(width), high_spec(width)] * 3


def read_shares(step, refs):
    own, *halves = refs
    shares = [own[...]]
    for low, high in zip(halves[0::2], halves[1::2]):
        shares.append(jnp.where(step < 2, low[...], high[...]))
    return shares


def project_kernel(
    me_ref, t0, t1a, t1b, t2a, t2b, t3a, t3b, wq, wk, wv,
    normed, inverse, q0, kv0, q1, kv1, q2, kv2, to_left, to_right,
):
    step = pl.program_id(0)
    me = me_ref[0]
    width = t0.shape[1]
    read = read_shares(step, (t0, t1a, t1b, t2a, t2b, t3a, t3b))
    shares = [share.astype(F32) for share in read]
    total = jnp.sum(shares[0] * shares[0], axis=1, keepdims=True)
    for share in shares[1:]:
        total = total + jnp.sum(share * share, axis=1, keepdims=True)
    inv = lax.rsqrt(total / (MP * width) + EPSILON)
    inverse[...] = jnp.broadcast_to(inv, inverse.shape)
    sums = [None, None, None]
    for r, share in enumerate(shares):
        part = (share * inv).astype(BF16)
        normed[:, r * width : (r + 1) * width] = part
        rows = share_rows(me, r, width)
        for n, w in enumerate((wq, wk, wv)):
            term = nn(part, w[rows, :])
            sums[n] = term if sums[n] is None else sums[n] + term
    fine = [s.astype(BF16) for s in sums]
    half = pool_matrix(BLOCK // 2, 2, 0.5)
    quarter = pool_matrix(BLOCK // 4, 4, 0.25)
    mid = [nn(half, x).astype(BF16) for x in fine]
    low = [nn(quarter, x).astype(BF16) for x in fine]
    q0[...] = fine[0]
    q1[...] = mid[0]
    q2[...] = low[0]
    half_rows = pl.ds(pl.multiple_of(256 + (step & 1) * 128, 128), 128)
    low_rows = pl.ds(pl.multiple_of(512 + step * 64, 64), 64)
    for n in range(2):
        kv0[n] = fine[1 + n]
        kv1[n] = mid[1 + n]
        kv2[n] = low[1 + n]
        to_left[n, low_rows, :] = low[1 + n]
        to_right[n, low_rows, :] = low[1 + n]

    @pl.when(step == 0)
    def _():
        for n in range(2):
            to_left[n, 0:BLOCK, :] = fine[1 + n]

    @pl.when(step < 2)
    def _():
        for n in range(2):
            to_left[n, half_rows, :] = mid[1 + n]

    @pl.when(step >= 2)
    def _():
        for n in range(2):
            to_right[n, half_rows, :] = mid[1 + n]

    @pl.when(step == 3)
    def _():
        for n in range(2):
            to_right[n, 0:BLOCK, :] = fine[1 + n]


def project(me, shares, wq, wk, wv):
    rows, width = shares[0].shape
    out = jax.ShapeDtypeStruct
    edge = out((2, 3 * BLOCK, width), BF16)
    pair_spec = lambda n: pl.BlockSpec((2, n, width), lambda i: (0, i, 0))
    return pl.pallas_call(
        project_kernel,
        grid=(rows // BLOCK,),
        in_specs=[SCALAR] + share_specs(width) + [whole(wq.shape)] * 3,
        out_specs=[
            rows_spec(BLOCK, MP * width),
            rows_spec(BLOCK, LANES),
            rows_spec(BLOCK, width),
            pair_spec(BLOCK),
            rows_spec(BLOCK // 2, width),
            pair_spec(BLOCK // 2),
            rows_spec(BLOCK // 4, width),
            pair_spec(BLOCK // 4),
            whole(edge.shape),
            whole(edge.shape),
        ],
        out_shape=[
            hbm_shape((rows, MP * width), BF16),
            hbm_shape((rows, LANES), F32),
            hbm_shape((rows, width), BF16),
            hbm_shape((2, rows, width), BF16),
            hbm_shape((rows // 2, width), BF16),
            hbm_shape((2, rows // 2, width), BF16),
            hbm_shape((rows // 4, width), BF16),
            hbm_shape((2, rows // 4, width), BF16),
            edge,
            edge,
        ],
        compiler_params=params(20),
        cost_estimate=SMALL,
        name="project",
    )(me, *in_hbm(shares[0]), *shares[1:], *in_hbm(wq, wk, wv))


def cotangent_kernel(me_ref, g0, g1, g2, g3, w_out, a0, a1, a2):
    me = me_ref[0]
    width = g0.shape[1]
    total = None
    for r, share in enumerate((g0, g1, g2, g3)):
        term = nt(share[...], w_out[:, share_rows(me, r, width)])
        total = term if total is None else total + term
    fine = total.astype(BF16)
    a0[...] = fine
    a1[...] = nn(pool_matrix(BLOCK // 2, 2, 1.0), fine).astype(BF16)
    a2[...] = nn(pool_matrix(BLOCK // 4, 4, 1.0), fine).astype(BF16)


def cotangent(me, shares, w_out):
    rows, width = shares[0].shape
    return pl.pallas_call(
        cotangent_kernel,
        grid=(rows // BLOCK,),
        in_specs=[SCALAR] + [rows_spec(BLOCK, width)] * 4 + [whole(w_out.shape)],
        out_specs=[rows_spec(BLOCK // n, width) for n in (1, 2, 4)],
        out_shape=[hbm_shape((rows // n, width), BF16) for n in (1, 2, 4)],
        compiler_params=params(12),
        cost_estimate=SMALL,
        name="cotangent",
    )(me, *in_hbm(shares[0]), *shares[1:], *in_hbm(w_out))


EDGE_UNITS = ((0, 0), (0, 3), (1, 0), (1, 1), (2, 0))
INNER_UNITS = ((0, 1), (0, 2))


def unit_keys(level, block):
    last = EXT_BLOCKS[level] - 1
    offsets = (0, 1, 2) if level == 0 else (0, 2)
    keys = []
    for offset in offsets:
        at = block + offset
        keys.append((at, 0 if at == 0 else 1 if at == last else None))
    return keys


def block_rows(block):
    return slice(block * BLOCK, (block + 1) * BLOCK)


def ext_rows(own, from_left, from_right, n, level, at):
    if at == 0:
        return from_left[n, block_rows(level), :]
    if at == EXT_BLOCKS[level] - 1:
        return from_right[n, block_rows(level), :]
    return own[level][n, block_rows(at - 1), :]


def head_part(lane, head, rows):
    mine = (lane >= head * HD) & (lane < (head + 1) * HD)
    return jnp.where(mine, rows, 0.0).astype(BF16)


def unit_scores(keys, key_rows, query, bias_ref):
    scores = []
    for (_, bias), rows in zip(keys, key_rows):
        s = nt(rows, query)
        scores.append(s if bias is None else s + bias_ref[bias])
    return scores


def add_spread(target, block, factor, rows):
    if factor == 1:
        target[block_rows(block), :] = target[block_rows(block), :] + rows
        return
    for s in range(factor):
        spread = pl.ds(block * factor * BLOCK + s, BLOCK, factor)
        target[spread, :] = target[spread, :] + rows


def forward_units(units, bias_ref, queries, own, from_left, from_right, stats, vt, out_f):
    lane = lax.broadcasted_iota(jnp.int32, (BLOCK, PAIR), 1)
    turned = set()
    for level, block in units:
        for at, _ in unit_keys(level, block):
            if (level, at) not in turned:
                turned.add((level, at))
                rows = ext_rows(own, from_left, from_right, 1, level, at)
                vt[FIRST_EXT[level] + at] = rows.T
    for u, (level, block) in enumerate(units):
        keys = unit_keys(level, block)
        key_rows = [ext_rows(own, from_left, from_right, 0, level, at) for at, _ in keys]
        q_rows = queries[level][block_rows(block), :] * HD ** (-0.5)
        outs = []
        for head in range(2):
            scores = unit_scores(keys, key_rows, head_part(lane, head, q_rows), bias_ref)
            top = scores[0].max(axis=0, keepdims=True)
            for s in scores[1:]:
                top = jnp.maximum(top, s.max(axis=0, keepdims=True))
            part = slice(head * HD, (head + 1) * HD)
            exps = [jnp.exp(s - top) for s in scores]
            total = exps[0].sum(axis=0, keepdims=True)
            for e in exps[1:]:
                total = total + e.sum(axis=0, keepdims=True)
            scale = 1.0 / total
            row = 4 * u + 2 * head
            stats[0, row : row + 1, :] = top
            stats[0, row + 1 : row + 2, :] = scale
            o_t = None
            for (at, _), e in zip(keys, exps):
                o = nn(vt[FIRST_EXT[level] + at, part, :], (e * scale).astype(BF16))
                o_t = o if o_t is None else o_t + o
            outs.append(o_t)
        add_spread(out_f, block, 2**level, jnp.concatenate(outs, axis=0).T)


def forward_inner_kernel(bias_ref, q0, kv0, out, stats, vt):
    out[...] = jnp.zeros_like(out)
    forward_units(INNER_UNITS, bias_ref, (q0,), (kv0,), None, None, stats, vt, out)


def forward_edge_kernel(
    bias_ref, q0, q1, q2, kv0, kv1, kv2, from_left, from_right, inner, attended, stats, vt, out_f
):
    out_f[...] = inner[...]
    forward_units(
        EDGE_UNITS, bias_ref, (q0, q1, q2), (kv0, kv1, kv2), from_left, from_right, stats, vt, out_f
    )
    stats[0, 20:24, :] = jnp.zeros((4, BLOCK), F32)
    attended[...] = out_f[...].astype(BF16)


def backward_units(
    units, bias_ref, queries, own, from_left, from_right, grads, stats, kt, dq_f, keep_key, keep_value
):
    lane = lax.broadcasted_iota(jnp.int32, (BLOCK, PAIR), 1)
    turned = set()
    for level, block in units:
        for at, _ in unit_keys(level, block):
            if (level, at) not in turned:
                turned.add((level, at))
                rows = ext_rows(own, from_left, from_right, 0, level, at)
                kt[FIRST_EXT[level] + at] = rows.T
    for u, (level, block) in enumerate(units):
        keys = unit_keys(level, block)
        key_rows = [ext_rows(own, from_left, from_right, 0, level, at) for at, _ in keys]
        value_rows = [ext_rows(own, from_left, from_right, 1, level, at) for at, _ in keys]
        q_rows = queries[level][block_rows(block), :] * HD ** (-0.5)
        a_rows = grads[level][block_rows(block), :]
        d_queries = []
        d_keys, d_values = [None] * len(keys), [None] * len(keys)
        for head in range(2):
            qm = head_part(lane, head, q_rows)
            am = head_part(lane, head, a_rows)
            row = 4 * u + 2 * head
            top, scale = stats[0, row : row + 1, :], stats[0, row + 1 : row + 2, :]
            scores = unit_scores(keys, key_rows, qm, bias_ref)
            probs = [jnp.exp(s - top) * scale for s in scores]
            d_weights = [nt(rows, am) for rows in value_rows]
            dots = None
            for p, dw in zip(probs, d_weights):
                d = (p * dw).sum(axis=0, keepdims=True)
                dots = d if dots is None else dots + d
            part = slice(head * HD, (head + 1) * HD)
            dq_t = None
            for n, (at, _) in enumerate(keys):
                gv = nn(probs[n].astype(BF16), am)
                d_scores = (probs[n] * (d_weights[n] - dots)).astype(BF16)
                gk = nn(d_scores, qm)
                g = nn(kt[FIRST_EXT[level] + at, part, :], d_scores)
                dq_t = g if dq_t is None else dq_t + g
                d_keys[n] = gk if head == 0 else d_keys[n] + gk
                d_values[n] = gv if head == 0 else d_values[n] + gv
            d_queries.append(dq_t)
        for n, (at, _) in enumerate(keys):
            keep_key(level, at, d_keys[n])
            keep_value(level, at, d_values[n])
        dq = jnp.concatenate(d_queries, axis=0).T * (HD ** (-0.5) / 2**level)
        add_spread(dq_f, block, 2**level, dq)


def edge_kernel(
    bias_ref, stats, q0, q1, q2, kv0, kv1, kv2, from_left, from_right, a0, a1, a2,
    dq_f, d_kv, to_left, to_right, kt, held, dq_s, sums,
):
    dq_s[...] = jnp.zeros_like(dq_s)
    seen = set()

    def keeper(n):
        def keep(level, at, rows):
            slot = FIRST_EXT[level] + at
            if (n, slot) in seen:
                held[n, slot] = held[n, slot] + rows
            else:
                seen.add((n, slot))
                held[n, slot] = rows

        return keep

    backward_units(
        EDGE_UNITS, bias_ref, (q0, q1, q2), (kv0, kv1, kv2), from_left, from_right,
        (a0, a1, a2), stats, kt, dq_s, keeper(0), keeper(1),
    )
    dq_f[...] = dq_s[...]
    for n in range(2):
        for level in range(LEVELS):
            first, last = FIRST_EXT[level], FIRST_EXT[level] + EXT_BLOCKS[level] - 1
            to_left[n, block_rows(level), :] = held[n, first].astype(BF16)
            to_right[n, block_rows(level), :] = held[n, last].astype(BF16)
        for b in range(4):
            sums[block_rows(b), :] = held[n, 1 + b]
        for b in range(2):
            add_spread(sums, b, 2, held[n, FIRST_EXT[1] + 1 + b] * 0.5)
        d_kv[n] = sums[...]


def inner_units_kernel(
    bias_ref, stats, q0, kv0, a0, dq_in, d_kv_in, d_query, d_kv, kt, dq_s
):
    dq_s[...] = dq_in[...]
    d_kv[...] = d_kv_in[...]

    def keeper(n):
        def keep(level, at, rows):
            d_kv[n, block_rows(at - 1), :] = d_kv[n, block_rows(at - 1), :] + rows

        return keep

    backward_units(
        INNER_UNITS, bias_ref, (q0,), (kv0,), None, None, (a0,), stats, kt, dq_s,
        keeper(0), keeper(1),
    )
    d_query[...] = dq_s[...].astype(BF16)


def lanes(n):
    return pl.BlockSpec((n, PAIR), lambda i: (0, i))


def lanes2(n):
    return pl.BlockSpec((2, n, PAIR), lambda i: (0, 0, i))


EDGE_STATS = pl.BlockSpec((1, 24, BLOCK), lambda i: (i, 0, 0))
INNER_STATS = pl.BlockSpec((1, 8, BLOCK), lambda i: (i, 0, 0))


def forward_inner(bias, q, kv):
    rows, width = q.shape
    out = jax.ShapeDtypeStruct
    return pl.pallas_call(
        forward_inner_kernel,
        grid=(width // PAIR,),
        in_specs=[SCALAR, lanes(rows), lanes2(rows)],
        out_specs=[lanes(rows), INNER_STATS],
        out_shape=[hbm_shape((rows, width), F32), hbm_shape((width // PAIR, 8, BLOCK), F32)],
        scratch_shapes=[pltpu.VMEM((EXT_BLOCKS[0], PAIR, BLOCK), BF16)],
        compiler_params=params(20),
        cost_estimate=SMALL,
        name="forward_inner",
    )(bias, *in_hbm(q, kv))


def forward_edge(bias, q, kv, from_left, from_right, inner):
    rows, width = q[0].shape
    out = jax.ShapeDtypeStruct
    return pl.pallas_call(
        forward_edge_kernel,
        grid=(width // PAIR,),
        in_specs=[SCALAR]
        + [lanes(rows // n) for n in (1, 2, 4)]
        + [lanes2(rows // n) for n in (1, 2, 4)]
        + [lanes2(3 * BLOCK)] * 2
        + [lanes(rows)],
        out_specs=[lanes(rows), EDGE_STATS],
        out_shape=[hbm_shape((rows, width), BF16), hbm_shape((width // PAIR, 24, BLOCK), F32)],
        scratch_shapes=[
            pltpu.VMEM((EXT_TOTAL, PAIR, BLOCK), BF16),
            pltpu.VMEM((rows, PAIR), F32),
        ],
        compiler_params=params(24),
        cost_estimate=SMALL,
        name="forward_edge",
    )(bias, *in_hbm(*q, *kv), from_left, from_right, inner)


def edge_backward(bias, stats, q, kv, from_left, from_right, d_level):
    rows, width = q[0].shape
    out = jax.ShapeDtypeStruct
    edge = out((2, 3 * BLOCK, width), BF16)
    return pl.pallas_call(
        edge_kernel,
        grid=(width // PAIR,),
        in_specs=[SCALAR, EDGE_STATS]
        + [lanes(rows // n) for n in (1, 2, 4)]
        + [lanes2(rows // n) for n in (1, 2, 4)]
        + [lanes2(3 * BLOCK)] * 2
        + [lanes(rows // n) for n in (1, 2, 4)],
        out_specs=[lanes(rows), lanes2(rows), lanes2(3 * BLOCK), lanes2(3 * BLOCK)],
        out_shape=[hbm_shape((rows, width), F32), hbm_shape((2, rows, width), F32), edge, edge],
        scratch_shapes=[
            pltpu.VMEM((EXT_TOTAL, PAIR, BLOCK), BF16),
            pltpu.VMEM((2, EXT_TOTAL, BLOCK, PAIR), F32),
            pltpu.VMEM((rows, PAIR), F32),
            pltpu.VMEM((rows, PAIR), F32),
        ],
        compiler_params=params(32),
        cost_estimate=SMALL,
        name="edge_backward",
    )(bias, *in_hbm(stats, *q, *kv), from_left, from_right, *d_level)


def inner_backward(bias, stats, q, kv, d_level, dq_f, d_kv):
    rows, width = q.shape
    out = jax.ShapeDtypeStruct
    return pl.pallas_call(
        inner_units_kernel,
        grid=(width // PAIR,),
        in_specs=[SCALAR, INNER_STATS, lanes(rows), lanes2(rows), lanes(rows), lanes(rows), lanes2(rows)],
        out_specs=[lanes(rows), lanes2(rows)],
        out_shape=[hbm_shape((rows, width), BF16), hbm_shape((2, rows, width), F32)],
        scratch_shapes=[
            pltpu.VMEM((EXT_BLOCKS[0], PAIR, BLOCK), BF16),
            pltpu.VMEM((rows, PAIR), F32),
        ],
        compiler_params=params(24),
        cost_estimate=SMALL,
        name="inner_backward",
    )(bias, *in_hbm(stats, q, kv), d_level, dq_f, d_kv)


def store_terms(step, terms, own, keep_right, keep_left, right, left):
    own[...] = terms[0]
    low = pl.ds(pl.multiple_of((step & 1) * BLOCK, BLOCK), BLOCK)
    high = pl.ds(pl.multiple_of(2 * BLOCK + (step & 1) * BLOCK, BLOCK), BLOCK)

    @pl.when(step < 2)
    def _():
        keep_right[low, :] = terms[1]
        right[high, :] = terms[2]
        left[low, :] = terms[3]

    @pl.when(step >= 2)
    def _():
        right[low, :] = terms[1]
        left[high, :] = terms[2]
        keep_left[low, :] = terms[3]


def term_outputs(rows, width, extra=0):
    out = jax.ShapeDtypeStruct
    shapes = [rows, rows // 2, rows // 2, rows + extra, rows + extra]
    return (
        [rows_spec(BLOCK, width)] + [whole((n, width)) for n in shapes[1:]],
        [hbm_shape((rows, width), BF16)] + [out((n, width), BF16) for n in shapes[1:]],
    )


def send_out_kernel(me_ref, attended, w_out, *outs):
    me = me_ref[0]
    width = attended.shape[1]
    rows = attended[...]
    terms = [nn(rows, w_out[:, share_rows(me, r, width)]).astype(BF16) for r in range(MP)]
    store_terms(pl.program_id(0), terms, *outs)


def out_terms(me, attended, w_out):
    rows, width = attended.shape
    specs, shapes = term_outputs(rows, width)
    return pl.pallas_call(
        send_out_kernel,
        grid=(rows // BLOCK,),
        in_specs=[SCALAR, rows_spec(BLOCK, width), whole(w_out.shape)],
        out_specs=specs,
        out_shape=shapes,
        compiler_params=params(12),
        cost_estimate=SMALL,
        name="out_terms",
    )(me, *in_hbm(attended, w_out))


def input_terms_kernel(
    me_ref, d_query, d_kv, from_left, from_right, t0, t1a, t1b, t2a, t2b, t3a, t3b, inverse,
    wq, wk, wv, d_proj, dots, own, keep_right, keep_left, right, left, dot_rows,
):
    step = pl.program_id(0)
    me = me_ref[0]
    width = d_query.shape[1]
    grads = [d_query[...]]
    half = spread_matrix(BLOCK // 2, 2, 0.5)
    quarter = spread_matrix(BLOCK // 4, 4, 0.25)
    half_rows = pl.ds(pl.multiple_of(256 + (step & 1) * 128, 128), 128)
    low_rows = pl.ds(pl.multiple_of(512 + step * 64, 64), 64)
    for n in range(2):
        total = d_kv[n]
        total = total + jnp.where(step == 0, from_left[n, 0:BLOCK, :].astype(F32), 0.0)
        total = total + jnp.where(step == 3, from_right[n, 0:BLOCK, :].astype(F32), 0.0)
        mid = jnp.where(step < 2, from_left[n, half_rows, :], from_right[n, half_rows, :])
        total = total + nn(half, mid)
        total = total + nn(quarter, from_left[n, low_rows, :])
        total = total + nn(quarter, from_right[n, low_rows, :])
        grads.append(total.astype(BF16))
    for n, grad in enumerate(grads):
        d_proj[:, n * width : (n + 1) * width] = grad
    shares = read_shares(step, (t0, t1a, t1b, t2a, t2b, t3a, t3b))
    terms, dot = [], None
    for r in range(MP):
        rows = share_rows(me, r, width)
        term = nt(grads[0], wq[rows, :]) + nt(grads[1], wk[rows, :]) + nt(grads[2], wv[rows, :])
        term = term.astype(BF16)
        terms.append(term)
        part = jnp.sum(term.astype(F32) * shares[r].astype(F32), axis=1, keepdims=True)
        dot = part if dot is None else dot + part
    dot = jnp.broadcast_to(dot * inverse[:, 0:1], (BLOCK, LANES)).T[0:1, :]
    high = dot.astype(BF16).astype(F32)
    middle = (dot - high).astype(BF16).astype(F32)
    for n, piece in enumerate((high, middle, dot - high - middle)):
        dot_rows[pl.ds(4 * n + step, 1), :] = piece
    store_terms(step, terms, own, keep_right, keep_left, right, left)

    @pl.when(step == 3)
    def _():
        dot_rows[12:16, :] = jnp.zeros((4, BLOCK), F32)
        pieces = dot_rows[...].astype(BF16)
        dots[...] = pieces
        right[4 * BLOCK :, :] = pieces
        left[4 * BLOCK :, :] = pieces


def input_terms(me, d_query, d_kv, from_left, from_right, shares, inverse, wq, wk, wv):
    rows, width = d_query.shape
    specs, shapes = term_outputs(rows, width, DOT_ROWS)
    out = jax.ShapeDtypeStruct
    return pl.pallas_call(
        input_terms_kernel,
        grid=(rows // BLOCK,),
        in_specs=[
            SCALAR,
            rows_spec(BLOCK, width),
            pl.BlockSpec((2, BLOCK, width), lambda i: (0, i, 0)),
            whole(from_left.shape),
            whole(from_right.shape),
        ]
        + share_specs(width)
        + [rows_spec(BLOCK, LANES)]
        + [whole(wq.shape)] * 3,
        out_specs=[rows_spec(BLOCK, 3 * width), whole((DOT_ROWS, width))] + specs,
        out_shape=[hbm_shape((rows, 3 * width), BF16), hbm_shape((DOT_ROWS, width), BF16)] + shapes,
        scratch_shapes=[pltpu.VMEM((DOT_ROWS, width), F32)],
        compiler_params=params(24),
        cost_estimate=SMALL,
        name="input_terms",
    )(
        me, d_query, d_kv, from_left, from_right, *in_hbm(shares[0]), *shares[1:],
        *in_hbm(inverse, wq, wk, wv)
    )


def relay_kernel(keep_right, keep_left, l1, r1, onward_right, onward_left):
    half = keep_right.shape[0]
    passed = l1[half : 2 * half, :].astype(F32)
    onward_right[0:half, :] = (keep_right[...].astype(F32) + passed).astype(BF16)
    passed = r1[half : 2 * half, :].astype(F32)
    onward_left[...] = (keep_left[...].astype(F32) + passed).astype(BF16)
    if onward_right.shape[0] > half:
        onward_right[half:, :] = l1[2 * half :, :]


def relay(keep_right, keep_left, l1, r1):
    half, width = keep_right.shape
    extra = l1.shape[0] - 2 * half
    out = jax.ShapeDtypeStruct
    return pl.pallas_call(
        relay_kernel,
        out_shape=[out((half + extra, width), BF16), out((half, width), BF16)],
        compiler_params=params(8),
        cost_estimate=SMALL,
        name="relay",
    )(keep_right, keep_left, l1, r1)


def summed(own, l1, r1, l2, r2):
    half = r2.shape[0]
    low = r1[0:half, :].astype(F32) + l2[0:half, :].astype(F32)
    high = l1[0:half, :].astype(F32) + r2[...].astype(F32)
    return own[0:half, :].astype(F32) + low, own[half:, :].astype(F32) + high


def finish_out_kernel(own, l1, r1, l2, r2, result):
    half = r2.shape[0]
    low, high = summed(own, l1, r1, l2, r2)
    result[0:half, :] = low.astype(BF16)
    result[half:, :] = high.astype(BF16)


def finish_out(own, l1, r1, l2, r2):
    rows, width = own.shape
    return pl.pallas_call(
        finish_out_kernel,
        out_shape=jax.ShapeDtypeStruct((rows, width), BF16),
        compiler_params=params(10),
        cost_estimate=SMALL,
        name="finish_out",
    )(*in_hbm(own, l1, r1, l2, r2))


def finish_grad_kernel(own, l1, r1, l2, r2, tokens, inverse, dots, result):
    rows, width = own.shape
    half = r2.shape[0]
    pieces = dots[...].astype(F32)
    for message, first in ((l1, rows), (r1, rows), (l2, half)):
        pieces = pieces + message[first : first + DOT_ROWS, :].astype(F32)
    means = (pieces[0:4] + pieces[4:8] + pieces[8:12]) / (MP * width)
    halves = summed(own, l1, r1, l2, r2)
    for b in range(rows // BLOCK):
        mean = jnp.broadcast_to(means[b : b + 1, :], (LANES, BLOCK)).T[:, 0:1]
        at = block_rows(b)
        inv = inverse[at, 0:1]
        total = halves[b // 2][block_rows(b % 2), :]
        result[at, :] = inv * (total - tokens[at, :].astype(F32) * inv * mean)


def finish_grad(own, l1, r1, l2, r2, tokens, inverse, dots):
    rows, width = own.shape
    return pl.pallas_call(
        finish_grad_kernel,
        out_shape=jax.ShapeDtypeStruct((rows, width), F32),
        compiler_params=params(16),
        cost_estimate=SMALL,
        name="finish_grad",
    )(*in_hbm(own), l1, r1, l2, r2, *in_hbm(tokens, inverse, dots))


def outer_kernel(g0, g1, g2, g3, attended, result):
    width = g0.shape[1]
    rows = attended[...]
    for r, share in enumerate((g0, g1, g2, g3)):
        result[r * width : (r + 1) * width, :] = tn(share[...], rows).astype(BF16)


def outer_terms(shares, attended):
    rows, width = attended.shape
    return pl.pallas_call(
        outer_kernel,
        out_shape=hbm_shape((MP * width, width), BF16),
        compiler_params=params(12),
        cost_estimate=SMALL,
        name="outer_terms",
    )(*in_hbm(shares[0]), *shares[1:], attended)


def inner_kernel(place, normed, d_proj, outer, mine, other, held):
    core = place[1]
    width = outer.shape[1]
    held[:, 0 : 3 * width] = tn(normed[...], d_proj[...]).astype(BF16)
    held[:, 3 * width :] = outer[...]
    for n in range(width // 64):
        rows = slice(n * 32, (n + 1) * 32)
        mine[rows, :] = held[pl.ds(pl.multiple_of(n * 64 + core * 32, 32), 32), :]
        other[rows, :] = held[pl.ds(pl.multiple_of(n * 64 + 32 - core * 32, 32), 32), :]


def inner_terms(place, normed, d_proj, outer):
    rows, total = normed.shape
    width = outer.shape[1]
    half = jax.ShapeDtypeStruct((total // 2, 4 * width), BF16)
    return pl.pallas_call(
        inner_kernel,
        grid=(total // width,),
        in_specs=[
            SCALAR,
            pl.BlockSpec((rows, width), lambda i: (0, i)),
            whole(d_proj.shape),
            rows_spec(width, width),
        ],
        out_specs=[rows_spec(width // 2, 4 * width)] * 2,
        out_shape=[half, half],
        scratch_shapes=[pltpu.VMEM((width, 4 * width), BF16)],
        compiler_params=params(16),
        cost_estimate=SMALL,
        name="inner_terms",
    )(place, *in_hbm(normed), d_proj, *in_hbm(outer))


def pair_sum_kernel(place, mine, got, *outs):
    x = place[2]
    for d, out in enumerate(outs):
        for y in range(4):
            rows = pl.ds(pl.multiple_of((4 * y + ((x + d) & 3)) * 32, 32), 32)
            total = mine[rows, :].astype(F32) + got[rows, :].astype(F32)
            out[32 * y : 32 * (y + 1), :] = total.astype(BF16)


def row_sum_kernel(place, a, b, c, d, *refs):
    *outs, total = refs
    first = place[3] - place[0] + 4
    total[...] = (
        a[...].astype(F32) + b[...].astype(F32) + c[...].astype(F32) + d[...].astype(F32)
    ).astype(BF16)
    for n, out in enumerate(outs):
        out[...] = total[pl.ds(pl.multiple_of(((first + n) & 3) * 32, 32), 32), :]


def last_sum_kernel(a, b, c, d, gq, gk, gv, go):
    width = gq.shape[1]
    total = a[...].astype(F32) + b[...].astype(F32) + c[...].astype(F32) + d[...].astype(F32)
    gq[...] = total[:, 0:width]
    gk[...] = total[:, width : 2 * width]
    gv[...] = total[:, 2 * width : 3 * width]
    go[...] = total[:, 3 * width :]


def sum_over_seq(place, mine, other):
    cols = mine.shape[1]
    out = jax.ShapeDtypeStruct
    vmem = pl.BlockSpec(memory_space=pltpu.VMEM)

    def sent(value, dy, dx, dc):
        pairs = []
        for i in range(32):
            c, a, b = i % 2, (i // 2) % 4, i // 8
            pairs.append((i, (((b + dy) % 4) * 4 + (a + dx) % 4) * 2 + (c + dc) % 2))
        return lax.ppermute(value, "seq", pairs)

    parts = pl.pallas_call(
        pair_sum_kernel,
        in_specs=[SCALAR, vmem, vmem],
        out_shape=[out((128, cols), BF16)] * 4,
        compiler_params=params(8),
        cost_estimate=SMALL,
        name="pair_sum",
    )(place, mine, sent(other, 0, 0, 1))
    parts = [parts[0]] + [sent(parts[d], 0, d, 0) for d in (1, 3, 2)]
    rows = pl.pallas_call(
        row_sum_kernel,
        in_specs=[SCALAR] + [vmem] * 4,
        out_shape=[out((32, cols), BF16)] * 4,
        scratch_shapes=[pltpu.VMEM((128, cols), BF16)],
        compiler_params=params(8),
        cost_estimate=SMALL,
        name="row_sum",
    )(place, *parts)
    rows = [rows[0]] + [sent(rows[d], d, 0, 0) for d in (1, 3, 2)]
    width = cols // 4
    return pl.pallas_call(
        last_sum_kernel,
        out_shape=[out((32, width), F32)] * 4,
        compiler_params=params(8),
        cost_estimate=SMALL,
        name="last_sum",
    )(*rows)


def to_next(value):
    return lax.ppermute(value, "mp", [(i, (i + 1) % MP) for i in range(MP)])


def to_previous(value):
    return lax.ppermute(value, "mp", [((i + 1) % MP, i) for i in range(MP)])


def gather_shares(share):
    half = share.shape[0] // 2
    low, high = share[:half], share[half:]
    after_low, before_high = to_previous(low), to_next(high)
    after_high, before_low = to_previous(high), to_next(low)
    far_low, far_high = to_previous(after_low), to_next(before_high)
    return [share, after_low, after_high, far_low, far_high, before_low, before_high]


def gather_direct(share):
    far = lax.ppermute(share, "mp", [(i, (i + 2) % MP) for i in range(MP)])
    return [share, to_previous(share), far, to_next(share)]


def exchange(to_left, to_right):
    count = lax.axis_size("seq")
    ends = count - 1
    from_left = lax.ppermute(to_right, "seq", [(i, i + 1) for i in range(ends)])
    from_right = lax.ppermute(to_left, "seq", [(i + 1, i) for i in range(ends)])
    return from_left, from_right


def tied(values, *others):
    flat, tree = jax.tree.flatten(values)
    flat = lax.optimization_barrier((*flat, *others))[: len(flat)]
    return jax.tree.unflatten(tree, flat)


def per_device(tokens, w_query, w_key, w_value, w_out, grad_out):
    count = lax.axis_size("seq")
    index = lax.axis_index("seq")
    me = jnp.stack([lax.axis_index("mp"), index & 1, (index >> 1) & 3, index >> 3])
    me = me.astype(jnp.int32)
    bias = jnp.stack(
        [
            jnp.where(index == 0, NEGATIVE, 0.0).astype(F32),
            jnp.where(index == count - 1, NEGATIVE, 0.0).astype(F32),
        ]
    )
    token_shares = gather_shares(tokens)
    *token_shares, grad_out = lax.optimization_barrier((*token_shares, grad_out))
    grad_shares = gather_direct(grad_out)
    normed, inverse, q0, kv0, q1, kv1, q2, kv2, to_left, to_right = project(
        me, token_shares, w_query, w_key, w_value
    )
    from_left, from_right = exchange(to_left, to_right)
    q, kv = (q0, q1, q2), (kv0, kv1, kv2)
    inner_out, inner_stats = forward_inner(bias, q0, kv0)
    attended, stats = forward_edge(bias, q, kv, from_left, from_right, inner_out)
    grad_shares = tied(grad_shares, attended)
    out_own, keep_right, keep_left, right, left = out_terms(me, attended, w_out)
    l1, r1 = to_next(right), to_previous(left)
    d_level = cotangent(me, grad_shares, w_out)
    dq_f, d_kv, to_left, to_right = edge_backward(
        bias, stats, q, kv, from_left, from_right, d_level
    )
    onward_right, onward_left = relay(keep_right, keep_left, l1, r1)
    l2, r2 = to_next(onward_right), to_previous(onward_left)
    from_left, from_right = exchange(to_left, to_right)
    dq_f = tied(dq_f, onward_right, onward_left)
    d_query, d_kv = inner_backward(bias, inner_stats, q0, kv0, d_level[0], dq_f, d_kv)
    d_query = tied(d_query, l2, r2)
    d_proj, dots, own, keep_right, keep_left, right, left = input_terms(
        me, d_query, d_kv, from_left, from_right, token_shares, inverse, w_query, w_key, w_value
    )
    attn_out = finish_out(out_own, l1, r1, l2, r2)
    l1, r1 = to_next(right), to_previous(left)
    outer = outer_terms(grad_shares, attended)
    mine, other = inner_terms(me, normed, d_proj, outer)
    onward_right, onward_left = relay(keep_right, keep_left, l1, r1)
    l2, r2 = to_next(onward_right), to_previous(onward_left)
    grad_tokens = finish_grad(own, l1, r1, l2, r2, tokens, inverse, dots)
    *weight_grads, grad_w_out = sum_over_seq(me, mine, other)
    return (attn_out, grad_tokens, *weight_grads, grad_w_out.T)


def solution(mesh):
    return jax.shard_map(
        per_device,
        mesh=mesh,
        in_specs=(
            P("seq", "mp"),
            P(None, "mp"),
            P(None, "mp"),
            P(None, "mp"),
            P("mp", None),
            P("seq", "mp"),
        ),
        out_specs=(
            P("seq", "mp"),
            P("seq", "mp"),
            P("seq", "mp"),
            P("seq", "mp"),
            P("seq", "mp"),
            P("mp", "seq"),
        ),
        check_vma=False,
    )
```

```python
import jax
import jax.numpy as jnp
from jax import lax
from jax.experimental import pallas as pl
from jax.experimental.pallas import tpu as pltpu
from jax.sharding import PartitionSpec as P

HD = 64
BLOCK = 256
LEVELS = 3
PAIR = 2 * HD
MP = 4
LANES = 128
DOT_ROWS = 16

EPSILON = 1e-06
NEGATIVE = -1e30

F32 = jnp.float32
BF16 = jnp.bfloat16

FIRST_EXT = (0, 6, 10)
EXT_BLOCKS = (6, 4, 3)
EXT_TOTAL = 13


def nn(left, right):
    return lax.dot_general(left, right, (((1,), (0,)), ((), ())), preferred_element_type=F32)


def nt(left, right):
    return lax.dot_general(left, right, (((1,), (1,)), ((), ())), preferred_element_type=F32)


def tn(left, right):
    return lax.dot_general(left, right, (((0,), (0,)), ((), ())), preferred_element_type=F32)


def pool_matrix(coarse, factor, value):
    shape = (coarse, coarse * factor)
    row = lax.broadcasted_iota(jnp.int32, shape, 0)
    low = row * factor
    col = lax.broadcasted_iota(jnp.int32, shape, 1)
    return jnp.where((col >= low) & (col < low + factor), value, 0.0).astype(BF16)


def spread_matrix(coarse, factor, value):
    shape = (coarse * factor, coarse)
    low = lax.broadcasted_iota(jnp.int32, shape, 1) * factor
    row = lax.broadcasted_iota(jnp.int32, shape, 0)
    return jnp.where((row >= low) & (row < low + factor), value, 0.0).astype(BF16)


def share_rows(me, step, width):
    return pl.ds(pl.multiple_of(((me + step) & (MP - 1)) * width, width), width)


SMALL = pl.CostEstimate(flops=10**6, bytes_accessed=10**4, transcendentals=0)
SCALAR = pl.BlockSpec(memory_space=pltpu.SMEM)
RESIDENT = pl.BlockSpec(memory_space=pltpu.VMEM)


def held(shape, dtype):
    return jax.ShapeDtypeStruct(shape, dtype)


def run(kernel, name, limit_mib, scalars, inputs, outputs, scratch=()):
    return pl.pallas_call(
        kernel,
        in_specs=[SCALAR] * len(scalars) + [RESIDENT] * len(inputs),
        out_specs=[RESIDENT] * len(outputs),
        out_shape=outputs,
        scratch_shapes=list(scratch),
        compiler_params=pltpu.CompilerParams(vmem_limit_bytes=limit_mib * 2**20),
        cost_estimate=SMALL,
        name=name,
    )(*scalars, *inputs)


def block_rows(block):
    return slice(block * BLOCK, (block + 1) * BLOCK)


def read_shares(step, refs):
    own, *halves = refs
    at = block_rows(step % 2)
    return [own[block_rows(step), :]] + [ref[at, :] for ref in halves[step // 2 :: 2]]


def level_rows(level, rows=4 * BLOCK):
    first = sum(rows // 2**n for n in range(level))
    return slice(first, first + rows // 2**level)


ALL_ROWS = 7 * BLOCK
LEVEL_BLOCK = (0, 4, 6)


def as_row(column):
    return jnp.broadcast_to(column, (column.shape[0], LANES)).T[0:1, :]


def as_column(row):
    return jnp.broadcast_to(row, (LANES, row.shape[1])).T[:, 0:1]


def project_kernel(
    place, t1a, t1b, t2a, t2b, t3a, t3b, t0_hbm, wq_hbm, wk_hbm, wv_hbm,
    inverse, q, kv, to_left, to_right, normed_hbm,
    t0, wq, wk, wv, normed, in_sems, out_sems,
):
    me = place[0]
    width = t0.shape[1]
    sources = (t0_hbm, wq_hbm, wk_hbm, wv_hbm)
    loads = [
        pltpu.make_async_copy(source, target, in_sems.at[n])
        for n, (source, target) in enumerate(zip(sources, (t0, wq, wk, wv)))
    ]
    for load in loads:
        load.start()
    half = pool_matrix(BLOCK // 2, 2, 0.5)
    quarter = pool_matrix(BLOCK // 4, 4, 0.25)
    inverse[4:8, :] = jnp.zeros((4, BLOCK), F32)
    stores = []
    for step in range(4):
        rows = block_rows(step)
        if step == 0:
            loads[0].wait()
        read = read_shares(step, (t0, t1a, t1b, t2a, t2b, t3a, t3b))
        shares = [share.astype(F32) for share in read]
        squares = shares[0] * shares[0]
        for share in shares[1:]:
            squares = squares + share * share
        total = jnp.sum(squares, axis=1, keepdims=True)
        inv = lax.rsqrt(total / (MP * width) + EPSILON)
        inverse[step : step + 1, :] = as_row(inv)
        parts = [(share * inv).astype(BF16) for share in shares]
        for r, part in enumerate(parts):
            normed[rows, r * width : (r + 1) * width] = part
        store = pltpu.make_async_copy(normed.at[rows], normed_hbm.at[rows], out_sems.at[step])
        store.start()
        stores.append(store)
        if step == 0:
            for load in loads[1:]:
                load.wait()
        sums = [None, None, None]
        for r, part in enumerate(parts):
            w_rows = share_rows(me, r, width)
            for n, w in enumerate((wq, wk, wv)):
                term = nn(part, w[w_rows, :])
                sums[n] = term if sums[n] is None else sums[n] + term
        fine = [x.astype(BF16) for x in sums]
        mid = [nn(half, x).astype(BF16) for x in fine]
        low = [nn(quarter, x).astype(BF16) for x in fine]
        mid_rows = slice(1024 + step * 128, 1024 + (step + 1) * 128)
        low_rows = slice(1536 + step * 64, 1536 + (step + 1) * 64)
        q[rows, :] = fine[0]
        q[mid_rows, :] = mid[0]
        q[low_rows, :] = low[0]
        edge_mid = slice(256 + (step % 2) * 128, 384 + (step % 2) * 128)
        edge_low = slice(512 + step * 64, 576 + step * 64)
        for n in range(2):
            kv[n, rows, :] = fine[1 + n]
            kv[n, mid_rows, :] = mid[1 + n]
            kv[n, low_rows, :] = low[1 + n]
            to_left[n, edge_low, :] = low[1 + n]
            to_right[n, edge_low, :] = low[1 + n]
            edge = to_left if step < 2 else to_right
            edge[n, edge_mid, :] = mid[1 + n]
            if step in (0, 3):
                edge[n, 0:BLOCK, :] = fine[1 + n]
    for store in stores:
        store.wait()


def project(place, shares, wq, wk, wv):
    rows, width = shares[0].shape
    out = jax.ShapeDtypeStruct
    edge = out((2, 3 * BLOCK, width), BF16)
    anywhere = pl.BlockSpec(memory_space=pl.ANY)
    share = pltpu.VMEM((rows, width), BF16)
    fixed = [
        pltpu.with_memory_space_constraint(value, pltpu.HBM)
        for value in (shares[0], wq, wk, wv)
    ]
    return pl.pallas_call(
        project_kernel,
        in_specs=[SCALAR] + [RESIDENT] * 6 + [anywhere] * 4,
        out_specs=[RESIDENT] * 5 + [anywhere],
        out_shape=[
            out((8, width), F32),
            out((ALL_ROWS, width), BF16),
            out((2, ALL_ROWS, width), BF16),
            edge,
            edge,
            pltpu.HBM((rows, MP * width), BF16),
        ],
        scratch_shapes=[share] * 4
        + [
            pltpu.VMEM((rows, MP * width), BF16),
            pltpu.SemaphoreType.DMA((4,)),
            pltpu.SemaphoreType.DMA((4,)),
        ],
        compiler_params=pltpu.CompilerParams(vmem_limit_bytes=20 * 2**20),
        cost_estimate=SMALL,
        name="project",
    )(place, *shares[1:], *fixed)


def cotangent_kernel(place, g0, g1, g2, g3, w_out, d_att):
    me = place[0]
    width = g0.shape[1]
    half = pool_matrix(BLOCK // 2, 2, 1.0)
    quarter = pool_matrix(BLOCK // 4, 4, 1.0)
    for step in range(4):
        rows = block_rows(step)
        total = None
        for r, share in enumerate((g0, g1, g2, g3)):
            term = nt(share[rows, :], w_out[:, share_rows(me, r, width)])
            total = term if total is None else total + term
        fine = total.astype(BF16)
        d_att[rows, :] = fine
        d_att[1024 + step * 128 : 1024 + (step + 1) * 128, :] = nn(half, fine).astype(BF16)
        d_att[1536 + step * 64 : 1536 + (step + 1) * 64, :] = nn(quarter, fine).astype(BF16)


def cotangent(place, shares, w_out):
    rows, width = shares[0].shape
    outputs = [held((ALL_ROWS, width), BF16)]
    return run(cotangent_kernel, "cotangent", 8, [place], [*shares, w_out], outputs)[0]


EDGE_UNITS = ((0, 0), (0, 3), (1, 0), (1, 1), (2, 0))
INNER_UNITS = ((0, 1), (0, 2))


def unit_keys(level, block):
    last = EXT_BLOCKS[level] - 1
    offsets = (0, 1, 2) if level == 0 else (0, 2)
    keys = []
    for offset in offsets:
        at = block + offset
        keys.append((at, 0 if at == 0 else 1 if at == last else None))
    return keys


def ext_rows(kv, from_left, from_right, n, level, at, lanes):
    if at == 0:
        return from_left[n, block_rows(level), lanes]
    if at == EXT_BLOCKS[level] - 1:
        return from_right[n, block_rows(level), lanes]
    return kv[n, block_rows(LEVEL_BLOCK[level] + at - 1), lanes]


def head_part(lane, head, rows):
    mine = (lane >= head * HD) & (lane < (head + 1) * HD)
    return jnp.where(mine, rows, 0.0).astype(BF16)


def unit_scores(keys, key_rows, query, bias_ref):
    scores = []
    for (_, bias), rows in zip(keys, key_rows):
        s = nt(rows, query)
        scores.append(s if bias is None else s + bias_ref[bias])
    return scores


def add_spread(target, block, factor, rows):
    if factor == 1:
        target[block_rows(block), :] = target[block_rows(block), :] + rows
        return
    for s in range(factor):
        spread = pl.ds(block * factor * BLOCK + s, BLOCK, factor)
        target[spread, :] = target[spread, :] + rows


def each_pair(width, body):
    def step(pair, _):
        body(pair, pl.ds(pl.multiple_of(pair * PAIR, PAIR), PAIR))
        return 0

    lax.fori_loop(0, width // PAIR, step, 0)


def head_part(lane, head, rows):
    mine = (lane >= head * HD) & (lane < (head + 1) * HD)
    return jnp.where(mine, rows, 0.0).astype(BF16)


def unit_scores(keys, key_rows, query, bias_ref):
    scores = []
    for (_, bias), rows in zip(keys, key_rows):
        s = nt(rows, query)
        scores.append(s if bias is None else s + bias_ref[bias])
    return scores


def add_spread(target, block, factor, rows):
    if factor == 1:
        target[block_rows(block), :] = target[block_rows(block), :] + rows
        return
    for s in range(factor):
        spread = pl.ds(block * factor * BLOCK + s, BLOCK, factor)
        target[spread, :] = target[spread, :] + rows


def forward_units(pair, lanes, units, bias_ref, q, kv, from_left, from_right, stats, vt, out_f):
    lane = lax.broadcasted_iota(jnp.int32, (BLOCK, PAIR), 1)
    done = set()
    for level, block in units:
        for at, _ in unit_keys(level, block):
            if (level, at) not in done:
                done.add((level, at))
                rows = ext_rows(kv, from_left, from_right, 1, level, at, lanes)
                vt[FIRST_EXT[level] + at] = rows.T

    def begin(u, head):
        level, block = units[u]
        keys = unit_keys(level, block)
        key_rows = [ext_rows(kv, from_left, from_right, 0, level, at, lanes) for at, _ in keys]
        q_rows = q[block_rows(LEVEL_BLOCK[level] + block), lanes] * HD ** (-0.5)
        return unit_scores(keys, key_rows, head_part(lane, head, q_rows), bias_ref)

    def finish(u, head, scores):
        level, block = units[u]
        top = scores[0].max(axis=0, keepdims=True)
        for s in scores[1:]:
            top = jnp.maximum(top, s.max(axis=0, keepdims=True))
        exps = [jnp.exp(s - top) for s in scores]
        total = exps[0].sum(axis=0, keepdims=True)
        for e in exps[1:]:
            total = total + e.sum(axis=0, keepdims=True)
        scale = 1.0 / total
        row = 4 * u + 2 * head
        stats[pair, row : row + 1, :] = top
        stats[pair, row + 1 : row + 2, :] = scale
        part = slice(head * HD, (head + 1) * HD)
        o_t = None
        for (at, _), e in zip(unit_keys(level, block), exps):
            o = nn(vt[FIRST_EXT[level] + at, part, :], (e * scale).astype(BF16))
            o_t = o if o_t is None else o_t + o
        return o_t

    items = [(u, head) for u in range(len(units)) for head in range(2)]
    scores, outs = begin(*items[0]), []
    for n, (u, head) in enumerate(items):
        following = begin(*items[n + 1]) if n + 1 < len(items) else None
        outs.append(finish(u, head, scores))
        scores = following
        if head == 1:
            level, block = units[u]
            add_spread(out_f, block, 2**level, jnp.concatenate(outs, axis=0).T)
            outs = []


def forward_inner_kernel(bias_ref, q, kv, out, stats, vt, out_f):
    def one(pair, lanes):
        out_f[...] = jnp.zeros_like(out_f)
        forward_units(pair, lanes, INNER_UNITS, bias_ref, q, kv, None, None, stats, vt, out_f)
        out[:, lanes] = out_f[BLOCK : 3 * BLOCK, :]

    each_pair(q.shape[1], one)


def forward_edge_kernel(
    bias_ref, q, kv, from_left, from_right, inner, attended, stats, vt, out_f
):
    def one(pair, lanes):
        out_f[0:BLOCK, :] = jnp.zeros((BLOCK, PAIR), F32)
        out_f[BLOCK : 3 * BLOCK, :] = inner[:, lanes]
        out_f[3 * BLOCK :, :] = jnp.zeros((BLOCK, PAIR), F32)
        forward_units(
            pair, lanes, EDGE_UNITS, bias_ref, q, kv, from_left, from_right, stats, vt, out_f
        )
        attended[:, lanes] = out_f[...].astype(BF16)

    each_pair(q.shape[1], one)


def backward_units(
    pair, lanes, units, bias_ref, q, kv, from_left, from_right, grads, stats, kt, dq_f, keep
):
    lane = lax.broadcasted_iota(jnp.int32, (BLOCK, PAIR), 1)
    done = set()
    for level, block in units:
        for at, _ in unit_keys(level, block):
            if (level, at) not in done:
                done.add((level, at))
                rows = ext_rows(kv, from_left, from_right, 0, level, at, lanes)
                kt[FIRST_EXT[level] + at] = rows.T

    def begin(u, head):
        level, block = units[u]
        keys = unit_keys(level, block)
        key_rows = [ext_rows(kv, from_left, from_right, 0, level, at, lanes) for at, _ in keys]
        value_rows = [ext_rows(kv, from_left, from_right, 1, level, at, lanes) for at, _ in keys]
        at = block_rows(LEVEL_BLOCK[level] + block)
        qm = head_part(lane, head, q[at, lanes] * HD ** (-0.5))
        am = head_part(lane, head, grads[at, lanes])
        scores = unit_scores(keys, key_rows, qm, bias_ref)
        return qm, am, scores, [nt(rows, am) for rows in value_rows]

    def finish(u, head, qm, am, scores, d_weights):
        level, block = units[u]
        row = 4 * u + 2 * head
        top, scale = stats[pair, row : row + 1, :], stats[pair, row + 1 : row + 2, :]
        probs = [jnp.exp(s - top) * scale for s in scores]
        dots = None
        for p, dw in zip(probs, d_weights):
            d = (p * dw).sum(axis=0, keepdims=True)
            dots = d if dots is None else dots + d
        part = slice(head * HD, (head + 1) * HD)
        dq_t, d_keys, d_values = None, [], []
        for (at, _), p, dw in zip(unit_keys(level, block), probs, d_weights):
            d_values.append(nn(p.astype(BF16), am))
            d_scores = (p * (dw - dots)).astype(BF16)
            d_keys.append(nn(d_scores, qm))
            g = nn(kt[FIRST_EXT[level] + at, part, :], d_scores)
            dq_t = g if dq_t is None else dq_t + g
        return dq_t, d_keys, d_values

    items = [(u, head) for u in range(len(units)) for head in range(2)]
    ready, first = begin(*items[0]), None
    for n, (u, head) in enumerate(items):
        following = begin(*items[n + 1]) if n + 1 < len(items) else None
        got = finish(u, head, *ready)
        ready = following
        if head == 0:
            first = got
            continue
        level, block = units[u]
        for m, (at, _) in enumerate(unit_keys(level, block)):
            keep(0, level, at, first[1][m] + got[1][m])
            keep(1, level, at, first[2][m] + got[2][m])
        dq = jnp.concatenate([first[0], got[0]], axis=0).T * (HD ** (-0.5) / 2**level)
        add_spread(dq_f, block, 2**level, dq)


def edge_kernel(
    bias_ref, stats, q, kv, from_left, from_right, grads,
    dq_f, d_kv, to_left, to_right, kt, ext, dq_s, sums,
):
    def one(pair, lanes):
        dq_s[...] = jnp.zeros_like(dq_s)
        seen = set()

        def keep(n, level, at, rows):
            slot = FIRST_EXT[level] + at
            if (n, slot) in seen:
                ext[n, slot] = ext[n, slot] + rows
            else:
                seen.add((n, slot))
                ext[n, slot] = rows

        backward_units(
            pair, lanes, EDGE_UNITS, bias_ref, q, kv, from_left, from_right, grads, stats, kt,
            dq_s, keep,
        )
        dq_f[:, lanes] = dq_s[...]
        for n in range(2):
            for level in range(LEVELS):
                first, last = FIRST_EXT[level], FIRST_EXT[level] + EXT_BLOCKS[level] - 1
                to_left[n, block_rows(level), lanes] = ext[n, first].astype(BF16)
                to_right[n, block_rows(level), lanes] = ext[n, last].astype(BF16)
            for b in range(4):
                sums[block_rows(b), :] = ext[n, 1 + b]
            for b in range(2):
                add_spread(sums, b, 2, ext[n, FIRST_EXT[1] + 1 + b] * 0.5)
            d_kv[n, :, lanes] = sums[...]

    each_pair(q.shape[1], one)


def inner_units_kernel(bias_ref, stats, q, kv, grads, dq_in, d_kv_in, d_query, d_kv, kt, dq_s):
    def one(pair, lanes):
        dq_s[...] = dq_in[:, lanes]
        d_kv[:, :, lanes] = d_kv_in[:, :, lanes]

        def keep(n, level, at, rows):
            where = block_rows(at - 1)
            d_kv[n, where, lanes] = d_kv[n, where, lanes] + rows

        backward_units(
            pair, lanes, INNER_UNITS, bias_ref, q, kv, None, None, grads, stats, kt, dq_s, keep
        )
        d_query[:, lanes] = dq_s[...].astype(BF16)

    each_pair(q.shape[1], one)


def turned(count):
    return pltpu.VMEM((count, PAIR, BLOCK), BF16)


def forward_inner(bias, q, kv):
    width = q.shape[1]
    outputs = [held((2 * BLOCK, width), F32), held((width // PAIR, 8, BLOCK), F32)]
    scratch = [turned(EXT_BLOCKS[0]), pltpu.VMEM((4 * BLOCK, PAIR), F32)]
    return run(forward_inner_kernel, "forward_inner", 12, [bias], [q, kv], outputs, scratch)


def forward_edge(bias, q, kv, from_left, from_right, inner):
    width = q.shape[1]
    inputs = [q, kv, from_left, from_right, inner]
    outputs = [held((4 * BLOCK, width), BF16), held((width // PAIR, 24, BLOCK), F32)]
    scratch = [turned(EXT_TOTAL), pltpu.VMEM((4 * BLOCK, PAIR), F32)]
    return run(forward_edge_kernel, "forward_edge", 12, [bias], inputs, outputs, scratch)


def edge_backward(bias, stats, q, kv, from_left, from_right, d_att):
    rows, width = 4 * BLOCK, q.shape[1]
    edge = held((2, 3 * BLOCK, width), BF16)
    inputs = [stats, q, kv, from_left, from_right, d_att]
    outputs = [held((rows, width), F32), held((2, rows, width), F32), edge, edge]
    scratch = [
        turned(EXT_TOTAL),
        pltpu.VMEM((2, EXT_TOTAL, BLOCK, PAIR), F32),
        pltpu.VMEM((rows, PAIR), F32),
        pltpu.VMEM((rows, PAIR), F32),
    ]
    return run(edge_kernel, "edge_backward", 20, [bias], inputs, outputs, scratch)


def inner_backward(bias, stats, q, kv, d_att, dq_f, d_kv):
    rows, width = 4 * BLOCK, q.shape[1]
    inputs = [stats, q, kv, d_att, dq_f, d_kv]
    outputs = [held((rows, width), BF16), held((2, rows, width), F32)]
    scratch = [turned(EXT_BLOCKS[0]), pltpu.VMEM((rows, PAIR), F32)]
    return run(inner_units_kernel, "inner_backward", 12, [bias], inputs, outputs, scratch)


def store_terms(step, terms, own, keep_right, keep_left, right, left):
    own[block_rows(step), :] = terms[0]
    low, high = block_rows(step % 2), block_rows(2 + step % 2)
    if step < 2:
        keep_right[low, :] = terms[1]
        right[high, :] = terms[2]
        left[low, :] = terms[3]
    else:
        right[low, :] = terms[1]
        left[high, :] = terms[2]
        keep_left[low, :] = terms[3]


def term_outputs(rows, width, extra=0):
    lengths = [rows, rows // 2, rows // 2, rows + extra, rows + extra]
    return [held((n, width), BF16) for n in lengths]


def out_terms_kernel(place, attended, w_out, *outs):
    me = place[0]
    width = attended.shape[1]
    for step in range(4):
        rows = attended[block_rows(step), :]
        terms = [nn(rows, w_out[:, share_rows(me, r, width)]).astype(BF16) for r in range(MP)]
        store_terms(step, terms, *outs)


def out_terms(place, attended, w_out):
    outputs = term_outputs(*attended.shape)
    return run(out_terms_kernel, "out_terms", 8, [place], [attended, w_out], outputs)


def input_terms_kernel(
    place, d_query, d_kv, from_left, from_right, normed, wq, wk, wv, d_proj,
    dots, own, keep_right, keep_left, right, left, dot_rows,
):
    me = place[0]
    width = d_query.shape[1]
    half = spread_matrix(BLOCK // 2, 2, 0.5)
    quarter = spread_matrix(BLOCK // 4, 4, 0.25)
    dot_rows[12:16, :] = jnp.zeros((4, BLOCK), F32)
    for step in range(4):
        rows = block_rows(step)
        grads = [d_query[rows, :]]
        mid_rows = slice(256 + (step % 2) * 128, 384 + (step % 2) * 128)
        low_rows = slice(512 + step * 64, 576 + step * 64)
        near = from_left if step < 2 else from_right
        for n in range(2):
            total = d_kv[n, rows, :]
            if step in (0, 3):
                total = total + near[n, 0:BLOCK, :].astype(F32)
            total = total + nn(half, near[n, mid_rows, :])
            total = total + nn(quarter, from_left[n, low_rows, :])
            total = total + nn(quarter, from_right[n, low_rows, :])
            grads.append(total.astype(BF16))
        for n, grad in enumerate(grads):
            d_proj[rows, n * width : (n + 1) * width] = grad
        terms, dot = [], None
        for r in range(MP):
            at = share_rows(me, r, width)
            term = nt(grads[0], wq[at, :]) + nt(grads[1], wk[at, :]) + nt(grads[2], wv[at, :])
            term = term.astype(BF16)
            terms.append(term)
            part = term.astype(F32) * normed[rows, r * width : (r + 1) * width].astype(F32)
            dot = part if dot is None else dot + part
        dot = as_row(jnp.sum(dot, axis=1, keepdims=True))
        first = dot.astype(BF16).astype(F32)
        second = (dot - first).astype(BF16).astype(F32)
        for n, piece in enumerate((first, second, dot - first - second)):
            dot_rows[4 * n + step : 4 * n + step + 1, :] = piece
        store_terms(step, terms, own, keep_right, keep_left, right, left)
    pieces = dot_rows[...].astype(BF16)
    dots[...] = pieces
    right[4 * BLOCK :, :] = pieces
    left[4 * BLOCK :, :] = pieces


def input_terms(place, d_query, d_kv, from_left, from_right, normed, wq, wk, wv):
    rows, width = d_query.shape
    inputs = [d_query, d_kv, from_left, from_right, normed, wq, wk, wv]
    outputs = [held((rows, 3 * width), BF16), held((DOT_ROWS, width), BF16)]
    outputs += term_outputs(rows, width, DOT_ROWS)
    scratch = [pltpu.VMEM((DOT_ROWS, width), F32)]
    return run(input_terms_kernel, "input_terms", 16, [place], inputs, outputs, scratch)


def relay_kernel(keep_right, keep_left, l1, r1, onward_right, onward_left):
    half = keep_right.shape[0]
    passed = l1[half : 2 * half, :].astype(F32)
    onward_right[0:half, :] = (keep_right[...].astype(F32) + passed).astype(BF16)
    passed = r1[half : 2 * half, :].astype(F32)
    onward_left[...] = (keep_left[...].astype(F32) + passed).astype(BF16)
    if onward_right.shape[0] > half:
        onward_right[half:, :] = l1[2 * half :, :]


def relay(keep_right, keep_left, l1, r1):
    half, width = keep_right.shape
    extra = l1.shape[0] - 2 * half
    outputs = [held((half + extra, width), BF16), held((half, width), BF16)]
    return run(relay_kernel, "relay", 4, [], [keep_right, keep_left, l1, r1], outputs)


def summed(own, l1, r1, l2, r2):
    half = r2.shape[0]
    low = r1[0:half, :].astype(F32) + l2[0:half, :].astype(F32)
    high = l1[0:half, :].astype(F32) + r2[...].astype(F32)
    return own[0:half, :].astype(F32) + low, own[half:, :].astype(F32) + high


def finish_out_kernel(own, l1, r1, l2, r2, result):
    half = r2.shape[0]
    low, high = summed(own, l1, r1, l2, r2)
    result[0:half, :] = low.astype(BF16)
    result[half:, :] = high.astype(BF16)


def finish_out(own, l1, r1, l2, r2):
    outputs = [jax.ShapeDtypeStruct(own.shape, BF16)]
    return run(finish_out_kernel, "finish_out", 8, [], [own, l1, r1, l2, r2], outputs)[0]


def finish_grad_kernel(own, l1, r1, l2, r2, tokens, inverse, dots, result):
    rows, width = own.shape
    half = r2.shape[0]
    pieces = dots[...].astype(F32)
    for message, first in ((l1, rows), (r1, rows), (l2, half)):
        pieces = pieces + message[first : first + DOT_ROWS, :].astype(F32)
    means = (pieces[0:4] + pieces[4:8] + pieces[8:12]) / (MP * width)
    halves = summed(own, l1, r1, l2, r2)
    for b in range(rows // BLOCK):
        mean = as_column(means[b : b + 1, :])
        inv = as_column(inverse[b : b + 1, :])
        at = block_rows(b)
        total = halves[b // 2][block_rows(b % 2), :]
        result[at, :] = inv * (total - tokens[at, :].astype(F32) * inv * mean)


def finish_grad(own, l1, r1, l2, r2, tokens, inverse, dots):
    inputs = [own, l1, r1, l2, r2, tokens, inverse, dots]
    outputs = [jax.ShapeDtypeStruct(own.shape, F32)]
    return run(finish_grad_kernel, "finish_grad", 8, [], inputs, outputs)[0]


def outer_kernel(g0, g1, g2, g3, attended, result):
    width = g0.shape[1]
    rows = attended[...]
    for r, share in enumerate((g0, g1, g2, g3)):
        result[r * width : (r + 1) * width, :] = tn(share[...], rows).astype(BF16)


def outer_terms(shares, attended):
    rows, width = attended.shape
    outputs = [held((MP * width, width), BF16)]
    return run(outer_kernel, "outer_terms", 10, [], [*shares, attended], outputs)[0]


def inner_kernel(place, normed, d_proj, outer, mine, other, rows_held):
    core = place[1]
    width = outer.shape[1]
    for block in range(MP):
        at = block_rows(block)
        rows_held[at, 0 : 3 * width] = tn(normed[:, at], d_proj[...]).astype(BF16)
        rows_held[at, 3 * width :] = outer[at, :]
        for n in range(width // 64):
            out = slice((4 * block + n) * 32, (4 * block + n + 1) * 32)
            first = block * width + n * 64
            mine[out, :] = rows_held[pl.ds(pl.multiple_of(first + core * 32, 32), 32), :]
            other[out, :] = rows_held[pl.ds(pl.multiple_of(first + 32 - core * 32, 32), 32), :]


def inner_terms(place, normed, d_proj, outer):
    total = normed.shape[1]
    width = outer.shape[1]
    outputs = [held((total // 2, 4 * width), BF16)] * 2
    scratch = [pltpu.VMEM((total, 4 * width), BF16)]
    return run(inner_kernel, "inner_terms", 16, [place], [normed, d_proj, outer], outputs, scratch)


def pair_sum_kernel(place, mine, got, *outs):
    x = place[2]
    for d, out in enumerate(outs):
        for y in range(4):
            rows = pl.ds(pl.multiple_of((4 * y + ((x + d) & 3)) * 32, 32), 32)
            total = mine[rows, :].astype(F32) + got[rows, :].astype(F32)
            out[32 * y : 32 * (y + 1), :] = total.astype(BF16)


def row_sum_kernel(place, a, b, c, d, *refs):
    *outs, total = refs
    first = place[3] - place[0] + 4
    total[...] = (
        a[...].astype(F32) + b[...].astype(F32) + c[...].astype(F32) + d[...].astype(F32)
    ).astype(BF16)
    for n, out in enumerate(outs):
        out[...] = total[pl.ds(pl.multiple_of(((first + n) & 3) * 32, 32), 32), :]


def last_sum_kernel(a, b, c, d, gq, gk, gv, go):
    width = gq.shape[1]
    total = a[...].astype(F32) + b[...].astype(F32) + c[...].astype(F32) + d[...].astype(F32)
    gq[...] = total[:, 0:width]
    gk[...] = total[:, width : 2 * width]
    gv[...] = total[:, 2 * width : 3 * width]
    go[...] = total[:, 3 * width :]


def sum_over_seq(place, mine, other):
    cols = mine.shape[1]

    def sent(value, dy, dx, dc):
        pairs = []
        for i in range(32):
            c, a, b = i % 2, (i // 2) % 4, i // 8
            pairs.append((i, (((b + dy) % 4) * 4 + (a + dx) % 4) * 2 + (c + dc) % 2))
        return lax.ppermute(value, "seq", pairs)

    parts = [held((128, cols), BF16)] * 4
    parts = run(pair_sum_kernel, "pair_sum", 6, [place], [mine, sent(other, 0, 0, 1)], parts)
    parts = [parts[0]] + [sent(parts[d], 0, d, 0) for d in (1, 3, 2)]
    rows = [held((32, cols), BF16)] * 4
    scratch = [pltpu.VMEM((128, cols), BF16)]
    rows = run(row_sum_kernel, "row_sum", 4, [place], parts, rows, scratch)
    rows = [rows[0]] + [sent(rows[d], d, 0, 0) for d in (1, 3, 2)]
    outputs = [held((32, cols // 4), F32)] * 4
    return run(last_sum_kernel, "last_sum", 4, [], rows, outputs)


def to_next(value):
    return lax.ppermute(value, "mp", [(i, (i + 1) % MP) for i in range(MP)])


def to_previous(value):
    return lax.ppermute(value, "mp", [((i + 1) % MP, i) for i in range(MP)])


def gather_shares(share):
    half = share.shape[0] // 2
    low, high = share[:half], share[half:]
    after_low, before_high = to_previous(low), to_next(high)
    after_high, before_low = to_previous(high), to_next(low)
    far_low, far_high = to_previous(after_low), to_next(before_high)
    return [share, after_low, after_high, far_low, far_high, before_low, before_high]


def gather_direct(share):
    far = lax.ppermute(share, "mp", [(i, (i + 2) % MP) for i in range(MP)])
    return [share, to_previous(share), far, to_next(share)]


def exchange(to_left, to_right):
    count = lax.axis_size("seq")
    ends = count - 1
    from_left = lax.ppermute(to_right, "seq", [(i, i + 1) for i in range(ends)])
    from_right = lax.ppermute(to_left, "seq", [(i + 1, i) for i in range(ends)])
    return from_left, from_right


def tied(values, *others):
    flat, tree = jax.tree.flatten(values)
    flat = lax.optimization_barrier((*flat, *others))[: len(flat)]
    return jax.tree.unflatten(tree, flat)


def per_device(tokens, w_query, w_key, w_value, w_out, grad_out):
    count = lax.axis_size("seq")
    index = lax.axis_index("seq")
    me = jnp.stack([lax.axis_index("mp"), index & 1, (index >> 1) & 3, index >> 3])
    me = me.astype(jnp.int32)
    bias = jnp.stack(
        [
            jnp.where(index == 0, NEGATIVE, 0.0).astype(F32),
            jnp.where(index == count - 1, NEGATIVE, 0.0).astype(F32),
        ]
    )
    token_shares = gather_shares(tokens)
    sent_grad = tied(grad_out, *token_shares)
    grad_shares = gather_direct(sent_grad)
    grad_shares[0] = grad_out
    inverse, q, kv, to_left, to_right, normed = project(
        me, token_shares, w_query, w_key, w_value
    )
    from_left, from_right = exchange(to_left, to_right)
    inner_out, inner_stats = forward_inner(bias, q, kv)
    attended, stats = forward_edge(bias, q, kv, from_left, from_right, inner_out)
    grad_shares = tied(grad_shares, attended)
    out_own, keep_right, keep_left, right, left = out_terms(me, attended, w_out)
    l1, r1 = to_next(right), to_previous(left)
    d_att = cotangent(me, grad_shares, w_out)
    dq_f, d_kv, to_left, to_right = edge_backward(
        bias, stats, q, kv, from_left, from_right, d_att
    )
    onward_right, onward_left = relay(keep_right, keep_left, l1, r1)
    l2, r2 = to_next(onward_right), to_previous(onward_left)
    from_left, from_right = exchange(to_left, to_right)
    dq_f = tied(dq_f, onward_right, onward_left)
    d_query, d_kv = inner_backward(bias, inner_stats, q, kv, d_att, dq_f, d_kv)
    d_query = tied(d_query, l2, r2)
    d_proj, dots, own, keep_right, keep_left, right, left = input_terms(
        me, d_query, d_kv, from_left, from_right, normed, w_query, w_key, w_value
    )
    attn_out = finish_out(out_own, l1, r1, l2, r2)
    l1, r1 = to_next(right), to_previous(left)
    outer = outer_terms(grad_shares, attended)
    mine, other = inner_terms(me, normed, d_proj, outer)
    onward_right, onward_left = relay(keep_right, keep_left, l1, r1)
    l2, r2 = to_next(onward_right), to_previous(onward_left)
    grad_tokens = finish_grad(own, l1, r1, l2, r2, tokens, inverse, dots)
    *weight_grads, grad_w_out = sum_over_seq(me, mine, other)
    return (attn_out, grad_tokens, *weight_grads, grad_w_out.T)


def solution(mesh):
    return jax.shard_map(
        per_device,
        mesh=mesh,
        in_specs=(
            P("seq", "mp"),
            P(None, "mp"),
            P(None, "mp"),
            P(None, "mp"),
            P("mp", None),
            P("seq", "mp"),
        ),
        out_specs=(
            P("seq", "mp"),
            P("seq", "mp"),
            P("seq", "mp"),
            P("seq", "mp"),
            P("seq", "mp"),
            P("mp", "seq"),
        ),
        check_vma=False,
    )
```

```python
import jax
import jax.numpy as jnp
from jax import lax
from jax.experimental import pallas as pl
from jax.experimental.pallas import tpu as pltpu
from jax.sharding import PartitionSpec as P

HD = 64
BLOCK = 256
LEVELS = 3
PAIR = 2 * HD
MP = 4
LANES = 128
DOT_ROWS = 16

EPSILON = 1e-06
NEGATIVE = -1e30

F32 = jnp.float32
BF16 = jnp.bfloat16

FIRST_EXT = (0, 6, 10)
EXT_BLOCKS = (6, 4, 3)
EXT_TOTAL = 13


def nn(left, right):
    return lax.dot_general(left, right, (((1,), (0,)), ((), ())), preferred_element_type=F32)


def nt(left, right):
    return lax.dot_general(left, right, (((1,), (1,)), ((), ())), preferred_element_type=F32)


def tn(left, right):
    return lax.dot_general(left, right, (((0,), (0,)), ((), ())), preferred_element_type=F32)


def pool_matrix(coarse, factor, value):
    shape = (coarse, coarse * factor)
    row = lax.broadcasted_iota(jnp.int32, shape, 0)
    low = row * factor
    col = lax.broadcasted_iota(jnp.int32, shape, 1)
    return jnp.where((col >= low) & (col < low + factor), value, 0.0).astype(BF16)


def spread_matrix(coarse, factor, value):
    shape = (coarse * factor, coarse)
    low = lax.broadcasted_iota(jnp.int32, shape, 1) * factor
    row = lax.broadcasted_iota(jnp.int32, shape, 0)
    return jnp.where((row >= low) & (row < low + factor), value, 0.0).astype(BF16)


def share_rows(me, step, width):
    return pl.ds(pl.multiple_of(((me + step) & (MP - 1)) * width, width), width)


SMALL = pl.CostEstimate(flops=10**6, bytes_accessed=10**4, transcendentals=0)
LARGE = pl.CostEstimate(flops=4 * 10**9, bytes_accessed=10**4, transcendentals=0)
LAST = pl.CostEstimate(flops=1 * 10**9, bytes_accessed=10**4, transcendentals=0)
SCALAR = pl.BlockSpec(memory_space=pltpu.SMEM)
RESIDENT = pl.BlockSpec(memory_space=pltpu.VMEM)


def held(shape, dtype):
    return jax.ShapeDtypeStruct(shape, dtype)


def run(kernel, name, limit_mib, scalars, inputs, outputs, scratch=(), cost=SMALL):
    return pl.pallas_call(
        kernel,
        in_specs=[SCALAR] * len(scalars) + [RESIDENT] * len(inputs),
        out_specs=[RESIDENT] * len(outputs),
        out_shape=outputs,
        scratch_shapes=list(scratch),
        compiler_params=pltpu.CompilerParams(vmem_limit_bytes=limit_mib * 2**20),
        cost_estimate=cost,
        name=name,
    )(*scalars, *inputs)


def block_rows(block):
    return slice(block * BLOCK, (block + 1) * BLOCK)


ALL_ROWS = 7 * BLOCK
LEVEL_BLOCK = (0, 4, 6)


def as_row(column):
    return jnp.broadcast_to(column, (column.shape[0], LANES)).T[0:1, :]


def as_column(row):
    return jnp.broadcast_to(row, (LANES, row.shape[1])).T[:, 0:1]


def project_kernel(
    place, t1a_any, t1b_any, t2a_any, t2b_any, t3a_any, t3b_any,
    t0_hbm, wq_hbm, wk_hbm, wv_hbm,
    inverse, q, kv, to_left, to_right, normed_hbm,
    t0, t1, t2, t3, wq, wk, wv, normed, in_sems, out_sems,
):
    me = place[0]
    width = t0.shape[1]
    low, high = pl.ds(0, 2 * BLOCK), pl.ds(2 * BLOCK, 2 * BLOCK)
    moves = [
        (t0_hbm, t0),
        (t1a_any, t1.at[low]),
        (t2a_any, t2.at[low]),
        (t3a_any, t3.at[low]),
        (t1b_any, t1.at[high]),
        (t2b_any, t2.at[high]),
        (t3b_any, t3.at[high]),
        (wq_hbm, wq),
        (wk_hbm, wk),
        (wv_hbm, wv),
    ]
    loads = [
        pltpu.make_async_copy(source, target, in_sems.at[n])
        for n, (source, target) in enumerate(moves)
    ]
    for load in loads:
        load.start()
    half = pool_matrix(BLOCK // 2, 2, 0.5)
    quarter = pool_matrix(BLOCK // 4, 4, 0.25)
    inverse[4:8, :] = jnp.zeros((4, BLOCK), F32)
    stores = []

    def normalise(step):
        if step in (0, 2):
            for load in loads[0:4] if step == 0 else loads[4:7]:
                load.wait()
        rows = block_rows(step)
        shares = [share[rows, :].astype(F32) for share in (t0, t1, t2, t3)]
        squares = shares[0] * shares[0]
        for share in shares[1:]:
            squares = squares + share * share
        total = jnp.sum(squares, axis=1, keepdims=True)
        inv = lax.rsqrt(total / (MP * width) + EPSILON)
        inverse[step : step + 1, :] = as_row(inv)
        parts = [(share * inv).astype(BF16) for share in shares]
        for r, part in enumerate(parts):
            normed[rows, r * width : (r + 1) * width] = part
        store = pltpu.make_async_copy(normed.at[rows], normed_hbm.at[rows], out_sems.at[step])
        store.start()
        stores.append(store)
        return parts

    def spread(step, parts):
        if step == 0:
            for load in loads[7:]:
                load.wait()
        rows = block_rows(step)
        sums = [None, None, None]
        for r, part in enumerate(parts):
            w_rows = share_rows(me, r, width)
            for n, w in enumerate((wq, wk, wv)):
                term = nn(part, w[w_rows, :])
                sums[n] = term if sums[n] is None else sums[n] + term
        fine = [x.astype(BF16) for x in sums]
        mid = [nn(half, x).astype(BF16) for x in fine]
        low = [nn(quarter, x).astype(BF16) for x in fine]
        mid_rows = slice(1024 + step * 128, 1024 + (step + 1) * 128)
        low_rows = slice(1536 + step * 64, 1536 + (step + 1) * 64)
        q[rows, :] = fine[0]
        q[mid_rows, :] = mid[0]
        q[low_rows, :] = low[0]
        edge_mid = slice(256 + (step % 2) * 128, 384 + (step % 2) * 128)
        edge_low = slice(512 + step * 64, 576 + step * 64)
        for n in range(2):
            kv[n, rows, :] = fine[1 + n]
            kv[n, mid_rows, :] = mid[1 + n]
            kv[n, low_rows, :] = low[1 + n]
            to_left[n, edge_low, :] = low[1 + n]
            to_right[n, edge_low, :] = low[1 + n]
            edge = to_left if step < 2 else to_right
            edge[n, edge_mid, :] = mid[1 + n]
            if step in (0, 3):
                edge[n, 0:BLOCK, :] = fine[1 + n]

    parts = normalise(0)
    for step in range(4):
        following = normalise(step + 1) if step < 3 else None
        spread(step, parts)
        parts = following
    for store in stores:
        store.wait()


def project(place, shares, wq, wk, wv):
    rows, width = shares[0].shape
    out = jax.ShapeDtypeStruct
    edge = out((2, 3 * BLOCK, width), BF16)
    anywhere = pl.BlockSpec(memory_space=pl.ANY)
    share = pltpu.VMEM((rows, width), BF16)
    fixed = [
        pltpu.with_memory_space_constraint(value, pltpu.HBM)
        for value in (shares[0], wq, wk, wv)
    ]
    return pl.pallas_call(
        project_kernel,
        in_specs=[SCALAR] + [anywhere] * 10,
        out_specs=[RESIDENT] * 5 + [anywhere],
        out_shape=[
            out((8, width), F32),
            out((ALL_ROWS, width), BF16),
            out((2, ALL_ROWS, width), BF16),
            edge,
            edge,
            pltpu.HBM((rows, MP * width), BF16),
        ],
        scratch_shapes=[share] * 7
        + [
            pltpu.VMEM((rows, MP * width), BF16),
            pltpu.SemaphoreType.DMA((10,)),
            pltpu.SemaphoreType.DMA((4,)),
        ],
        compiler_params=pltpu.CompilerParams(vmem_limit_bytes=20 * 2**20),
        cost_estimate=SMALL,
        name="project",
    )(place, *shares[1:], *fixed)


def cotangent_kernel(place, g0, g1, g2, g3, w_out, d_att):
    me = place[0]
    width = g0.shape[1]
    half = pool_matrix(BLOCK // 2, 2, 1.0)
    quarter = pool_matrix(BLOCK // 4, 4, 1.0)
    for step in range(4):
        rows = block_rows(step)
        total = None
        for r, share in enumerate((g0, g1, g2, g3)):
            term = nt(share[rows, :], w_out[:, share_rows(me, r, width)])
            total = term if total is None else total + term
        fine = total.astype(BF16)
        d_att[rows, :] = fine
        d_att[1024 + step * 128 : 1024 + (step + 1) * 128, :] = nn(half, fine).astype(BF16)
        d_att[1536 + step * 64 : 1536 + (step + 1) * 64, :] = nn(quarter, fine).astype(BF16)


def cotangent(place, shares, w_out):
    rows, width = shares[0].shape
    outputs = [held((ALL_ROWS, width), BF16)]
    return run(cotangent_kernel, "cotangent", 8, [place], [*shares, w_out], outputs)[0]


EDGE_UNITS = ((0, 0), (0, 3), (1, 0), (1, 1), (2, 0))
INNER_UNITS = ((0, 1), (0, 2))


def unit_keys(level, block):
    last = EXT_BLOCKS[level] - 1
    offsets = (0, 1, 2) if level == 0 else (0, 2)
    keys = []
    for offset in offsets:
        at = block + offset
        keys.append((at, 0 if at == 0 else 1 if at == last else None))
    return keys


def ext_rows(kv, from_left, from_right, n, level, at, lanes):
    if at == 0:
        return from_left[n, block_rows(level), lanes]
    if at == EXT_BLOCKS[level] - 1:
        return from_right[n, block_rows(level), lanes]
    return kv[n, block_rows(LEVEL_BLOCK[level] + at - 1), lanes]


def head_part(lane, head, rows):
    mine = (lane >= head * HD) & (lane < (head + 1) * HD)
    return jnp.where(mine, rows, 0.0).astype(BF16)


def unit_scores(keys, key_rows, query, bias_ref):
    scores = []
    for (_, bias), rows in zip(keys, key_rows):
        s = nt(rows, query)
        scores.append(s if bias is None else s + bias_ref[bias])
    return scores


def add_spread(target, block, factor, rows):
    if factor == 1:
        target[block_rows(block), :] = target[block_rows(block), :] + rows
        return
    for s in range(factor):
        spread = pl.ds(block * factor * BLOCK + s, BLOCK, factor)
        target[spread, :] = target[spread, :] + rows


def each_pair(width, body):
    def step(pair, _):
        body(pair, pl.ds(pl.multiple_of(pair * PAIR, PAIR), PAIR))
        return 0

    lax.fori_loop(0, width // PAIR, step, 0)


def head_part(lane, head, rows):
    mine = (lane >= head * HD) & (lane < (head + 1) * HD)
    return jnp.where(mine, rows, 0.0).astype(BF16)


def unit_scores(keys, key_rows, query, bias_ref):
    scores = []
    for (_, bias), rows in zip(keys, key_rows):
        s = nt(rows, query)
        scores.append(s if bias is None else s + bias_ref[bias])
    return scores


def add_spread(target, block, factor, rows):
    if factor == 1:
        target[block_rows(block), :] = target[block_rows(block), :] + rows
        return
    for s in range(factor):
        spread = pl.ds(block * factor * BLOCK + s, BLOCK, factor)
        target[spread, :] = target[spread, :] + rows


def forward_units(pair, lanes, units, bias_ref, q, kv, from_left, from_right, stats, vt, out_f):
    lane = lax.broadcasted_iota(jnp.int32, (BLOCK, PAIR), 1)
    done = set()
    for level, block in units:
        for at, _ in unit_keys(level, block):
            if (level, at) not in done:
                done.add((level, at))
                rows = ext_rows(kv, from_left, from_right, 1, level, at, lanes)
                vt[FIRST_EXT[level] + at] = rows.T

    def begin(u, head):
        level, block = units[u]
        keys = unit_keys(level, block)
        key_rows = [ext_rows(kv, from_left, from_right, 0, level, at, lanes) for at, _ in keys]
        q_rows = q[block_rows(LEVEL_BLOCK[level] + block), lanes] * HD ** (-0.5)
        return unit_scores(keys, key_rows, head_part(lane, head, q_rows), bias_ref)

    def finish(u, head, scores):
        level, block = units[u]
        top = scores[0].max(axis=0, keepdims=True)
        for s in scores[1:]:
            top = jnp.maximum(top, s.max(axis=0, keepdims=True))
        exps = [jnp.exp(s - top) for s in scores]
        total = exps[0].sum(axis=0, keepdims=True)
        for e in exps[1:]:
            total = total + e.sum(axis=0, keepdims=True)
        scale = 1.0 / total
        row = 4 * u + 2 * head
        stats[pair, row : row + 1, :] = top
        stats[pair, row + 1 : row + 2, :] = scale
        part = slice(head * HD, (head + 1) * HD)
        o_t = None
        for (at, _), e in zip(unit_keys(level, block), exps):
            o = nn(vt[FIRST_EXT[level] + at, part, :], (e * scale).astype(BF16))
            o_t = o if o_t is None else o_t + o
        return o_t

    items = [(u, head) for u in range(len(units)) for head in range(2)]
    scores, outs = begin(*items[0]), []
    for n, (u, head) in enumerate(items):
        following = begin(*items[n + 1]) if n + 1 < len(items) else None
        outs.append(finish(u, head, scores))
        scores = following
        if head == 1:
            level, block = units[u]
            add_spread(out_f, block, 2**level, jnp.concatenate(outs, axis=0).T)
            outs = []


def forward_inner_kernel(bias_ref, q, kv, out, stats, vt, out_f):
    def one(pair, lanes):
        out_f[...] = jnp.zeros_like(out_f)
        forward_units(pair, lanes, INNER_UNITS, bias_ref, q, kv, None, None, stats, vt, out_f)
        out[:, lanes] = out_f[BLOCK : 3 * BLOCK, :]

    each_pair(q.shape[1], one)


def forward_edge_kernel(
    bias_ref, q, kv, from_left, from_right, inner, attended, stats, vt, out_f
):
    def one(pair, lanes):
        out_f[0:BLOCK, :] = jnp.zeros((BLOCK, PAIR), F32)
        out_f[BLOCK : 3 * BLOCK, :] = inner[:, lanes]
        out_f[3 * BLOCK :, :] = jnp.zeros((BLOCK, PAIR), F32)
        forward_units(
            pair, lanes, EDGE_UNITS, bias_ref, q, kv, from_left, from_right, stats, vt, out_f
        )
        attended[:, lanes] = out_f[...].astype(BF16)

    each_pair(q.shape[1], one)


def backward_units(
    pair, lanes, units, bias_ref, q, kv, from_left, from_right, grads, stats, kt, dq_f, keep
):
    lane = lax.broadcasted_iota(jnp.int32, (BLOCK, PAIR), 1)
    done = set()
    for level, block in units:
        for at, _ in unit_keys(level, block):
            if (level, at) not in done:
                done.add((level, at))
                rows = ext_rows(kv, from_left, from_right, 0, level, at, lanes)
                kt[FIRST_EXT[level] + at] = rows.T

    def begin(u, head):
        level, block = units[u]
        keys = unit_keys(level, block)
        key_rows = [ext_rows(kv, from_left, from_right, 0, level, at, lanes) for at, _ in keys]
        value_rows = [ext_rows(kv, from_left, from_right, 1, level, at, lanes) for at, _ in keys]
        at = block_rows(LEVEL_BLOCK[level] + block)
        qm = head_part(lane, head, q[at, lanes] * HD ** (-0.5))
        am = head_part(lane, head, grads[at, lanes])
        scores = unit_scores(keys, key_rows, qm, bias_ref)
        return qm, am, scores, [nt(rows, am) for rows in value_rows]

    def finish(u, head, qm, am, scores, d_weights):
        level, block = units[u]
        row = 4 * u + 2 * head
        top, scale = stats[pair, row : row + 1, :], stats[pair, row + 1 : row + 2, :]
        probs = [jnp.exp(s - top) * scale for s in scores]
        dots = None
        for p, dw in zip(probs, d_weights):
            d = (p * dw).sum(axis=0, keepdims=True)
            dots = d if dots is None else dots + d
        part = slice(head * HD, (head + 1) * HD)
        dq_t, d_keys, d_values = None, [], []
        for (at, _), p, dw in zip(unit_keys(level, block), probs, d_weights):
            d_values.append(nn(p.astype(BF16), am))
            d_scores = (p * (dw - dots)).astype(BF16)
            d_keys.append(nn(d_scores, qm))
            g = nn(kt[FIRST_EXT[level] + at, part, :], d_scores)
            dq_t = g if dq_t is None else dq_t + g
        return dq_t, d_keys, d_values

    items = [(u, head) for u in range(len(units)) for head in range(2)]
    ready, first = begin(*items[0]), None
    for n, (u, head) in enumerate(items):
        following = begin(*items[n + 1]) if n + 1 < len(items) else None
        got = finish(u, head, *ready)
        ready = following
        if head == 0:
            first = got
            continue
        level, block = units[u]
        for m, (at, _) in enumerate(unit_keys(level, block)):
            keep(0, level, at, first[1][m] + got[1][m])
            keep(1, level, at, first[2][m] + got[2][m])
        dq = jnp.concatenate([first[0], got[0]], axis=0).T * (HD ** (-0.5) / 2**level)
        add_spread(dq_f, block, 2**level, dq)


def edge_kernel(
    bias_ref, stats, q, kv, from_left, from_right, grads,
    dq_f, d_kv, to_left, to_right, kt, ext, dq_s, sums,
):
    def one(pair, lanes):
        dq_s[...] = jnp.zeros_like(dq_s)
        seen = set()

        def keep(n, level, at, rows):
            slot = FIRST_EXT[level] + at
            if (n, slot) in seen:
                ext[n, slot] = ext[n, slot] + rows
            else:
                seen.add((n, slot))
                ext[n, slot] = rows

        backward_units(
            pair, lanes, EDGE_UNITS, bias_ref, q, kv, from_left, from_right, grads, stats, kt,
            dq_s, keep,
        )
        dq_f[:, lanes] = dq_s[...]
        for n in range(2):
            for level in range(LEVELS):
                first, last = FIRST_EXT[level], FIRST_EXT[level] + EXT_BLOCKS[level] - 1
                to_left[n, block_rows(level), lanes] = ext[n, first].astype(BF16)
                to_right[n, block_rows(level), lanes] = ext[n, last].astype(BF16)
            for b in range(4):
                sums[block_rows(b), :] = ext[n, 1 + b]
            for b in range(2):
                add_spread(sums, b, 2, ext[n, FIRST_EXT[1] + 1 + b] * 0.5)
            d_kv[n, :, lanes] = sums[...]

    each_pair(q.shape[1], one)


def inner_units_kernel(bias_ref, stats, q, kv, grads, dq_in, d_kv_in, d_query, d_kv, kt, dq_s):
    def one(pair, lanes):
        dq_s[...] = dq_in[:, lanes]
        d_kv[:, :, lanes] = d_kv_in[:, :, lanes]

        def keep(n, level, at, rows):
            where = block_rows(at - 1)
            d_kv[n, where, lanes] = d_kv[n, where, lanes] + rows

        backward_units(
            pair, lanes, INNER_UNITS, bias_ref, q, kv, None, None, grads, stats, kt, dq_s, keep
        )
        d_query[:, lanes] = dq_s[...].astype(BF16)

    each_pair(q.shape[1], one)


def turned(count):
    return pltpu.VMEM((count, PAIR, BLOCK), BF16)


def forward_inner(bias, q, kv):
    width = q.shape[1]
    outputs = [held((2 * BLOCK, width), F32), held((width // PAIR, 8, BLOCK), F32)]
    scratch = [turned(EXT_BLOCKS[0]), pltpu.VMEM((4 * BLOCK, PAIR), F32)]
    return run(forward_inner_kernel, "forward_inner", 12, [bias], [q, kv], outputs, scratch, LARGE)


def forward_edge(bias, q, kv, from_left, from_right, inner):
    width = q.shape[1]
    inputs = [q, kv, from_left, from_right, inner]
    outputs = [held((4 * BLOCK, width), BF16), held((width // PAIR, 24, BLOCK), F32)]
    scratch = [turned(EXT_TOTAL), pltpu.VMEM((4 * BLOCK, PAIR), F32)]
    return run(forward_edge_kernel, "forward_edge", 12, [bias], inputs, outputs, scratch)


def edge_backward(bias, stats, q, kv, from_left, from_right, d_att):
    rows, width = 4 * BLOCK, q.shape[1]
    edge = held((2, 3 * BLOCK, width), BF16)
    inputs = [stats, q, kv, from_left, from_right, d_att]
    outputs = [held((rows, width), F32), held((2, rows, width), F32), edge, edge]
    scratch = [
        turned(EXT_TOTAL),
        pltpu.VMEM((2, EXT_TOTAL, BLOCK, PAIR), F32),
        pltpu.VMEM((rows, PAIR), F32),
        pltpu.VMEM((rows, PAIR), F32),
    ]
    return run(edge_kernel, "edge_backward", 20, [bias], inputs, outputs, scratch)


def inner_backward(bias, stats, q, kv, d_att, dq_f, d_kv):
    rows, width = 4 * BLOCK, q.shape[1]
    inputs = [stats, q, kv, d_att, dq_f, d_kv]
    outputs = [held((rows, width), BF16), held((2, rows, width), F32)]
    scratch = [turned(EXT_BLOCKS[0]), pltpu.VMEM((rows, PAIR), F32)]
    return run(inner_units_kernel, "inner_backward", 12, [bias], inputs, outputs, scratch, LARGE)


def term_outputs(rows, width, extra=0):
    return [held((rows, width), BF16)] + [held((rows + extra, width), BF16)] * (MP - 1)


def out_terms_kernel(place, attended, w_out, *outs):
    me = place[0]
    width = attended.shape[1]
    for step in range(4):
        rows = attended[block_rows(step), :]
        for r, out in enumerate(outs):
            term = nn(rows, w_out[:, share_rows(me, r, width)])
            out[block_rows(step), :] = term.astype(BF16)


def out_terms(place, attended, w_out):
    outputs = term_outputs(*attended.shape)
    return run(out_terms_kernel, "out_terms", 8, [place], [attended, w_out], outputs)


def input_terms_kernel(
    place, d_query, d_kv, from_left, from_right, normed, wq, wk, wv, d_proj,
    dots, own, one, two, three, dot_rows,
):
    me = place[0]
    width = d_query.shape[1]
    half = spread_matrix(BLOCK // 2, 2, 0.5)
    quarter = spread_matrix(BLOCK // 4, 4, 0.25)
    dot_rows[12:16, :] = jnp.zeros((4, BLOCK), F32)
    for step in range(4):
        rows = block_rows(step)
        grads = [d_query[rows, :]]
        mid_rows = slice(256 + (step % 2) * 128, 384 + (step % 2) * 128)
        low_rows = slice(512 + step * 64, 576 + step * 64)
        near = from_left if step < 2 else from_right
        for n in range(2):
            total = d_kv[n, rows, :]
            if step in (0, 3):
                total = total + near[n, 0:BLOCK, :].astype(F32)
            total = total + nn(half, near[n, mid_rows, :])
            total = total + nn(quarter, from_left[n, low_rows, :])
            total = total + nn(quarter, from_right[n, low_rows, :])
            grads.append(total.astype(BF16))
        for n, grad in enumerate(grads):
            d_proj[rows, n * width : (n + 1) * width] = grad
        dot = None
        for r, out in enumerate((own, one, two, three)):
            at = share_rows(me, r, width)
            term = nt(grads[0], wq[at, :]) + nt(grads[1], wk[at, :]) + nt(grads[2], wv[at, :])
            term = term.astype(BF16)
            out[rows, :] = term
            part = term.astype(F32) * normed[rows, r * width : (r + 1) * width].astype(F32)
            dot = part if dot is None else dot + part
        dot = as_row(jnp.sum(dot, axis=1, keepdims=True))
        first = dot.astype(BF16).astype(F32)
        second = (dot - first).astype(BF16).astype(F32)
        for n, piece in enumerate((first, second, dot - first - second)):
            dot_rows[4 * n + step : 4 * n + step + 1, :] = piece
    pieces = dot_rows[...].astype(BF16)
    dots[...] = pieces
    for out in (one, two, three):
        out[4 * BLOCK :, :] = pieces


def input_terms(place, d_query, d_kv, from_left, from_right, normed, wq, wk, wv):
    rows, width = d_query.shape
    inputs = [d_query, d_kv, from_left, from_right, normed, wq, wk, wv]
    outputs = [held((rows, 3 * width), BF16), held((DOT_ROWS, width), BF16)]
    outputs += term_outputs(rows, width, DOT_ROWS)
    scratch = [pltpu.VMEM((DOT_ROWS, width), F32)]
    return run(input_terms_kernel, "input_terms", 16, [place], inputs, outputs, scratch)


def sum_terms(own, received, at):
    total = own[at, :].astype(F32)
    for term in received:
        total = total + term[at, :].astype(F32)
    return total


def finish_out_kernel(own, one, two, three, result):
    for b in range(4):
        at = block_rows(b)
        result[at, :] = sum_terms(own, (one, two, three), at).astype(BF16)


def finish_out(own, received):
    outputs = [held(own.shape, BF16)]
    return run(finish_out_kernel, "finish_out", 8, [], [own, *received], outputs)[0]


def finish_grad_kernel(own, one, two, three, tokens, inverse, dots, result):
    rows, width = own.shape
    pieces = dots[...].astype(F32)
    for term in (one, two, three):
        pieces = pieces + term[rows:, :].astype(F32)
    means = (pieces[0:4] + pieces[4:8] + pieces[8:12]) / (MP * width)
    for b in range(rows // BLOCK):
        at = block_rows(b)
        mean = as_column(means[b : b + 1, :])
        inv = as_column(inverse[b : b + 1, :])
        total = sum_terms(own, (one, two, three), at)
        result[at, :] = inv * (total - tokens[at, :].astype(F32) * inv * mean)


def finish_grad(own, received, tokens, inverse, dots):
    inputs = [own, *received, tokens, inverse, dots]
    outputs = [held(own.shape, F32)]
    return run(finish_grad_kernel, "finish_grad", 8, [], inputs, outputs, (), LAST)[0]


def outer_kernel(g0, g1, g2, g3, attended, result):
    width = g0.shape[1]
    rows = attended[...]
    for r, share in enumerate((g0, g1, g2, g3)):
        result[r * width : (r + 1) * width, :] = tn(share[...], rows).astype(BF16)


def outer_terms(shares, attended):
    rows, width = attended.shape
    outputs = [held((MP * width, width), BF16)]
    return run(outer_kernel, "outer_terms", 10, [], [*shares, attended], outputs)[0]


def inner_kernel(place, normed, d_proj, outer, mine, other, rows_held):
    core = place[1]
    width = outer.shape[1]
    for block in range(MP):
        at = block_rows(block)
        rows_held[at, 0 : 3 * width] = tn(normed[:, at], d_proj[...]).astype(BF16)
        rows_held[at, 3 * width :] = outer[at, :]
        for n in range(width // 64):
            out = slice((4 * block + n) * 32, (4 * block + n + 1) * 32)
            first = block * width + n * 64
            mine[out, :] = rows_held[pl.ds(pl.multiple_of(first + core * 32, 32), 32), :]
            other[out, :] = rows_held[pl.ds(pl.multiple_of(first + 32 - core * 32, 32), 32), :]


def inner_terms(place, normed, d_proj, outer):
    total = normed.shape[1]
    width = outer.shape[1]
    outputs = [held((total // 2, 4 * width), BF16)] * 2
    scratch = [pltpu.VMEM((total, 4 * width), BF16)]
    return run(inner_kernel, "inner_terms", 16, [place], [normed, d_proj, outer], outputs, scratch)


def pair_sum_kernel(place, mine, got, *outs):
    z, core, x, y = place[0], place[1], place[2], place[3]
    for d, out in enumerate(outs):
        for n in range(4):
            chunk = jnp.where(core == 0, 4 * n + ((x + d) & 3), 4 * ((y + d - z + 4) & 3) + n)
            rows = pl.ds(pl.multiple_of(chunk * 32, 32), 32)
            total = mine[rows, :].astype(F32) + got[rows, :].astype(F32)
            out[32 * n : 32 * (n + 1), :] = total.astype(BF16)


def row_sum_kernel(place, a, b, c, d, *refs):
    *outs, total = refs
    z, core, x, y = place[0], place[1], place[2], place[3]
    first = jnp.where(core == 0, y - z + 4, x)
    total[...] = (
        a[...].astype(F32) + b[...].astype(F32) + c[...].astype(F32) + d[...].astype(F32)
    ).astype(BF16)
    for n, out in enumerate(outs):
        out[...] = total[pl.ds(pl.multiple_of(((first + n) & 3) * 32, 32), 32), :]


def last_sum_kernel(a, b, c, d, gq, gk, gv, go):
    width = gq.shape[1]
    total = a[...].astype(F32) + b[...].astype(F32) + c[...].astype(F32) + d[...].astype(F32)
    gq[...] = total[:, 0:width]
    gk[...] = total[:, width : 2 * width]
    gv[...] = total[:, 2 * width : 3 * width]
    go[...] = total[:, 3 * width :]


def sum_over_seq(place, mine, other):
    cols = mine.shape[1]

    def sent(value, stage, d):
        pairs = []
        for i in range(32):
            core, x, y = i % 2, (i // 2) % 4, i // 8
            if stage == core:
                x = (x + d) % 4
            else:
                y = (y + d) % 4
            pairs.append((i, (y * 4 + x) * 2 + core))
        return lax.ppermute(value, "seq", pairs)

    got = lax.ppermute(other, "seq", [(i, i ^ 1) for i in range(32)])
    parts = [held((128, cols), BF16)] * 4
    parts = run(pair_sum_kernel, "pair_sum", 6, [place], [mine, got], parts)
    parts = [parts[0]] + [sent(parts[d], 0, d) for d in (1, 2, 3)]
    rows = [held((32, cols), BF16)] * 4
    scratch = [pltpu.VMEM((128, cols), BF16)]
    rows = run(row_sum_kernel, "row_sum", 4, [place], parts, rows, scratch)
    rows = [rows[0]] + [sent(rows[d], 1, d) for d in (1, 2, 3)]
    outputs = [held((32, cols // 4), F32)] * 4
    return run(last_sum_kernel, "last_sum", 4, [], rows, outputs)


def to_next(value):
    return lax.ppermute(value, "mp", [(i, (i + 1) % MP) for i in range(MP)])


def to_previous(value):
    return lax.ppermute(value, "mp", [((i + 1) % MP, i) for i in range(MP)])


def gather_shares(share):
    half = share.shape[0] // 2
    low, high = share[:half], share[half:]
    after_low, before_high = to_previous(low), to_next(high)
    after_high, before_low = to_previous(high), to_next(low)
    far_low, far_high = to_previous(after_low), to_next(before_high)
    return [share, after_low, after_high, far_low, far_high, before_low, before_high]


def turned_by(value, step):
    return lax.ppermute(value, "mp", [(i, (i + step) % MP) for i in range(MP)])


def sum_over_mp(terms):
    return [turned_by(term, step) for step, term in zip((1, 2, 3), terms)]


def exchange(to_left, to_right):
    count = lax.axis_size("seq")
    ends = count - 1
    from_left = lax.ppermute(to_right, "seq", [(i, i + 1) for i in range(ends)])
    from_right = lax.ppermute(to_left, "seq", [(i + 1, i) for i in range(ends)])
    return from_left, from_right


def tied(values, *others):
    flat, tree = jax.tree.flatten(values)
    flat = lax.optimization_barrier((*flat, *others))[: len(flat)]
    return jax.tree.unflatten(tree, flat)


def per_device(tokens, w_query, w_key, w_value, w_out, grad_out):
    count = lax.axis_size("seq")
    index = lax.axis_index("seq")
    me = jnp.stack([lax.axis_index("mp"), index & 1, (index >> 1) & 3, index >> 3])
    me = me.astype(jnp.int32)
    bias = jnp.stack(
        [
            jnp.where(index == 0, NEGATIVE, 0.0).astype(F32),
            jnp.where(index == count - 1, NEGATIVE, 0.0).astype(F32),
        ]
    )
    token_shares = gather_shares(tokens)
    near_grad = tied(grad_out, *(token_shares[n] for n in (1, 2, 5, 6)))
    far_grad = tied(grad_out, *token_shares)
    far = turned_by(far_grad, 2)
    grad_shares = [grad_out, to_previous(near_grad), far, to_next(near_grad)]
    inverse, q, kv, to_left, to_right, normed = project(
        me, token_shares, w_query, w_key, w_value
    )
    from_left, from_right = exchange(to_left, to_right)
    near_q = tied(q, grad_shares[1], grad_shares[3])
    inner_out, inner_stats = forward_inner(bias, near_q, kv)
    attended, stats = forward_edge(bias, q, kv, from_left, from_right, inner_out)
    out_own, *terms = out_terms(me, attended, w_out)
    out_received = sum_over_mp(terms)
    grad_shares = tied(grad_shares, out_own)
    d_att = cotangent(me, grad_shares, w_out)
    dq_f, d_kv, to_left, to_right = edge_backward(
        bias, stats, q, kv, from_left, from_right, d_att
    )
    from_left, from_right = exchange(to_left, to_right)
    dq_f = tied(dq_f, *out_received)
    d_query, d_kv = inner_backward(bias, inner_stats, q, kv, d_att, dq_f, d_kv)
    d_proj, dots, own, *terms = input_terms(
        me, d_query, d_kv, from_left, from_right, normed, w_query, w_key, w_value
    )
    received = sum_over_mp(terms)
    attn_out = finish_out(out_own, out_received)
    outer = outer_terms(grad_shares, attended)
    mine, other = inner_terms(me, normed, d_proj, outer)
    grad_tokens = finish_grad(own, received, tokens, inverse, dots)
    *weight_grads, grad_w_out = sum_over_seq(me, mine, other)
    return (attn_out, grad_tokens, *weight_grads, grad_w_out.T)


def solution(mesh):
    return jax.shard_map(
        per_device,
        mesh=mesh,
        in_specs=(
            P("seq", "mp"),
            P(None, "mp"),
            P(None, "mp"),
            P(None, "mp"),
            P("mp", None),
            P("seq", "mp"),
        ),
        out_specs=(
            P("seq", "mp"),
            P("seq", "mp"),
            P("seq", "mp"),
            P("seq", "mp"),
            P("seq", "mp"),
            P("mp", "seq"),
        ),
        check_vma=False,
    )
```

```python
import jax
import jax.numpy as jnp
from jax import lax
from jax.experimental import pallas as pl
from jax.experimental.pallas import tpu as pltpu
from jax.sharding import PartitionSpec as P

HD = 64
BLOCK = 256
LEVELS = 3
PAIR = 2 * HD
MP = 4
LANES = 128
DOT_ROWS = 16

EPSILON = 1e-06
NEGATIVE = -1e30

F32 = jnp.float32
BF16 = jnp.bfloat16

FIRST_EXT = (0, 6, 10)
EXT_BLOCKS = (6, 4, 3)
EXT_TOTAL = 13


def nn(left, right):
    return lax.dot_general(left, right, (((1,), (0,)), ((), ())), preferred_element_type=F32)


def nt(left, right):
    return lax.dot_general(left, right, (((1,), (1,)), ((), ())), preferred_element_type=F32)


def tn(left, right):
    return lax.dot_general(left, right, (((0,), (0,)), ((), ())), preferred_element_type=F32)


def pool_matrix(coarse, factor, value):
    shape = (coarse, coarse * factor)
    row = lax.broadcasted_iota(jnp.int32, shape, 0)
    low = row * factor
    col = lax.broadcasted_iota(jnp.int32, shape, 1)
    return jnp.where((col >= low) & (col < low + factor), value, 0.0).astype(BF16)


def spread_matrix(coarse, factor, value):
    shape = (coarse * factor, coarse)
    low = lax.broadcasted_iota(jnp.int32, shape, 1) * factor
    row = lax.broadcasted_iota(jnp.int32, shape, 0)
    return jnp.where((row >= low) & (row < low + factor), value, 0.0).astype(BF16)


def share_rows(me, step, width):
    return pl.ds(pl.multiple_of(((me + step) & (MP - 1)) * width, width), width)


SMALL = pl.CostEstimate(flops=10**6, bytes_accessed=10**4, transcendentals=0)
LARGE = pl.CostEstimate(flops=4 * 10**9, bytes_accessed=10**4, transcendentals=0)
LAST = pl.CostEstimate(flops=1 * 10**9, bytes_accessed=10**4, transcendentals=0)
SCALAR = pl.BlockSpec(memory_space=pltpu.SMEM)
RESIDENT = pl.BlockSpec(memory_space=pltpu.VMEM)


def held(shape, dtype):
    return jax.ShapeDtypeStruct(shape, dtype)


def run(kernel, name, limit_mib, scalars, inputs, outputs, scratch=(), cost=SMALL):
    return pl.pallas_call(
        kernel,
        in_specs=[SCALAR] * len(scalars) + [RESIDENT] * len(inputs),
        out_specs=[RESIDENT] * len(outputs),
        out_shape=outputs,
        scratch_shapes=list(scratch),
        compiler_params=pltpu.CompilerParams(vmem_limit_bytes=limit_mib * 2**20),
        cost_estimate=cost,
        name=name,
    )(*scalars, *inputs)


def block_rows(block):
    return slice(block * BLOCK, (block + 1) * BLOCK)


ALL_ROWS = 7 * BLOCK
LEVEL_BLOCK = (0, 4, 6)


def as_row(column):
    return jnp.broadcast_to(column, (column.shape[0], LANES)).T[0:1, :]


def as_column(row):
    return jnp.broadcast_to(row, (LANES, row.shape[1])).T[:, 0:1]


def project_kernel(
    place, t1a_any, t1b_any, t2a_any, t2b_any, t3a_any, t3b_any,
    t0_hbm, wq_hbm, wk_hbm, wv_hbm,
    inverse, q, kv, to_left, to_right, normed_hbm,
    t0, t1, t2, t3, wq, wk, wv, normed, in_sems, out_sems,
):
    me = place[0]
    width = t0.shape[1]
    low, high = pl.ds(0, 2 * BLOCK), pl.ds(2 * BLOCK, 2 * BLOCK)
    moves = [
        (t0_hbm, t0),
        (t1a_any, t1.at[low]),
        (t2a_any, t2.at[low]),
        (t3a_any, t3.at[low]),
        (t1b_any, t1.at[high]),
        (t2b_any, t2.at[high]),
        (t3b_any, t3.at[high]),
        (wq_hbm, wq),
        (wk_hbm, wk),
        (wv_hbm, wv),
    ]
    loads = [
        pltpu.make_async_copy(source, target, in_sems.at[n])
        for n, (source, target) in enumerate(moves)
    ]
    for load in loads:
        load.start()
    half = pool_matrix(BLOCK // 2, 2, 0.5)
    quarter = pool_matrix(BLOCK // 4, 4, 0.25)
    inverse[4:8, :] = jnp.zeros((4, BLOCK), F32)
    stores = []

    def normalise(step):
        if step in (0, 2):
            for load in loads[0:4] if step == 0 else loads[4:7]:
                load.wait()
        rows = block_rows(step)
        shares = [share[rows, :].astype(F32) for share in (t0, t1, t2, t3)]
        squares = shares[0] * shares[0]
        for share in shares[1:]:
            squares = squares + share * share
        total = jnp.sum(squares, axis=1, keepdims=True)
        inv = lax.rsqrt(total / (MP * width) + EPSILON)
        inverse[step : step + 1, :] = as_row(inv)
        parts = [(share * inv).astype(BF16) for share in shares]
        for r, part in enumerate(parts):
            normed[rows, r * width : (r + 1) * width] = part
        store = pltpu.make_async_copy(normed.at[rows], normed_hbm.at[rows], out_sems.at[step])
        store.start()
        stores.append(store)
        return parts

    def spread(step, parts):
        if step == 0:
            for load in loads[7:]:
                load.wait()
        rows = block_rows(step)
        sums = [None, None, None]
        for r, part in enumerate(parts):
            w_rows = share_rows(me, r, width)
            for n, w in enumerate((wq, wk, wv)):
                term = nn(part, w[w_rows, :])
                sums[n] = term if sums[n] is None else sums[n] + term
        fine = [x.astype(BF16) for x in sums]
        mid = [nn(half, x).astype(BF16) for x in fine]
        low = [nn(quarter, x).astype(BF16) for x in fine]
        mid_rows = slice(1024 + step * 128, 1024 + (step + 1) * 128)
        low_rows = slice(1536 + step * 64, 1536 + (step + 1) * 64)
        q[rows, :] = fine[0]
        q[mid_rows, :] = mid[0]
        q[low_rows, :] = low[0]
        edge_mid = slice(256 + (step % 2) * 128, 384 + (step % 2) * 128)
        edge_low = slice(512 + step * 64, 576 + step * 64)
        for n in range(2):
            kv[n, rows, :] = fine[1 + n]
            kv[n, mid_rows, :] = mid[1 + n]
            kv[n, low_rows, :] = low[1 + n]
            to_left[n, edge_low, :] = low[1 + n]
            to_right[n, edge_low, :] = low[1 + n]
            edge = to_left if step < 2 else to_right
            edge[n, edge_mid, :] = mid[1 + n]
            if step in (0, 3):
                edge[n, 0:BLOCK, :] = fine[1 + n]

    parts = normalise(0)
    for step in range(4):
        following = normalise(step + 1) if step < 3 else None
        spread(step, parts)
        parts = following
    for store in stores:
        store.wait()


def project(place, shares, wq, wk, wv):
    rows, width = shares[0].shape
    out = jax.ShapeDtypeStruct
    edge = out((2, 3 * BLOCK, width), BF16)
    anywhere = pl.BlockSpec(memory_space=pl.ANY)
    share = pltpu.VMEM((rows, width), BF16)
    fixed = [
        pltpu.with_memory_space_constraint(value, pltpu.HBM)
        for value in (*shares[1:], shares[0], wq, wk, wv)
    ]
    return pl.pallas_call(
        project_kernel,
        in_specs=[SCALAR] + [anywhere] * 10,
        out_specs=[RESIDENT] * 5 + [anywhere],
        out_shape=[
            out((8, width), F32),
            out((ALL_ROWS, width), BF16),
            out((2, ALL_ROWS, width), BF16),
            edge,
            edge,
            pltpu.HBM((rows, MP * width), BF16),
        ],
        scratch_shapes=[share] * 7
        + [
            pltpu.VMEM((rows, MP * width), BF16),
            pltpu.SemaphoreType.DMA((10,)),
            pltpu.SemaphoreType.DMA((4,)),
        ],
        compiler_params=pltpu.CompilerParams(vmem_limit_bytes=20 * 2**20),
        cost_estimate=SMALL,
        name="project",
    )(place, *fixed)


def cotangent_kernel(place, g0, g1, g2, g3, w_out, d_att):
    me = place[0]
    width = g0.shape[1]
    half = pool_matrix(BLOCK // 2, 2, 1.0)
    quarter = pool_matrix(BLOCK // 4, 4, 1.0)
    for step in range(4):
        rows = block_rows(step)
        total = None
        for r, share in enumerate((g0, g1, g2, g3)):
            term = nt(share[rows, :], w_out[:, share_rows(me, r, width)])
            total = term if total is None else total + term
        fine = total.astype(BF16)
        d_att[rows, :] = fine
        d_att[1024 + step * 128 : 1024 + (step + 1) * 128, :] = nn(half, fine).astype(BF16)
        d_att[1536 + step * 64 : 1536 + (step + 1) * 64, :] = nn(quarter, fine).astype(BF16)


def cotangent(place, shares, w_out):
    rows, width = shares[0].shape
    outputs = [held((ALL_ROWS, width), BF16)]
    return run(cotangent_kernel, "cotangent", 8, [place], [*shares, w_out], outputs)[0]


EDGE_UNITS = ((0, 0), (0, 3), (1, 0), (1, 1), (2, 0))
INNER_UNITS = ((0, 1), (0, 2))


def unit_keys(level, block):
    last = EXT_BLOCKS[level] - 1
    offsets = (0, 1, 2) if level == 0 else (0, 2)
    keys = []
    for offset in offsets:
        at = block + offset
        keys.append((at, 0 if at == 0 else 1 if at == last else None))
    return keys


def ext_rows(kv, from_left, from_right, n, level, at, lanes):
    if at == 0:
        return from_left[n, block_rows(level), lanes]
    if at == EXT_BLOCKS[level] - 1:
        return from_right[n, block_rows(level), lanes]
    return kv[n, block_rows(LEVEL_BLOCK[level] + at - 1), lanes]


def head_part(lane, head, rows):
    mine = (lane >= head * HD) & (lane < (head + 1) * HD)
    return jnp.where(mine, rows, 0.0).astype(BF16)


def unit_scores(keys, key_rows, query, bias_ref):
    scores = []
    for (_, bias), rows in zip(keys, key_rows):
        s = nt(rows, query)
        scores.append(s if bias is None else s + bias_ref[bias])
    return scores


def add_spread(target, block, factor, rows):
    if factor == 1:
        target[block_rows(block), :] = target[block_rows(block), :] + rows
        return
    for s in range(factor):
        spread = pl.ds(block * factor * BLOCK + s, BLOCK, factor)
        target[spread, :] = target[spread, :] + rows


def each_pair(width, body):
    def step(pair, _):
        body(pair, pl.ds(pl.multiple_of(pair * PAIR, PAIR), PAIR))
        return 0

    lax.fori_loop(0, width // PAIR, step, 0)


def head_part(lane, head, rows):
    mine = (lane >= head * HD) & (lane < (head + 1) * HD)
    return jnp.where(mine, rows, 0.0).astype(BF16)


def unit_scores(keys, key_rows, query, bias_ref):
    scores = []
    for (_, bias), rows in zip(keys, key_rows):
        s = nt(rows, query)
        scores.append(s if bias is None else s + bias_ref[bias])
    return scores


def add_spread(target, block, factor, rows):
    if factor == 1:
        target[block_rows(block), :] = target[block_rows(block), :] + rows
        return
    for s in range(factor):
        spread = pl.ds(block * factor * BLOCK + s, BLOCK, factor)
        target[spread, :] = target[spread, :] + rows


def forward_units(pair, lanes, units, bias_ref, q, kv, from_left, from_right, stats, vt, out_f):
    lane = lax.broadcasted_iota(jnp.int32, (BLOCK, PAIR), 1)
    done = set()
    for level, block in units:
        for at, _ in unit_keys(level, block):
            if (level, at) not in done:
                done.add((level, at))
                rows = ext_rows(kv, from_left, from_right, 1, level, at, lanes)
                vt[FIRST_EXT[level] + at] = rows.T

    def begin(u, head):
        level, block = units[u]
        keys = unit_keys(level, block)
        key_rows = [ext_rows(kv, from_left, from_right, 0, level, at, lanes) for at, _ in keys]
        q_rows = q[block_rows(LEVEL_BLOCK[level] + block), lanes] * HD ** (-0.5)
        return unit_scores(keys, key_rows, head_part(lane, head, q_rows), bias_ref)

    def finish(u, head, scores):
        level, block = units[u]
        top = scores[0].max(axis=0, keepdims=True)
        for s in scores[1:]:
            top = jnp.maximum(top, s.max(axis=0, keepdims=True))
        exps = [jnp.exp(s - top) for s in scores]
        total = exps[0].sum(axis=0, keepdims=True)
        for e in exps[1:]:
            total = total + e.sum(axis=0, keepdims=True)
        scale = 1.0 / total
        row = 4 * u + 2 * head
        stats[pair, row : row + 1, :] = top
        stats[pair, row + 1 : row + 2, :] = scale
        return [(e * scale).astype(BF16) for e in exps]

    outs = []

    def give(u, head, weights):
        level, block = units[u]
        part = slice(head * HD, (head + 1) * HD)
        o_t = None
        for (at, _), w in zip(unit_keys(level, block), weights):
            o = nn(vt[FIRST_EXT[level] + at, part, :], w)
            o_t = o if o_t is None else o_t + o
        outs.append(o_t)
        if head == 1:
            add_spread(out_f, block, 2**level, jnp.concatenate(outs, axis=0).T)
            outs.clear()

    items = [(u, head) for u in range(len(units)) for head in range(2)]
    scores, last = begin(*items[0]), None
    for n, item in enumerate(items):
        following = begin(*items[n + 1]) if n + 1 < len(items) else None
        if last is not None:
            give(*items[n - 1], last)
        last = finish(*item, scores)
        scores = following
    give(*items[-1], last)


def forward_inner_kernel(bias_ref, q, kv, out, stats, vt, out_f):
    def one(pair, lanes):
        out_f[...] = jnp.zeros_like(out_f)
        forward_units(pair, lanes, INNER_UNITS, bias_ref, q, kv, None, None, stats, vt, out_f)
        out[:, lanes] = out_f[BLOCK : 3 * BLOCK, :]

    each_pair(q.shape[1], one)


def forward_edge_kernel(
    bias_ref, q, kv, from_left, from_right, inner, attended, stats, vt, out_f
):
    def one(pair, lanes):
        out_f[0:BLOCK, :] = jnp.zeros((BLOCK, PAIR), F32)
        out_f[BLOCK : 3 * BLOCK, :] = inner[:, lanes]
        out_f[3 * BLOCK :, :] = jnp.zeros((BLOCK, PAIR), F32)
        forward_units(
            pair, lanes, EDGE_UNITS, bias_ref, q, kv, from_left, from_right, stats, vt, out_f
        )
        attended[:, lanes] = out_f[...].astype(BF16)

    each_pair(q.shape[1], one)


def backward_units(
    pair, lanes, units, bias_ref, q, kv, from_left, from_right, grads, stats, kt, dq_f, keep
):
    lane = lax.broadcasted_iota(jnp.int32, (BLOCK, PAIR), 1)
    done = set()
    for level, block in units:
        for at, _ in unit_keys(level, block):
            if (level, at) not in done:
                done.add((level, at))
                rows = ext_rows(kv, from_left, from_right, 0, level, at, lanes)
                kt[FIRST_EXT[level] + at] = rows.T

    def begin(u, head):
        level, block = units[u]
        keys = unit_keys(level, block)
        key_rows = [ext_rows(kv, from_left, from_right, 0, level, at, lanes) for at, _ in keys]
        value_rows = [ext_rows(kv, from_left, from_right, 1, level, at, lanes) for at, _ in keys]
        at = block_rows(LEVEL_BLOCK[level] + block)
        qm = head_part(lane, head, q[at, lanes] * HD ** (-0.5))
        am = head_part(lane, head, grads[at, lanes])
        scores = unit_scores(keys, key_rows, qm, bias_ref)
        return qm, am, scores, [nt(rows, am) for rows in value_rows]

    def finish(u, head, qm, am, scores, d_weights):
        level, block = units[u]
        row = 4 * u + 2 * head
        top, scale = stats[pair, row : row + 1, :], stats[pair, row + 1 : row + 2, :]
        probs = [jnp.exp(s - top) * scale for s in scores]
        dots = None
        for p, dw in zip(probs, d_weights):
            d = (p * dw).sum(axis=0, keepdims=True)
            dots = d if dots is None else dots + d
        weights = [p.astype(BF16) for p in probs]
        d_scores = [(p * (dw - dots)).astype(BF16) for p, dw in zip(probs, d_weights)]
        return qm, am, weights, d_scores

    first = []

    def give(u, head, qm, am, weights, d_scores):
        level, block = units[u]
        keys = unit_keys(level, block)
        part = slice(head * HD, (head + 1) * HD)
        d_values = [nn(w, am) for w in weights]
        d_keys = [nn(ds, qm) for ds in d_scores]
        dq_t = None
        for (at, _), ds in zip(keys, d_scores):
            g = nn(kt[FIRST_EXT[level] + at, part, :], ds)
            dq_t = g if dq_t is None else dq_t + g
        if head == 0:
            first.append((dq_t, d_keys, d_values))
            return
        dq_first, k_first, v_first = first.pop()
        for n, (at, _) in enumerate(keys):
            keep(0, level, at, k_first[n] + d_keys[n])
            keep(1, level, at, v_first[n] + d_values[n])
        dq = jnp.concatenate([dq_first, dq_t], axis=0).T * (HD ** (-0.5) / 2**level)
        add_spread(dq_f, block, 2**level, dq)

    items = [(u, head) for u in range(len(units)) for head in range(2)]
    ready, last = begin(*items[0]), None
    for n, item in enumerate(items):
        following = begin(*items[n + 1]) if n + 1 < len(items) else None
        if last is not None:
            give(*items[n - 1], *last)
        last = finish(*item, *ready)
        ready = following
    give(*items[-1], *last)


def edge_kernel(
    bias_ref, stats, q, kv, from_left, from_right, grads,
    dq_f, d_kv, to_left, to_right, kt, ext, dq_s, sums,
):
    def one(pair, lanes):
        dq_s[...] = jnp.zeros_like(dq_s)
        seen = set()

        def keep(n, level, at, rows):
            slot = FIRST_EXT[level] + at
            if (n, slot) in seen:
                ext[n, slot] = ext[n, slot] + rows
            else:
                seen.add((n, slot))
                ext[n, slot] = rows

        backward_units(
            pair, lanes, EDGE_UNITS, bias_ref, q, kv, from_left, from_right, grads, stats, kt,
            dq_s, keep,
        )
        dq_f[:, lanes] = dq_s[...]
        for n in range(2):
            for level in range(LEVELS):
                first, last = FIRST_EXT[level], FIRST_EXT[level] + EXT_BLOCKS[level] - 1
                to_left[n, block_rows(level), lanes] = ext[n, first].astype(BF16)
                to_right[n, block_rows(level), lanes] = ext[n, last].astype(BF16)
            for b in range(4):
                sums[block_rows(b), :] = ext[n, 1 + b]
            for b in range(2):
                add_spread(sums, b, 2, ext[n, FIRST_EXT[1] + 1 + b] * 0.5)
            d_kv[n, :, lanes] = sums[...]

    each_pair(q.shape[1], one)


def inner_units_kernel(bias_ref, stats, q, kv, grads, dq_in, d_kv_in, d_query, d_kv, kt, dq_s):
    def one(pair, lanes):
        dq_s[...] = dq_in[:, lanes]
        d_kv[:, :, lanes] = d_kv_in[:, :, lanes]

        def keep(n, level, at, rows):
            where = block_rows(at - 1)
            d_kv[n, where, lanes] = d_kv[n, where, lanes] + rows

        backward_units(
            pair, lanes, INNER_UNITS, bias_ref, q, kv, None, None, grads, stats, kt, dq_s, keep
        )
        d_query[:, lanes] = dq_s[...].astype(BF16)

    each_pair(q.shape[1], one)


def turned(count):
    return pltpu.VMEM((count, PAIR, BLOCK), BF16)


def forward_inner(bias, q, kv):
    width = q.shape[1]
    outputs = [held((2 * BLOCK, width), F32), held((width // PAIR, 8, BLOCK), F32)]
    scratch = [turned(EXT_BLOCKS[0]), pltpu.VMEM((4 * BLOCK, PAIR), F32)]
    return run(forward_inner_kernel, "forward_inner", 12, [bias], [q, kv], outputs, scratch, LARGE)


def forward_edge(bias, q, kv, from_left, from_right, inner):
    width = q.shape[1]
    inputs = [q, kv, from_left, from_right, inner]
    outputs = [held((4 * BLOCK, width), BF16), held((width // PAIR, 24, BLOCK), F32)]
    scratch = [turned(EXT_TOTAL), pltpu.VMEM((4 * BLOCK, PAIR), F32)]
    return run(forward_edge_kernel, "forward_edge", 12, [bias], inputs, outputs, scratch)


def edge_backward(bias, stats, q, kv, from_left, from_right, d_att):
    rows, width = 4 * BLOCK, q.shape[1]
    edge = held((2, 3 * BLOCK, width), BF16)
    inputs = [stats, q, kv, from_left, from_right, d_att]
    outputs = [held((rows, width), F32), held((2, rows, width), F32), edge, edge]
    scratch = [
        turned(EXT_TOTAL),
        pltpu.VMEM((2, EXT_TOTAL, BLOCK, PAIR), F32),
        pltpu.VMEM((rows, PAIR), F32),
        pltpu.VMEM((rows, PAIR), F32),
    ]
    return run(edge_kernel, "edge_backward", 20, [bias], inputs, outputs, scratch)


def inner_backward(bias, stats, q, kv, d_att, dq_f, d_kv):
    rows, width = 4 * BLOCK, q.shape[1]
    inputs = [stats, q, kv, d_att, dq_f, d_kv]
    outputs = [held((rows, width), BF16), held((2, rows, width), F32)]
    scratch = [turned(EXT_BLOCKS[0]), pltpu.VMEM((rows, PAIR), F32)]
    return run(inner_units_kernel, "inner_backward", 12, [bias], inputs, outputs, scratch)


def term_outputs(rows, width, extra=0):
    return [held((rows, width), BF16)] + [held((rows + extra, width), BF16)] * (MP - 1)


def out_terms_kernel(place, attended, w_out, *outs):
    me = place[0]
    width = attended.shape[1]
    for step in range(4):
        rows = attended[block_rows(step), :]
        for r, out in enumerate(outs):
            term = nn(rows, w_out[:, share_rows(me, r, width)])
            out[block_rows(step), :] = term.astype(BF16)


def out_terms(place, attended, w_out):
    outputs = term_outputs(*attended.shape)
    return run(out_terms_kernel, "out_terms", 8, [place], [attended, w_out], outputs)


def input_terms_kernel(
    place, d_query, d_kv, from_left, from_right, normed, wq, wk, wv, d_proj,
    dots, own, one, two, three, dot_rows,
):
    me = place[0]
    width = d_query.shape[1]
    half = spread_matrix(BLOCK // 2, 2, 0.5)
    quarter = spread_matrix(BLOCK // 4, 4, 0.25)
    dot_rows[12:16, :] = jnp.zeros((4, BLOCK), F32)
    for step in range(4):
        rows = block_rows(step)
        grads = [d_query[rows, :]]
        mid_rows = slice(256 + (step % 2) * 128, 384 + (step % 2) * 128)
        low_rows = slice(512 + step * 64, 576 + step * 64)
        near = from_left if step < 2 else from_right
        for n in range(2):
            total = d_kv[n, rows, :]
            if step in (0, 3):
                total = total + near[n, 0:BLOCK, :].astype(F32)
            total = total + nn(half, near[n, mid_rows, :])
            total = total + nn(quarter, from_left[n, low_rows, :])
            total = total + nn(quarter, from_right[n, low_rows, :])
            grads.append(total.astype(BF16))
        for n, grad in enumerate(grads[1:]):
            d_proj[rows, n * width : (n + 1) * width] = grad
        dot = None
        for r, out in enumerate((own, one, two, three)):
            at = share_rows(me, r, width)
            term = nt(grads[0], wq[at, :]) + nt(grads[1], wk[at, :]) + nt(grads[2], wv[at, :])
            term = term.astype(BF16)
            out[rows, :] = term
            part = term.astype(F32) * normed[rows, r * width : (r + 1) * width].astype(F32)
            dot = part if dot is None else dot + part
        dot = as_row(jnp.sum(dot, axis=1, keepdims=True))
        first = dot.astype(BF16).astype(F32)
        second = (dot - first).astype(BF16).astype(F32)
        for n, piece in enumerate((first, second, dot - first - second)):
            dot_rows[4 * n + step : 4 * n + step + 1, :] = piece
    pieces = dot_rows[...].astype(BF16)
    dots[...] = pieces
    for out in (one, two, three):
        out[4 * BLOCK :, :] = pieces


def input_terms(place, d_query, d_kv, from_left, from_right, normed, wq, wk, wv):
    rows, width = d_query.shape
    inputs = [d_query, d_kv, from_left, from_right, normed, wq, wk, wv]
    outputs = [held((rows, 2 * width), BF16), held((DOT_ROWS, width), BF16)]
    outputs += term_outputs(rows, width, DOT_ROWS)
    scratch = [pltpu.VMEM((DOT_ROWS, width), F32)]
    return run(input_terms_kernel, "input_terms", 16, [place], inputs, outputs, scratch)


def sum_terms(own, received, at):
    total = own[at, :].astype(F32)
    for term in received:
        total = total + term[at, :].astype(F32)
    return total


def finish_out_kernel(own, one, two, three, result):
    for b in range(4):
        at = block_rows(b)
        result[at, :] = sum_terms(own, (one, two, three), at).astype(BF16)


def finish_out(own, received):
    outputs = [held(own.shape, BF16)]
    return run(finish_out_kernel, "finish_out", 8, [], [own, *received], outputs)[0]


def finish_grad_kernel(own, one, two, three, tokens, inverse, dots, result):
    rows, width = own.shape
    pieces = dots[...].astype(F32)
    for term in (one, two, three):
        pieces = pieces + term[rows:, :].astype(F32)
    means = (pieces[0:4] + pieces[4:8] + pieces[8:12]) / (MP * width)
    for b in range(rows // BLOCK):
        at = block_rows(b)
        mean = as_column(means[b : b + 1, :])
        inv = as_column(inverse[b : b + 1, :])
        total = sum_terms(own, (one, two, three), at)
        result[at, :] = inv * (total - tokens[at, :].astype(F32) * inv * mean)


def finish_grad(own, received, tokens, inverse, dots):
    inputs = [own, *received, tokens, inverse, dots]
    outputs = [held(own.shape, F32)]
    return run(finish_grad_kernel, "finish_grad", 8, [], inputs, outputs, (), LAST)[0]


def early_kernel(g0, g1, g2, g3, attended, normed, d_query, outer, inner):
    width = g0.shape[1]
    rows = attended[...]
    for r, share in enumerate((g0, g1, g2, g3)):
        at = slice(r * width, (r + 1) * width)
        outer[at, :] = tn(share[...], rows).astype(BF16)
        inner[at, :] = tn(normed[:, at], d_query[...]).astype(BF16)


def early_terms(shares, attended, normed, d_query):
    width = attended.shape[1]
    inputs = [*shares, attended, normed, d_query]
    outputs = [held((MP * width, width), BF16)] * 2
    return run(early_kernel, "early_terms", 14, [], inputs, outputs, (), LARGE)


def inner_kernel(place, normed, d_proj, inner, outer, mine, other, rows_held):
    core = place[1]
    width = outer.shape[1]
    for block in range(MP):
        at = block_rows(block)
        rows_held[at, 0:width] = inner[at, :]
        rows_held[at, width : 3 * width] = tn(normed[:, at], d_proj[...]).astype(BF16)
        rows_held[at, 3 * width :] = outer[at, :]
        for n in range(width // 64):
            out = slice((4 * block + n) * 32, (4 * block + n + 1) * 32)
            first = block * width + n * 64
            mine[out, :] = rows_held[pl.ds(pl.multiple_of(first + core * 32, 32), 32), :]
            other[out, :] = rows_held[pl.ds(pl.multiple_of(first + 32 - core * 32, 32), 32), :]


def inner_terms(place, normed, d_proj, inner, outer):
    total = normed.shape[1]
    width = outer.shape[1]
    outputs = [held((total // 2, 4 * width), BF16)] * 2
    scratch = [pltpu.VMEM((total, 4 * width), BF16)]
    return run(inner_kernel, "inner_terms", 16, [place], [normed, d_proj, inner, outer], outputs, scratch)


def pair_sum_kernel(place, mine, got, *outs):
    z, core, x, y = place[0], place[1], place[2], place[3]
    for d, out in enumerate(outs):
        for n in range(4):
            chunk = jnp.where(core == 0, 4 * n + ((x + d) & 3), 4 * ((y + d - z + 4) & 3) + n)
            rows = pl.ds(pl.multiple_of(chunk * 32, 32), 32)
            total = mine[rows, :].astype(F32) + got[rows, :].astype(F32)
            out[32 * n : 32 * (n + 1), :] = total.astype(BF16)


def row_sum_kernel(place, a, b, c, d, *refs):
    *outs, total = refs
    z, core, x, y = place[0], place[1], place[2], place[3]
    first = jnp.where(core == 0, y - z + 4, x)
    total[...] = (
        a[...].astype(F32) + b[...].astype(F32) + c[...].astype(F32) + d[...].astype(F32)
    ).astype(BF16)
    for n, out in enumerate(outs):
        out[...] = total[pl.ds(pl.multiple_of(((first + n) & 3) * 32, 32), 32), :]


def last_sum_kernel(a, b, c, d, gq, gk, gv, go):
    width = gq.shape[1]
    total = a[...].astype(F32) + b[...].astype(F32) + c[...].astype(F32) + d[...].astype(F32)
    gq[...] = total[:, 0:width]
    gk[...] = total[:, width : 2 * width]
    gv[...] = total[:, 2 * width : 3 * width]
    go[...] = total[:, 3 * width :]


def sum_over_seq(place, mine, other):
    cols = mine.shape[1]

    def sent(value, stage, d):
        pairs = []
        for i in range(32):
            core, x, y = i % 2, (i // 2) % 4, i // 8
            if stage == core:
                x = (x + d) % 4
            else:
                y = (y + d) % 4
            pairs.append((i, (y * 4 + x) * 2 + core))
        return lax.ppermute(value, "seq", pairs)

    got = lax.ppermute(other, "seq", [(i, i ^ 1) for i in range(32)])
    parts = [held((128, cols), BF16)] * 4
    parts = run(pair_sum_kernel, "pair_sum", 6, [place], [mine, got], parts)
    parts = [parts[0]] + [sent(parts[d], 0, d) for d in (1, 2, 3)]
    rows = [held((32, cols), BF16)] * 4
    scratch = [pltpu.VMEM((128, cols), BF16)]
    rows = run(row_sum_kernel, "row_sum", 4, [place], parts, rows, scratch)
    rows = [rows[0]] + [sent(rows[d], 1, d) for d in (1, 2, 3)]
    outputs = [held((32, cols // 4), F32)] * 4
    return run(last_sum_kernel, "last_sum", 4, [], rows, outputs)


def to_next(value):
    return lax.ppermute(value, "mp", [(i, (i + 1) % MP) for i in range(MP)])


def to_previous(value):
    return lax.ppermute(value, "mp", [((i + 1) % MP, i) for i in range(MP)])


def gather_shares(share):
    half = share.shape[0] // 2
    low, high = share[:half], share[half:]
    after_low, before_high = to_previous(low), to_next(high)
    after_high, before_low = to_previous(high), to_next(low)
    far_low, far_high = to_previous(after_low), to_next(before_high)
    return [share, after_low, after_high, far_low, far_high, before_low, before_high]


def turned_by(value, step):
    return lax.ppermute(value, "mp", [(i, (i + step) % MP) for i in range(MP)])


def sum_over_mp(terms):
    return [turned_by(term, step) for step, term in zip((1, 2, 3), terms)]


def exchange(to_left, to_right):
    count = lax.axis_size("seq")
    ends = count - 1
    from_left = lax.ppermute(to_right, "seq", [(i, i + 1) for i in range(ends)])
    from_right = lax.ppermute(to_left, "seq", [(i + 1, i) for i in range(ends)])
    return from_left, from_right


def tied(values, *others):
    flat, tree = jax.tree.flatten(values)
    flat = lax.optimization_barrier((*flat, *others))[: len(flat)]
    return jax.tree.unflatten(tree, flat)


def per_device(tokens, w_query, w_key, w_value, w_out, grad_out):
    count = lax.axis_size("seq")
    index = lax.axis_index("seq")
    me = jnp.stack([lax.axis_index("mp"), index & 1, (index >> 1) & 3, index >> 3])
    me = me.astype(jnp.int32)
    bias = jnp.stack(
        [
            jnp.where(index == 0, NEGATIVE, 0.0).astype(F32),
            jnp.where(index == count - 1, NEGATIVE, 0.0).astype(F32),
        ]
    )
    token_shares = gather_shares(tokens)
    near_grad = tied(grad_out, *(token_shares[n] for n in (1, 2, 5, 6)))
    far_grad = tied(grad_out, *token_shares)
    far = turned_by(far_grad, 2)
    grad_shares = [grad_out, to_previous(near_grad), far, to_next(near_grad)]
    inverse, q, kv, to_left, to_right, normed = project(
        me, token_shares, w_query, w_key, w_value
    )
    from_left, from_right = exchange(to_left, to_right)
    near_q = tied(q, grad_shares[1], grad_shares[3])
    inner_out, inner_stats = forward_inner(bias, near_q, kv)
    attended, stats = forward_edge(bias, q, kv, from_left, from_right, inner_out)
    out_own, *terms = out_terms(me, attended, w_out)
    out_received = sum_over_mp(terms)
    grad_shares = tied(grad_shares, out_own)
    d_att = cotangent(me, grad_shares, w_out)
    dq_f, d_kv, to_left, to_right = edge_backward(
        bias, stats, q, kv, from_left, from_right, d_att
    )
    from_left, from_right = exchange(to_left, to_right)
    d_query, d_kv = inner_backward(bias, inner_stats, q, kv, d_att, dq_f, d_kv)
    attended = tied(attended, *out_received)
    outer, inner = early_terms(grad_shares, attended, normed, d_query)
    d_query = tied(d_query, outer)
    d_proj, dots, own, *terms = input_terms(
        me, d_query, d_kv, from_left, from_right, normed, w_query, w_key, w_value
    )
    received = sum_over_mp(terms)
    attn_out = finish_out(out_own, out_received)
    mine, other = inner_terms(me, normed, d_proj, inner, outer)
    grad_tokens = finish_grad(own, received, tokens, inverse, dots)
    *weight_grads, grad_w_out = sum_over_seq(me, mine, other)
    return (attn_out, grad_tokens, *weight_grads, grad_w_out.T)


def solution(mesh):
    return jax.shard_map(
        per_device,
        mesh=mesh,
        in_specs=(
            P("seq", "mp"),
            P(None, "mp"),
            P(None, "mp"),
            P(None, "mp"),
            P("mp", None),
            P("seq", "mp"),
        ),
        out_specs=(
            P("seq", "mp"),
            P("seq", "mp"),
            P("seq", "mp"),
            P("seq", "mp"),
            P("seq", "mp"),
            P("mp", "seq"),
        ),
        check_vma=False,
    )
```

```python
import jax
import jax.numpy as jnp
from jax import lax
from jax.experimental import pallas as pl
from jax.experimental.pallas import tpu as pltpu
from jax.sharding import PartitionSpec as P

HD = 64
BLOCK = 256
LEVELS = 3
PAIR = 2 * HD
MP = 4
LANES = 128
DOT_ROWS = 16

EPSILON = 1e-06
NEGATIVE = -1e30

F32 = jnp.float32
BF16 = jnp.bfloat16

FIRST_EXT = (0, 6, 10)
EXT_BLOCKS = (6, 4, 3)
EXT_TOTAL = 13


def nn(left, right):
    return lax.dot_general(left, right, (((1,), (0,)), ((), ())), preferred_element_type=F32)


def nt(left, right):
    return lax.dot_general(left, right, (((1,), (1,)), ((), ())), preferred_element_type=F32)


def tn(left, right):
    return lax.dot_general(left, right, (((0,), (0,)), ((), ())), preferred_element_type=F32)


def pool_matrix(coarse, factor, value):
    shape = (coarse, coarse * factor)
    row = lax.broadcasted_iota(jnp.int32, shape, 0)
    low = row * factor
    col = lax.broadcasted_iota(jnp.int32, shape, 1)
    return jnp.where((col >= low) & (col < low + factor), value, 0.0).astype(BF16)


def spread_matrix(coarse, factor, value):
    shape = (coarse * factor, coarse)
    low = lax.broadcasted_iota(jnp.int32, shape, 1) * factor
    row = lax.broadcasted_iota(jnp.int32, shape, 0)
    return jnp.where((row >= low) & (row < low + factor), value, 0.0).astype(BF16)


def share_rows(me, step, width):
    return pl.ds(pl.multiple_of(((me + step) & (MP - 1)) * width, width), width)


SMALL = pl.CostEstimate(flops=10**6, bytes_accessed=10**4, transcendentals=0)
LARGE = pl.CostEstimate(flops=4 * 10**9, bytes_accessed=10**4, transcendentals=0)
SCALAR = pl.BlockSpec(memory_space=pltpu.SMEM)
RESIDENT = pl.BlockSpec(memory_space=pltpu.VMEM)


def held(shape, dtype):
    return jax.ShapeDtypeStruct(shape, dtype)


def run(kernel, name, limit_mib, scalars, inputs, outputs, scratch=(), cost=SMALL):
    return pl.pallas_call(
        kernel,
        in_specs=[SCALAR] * len(scalars) + [RESIDENT] * len(inputs),
        out_specs=[RESIDENT] * len(outputs),
        out_shape=outputs,
        scratch_shapes=list(scratch),
        compiler_params=pltpu.CompilerParams(vmem_limit_bytes=limit_mib * 2**20),
        cost_estimate=cost,
        name=name,
    )(*scalars, *inputs)


def block_rows(block):
    return slice(block * BLOCK, (block + 1) * BLOCK)


ALL_ROWS = 7 * BLOCK
LEVEL_BLOCK = (0, 4, 6)


def as_row(column):
    return jnp.broadcast_to(column, (column.shape[0], LANES)).T[0:1, :]


def as_column(row):
    return jnp.broadcast_to(row, (LANES, row.shape[1])).T[:, 0:1]


def project_kernel(
    place, t1a_any, t1b_any, t2a_any, t2b_any, t3a_any, t3b_any,
    t0_hbm, wq_hbm, wk_hbm, wv_hbm,
    inverse, q, kv, to_left, to_right, normed_hbm, w_hbm,
    t0, t1, t2, t3, w, normed, in_sems, out_sems,
):
    me = place[0]
    width = t0.shape[1]
    low, high = pl.ds(0, 2 * BLOCK), pl.ds(2 * BLOCK, 2 * BLOCK)
    moves = [
        (t0_hbm, t0),
        (t1a_any, t1.at[low]),
        (t2a_any, t2.at[low]),
        (t3a_any, t3.at[low]),
        (t1b_any, t1.at[high]),
        (t2b_any, t2.at[high]),
        (t3b_any, t3.at[high]),
    ]
    for n, source in enumerate((wq_hbm, wk_hbm, wv_hbm)):
        for r in range(MP):
            target = w.at[pl.ds(r * width, width), pl.ds(n * width, width)]
            moves.append((source.at[share_rows(me, r, width), :], target))
    loads = [
        pltpu.make_async_copy(source, target, in_sems.at[n])
        for n, (source, target) in enumerate(moves)
    ]
    for load in loads:
        load.start()
    half = pool_matrix(BLOCK // 2, 2, 0.5)
    quarter = pool_matrix(BLOCK // 4, 4, 0.25)
    inverse[4:8, :] = jnp.zeros((4, BLOCK), F32)
    stores = []

    def normalise(step):
        if step in (0, 2):
            for load in loads[0:4] if step == 0 else loads[4:7]:
                load.wait()
        rows = block_rows(step)
        shares = [share[rows, :].astype(F32) for share in (t0, t1, t2, t3)]
        squares = shares[0] * shares[0]
        for share in shares[1:]:
            squares = squares + share * share
        total = jnp.sum(squares, axis=1, keepdims=True)
        inv = lax.rsqrt(total / (MP * width) + EPSILON)
        inverse[step : step + 1, :] = as_row(inv)
        parts = [(share * inv).astype(BF16) for share in shares]
        for r, part in enumerate(parts):
            normed[rows, r * width : (r + 1) * width] = part
        store = pltpu.make_async_copy(normed.at[rows], normed_hbm.at[rows], out_sems.at[step])
        store.start()
        stores.append(store)
        return jnp.concatenate(parts, axis=1)

    def spread(step, whole):
        if step == 0:
            for load in loads[7:]:
                load.wait()
            store = pltpu.make_async_copy(w, w_hbm, out_sems.at[4])
            store.start()
            stores.append(store)
        rows = block_rows(step)
        fine = [nn(whole, w[:, n * width : (n + 1) * width]).astype(BF16) for n in range(3)]
        mid = [nn(half, x).astype(BF16) for x in fine]
        low = [nn(quarter, x).astype(BF16) for x in fine]
        mid_rows = slice(1024 + step * 128, 1024 + (step + 1) * 128)
        low_rows = slice(1536 + step * 64, 1536 + (step + 1) * 64)
        q[rows, :] = fine[0]
        q[mid_rows, :] = mid[0]
        q[low_rows, :] = low[0]
        edge_mid = slice(256 + (step % 2) * 128, 384 + (step % 2) * 128)
        edge_low = slice(512 + step * 64, 576 + step * 64)
        for n in range(2):
            kv[n, rows, :] = fine[1 + n]
            kv[n, mid_rows, :] = mid[1 + n]
            kv[n, low_rows, :] = low[1 + n]
            to_left[n, edge_low, :] = low[1 + n]
            to_right[n, edge_low, :] = low[1 + n]
            edge = to_left if step < 2 else to_right
            edge[n, edge_mid, :] = mid[1 + n]
            if step in (0, 3):
                edge[n, 0:BLOCK, :] = fine[1 + n]

    parts = normalise(0)
    for step in range(4):
        following = normalise(step + 1) if step < 3 else None
        spread(step, parts)
        parts = following
    for store in stores:
        store.wait()


def project(place, shares, wq, wk, wv):
    rows, width = shares[0].shape
    out = jax.ShapeDtypeStruct
    edge = out((2, 3 * BLOCK, width), BF16)
    anywhere = pl.BlockSpec(memory_space=pl.ANY)
    share = pltpu.VMEM((rows, width), BF16)
    fixed = [
        pltpu.with_memory_space_constraint(value, pltpu.HBM)
        for value in (*shares[1:], shares[0], wq, wk, wv)
    ]
    return pl.pallas_call(
        project_kernel,
        in_specs=[SCALAR] + [anywhere] * 10,
        out_specs=[RESIDENT] * 5 + [anywhere] * 2,
        out_shape=[
            out((8, width), F32),
            out((ALL_ROWS, width), BF16),
            out((2, ALL_ROWS, width), BF16),
            edge,
            edge,
            pltpu.HBM((rows, MP * width), BF16),
            pltpu.HBM((MP * width, 3 * width), BF16),
        ],
        scratch_shapes=[share] * 4
        + [
            pltpu.VMEM((MP * width, 3 * width), BF16),
            pltpu.VMEM((rows, MP * width), BF16),
            pltpu.SemaphoreType.DMA((19,)),
            pltpu.SemaphoreType.DMA((5,)),
        ],
        compiler_params=pltpu.CompilerParams(vmem_limit_bytes=20 * 2**20),
        cost_estimate=SMALL,
        name="project",
    )(place, *fixed)


def cotangent_kernel(place, g0, g1, g2, g3, w_out, d_att):
    me = place[0]
    width = g0.shape[1]
    half = pool_matrix(BLOCK // 2, 2, 1.0)
    quarter = pool_matrix(BLOCK // 4, 4, 1.0)
    columns = [w_out[:, share_rows(me, r, width)] for r in range(MP)]
    turned_w = jnp.concatenate(columns, axis=1)
    for step in range(4):
        rows = block_rows(step)
        shares = jnp.concatenate([share[rows, :] for share in (g0, g1, g2, g3)], axis=1)
        fine = nt(shares, turned_w).astype(BF16)
        d_att[rows, :] = fine
        d_att[1024 + step * 128 : 1024 + (step + 1) * 128, :] = nn(half, fine).astype(BF16)
        d_att[1536 + step * 64 : 1536 + (step + 1) * 64, :] = nn(quarter, fine).astype(BF16)


def cotangent(place, shares, w_out):
    rows, width = shares[0].shape
    outputs = [held((ALL_ROWS, width), BF16)]
    return run(cotangent_kernel, "cotangent", 10, [place], [*shares, w_out], outputs, (), LARGE)[0]


EDGE_UNITS = ((0, 0), (0, 3), (1, 0), (1, 1), (2, 0))
INNER_UNITS = ((0, 1), (0, 2))


def unit_keys(level, block):
    last = EXT_BLOCKS[level] - 1
    offsets = (0, 1, 2) if level == 0 else (0, 2)
    keys = []
    for offset in offsets:
        at = block + offset
        keys.append((at, 0 if at == 0 else 1 if at == last else None))
    return keys


def ext_rows(kv, from_left, from_right, n, level, at, lanes):
    if at == 0:
        return from_left[n, block_rows(level), lanes]
    if at == EXT_BLOCKS[level] - 1:
        return from_right[n, block_rows(level), lanes]
    return kv[n, block_rows(LEVEL_BLOCK[level] + at - 1), lanes]


def head_part(lane, head, rows):
    mine = (lane >= head * HD) & (lane < (head + 1) * HD)
    return jnp.where(mine, rows, 0.0).astype(BF16)


def unit_scores(keys, key_rows, query, bias_ref):
    scores = []
    for (_, bias), rows in zip(keys, key_rows):
        s = nt(rows, query)
        scores.append(s if bias is None else s + bias_ref[bias])
    return scores


def add_spread(target, block, factor, rows):
    if factor == 1:
        target[block_rows(block), :] = target[block_rows(block), :] + rows
        return
    for s in range(factor):
        spread = pl.ds(block * factor * BLOCK + s, BLOCK, factor)
        target[spread, :] = target[spread, :] + rows


def each_pair(width, body):
    def step(pair, _):
        body(pair, pl.ds(pl.multiple_of(pair * PAIR, PAIR), PAIR))
        return 0

    lax.fori_loop(0, width // PAIR, step, 0)


def head_part(lane, head, rows):
    mine = (lane >= head * HD) & (lane < (head + 1) * HD)
    return jnp.where(mine, rows, 0.0).astype(BF16)


def unit_scores(keys, key_rows, query, bias_ref):
    scores = []
    for (_, bias), rows in zip(keys, key_rows):
        s = nt(rows, query)
        scores.append(s if bias is None else s + bias_ref[bias])
    return scores


def add_spread(target, block, factor, rows):
    if factor == 1:
        target[block_rows(block), :] = target[block_rows(block), :] + rows
        return
    for s in range(factor):
        spread = pl.ds(block * factor * BLOCK + s, BLOCK, factor)
        target[spread, :] = target[spread, :] + rows


def forward_units(pair, lanes, units, bias_ref, q, kv, from_left, from_right, stats, vt, out_f):
    lane = lax.broadcasted_iota(jnp.int32, (BLOCK, PAIR), 1)
    done = set()
    for level, block in units:
        for at, _ in unit_keys(level, block):
            if (level, at) not in done:
                done.add((level, at))
                rows = ext_rows(kv, from_left, from_right, 1, level, at, lanes)
                vt[FIRST_EXT[level] + at] = rows.T

    def begin(u, head):
        level, block = units[u]
        keys = unit_keys(level, block)
        key_rows = [ext_rows(kv, from_left, from_right, 0, level, at, lanes) for at, _ in keys]
        q_rows = q[block_rows(LEVEL_BLOCK[level] + block), lanes] * HD ** (-0.5)
        return unit_scores(keys, key_rows, head_part(lane, head, q_rows), bias_ref)

    def finish(u, head, scores):
        level, block = units[u]
        top = scores[0].max(axis=0, keepdims=True)
        for s in scores[1:]:
            top = jnp.maximum(top, s.max(axis=0, keepdims=True))
        exps = [jnp.exp(s - top) for s in scores]
        total = exps[0].sum(axis=0, keepdims=True)
        for e in exps[1:]:
            total = total + e.sum(axis=0, keepdims=True)
        scale = 1.0 / total
        row = 4 * u + 2 * head
        stats[pair, row : row + 1, :] = top
        stats[pair, row + 1 : row + 2, :] = scale
        return [(e * scale).astype(BF16) for e in exps]

    outs = []

    def give(u, head, weights):
        level, block = units[u]
        part = slice(head * HD, (head + 1) * HD)
        o_t = None
        for (at, _), w in zip(unit_keys(level, block), weights):
            o = nn(vt[FIRST_EXT[level] + at, part, :], w)
            o_t = o if o_t is None else o_t + o
        outs.append(o_t)
        if head == 1:
            add_spread(out_f, block, 2**level, jnp.concatenate(outs, axis=0).T)
            outs.clear()

    items = [(u, head) for u in range(len(units)) for head in range(2)]
    scores, last = begin(*items[0]), None
    for n, item in enumerate(items):
        following = begin(*items[n + 1]) if n + 1 < len(items) else None
        if last is not None:
            give(*items[n - 1], last)
        last = finish(*item, scores)
        scores = following
    give(*items[-1], last)


def forward_inner_kernel(bias_ref, q, kv, out, stats, vt, out_f):
    def one(pair, lanes):
        out_f[...] = jnp.zeros_like(out_f)
        forward_units(pair, lanes, INNER_UNITS, bias_ref, q, kv, None, None, stats, vt, out_f)
        out[:, lanes] = out_f[BLOCK : 3 * BLOCK, :]

    each_pair(q.shape[1], one)


def forward_edge_kernel(
    bias_ref, q, kv, from_left, from_right, inner, attended, stats, vt, out_f
):
    def one(pair, lanes):
        out_f[0:BLOCK, :] = jnp.zeros((BLOCK, PAIR), F32)
        out_f[BLOCK : 3 * BLOCK, :] = inner[:, lanes]
        out_f[3 * BLOCK :, :] = jnp.zeros((BLOCK, PAIR), F32)
        forward_units(
            pair, lanes, EDGE_UNITS, bias_ref, q, kv, from_left, from_right, stats, vt, out_f
        )
        attended[:, lanes] = out_f[...].astype(BF16)

    each_pair(q.shape[1], one)


def backward_units(
    pair, lanes, units, bias_ref, q, kv, from_left, from_right, grads, stats, kt, dq_f, keep
):
    lane = lax.broadcasted_iota(jnp.int32, (BLOCK, PAIR), 1)
    done = set()
    for level, block in units:
        for at, _ in unit_keys(level, block):
            if (level, at) not in done:
                done.add((level, at))
                rows = ext_rows(kv, from_left, from_right, 0, level, at, lanes)
                kt[FIRST_EXT[level] + at] = rows.T

    def begin(u, head):
        level, block = units[u]
        keys = unit_keys(level, block)
        key_rows = [ext_rows(kv, from_left, from_right, 0, level, at, lanes) for at, _ in keys]
        value_rows = [ext_rows(kv, from_left, from_right, 1, level, at, lanes) for at, _ in keys]
        at = block_rows(LEVEL_BLOCK[level] + block)
        qm = head_part(lane, head, q[at, lanes] * HD ** (-0.5))
        am = head_part(lane, head, grads[at, lanes])
        scores = unit_scores(keys, key_rows, qm, bias_ref)
        return qm, am, scores, [nt(rows, am) for rows in value_rows]

    def finish(u, head, qm, am, scores, d_weights):
        level, block = units[u]
        row = 4 * u + 2 * head
        top, scale = stats[pair, row : row + 1, :], stats[pair, row + 1 : row + 2, :]
        probs = [jnp.exp(s - top) * scale for s in scores]
        dots = None
        for p, dw in zip(probs, d_weights):
            d = (p * dw).sum(axis=0, keepdims=True)
            dots = d if dots is None else dots + d
        weights = [p.astype(BF16) for p in probs]
        d_scores = [(p * (dw - dots)).astype(BF16) for p, dw in zip(probs, d_weights)]
        return qm, am, weights, d_scores

    first = []

    def give(u, head, qm, am, weights, d_scores):
        level, block = units[u]
        keys = unit_keys(level, block)
        part = slice(head * HD, (head + 1) * HD)
        d_values = [nn(w, am) for w in weights]
        d_keys = [nn(ds, qm) for ds in d_scores]
        dq_t = None
        for (at, _), ds in zip(keys, d_scores):
            g = nn(kt[FIRST_EXT[level] + at, part, :], ds)
            dq_t = g if dq_t is None else dq_t + g
        if head == 0:
            first.append((dq_t, d_keys, d_values))
            return
        dq_first, k_first, v_first = first.pop()
        for n, (at, _) in enumerate(keys):
            keep(0, level, at, k_first[n] + d_keys[n])
            keep(1, level, at, v_first[n] + d_values[n])
        dq = jnp.concatenate([dq_first, dq_t], axis=0).T * (HD ** (-0.5) / 2**level)
        add_spread(dq_f, block, 2**level, dq)

    items = [(u, head) for u in range(len(units)) for head in range(2)]
    ready, last = begin(*items[0]), None
    for n, item in enumerate(items):
        following = begin(*items[n + 1]) if n + 1 < len(items) else None
        if last is not None:
            give(*items[n - 1], *last)
        last = finish(*item, *ready)
        ready = following
    give(*items[-1], *last)


def edge_kernel(
    bias_ref, stats, q, kv, from_left, from_right, grads,
    dq_f, d_kv, to_left, to_right, kt, ext, dq_s, sums,
):
    def one(pair, lanes):
        dq_s[...] = jnp.zeros_like(dq_s)
        seen = set()

        def keep(n, level, at, rows):
            slot = FIRST_EXT[level] + at
            if (n, slot) in seen:
                ext[n, slot] = ext[n, slot] + rows
            else:
                seen.add((n, slot))
                ext[n, slot] = rows

        backward_units(
            pair, lanes, EDGE_UNITS, bias_ref, q, kv, from_left, from_right, grads, stats, kt,
            dq_s, keep,
        )
        dq_f[:, lanes] = dq_s[...]
        for n in range(2):
            for level in range(LEVELS):
                first, last = FIRST_EXT[level], FIRST_EXT[level] + EXT_BLOCKS[level] - 1
                to_left[n, block_rows(level), lanes] = ext[n, first].astype(BF16)
                to_right[n, block_rows(level), lanes] = ext[n, last].astype(BF16)
            for b in range(4):
                sums[block_rows(b), :] = ext[n, 1 + b]
            for b in range(2):
                add_spread(sums, b, 2, ext[n, FIRST_EXT[1] + 1 + b] * 0.5)
            d_kv[n, :, lanes] = sums[...]

    each_pair(q.shape[1], one)


def inner_units_kernel(bias_ref, stats, q, kv, grads, dq_in, d_kv_in, d_query, d_kv, kt, dq_s):
    def one(pair, lanes):
        dq_s[...] = dq_in[:, lanes]
        d_kv[:, :, lanes] = d_kv_in[:, :, lanes]

        def keep(n, level, at, rows):
            where = block_rows(at - 1)
            d_kv[n, where, lanes] = d_kv[n, where, lanes] + rows

        backward_units(
            pair, lanes, INNER_UNITS, bias_ref, q, kv, None, None, grads, stats, kt, dq_s, keep
        )
        d_query[:, lanes] = dq_s[...].astype(BF16)

    each_pair(q.shape[1], one)


def turned(count):
    return pltpu.VMEM((count, PAIR, BLOCK), BF16)


def forward_inner(bias, q, kv):
    width = q.shape[1]
    outputs = [held((2 * BLOCK, width), F32), held((width // PAIR, 8, BLOCK), F32)]
    scratch = [turned(EXT_BLOCKS[0]), pltpu.VMEM((4 * BLOCK, PAIR), F32)]
    return run(forward_inner_kernel, "forward_inner", 12, [bias], [q, kv], outputs, scratch)


def forward_edge(bias, q, kv, from_left, from_right, inner):
    width = q.shape[1]
    inputs = [q, kv, from_left, from_right, inner]
    outputs = [held((4 * BLOCK, width), BF16), held((width // PAIR, 24, BLOCK), F32)]
    scratch = [turned(EXT_TOTAL), pltpu.VMEM((4 * BLOCK, PAIR), F32)]
    return run(forward_edge_kernel, "forward_edge", 12, [bias], inputs, outputs, scratch)


def edge_backward(bias, stats, q, kv, from_left, from_right, d_att):
    rows, width = 4 * BLOCK, q.shape[1]
    edge = held((2, 3 * BLOCK, width), BF16)
    inputs = [stats, q, kv, from_left, from_right, d_att]
    outputs = [held((rows, width), F32), held((2, rows, width), F32), edge, edge]
    scratch = [
        turned(EXT_TOTAL),
        pltpu.VMEM((2, EXT_TOTAL, BLOCK, PAIR), F32),
        pltpu.VMEM((rows, PAIR), F32),
        pltpu.VMEM((rows, PAIR), F32),
    ]
    return run(edge_kernel, "edge_backward", 20, [bias], inputs, outputs, scratch)


def inner_backward(bias, stats, q, kv, d_att, dq_f, d_kv):
    rows, width = 4 * BLOCK, q.shape[1]
    inputs = [stats, q, kv, d_att, dq_f, d_kv]
    outputs = [held((rows, width), BF16), held((2, rows, width), F32)]
    scratch = [turned(EXT_BLOCKS[0]), pltpu.VMEM((rows, PAIR), F32)]
    return run(inner_units_kernel, "inner_backward", 12, [bias], inputs, outputs, scratch)


def term_outputs(rows, width, extra=0):
    return [held((rows, width), BF16)] + [held((rows + extra, width), BF16)] * (MP - 1)


def out_terms_kernel(place, attended, w_out, *outs):
    me = place[0]
    width = attended.shape[1]
    for step in range(4):
        rows = attended[block_rows(step), :]
        for r, out in enumerate(outs):
            term = nn(rows, w_out[:, share_rows(me, r, width)])
            out[block_rows(step), :] = term.astype(BF16)


def out_terms(place, attended, w_out):
    outputs = term_outputs(*attended.shape)
    return run(out_terms_kernel, "out_terms", 8, [place], [attended, w_out], outputs)


def input_terms_kernel(
    d_query, d_kv, from_left, from_right, normed, w, d_proj,
    dots, own, one, two, three, dot_rows,
):
    width = d_query.shape[1]
    half = spread_matrix(BLOCK // 2, 2, 0.5)
    quarter = spread_matrix(BLOCK // 4, 4, 0.25)
    dot_rows[12:16, :] = jnp.zeros((4, BLOCK), F32)
    for step in range(4):
        rows = block_rows(step)
        grads = [d_query[rows, :]]
        mid_rows = slice(256 + (step % 2) * 128, 384 + (step % 2) * 128)
        low_rows = slice(512 + step * 64, 576 + step * 64)
        near = from_left if step < 2 else from_right
        for n in range(2):
            total = d_kv[n, rows, :]
            if step in (0, 3):
                total = total + near[n, 0:BLOCK, :].astype(F32)
            total = total + nn(half, near[n, mid_rows, :])
            total = total + nn(quarter, from_left[n, low_rows, :])
            total = total + nn(quarter, from_right[n, low_rows, :])
            grads.append(total.astype(BF16))
        for n, grad in enumerate(grads[1:]):
            d_proj[rows, n * width : (n + 1) * width] = grad
        dot = None
        every = jnp.concatenate(grads, axis=1)
        for r, out in enumerate((own, one, two, three)):
            term = nt(every, w[r * width : (r + 1) * width, :]).astype(BF16)
            out[rows, :] = term
            part = term.astype(F32) * normed[rows, r * width : (r + 1) * width].astype(F32)
            dot = part if dot is None else dot + part
        dot = as_row(jnp.sum(dot, axis=1, keepdims=True))
        first = dot.astype(BF16).astype(F32)
        second = (dot - first).astype(BF16).astype(F32)
        for n, piece in enumerate((first, second, dot - first - second)):
            dot_rows[4 * n + step : 4 * n + step + 1, :] = piece
    pieces = dot_rows[...].astype(BF16)
    dots[...] = pieces
    for out in (one, two, three):
        out[4 * BLOCK :, :] = pieces


def input_terms(d_query, d_kv, from_left, from_right, normed, w):
    rows, width = d_query.shape
    inputs = [d_query, d_kv, from_left, from_right, normed, w]
    outputs = [held((rows, 2 * width), BF16), held((DOT_ROWS, width), BF16)]
    outputs += term_outputs(rows, width, DOT_ROWS)
    scratch = [pltpu.VMEM((DOT_ROWS, width), F32)]
    return run(input_terms_kernel, "input_terms", 16, [], inputs, outputs, scratch)


def sum_terms(own, received, at):
    total = own[at, :].astype(F32)
    for term in received:
        total = total + term[at, :].astype(F32)
    return total


def finish_out_kernel(own, one, two, three, result):
    for b in range(4):
        at = block_rows(b)
        result[at, :] = sum_terms(own, (one, two, three), at).astype(BF16)


def finish_out(own, received):
    outputs = [held(own.shape, BF16)]
    return run(finish_out_kernel, "finish_out", 8, [], [own, *received], outputs)[0]


def near_sum_kernel(own, one, three, dots, total, pieces):
    rows = own.shape[0]
    for b in range(rows // BLOCK):
        at = block_rows(b)
        total[at, :] = sum_terms(own, (one, three), at)
    pieces[...] = dots[...].astype(F32) + one[rows:, :].astype(F32) + three[rows:, :].astype(F32)


def finish_grad_kernel(near, pieces, far, tokens, inverse, result):
    rows, width = near.shape
    every = pieces[...] + far[rows:, :].astype(F32)
    means = (every[0:4] + every[4:8] + every[8:12]) / (MP * width)
    for b in range(rows // BLOCK):
        at = block_rows(b)
        mean = as_column(means[b : b + 1, :])
        inv = as_column(inverse[b : b + 1, :])
        total = near[at, :] + far[at, :].astype(F32)
        result[at, :] = inv * (total - tokens[at, :].astype(F32) * inv * mean)


def finish_grad(own, received, tokens, inverse, dots):
    one, two, three = received
    outputs = [held(own.shape, F32), held(dots.shape, F32)]
    inputs = [own, one, three, dots]
    near, pieces = run(near_sum_kernel, "near_sum", 8, [], inputs, outputs, (), LARGE)
    inputs = [near, pieces, two, tokens, inverse]
    outputs = [held(own.shape, F32)]
    return run(finish_grad_kernel, "finish_grad", 8, [], inputs, outputs)[0]


def early_kernel(g0, g1, g2, g3, attended, normed, d_query, outer, inner):
    width = g0.shape[1]
    rows = attended[...]
    for r, share in enumerate((g0, g1, g2, g3)):
        at = slice(r * width, (r + 1) * width)
        outer[at, :] = tn(share[...], rows).astype(BF16)
        inner[at, :] = tn(normed[:, at], d_query[...]).astype(BF16)


def early_terms(shares, attended, normed, d_query):
    width = attended.shape[1]
    inputs = [*shares, attended, normed, d_query]
    outputs = [held((MP * width, width), BF16)] * 2
    return run(early_kernel, "early_terms", 14, [], inputs, outputs, (), LARGE)


def inner_kernel(place, normed, d_proj, inner, outer, mine, other, rows_held):
    core = place[1]
    width = outer.shape[1]
    for block in range(MP):
        at = block_rows(block)
        rows_held[at, 0:width] = inner[at, :]
        rows_held[at, width : 3 * width] = tn(normed[:, at], d_proj[...]).astype(BF16)
        rows_held[at, 3 * width :] = outer[at, :]
        for n in range(width // 64):
            out = slice((4 * block + n) * 32, (4 * block + n + 1) * 32)
            first = block * width + n * 64
            mine[out, :] = rows_held[pl.ds(pl.multiple_of(first + core * 32, 32), 32), :]
            other[out, :] = rows_held[pl.ds(pl.multiple_of(first + 32 - core * 32, 32), 32), :]


def inner_terms(place, normed, d_proj, inner, outer):
    total = normed.shape[1]
    width = outer.shape[1]
    outputs = [held((total // 2, 4 * width), BF16)] * 2
    scratch = [pltpu.VMEM((total, 4 * width), BF16)]
    return run(inner_kernel, "inner_terms", 16, [place], [normed, d_proj, inner, outer], outputs, scratch)


def pair_sum_kernel(place, mine, got, *outs):
    z, core, x, y = place[0], place[1], place[2], place[3]
    for d, out in enumerate(outs):
        for n in range(4):
            chunk = jnp.where(core == 0, 4 * n + ((x + d) & 3), 4 * ((y + d - z + 4) & 3) + n)
            rows = pl.ds(pl.multiple_of(chunk * 32, 32), 32)
            total = mine[rows, :].astype(F32) + got[rows, :].astype(F32)
            out[32 * n : 32 * (n + 1), :] = total.astype(BF16)


def row_sum_kernel(place, a, b, c, d, *refs):
    *outs, total = refs
    z, core, x, y = place[0], place[1], place[2], place[3]
    first = jnp.where(core == 0, y - z + 4, x)
    total[...] = (
        a[...].astype(F32) + b[...].astype(F32) + c[...].astype(F32) + d[...].astype(F32)
    ).astype(BF16)
    for n, out in enumerate(outs):
        out[...] = total[pl.ds(pl.multiple_of(((first + n) & 3) * 32, 32), 32), :]


def last_sum_kernel(a, b, c, d, gq, gk, gv, go):
    width = gq.shape[1]
    total = a[...].astype(F32) + b[...].astype(F32) + c[...].astype(F32) + d[...].astype(F32)
    gq[...] = total[:, 0:width]
    gk[...] = total[:, width : 2 * width]
    gv[...] = total[:, 2 * width : 3 * width]
    go[...] = total[:, 3 * width :]


def sum_over_core(place, mine, other):
    got = lax.ppermute(other, "seq", [(i, i ^ 1) for i in range(32)])
    parts = [held((128, mine.shape[1]), BF16)] * 4
    return run(pair_sum_kernel, "pair_sum", 6, [place], [mine, got], parts)


def sum_over_seq(place, parts):
    cols = parts[0].shape[1]

    def sent(value, stage, d):
        pairs = []
        for i in range(32):
            core, x, y = i % 2, (i // 2) % 4, i // 8
            if stage == core:
                x = (x + d) % 4
            else:
                y = (y + d) % 4
            pairs.append((i, (y * 4 + x) * 2 + core))
        return lax.ppermute(value, "seq", pairs)

    parts = [parts[0]] + [sent(parts[d], 0, d) for d in (1, 2, 3)]
    rows = [held((32, cols), BF16)] * 4
    scratch = [pltpu.VMEM((128, cols), BF16)]
    rows = run(row_sum_kernel, "row_sum", 4, [place], parts, rows, scratch)
    rows = [rows[0]] + [sent(rows[d], 1, d) for d in (1, 2, 3)]
    outputs = [held((32, cols // 4), F32)] * 4
    return run(last_sum_kernel, "last_sum", 4, [], rows, outputs)


def to_next(value):
    return lax.ppermute(value, "mp", [(i, (i + 1) % MP) for i in range(MP)])


def to_previous(value):
    return lax.ppermute(value, "mp", [((i + 1) % MP, i) for i in range(MP)])


def gather_shares(share):
    half = share.shape[0] // 2
    low, high = share[:half], share[half:]
    after_low, before_high = to_previous(low), to_next(high)
    after_high, before_low = to_previous(high), to_next(low)
    far_low, far_high = to_previous(after_low), to_next(before_high)
    return [share, after_low, after_high, far_low, far_high, before_low, before_high]


def turned_by(value, step):
    return lax.ppermute(value, "mp", [(i, (i + step) % MP) for i in range(MP)])


def sum_over_mp(terms):
    return [turned_by(term, step) for step, term in zip((1, 2, 3), terms)]


def exchange(to_left, to_right):
    count = lax.axis_size("seq")
    ends = count - 1
    from_left = lax.ppermute(to_right, "seq", [(i, i + 1) for i in range(ends)])
    from_right = lax.ppermute(to_left, "seq", [(i + 1, i) for i in range(ends)])
    return from_left, from_right


def tied(values, *others):
    flat, tree = jax.tree.flatten(values)
    flat = lax.optimization_barrier((*flat, *others))[: len(flat)]
    return jax.tree.unflatten(tree, flat)


def per_device(tokens, w_query, w_key, w_value, w_out, grad_out):
    count = lax.axis_size("seq")
    index = lax.axis_index("seq")
    me = jnp.stack([lax.axis_index("mp"), index & 1, (index >> 1) & 3, index >> 3])
    me = me.astype(jnp.int32)
    bias = jnp.stack(
        [
            jnp.where(index == 0, NEGATIVE, 0.0).astype(F32),
            jnp.where(index == count - 1, NEGATIVE, 0.0).astype(F32),
        ]
    )
    token_shares = gather_shares(tokens)
    sent_grad = tied(grad_out, *(token_shares[n] for n in (1, 2, 5, 6)))
    grad_shares = [
        grad_out, to_previous(sent_grad), turned_by(sent_grad, 2), to_next(sent_grad)
    ]
    inverse, q, kv, to_left, to_right, normed, w = project(
        me, token_shares, w_query, w_key, w_value
    )
    from_left, from_right = exchange(to_left, to_right)
    inner_out, inner_stats = forward_inner(bias, q, kv)
    grad_shares = tied(grad_shares, inner_out)
    d_att = cotangent(me, grad_shares, w_out)
    inner_out = tied(inner_out, d_att)
    attended, stats = forward_edge(bias, q, kv, from_left, from_right, inner_out)
    out_own, *terms = out_terms(me, attended, w_out)
    out_received = sum_over_mp(terms)
    stats = tied(stats, out_own)
    dq_f, d_kv, to_left, to_right = edge_backward(
        bias, stats, q, kv, from_left, from_right, d_att
    )
    from_left, from_right = exchange(to_left, to_right)
    d_query, d_kv = inner_backward(bias, inner_stats, q, kv, d_att, dq_f, d_kv)
    attended = tied(attended, *out_received)
    outer, inner = early_terms(grad_shares, attended, normed, d_query)
    d_query = tied(d_query, outer)
    d_proj, dots, own, *terms = input_terms(
        d_query, d_kv, from_left, from_right, normed, w
    )
    attn_out = finish_out(out_own, out_received)
    mine, other = inner_terms(me, normed, d_proj, inner, outer)
    core_sums = sum_over_core(me, mine, other)
    terms[1] = tied(terms[1], core_sums[0])
    received = sum_over_mp(terms)
    grad_tokens = finish_grad(own, received, tokens, inverse, dots)
    *weight_grads, grad_w_out = sum_over_seq(me, core_sums)
    return (attn_out, grad_tokens, *weight_grads, grad_w_out.T)


def solution(mesh):
    return jax.shard_map(
        per_device,
        mesh=mesh,
        in_specs=(
            P("seq", "mp"),
            P(None, "mp"),
            P(None, "mp"),
            P(None, "mp"),
            P("mp", None),
            P("seq", "mp"),
        ),
        out_specs=(
            P("seq", "mp"),
            P("seq", "mp"),
            P("seq", "mp"),
            P("seq", "mp"),
            P("seq", "mp"),
            P("mp", "seq"),
        ),
        check_vma=False,
    )
```

```python
import jax
import jax.numpy as jnp
from jax import lax
from jax.experimental import pallas as pl
from jax.experimental.pallas import tpu as pltpu
from jax.sharding import PartitionSpec as P

HD = 64
BLOCK = 256
LEVELS = 3
PAIR = 2 * HD
MP = 4
LANES = 128
DOT_ROWS = 16

EPSILON = 1e-06
NEGATIVE = -1e30

F32 = jnp.float32
BF16 = jnp.bfloat16

FIRST_EXT = (0, 6, 10)
EXT_BLOCKS = (6, 4, 3)
EXT_TOTAL = 13


def nn(left, right):
    return lax.dot_general(left, right, (((1,), (0,)), ((), ())), preferred_element_type=F32)


def nt(left, right):
    return lax.dot_general(left, right, (((1,), (1,)), ((), ())), preferred_element_type=F32)


def tn(left, right):
    return lax.dot_general(left, right, (((0,), (0,)), ((), ())), preferred_element_type=F32)


def pool_matrix(coarse, factor, value):
    shape = (coarse, coarse * factor)
    row = lax.broadcasted_iota(jnp.int32, shape, 0)
    low = row * factor
    col = lax.broadcasted_iota(jnp.int32, shape, 1)
    return jnp.where((col >= low) & (col < low + factor), value, 0.0).astype(BF16)


def pool_both(half, quarter):
    parts = [pool_matrix(BLOCK // 2, 2, half), pool_matrix(BLOCK // 4, 4, quarter)]
    return jnp.concatenate(parts, axis=0)


def spread_matrix(coarse, factor, value):
    shape = (coarse * factor, coarse)
    low = lax.broadcasted_iota(jnp.int32, shape, 1) * factor
    row = lax.broadcasted_iota(jnp.int32, shape, 0)
    return jnp.where((row >= low) & (row < low + factor), value, 0.0).astype(BF16)


def share_rows(me, step, width):
    return pl.ds(pl.multiple_of(((me + step) & (MP - 1)) * width, width), width)


SMALL = pl.CostEstimate(flops=10**6, bytes_accessed=10**4, transcendentals=0)
LARGE = pl.CostEstimate(flops=4 * 10**9, bytes_accessed=10**4, transcendentals=0)
RELAY = pl.CostEstimate(flops=10**9, bytes_accessed=10**4, transcendentals=0)
SCALAR = pl.BlockSpec(memory_space=pltpu.SMEM)
RESIDENT = pl.BlockSpec(memory_space=pltpu.VMEM)


def held(shape, dtype):
    return jax.ShapeDtypeStruct(shape, dtype)


def run(kernel, name, limit_mib, scalars, inputs, outputs, scratch=(), cost=SMALL):
    return pl.pallas_call(
        kernel,
        in_specs=[SCALAR] * len(scalars) + [RESIDENT] * len(inputs),
        out_specs=[RESIDENT] * len(outputs),
        out_shape=outputs,
        scratch_shapes=list(scratch),
        compiler_params=pltpu.CompilerParams(vmem_limit_bytes=limit_mib * 2**20),
        cost_estimate=cost,
        name=name,
    )(*scalars, *inputs)


def block_rows(block):
    return slice(block * BLOCK, (block + 1) * BLOCK)


ALL_ROWS = 7 * BLOCK
LEVEL_BLOCK = (0, 4, 6)


def as_row(column):
    return jnp.broadcast_to(column, (column.shape[0], LANES)).T[0:1, :]


def as_column(row):
    return jnp.broadcast_to(row, (LANES, row.shape[1])).T[:, 0:1]


def project_kernel(
    place, t1a_any, t1b_any, t2a_any, t2b_any, t3a_any, t3b_any,
    t0_hbm, wq_hbm, wk_hbm, wv_hbm,
    inverse, q, kv, to_left, to_right, normed_hbm, w_hbm,
    t0, t1, t2, t3, w, normed, in_sems, out_sems,
):
    me = place[0]
    width = t0.shape[1]
    low, high = pl.ds(0, 2 * BLOCK), pl.ds(2 * BLOCK, 2 * BLOCK)
    moves = [
        (t0_hbm, t0),
        (t1a_any, t1.at[low]),
        (t2a_any, t2.at[low]),
        (t3a_any, t3.at[low]),
        (t1b_any, t1.at[high]),
        (t2b_any, t2.at[high]),
        (t3b_any, t3.at[high]),
    ]
    for n, source in enumerate((wq_hbm, wk_hbm, wv_hbm)):
        for r in range(MP):
            target = w.at[pl.ds(r * width, width), pl.ds(n * width, width)]
            moves.append((source.at[share_rows(me, r, width), :], target))
    loads = [
        pltpu.make_async_copy(source, target, in_sems.at[n])
        for n, (source, target) in enumerate(moves)
    ]
    for load in loads:
        load.start()
    pools = pool_both(0.5, 0.25)
    inverse[4:8, :] = jnp.zeros((4, BLOCK), F32)
    stores = []

    def normalise(step):
        if step in (0, 2):
            for load in loads[0:4] if step == 0 else loads[4:7]:
                load.wait()
        rows = block_rows(step)
        shares = [share[rows, :].astype(F32) for share in (t0, t1, t2, t3)]
        squares = shares[0] * shares[0]
        for share in shares[1:]:
            squares = squares + share * share
        total = jnp.sum(squares, axis=1, keepdims=True)
        inv = lax.rsqrt(total / (MP * width) + EPSILON)
        inverse[step : step + 1, :] = as_row(inv)
        parts = [(share * inv).astype(BF16) for share in shares]
        for r, part in enumerate(parts):
            normed[rows, r * width : (r + 1) * width] = part
        store = pltpu.make_async_copy(normed.at[rows], normed_hbm.at[rows], out_sems.at[step])
        store.start()
        stores.append(store)
        return jnp.concatenate(parts, axis=1)

    def spread(step, whole):
        if step == 0:
            for load in loads[7:]:
                load.wait()
            store = pltpu.make_async_copy(w, w_hbm, out_sems.at[4])
            store.start()
            stores.append(store)
        rows = block_rows(step)
        fine = [nn(whole, w[:, n * width : (n + 1) * width]).astype(BF16) for n in range(3)]
        coarse = [nn(pools, x).astype(BF16) for x in fine]
        mid = [x[0:128] for x in coarse]
        low = [x[128:192] for x in coarse]
        mid_rows = slice(1024 + step * 128, 1024 + (step + 1) * 128)
        low_rows = slice(1536 + step * 64, 1536 + (step + 1) * 64)
        q[rows, :] = fine[0]
        q[mid_rows, :] = mid[0]
        q[low_rows, :] = low[0]
        edge_mid = slice(256 + (step % 2) * 128, 384 + (step % 2) * 128)
        edge_low = slice(512 + step * 64, 576 + step * 64)
        for n in range(2):
            kv[n, rows, :] = fine[1 + n]
            kv[n, mid_rows, :] = mid[1 + n]
            kv[n, low_rows, :] = low[1 + n]
            to_left[n, edge_low, :] = low[1 + n]
            to_right[n, edge_low, :] = low[1 + n]
            edge = to_left if step < 2 else to_right
            edge[n, edge_mid, :] = mid[1 + n]
            if step in (0, 3):
                edge[n, 0:BLOCK, :] = fine[1 + n]

    parts = normalise(0)
    for step in range(4):
        following = normalise(step + 1) if step < 3 else None
        spread(step, parts)
        parts = following
    for store in stores:
        store.wait()


def project(place, shares, wq, wk, wv):
    rows, width = shares[0].shape
    out = jax.ShapeDtypeStruct
    edge = out((2, 3 * BLOCK, width), BF16)
    anywhere = pl.BlockSpec(memory_space=pl.ANY)
    share = pltpu.VMEM((rows, width), BF16)
    fixed = [
        pltpu.with_memory_space_constraint(value, pltpu.HBM)
        for value in (*shares[1:], shares[0], wq, wk, wv)
    ]
    return pl.pallas_call(
        project_kernel,
        in_specs=[SCALAR] + [anywhere] * 10,
        out_specs=[RESIDENT] * 5 + [anywhere] * 2,
        out_shape=[
            out((8, width), F32),
            out((ALL_ROWS, width), BF16),
            out((2, ALL_ROWS, width), BF16),
            edge,
            edge,
            pltpu.HBM((rows, MP * width), BF16),
            pltpu.HBM((MP * width, 3 * width), BF16),
        ],
        scratch_shapes=[share] * 4
        + [
            pltpu.VMEM((MP * width, 3 * width), BF16),
            pltpu.VMEM((rows, MP * width), BF16),
            pltpu.SemaphoreType.DMA((19,)),
            pltpu.SemaphoreType.DMA((5,)),
        ],
        compiler_params=pltpu.CompilerParams(vmem_limit_bytes=20 * 2**20),
        cost_estimate=SMALL,
        name="project",
    )(place, *fixed)


def cotangent_kernel(place, g0, g1, g2, g3, w_out, d_att, w_turned):
    me = place[0]
    width = g0.shape[1]
    pools = pool_both(1.0, 1.0)
    for r in range(MP):
        w_turned[block_rows(r), :] = w_out[:, share_rows(me, r, width)].T
    for step in range(4):
        rows = block_rows(step)
        shares = jnp.concatenate([share[rows, :] for share in (g0, g1, g2, g3)], axis=1)
        fine = nn(shares, w_turned[...]).astype(BF16)
        d_att[rows, :] = fine
        coarse = nn(pools, fine).astype(BF16)
        d_att[1024 + step * 128 : 1024 + (step + 1) * 128, :] = coarse[0:128]
        d_att[1536 + step * 64 : 1536 + (step + 1) * 64, :] = coarse[128:192]


def cotangent(place, shares, w_out):
    rows, width = shares[0].shape
    outputs = [held((ALL_ROWS, width), BF16)]
    scratch = [pltpu.VMEM((MP * width, width), BF16)]
    return run(cotangent_kernel, "cotangent", 10, [place], [*shares, w_out], outputs, scratch)[0]


EDGE_UNITS = ((0, 0), (0, 3), (1, 0), (1, 1), (2, 0))
INNER_UNITS = ((0, 1), (0, 2))


def unit_keys(level, block):
    last = EXT_BLOCKS[level] - 1
    offsets = (0, 1, 2) if level == 0 else (0, 2)
    keys = []
    for offset in offsets:
        at = block + offset
        keys.append((at, 0 if at == 0 else 1 if at == last else None))
    return keys


def ext_rows(kv, from_left, from_right, n, level, at, lanes):
    if at == 0:
        return from_left[n, block_rows(level), lanes]
    if at == EXT_BLOCKS[level] - 1:
        return from_right[n, block_rows(level), lanes]
    return kv[n, block_rows(LEVEL_BLOCK[level] + at - 1), lanes]


def head_part(lane, head, rows):
    mine = (lane >= head * HD) & (lane < (head + 1) * HD)
    return jnp.where(mine, rows, 0.0).astype(BF16)


def unit_scores(keys, key_rows, query, bias_ref):
    scores = []
    for (_, bias), rows in zip(keys, key_rows):
        s = nt(rows, query)
        scores.append(s if bias is None else s + bias_ref[bias])
    return scores


def add_spread(target, block, factor, rows):
    if factor == 1:
        target[block_rows(block), :] = target[block_rows(block), :] + rows
        return
    for s in range(factor):
        spread = pl.ds(block * factor * BLOCK + s, BLOCK, factor)
        target[spread, :] = target[spread, :] + rows


def each_pair(width, body):
    def step(pair, _):
        body(pair, pl.ds(pl.multiple_of(pair * PAIR, PAIR), PAIR))
        return 0

    lax.fori_loop(0, width // PAIR, step, 0)


def head_part(lane, head, rows):
    mine = (lane >= head * HD) & (lane < (head + 1) * HD)
    return jnp.where(mine, rows, 0.0).astype(BF16)


def unit_scores(keys, key_rows, query, bias_ref):
    scores = []
    for (_, bias), rows in zip(keys, key_rows):
        s = nt(rows, query)
        scores.append(s if bias is None else s + bias_ref[bias])
    return scores


def add_spread(target, block, factor, rows):
    if factor == 1:
        target[block_rows(block), :] = target[block_rows(block), :] + rows
        return
    for s in range(factor):
        spread = pl.ds(block * factor * BLOCK + s, BLOCK, factor)
        target[spread, :] = target[spread, :] + rows


def forward_units(pair, lanes, units, bias_ref, q, kv, from_left, from_right, stats, vt, out_f):
    lane = lax.broadcasted_iota(jnp.int32, (BLOCK, PAIR), 1)
    done = set()
    for level, block in units:
        for at, _ in unit_keys(level, block):
            if (level, at) not in done:
                done.add((level, at))
                rows = ext_rows(kv, from_left, from_right, 1, level, at, lanes)
                vt[FIRST_EXT[level] + at] = rows.T

    def begin(u, head):
        level, block = units[u]
        keys = unit_keys(level, block)
        key_rows = [ext_rows(kv, from_left, from_right, 0, level, at, lanes) for at, _ in keys]
        q_rows = q[block_rows(LEVEL_BLOCK[level] + block), lanes] * HD ** (-0.5)
        return unit_scores(keys, key_rows, head_part(lane, head, q_rows), bias_ref)

    def finish(u, head, scores):
        level, block = units[u]
        top = scores[0].max(axis=0, keepdims=True)
        for s in scores[1:]:
            top = jnp.maximum(top, s.max(axis=0, keepdims=True))
        exps = [jnp.exp(s - top) for s in scores]
        total = exps[0].sum(axis=0, keepdims=True)
        for e in exps[1:]:
            total = total + e.sum(axis=0, keepdims=True)
        scale = 1.0 / total
        row = 4 * u + 2 * head
        stats[pair, row : row + 1, :] = top
        stats[pair, row + 1 : row + 2, :] = scale
        return [(e * scale).astype(BF16) for e in exps]

    outs = []

    def give(u, head, weights):
        level, block = units[u]
        part = slice(head * HD, (head + 1) * HD)
        o_t = None
        for (at, _), w in zip(unit_keys(level, block), weights):
            o = nn(vt[FIRST_EXT[level] + at, part, :], w)
            o_t = o if o_t is None else o_t + o
        outs.append(o_t)
        if head == 1:
            add_spread(out_f, block, 2**level, jnp.concatenate(outs, axis=0).T)
            outs.clear()

    items = [(u, head) for u in range(len(units)) for head in range(2)]
    scores, last = begin(*items[0]), None
    for n, item in enumerate(items):
        following = begin(*items[n + 1]) if n + 1 < len(items) else None
        if last is not None:
            give(*items[n - 1], last)
        last = finish(*item, scores)
        scores = following
    give(*items[-1], last)


def forward_inner_kernel(bias_ref, q, kv, out, stats, vt, out_f):
    def one(pair, lanes):
        out_f[...] = jnp.zeros_like(out_f)
        forward_units(pair, lanes, INNER_UNITS, bias_ref, q, kv, None, None, stats, vt, out_f)
        out[:, lanes] = out_f[BLOCK : 3 * BLOCK, :]

    each_pair(q.shape[1], one)


def forward_edge_kernel(
    bias_ref, q, kv, from_left, from_right, inner, attended, stats, vt, out_f
):
    def one(pair, lanes):
        out_f[0:BLOCK, :] = jnp.zeros((BLOCK, PAIR), F32)
        out_f[BLOCK : 3 * BLOCK, :] = inner[:, lanes]
        out_f[3 * BLOCK :, :] = jnp.zeros((BLOCK, PAIR), F32)
        forward_units(
            pair, lanes, EDGE_UNITS, bias_ref, q, kv, from_left, from_right, stats, vt, out_f
        )
        attended[:, lanes] = out_f[...].astype(BF16)

    each_pair(q.shape[1], one)


def backward_units(
    pair, lanes, units, bias_ref, q, kv, from_left, from_right, grads, stats, kt, dq_f, keep
):
    lane = lax.broadcasted_iota(jnp.int32, (BLOCK, PAIR), 1)
    done = set()
    for level, block in units:
        for at, _ in unit_keys(level, block):
            if (level, at) not in done:
                done.add((level, at))
                rows = ext_rows(kv, from_left, from_right, 0, level, at, lanes)
                kt[FIRST_EXT[level] + at] = rows.T

    def begin(u, head):
        level, block = units[u]
        keys = unit_keys(level, block)
        key_rows = [ext_rows(kv, from_left, from_right, 0, level, at, lanes) for at, _ in keys]
        value_rows = [ext_rows(kv, from_left, from_right, 1, level, at, lanes) for at, _ in keys]
        at = block_rows(LEVEL_BLOCK[level] + block)
        qm = head_part(lane, head, q[at, lanes] * HD ** (-0.5))
        am = head_part(lane, head, grads[at, lanes])
        scores = unit_scores(keys, key_rows, qm, bias_ref)
        return qm, am, scores, [nt(rows, am) for rows in value_rows]

    def finish(u, head, qm, am, scores, d_weights):
        level, block = units[u]
        row = 4 * u + 2 * head
        top, scale = stats[pair, row : row + 1, :], stats[pair, row + 1 : row + 2, :]
        probs = [jnp.exp(s - top) * scale for s in scores]
        dots = None
        for p, dw in zip(probs, d_weights):
            d = (p * dw).sum(axis=0, keepdims=True)
            dots = d if dots is None else dots + d
        weights = [p.astype(BF16) for p in probs]
        d_scores = [(p * (dw - dots)).astype(BF16) for p, dw in zip(probs, d_weights)]
        return qm, am, weights, d_scores

    first = []

    def give(u, head, qm, am, weights, d_scores):
        level, block = units[u]
        keys = unit_keys(level, block)
        part = slice(head * HD, (head + 1) * HD)
        d_values = [nn(w, am) for w in weights]
        d_keys = [nn(ds, qm) for ds in d_scores]
        dq_t = None
        for (at, _), ds in zip(keys, d_scores):
            g = nn(kt[FIRST_EXT[level] + at, part, :], ds)
            dq_t = g if dq_t is None else dq_t + g
        if head == 0:
            first.append((dq_t, d_keys, d_values))
            return
        dq_first, k_first, v_first = first.pop()
        for n, (at, _) in enumerate(keys):
            keep(0, level, at, k_first[n] + d_keys[n])
            keep(1, level, at, v_first[n] + d_values[n])
        dq = jnp.concatenate([dq_first, dq_t], axis=0).T * (HD ** (-0.5) / 2**level)
        add_spread(dq_f, block, 2**level, dq)

    items = [(u, head) for u in range(len(units)) for head in range(2)]
    ready, last = begin(*items[0]), None
    for n, item in enumerate(items):
        following = begin(*items[n + 1]) if n + 1 < len(items) else None
        if last is not None:
            give(*items[n - 1], *last)
        last = finish(*item, *ready)
        ready = following
    give(*items[-1], *last)


def edge_kernel(
    bias_ref, stats, q, kv, from_left, from_right, grads,
    dq_f, d_kv, to_left, to_right, kt, ext, dq_s, sums,
):
    def one(pair, lanes):
        dq_s[...] = jnp.zeros_like(dq_s)
        seen = set()

        def keep(n, level, at, rows):
            slot = FIRST_EXT[level] + at
            if (n, slot) in seen:
                ext[n, slot] = ext[n, slot] + rows
            else:
                seen.add((n, slot))
                ext[n, slot] = rows

        backward_units(
            pair, lanes, EDGE_UNITS, bias_ref, q, kv, from_left, from_right, grads, stats, kt,
            dq_s, keep,
        )
        dq_f[:, lanes] = dq_s[...]
        for n in range(2):
            for level in range(LEVELS):
                first, last = FIRST_EXT[level], FIRST_EXT[level] + EXT_BLOCKS[level] - 1
                to_left[n, block_rows(level), lanes] = ext[n, first].astype(BF16)
                to_right[n, block_rows(level), lanes] = ext[n, last].astype(BF16)
            for b in range(4):
                sums[block_rows(b), :] = ext[n, 1 + b]
            for b in range(2):
                add_spread(sums, b, 2, ext[n, FIRST_EXT[1] + 1 + b] * 0.5)
            d_kv[n, :, lanes] = sums[...]

    each_pair(q.shape[1], one)


def inner_units_kernel(bias_ref, stats, q, kv, grads, dq_in, d_kv_in, d_query, d_kv, kt, dq_s):
    def one(pair, lanes):
        dq_s[...] = dq_in[:, lanes]
        d_kv[:, :, lanes] = d_kv_in[:, :, lanes]

        def keep(n, level, at, rows):
            where = block_rows(at - 1)
            d_kv[n, where, lanes] = d_kv[n, where, lanes] + rows

        backward_units(
            pair, lanes, INNER_UNITS, bias_ref, q, kv, None, None, grads, stats, kt, dq_s, keep
        )
        d_query[:, lanes] = dq_s[...].astype(BF16)

    each_pair(q.shape[1], one)


def turned(count):
    return pltpu.VMEM((count, PAIR, BLOCK), BF16)


def forward_inner(bias, q, kv):
    width = q.shape[1]
    outputs = [held((2 * BLOCK, width), F32), held((width // PAIR, 8, BLOCK), F32)]
    scratch = [turned(EXT_BLOCKS[0]), pltpu.VMEM((4 * BLOCK, PAIR), F32)]
    return run(forward_inner_kernel, "forward_inner", 12, [bias], [q, kv], outputs, scratch, LARGE)


def forward_edge(bias, q, kv, from_left, from_right, inner):
    width = q.shape[1]
    inputs = [q, kv, from_left, from_right, inner]
    outputs = [held((4 * BLOCK, width), BF16), held((width // PAIR, 24, BLOCK), F32)]
    scratch = [turned(EXT_TOTAL), pltpu.VMEM((4 * BLOCK, PAIR), F32)]
    return run(forward_edge_kernel, "forward_edge", 12, [bias], inputs, outputs, scratch)


def edge_backward(bias, stats, q, kv, from_left, from_right, d_att):
    rows, width = 4 * BLOCK, q.shape[1]
    edge = held((2, 3 * BLOCK, width), BF16)
    inputs = [stats, q, kv, from_left, from_right, d_att]
    outputs = [held((rows, width), F32), held((2, rows, width), F32), edge, edge]
    scratch = [
        turned(EXT_TOTAL),
        pltpu.VMEM((2, EXT_TOTAL, BLOCK, PAIR), F32),
        pltpu.VMEM((rows, PAIR), F32),
        pltpu.VMEM((rows, PAIR), F32),
    ]
    return run(edge_kernel, "edge_backward", 20, [bias], inputs, outputs, scratch)


def inner_backward(bias, stats, q, kv, d_att, dq_f, d_kv):
    rows, width = 4 * BLOCK, q.shape[1]
    inputs = [stats, q, kv, d_att, dq_f, d_kv]
    outputs = [held((rows, width), BF16), held((2, rows, width), F32)]
    scratch = [turned(EXT_BLOCKS[0]), pltpu.VMEM((rows, PAIR), F32)]
    return run(inner_units_kernel, "inner_backward", 12, [bias], inputs, outputs, scratch)


def term_outputs(rows, width):
    return [held((rows, width), BF16)] * MP


def store_terms(step, terms, own, keep_right, keep_left, right, left):
    own[block_rows(step), :] = terms[0]
    low, high = block_rows(step % 2), block_rows(2 + step % 2)
    if step < 2:
        keep_right[low, :] = terms[1]
        right[high, :] = terms[2]
        left[low, :] = terms[3]
    else:
        right[low, :] = terms[1]
        left[high, :] = terms[2]
        keep_left[low, :] = terms[3]


def out_terms_kernel(place, attended, w_out, *outs):
    me = place[0]
    width = attended.shape[1]
    for step in range(4):
        rows = attended[block_rows(step), :]
        for r, out in enumerate(outs):
            term = nn(rows, w_out[:, share_rows(me, r, width)])
            out[block_rows(step), :] = term.astype(BF16)


def out_terms(place, attended, w_out):
    outputs = term_outputs(*attended.shape)
    return run(out_terms_kernel, "out_terms", 8, [place], [attended, w_out], outputs)


def input_terms_kernel(
    d_query, d_kv, from_left, from_right, normed, w, d_proj,
    dots, own, keep_right, keep_left, right, left, dot_rows, w_turned,
):
    width = d_query.shape[1]
    half = spread_matrix(BLOCK // 2, 2, 0.5)
    quarter = spread_matrix(BLOCK // 4, 4, 0.25)
    dot_rows[12:16, :] = jnp.zeros((4, BLOCK), F32)
    for r in range(MP):
        for n in range(3):
            at = slice(r * width, (r + 1) * width)
            w_turned[block_rows(n), at] = w[at, n * width : (n + 1) * width].T
    for step in range(4):
        rows = block_rows(step)
        grads = [d_query[rows, :]]
        mid_rows = slice(256 + (step % 2) * 128, 384 + (step % 2) * 128)
        low_rows = slice(512 + step * 64, 576 + step * 64)
        near = from_left if step < 2 else from_right
        for n in range(2):
            total = d_kv[n, rows, :]
            if step in (0, 3):
                total = total + near[n, 0:BLOCK, :].astype(F32)
            total = total + nn(half, near[n, mid_rows, :])
            total = total + nn(quarter, from_left[n, low_rows, :])
            total = total + nn(quarter, from_right[n, low_rows, :])
            grads.append(total.astype(BF16))
        for n, grad in enumerate(grads[1:]):
            d_proj[rows, n * width : (n + 1) * width] = grad
        dot = None
        every = jnp.concatenate(grads, axis=1)
        terms = []
        for r in range(MP):
            term = nn(every, w_turned[:, r * width : (r + 1) * width]).astype(BF16)
            terms.append(term)
            part = term.astype(F32) * normed[rows, r * width : (r + 1) * width].astype(F32)
            dot = part if dot is None else dot + part
        store_terms(step, terms, own, keep_right, keep_left, right, left)
        dot = as_row(jnp.sum(dot, axis=1, keepdims=True))
        first = dot.astype(BF16).astype(F32)
        second = (dot - first).astype(BF16).astype(F32)
        for n, piece in enumerate((first, second, dot - first - second)):
            dot_rows[4 * n + step : 4 * n + step + 1, :] = piece
    pieces = dot_rows[...].astype(BF16)
    dots[...] = pieces
    right[4 * BLOCK :, :] = pieces
    left[4 * BLOCK :, :] = pieces


def input_terms(d_query, d_kv, from_left, from_right, normed, w):
    rows, width = d_query.shape
    inputs = [d_query, d_kv, from_left, from_right, normed, w]
    outputs = [held((rows, 2 * width), BF16), held((DOT_ROWS, width), BF16)]
    lengths = [rows, rows // 2, rows // 2, rows + DOT_ROWS, rows + DOT_ROWS]
    outputs += [held((n, width), BF16) for n in lengths]
    scratch = [pltpu.VMEM((DOT_ROWS, width), F32), pltpu.VMEM((3 * width, MP * width), BF16)]
    return run(input_terms_kernel, "input_terms", 18, [], inputs, outputs, scratch)


def sum_terms(own, received, at):
    total = own[at, :].astype(F32)
    for term in received:
        total = total + term[at, :].astype(F32)
    return total


def finish_out_kernel(own, one, two, three, result):
    for b in range(4):
        at = block_rows(b)
        result[at, :] = sum_terms(own, (one, two, three), at).astype(BF16)


def finish_out(own, received):
    outputs = [held(own.shape, BF16)]
    return run(finish_out_kernel, "finish_out", 8, [], [own, *received], outputs)[0]


def relay_kernel(keep_right, keep_left, l1, r1, onward_right, onward_left):
    half = keep_right.shape[0]
    passed = l1[half : 2 * half, :].astype(F32)
    onward_right[0:half, :] = (keep_right[...].astype(F32) + passed).astype(BF16)
    passed = r1[half : 2 * half, :].astype(F32)
    onward_left[...] = (keep_left[...].astype(F32) + passed).astype(BF16)
    if onward_right.shape[0] > half:
        onward_right[half:, :] = l1[2 * half :, :]


def relay(keep_right, keep_left, l1, r1):
    half, width = keep_right.shape
    outputs = [held((half + DOT_ROWS, width), BF16), held((half, width), BF16)]
    return run(relay_kernel, "relay", 4, [], [keep_right, keep_left, l1, r1], outputs, (), RELAY)


def finish_grad_kernel(own, l1, r1, l2, r2, tokens, inverse, dots, result):
    rows, width = own.shape
    half = r2.shape[0]
    pieces = dots[...].astype(F32)
    for message, first in ((l1, rows), (r1, rows), (l2, half)):
        pieces = pieces + message[first : first + DOT_ROWS, :].astype(F32)
    means = (pieces[0:4] + pieces[4:8] + pieces[8:12]) / (MP * width)
    for b in range(rows // BLOCK):
        at, near = block_rows(b), block_rows(b % 2)
        mean = as_column(means[b : b + 1, :])
        inv = as_column(inverse[b : b + 1, :])
        total = own[at, :].astype(F32)
        for part in (r1, l2) if b < 2 else (l1, r2):
            total = total + part[near, :].astype(F32)
        result[at, :] = inv * (total - tokens[at, :].astype(F32) * inv * mean)


def finish_grad(own, l1, r1, l2, r2, tokens, inverse, dots):
    inputs = [own, l1, r1, l2, r2, tokens, inverse, dots]
    outputs = [held(own.shape, F32)]
    return run(finish_grad_kernel, "finish_grad", 8, [], inputs, outputs)[0]


def early_kernel(g0, g1, g2, g3, attended, normed, d_query, outer, inner):
    width = g0.shape[1]
    rows = attended[...]
    for r, share in enumerate((g0, g1, g2, g3)):
        at = slice(r * width, (r + 1) * width)
        outer[at, :] = tn(share[...], rows).astype(BF16)
        inner[at, :] = tn(normed[:, at], d_query[...]).astype(BF16)


def early_terms(shares, attended, normed, d_query):
    width = attended.shape[1]
    inputs = [*shares, attended, normed, d_query]
    outputs = [held((MP * width, width), BF16)] * 2
    return run(early_kernel, "early_terms", 14, [], inputs, outputs, (), LARGE)


def inner_kernel(place, normed, d_proj, inner, outer, mine, other_low, other_high, rows_held):
    core = place[1]
    width = outer.shape[1]
    for block in range(MP):
        at = block_rows(block)
        rows_held[at, 0:width] = inner[at, :]
        rows_held[at, width : 3 * width] = tn(normed[:, at], d_proj[...]).astype(BF16)
        rows_held[at, 3 * width :] = outer[at, :]
        for n in range(width // 64):
            out = slice((4 * block + n) * 32, (4 * block + n + 1) * 32)
            first = block * width + n * 64
            mine[out, :] = rows_held[pl.ds(pl.multiple_of(first + core * 32, 32), 32), :]
            other, start = (other_low, 0) if block < 2 else (other_high, 256)
            other[out.start - start : out.stop - start, :] = rows_held[pl.ds(pl.multiple_of(first + 32 - core * 32, 32), 32), :]


def inner_terms(place, normed, d_proj, inner, outer):
    total = normed.shape[1]
    width = outer.shape[1]
    outputs = [held((n, 4 * width), BF16) for n in (total // 2, total // 4, total // 4)]
    scratch = [pltpu.VMEM((total, 4 * width), BF16)]
    return run(inner_kernel, "inner_terms", 16, [place], [normed, d_proj, inner, outer], outputs, scratch)


def pair_sum_kernel(place, mine, got_low, got_high, *outs):
    z, core, x, y = place[0], place[1], place[2], place[3]
    for d, out in enumerate(outs):
        for n in range(4):
            chunk = jnp.where(core == 0, 4 * n + ((x + d) & 3), 4 * ((y + d - z + 4) & 3) + n)
            rows = pl.ds(pl.multiple_of(chunk * 32, 32), 32)
            half = pl.ds(pl.multiple_of((chunk & 7) * 32, 32), 32)
            got = jnp.where(chunk < 8, got_low[half, :], got_high[half, :])
            total = mine[rows, :].astype(F32) + got.astype(F32)
            out[32 * n : 32 * (n + 1), :] = total.astype(BF16)


def row_sum_kernel(place, a, b, c, d, *refs):
    *outs, total = refs
    z, core, x, y = place[0], place[1], place[2], place[3]
    first = jnp.where(core == 0, y - z + 4, x)
    total[...] = (
        a[...].astype(F32) + b[...].astype(F32) + c[...].astype(F32) + d[...].astype(F32)
    ).astype(BF16)
    for n, out in enumerate(outs):
        out[...] = total[pl.ds(pl.multiple_of(((first + n) & 3) * 32, 32), 32), :]


def last_sum_kernel(a, b, c, d, gq, gk, gv, go):
    width = gq.shape[1]
    total = a[...].astype(F32) + b[...].astype(F32) + c[...].astype(F32) + d[...].astype(F32)
    gq[...] = total[:, 0:width]
    gk[...] = total[:, width : 2 * width]
    gv[...] = total[:, 2 * width : 3 * width]
    go[...] = total[:, 3 * width :]


def sum_over_core(place, mine, *others):
    got = [lax.ppermute(other, "seq", [(i, i ^ 1) for i in range(32)]) for other in others]
    parts = [held((128, mine.shape[1]), BF16)] * 4
    return run(pair_sum_kernel, "pair_sum", 6, [place], [mine, *got], parts)


def sum_over_seq(place, parts, *first):
    cols = parts[0].shape[1]

    def sent(value, stage, d):
        pairs = []
        for i in range(32):
            core, x, y = i % 2, (i // 2) % 4, i // 8
            if stage == core:
                x = (x + d) % 4
            else:
                y = (y + d) % 4
            pairs.append((i, (y * 4 + x) * 2 + core))
        return lax.ppermute(value, "seq", pairs)

    parts = [parts[0]] + [sent(parts[d], 0, d) for d in (1, 2, 3)]
    parts = tied(parts, *first)
    rows = [held((32, cols), BF16)] * 4
    scratch = [pltpu.VMEM((128, cols), BF16)]
    rows = run(row_sum_kernel, "row_sum", 4, [place], parts, rows, scratch)
    rows = [rows[0]] + [sent(rows[d], 1, d) for d in (1, 2, 3)]
    outputs = [held((32, cols // 4), F32)] * 4
    return run(last_sum_kernel, "last_sum", 4, [], rows, outputs)


def to_next(value):
    return lax.ppermute(value, "mp", [(i, (i + 1) % MP) for i in range(MP)])


def to_previous(value):
    return lax.ppermute(value, "mp", [((i + 1) % MP, i) for i in range(MP)])


def gather_shares(share):
    half = share.shape[0] // 2
    low, high = share[:half], share[half:]
    after_low, before_high = to_previous(low), to_next(high)
    after_high, before_low = to_previous(high), to_next(low)
    far_low, far_high = to_previous(after_low), to_next(before_high)
    return [share, after_low, after_high, far_low, far_high, before_low, before_high]


def turned_by(value, step):
    return lax.ppermute(value, "mp", [(i, (i + step) % MP) for i in range(MP)])


def sum_over_mp(terms):
    return [turned_by(term, step) for step, term in zip((1, 2, 3), terms)]


def exchange(to_left, to_right):
    count = lax.axis_size("seq")
    ends = count - 1
    from_left = lax.ppermute(to_right, "seq", [(i, i + 1) for i in range(ends)])
    from_right = lax.ppermute(to_left, "seq", [(i + 1, i) for i in range(ends)])
    return from_left, from_right


def tied(values, *others):
    flat, tree = jax.tree.flatten(values)
    flat = lax.optimization_barrier((*flat, *others))[: len(flat)]
    return jax.tree.unflatten(tree, flat)


def per_device(tokens, w_query, w_key, w_value, w_out, grad_out):
    count = lax.axis_size("seq")
    index = lax.axis_index("seq")
    me = jnp.stack([lax.axis_index("mp"), index & 1, (index >> 1) & 3, index >> 3])
    me = me.astype(jnp.int32)
    bias = jnp.stack(
        [
            jnp.where(index == 0, NEGATIVE, 0.0).astype(F32),
            jnp.where(index == count - 1, NEGATIVE, 0.0).astype(F32),
        ]
    )
    token_shares = gather_shares(tokens)
    near_grad = tied(grad_out, *(token_shares[n] for n in (1, 2, 5, 6)))
    far_grad = tied(grad_out, *token_shares)
    far = turned_by(far_grad, 2)
    grad_shares = [grad_out, to_previous(near_grad), far, to_next(near_grad)]
    inverse, q, kv, to_left, to_right, normed, w = project(
        me, token_shares, w_query, w_key, w_value
    )
    from_left, from_right = exchange(to_left, to_right)
    near_q = tied(q, grad_shares[1], grad_shares[3])
    inner_out, inner_stats = forward_inner(bias, near_q, kv)
    attended, stats = forward_edge(bias, q, kv, from_left, from_right, inner_out)
    out_own, *terms = out_terms(me, attended, w_out)
    out_received = sum_over_mp(terms)
    grad_shares = tied(grad_shares, out_own)
    d_att = cotangent(me, grad_shares, w_out)
    dq_f, d_kv, to_left, to_right = edge_backward(
        bias, stats, q, kv, from_left, from_right, d_att
    )
    from_left, from_right = exchange(to_left, to_right)
    d_query, d_kv = inner_backward(bias, inner_stats, q, kv, d_att, dq_f, d_kv)
    attended = tied(attended, *out_received)
    outer, inner = early_terms(grad_shares, attended, normed, d_query)
    d_query = tied(d_query, outer)
    d_proj, dots, own, keep_right, keep_left, right, left = input_terms(
        d_query, d_kv, from_left, from_right, normed, w
    )
    attn_out = finish_out(out_own, out_received)
    mine, *others = inner_terms(me, normed, d_proj, inner, outer)
    core_sums = sum_over_core(me, mine, *others)
    l1, r1 = to_next(right), to_previous(left)
    onward_right, onward_left = relay(keep_right, keep_left, l1, r1)
    l2, r2 = to_next(onward_right), to_previous(onward_left)
    grad_tokens = finish_grad(own, l1, r1, l2, r2, tokens, inverse, dots)
    *weight_grads, grad_w_out = sum_over_seq(me, core_sums, onward_right)
    return (attn_out, grad_tokens, *weight_grads, grad_w_out.T)


def solution(mesh):
    return jax.shard_map(
        per_device,
        mesh=mesh,
        in_specs=(
            P("seq", "mp"),
            P(None, "mp"),
            P(None, "mp"),
            P(None, "mp"),
            P("mp", None),
            P("seq", "mp"),
        ),
        out_specs=(
            P("seq", "mp"),
            P("seq", "mp"),
            P("seq", "mp"),
            P("seq", "mp"),
            P("seq", "mp"),
            P("mp", "seq"),
        ),
        check_vma=False,
    )
```

```python
import jax
import jax.numpy as jnp
from jax import lax
from jax.experimental import pallas as pl
from jax.experimental.pallas import tpu as pltpu
from jax.sharding import PartitionSpec as P

HD = 64
BLOCK = 256
LEVELS = 3
PAIR = 2 * HD
MP = 4
LANES = 128
DOT_ROWS = 16

EPSILON = 1e-06
NEGATIVE = -1e30

F32 = jnp.float32
BF16 = jnp.bfloat16

FIRST_EXT = (0, 6, 10)
EXT_BLOCKS = (6, 4, 3)
EXT_TOTAL = 13


def nn(left, right):
    return lax.dot_general(left, right, (((1,), (0,)), ((), ())), preferred_element_type=F32)


def nt(left, right):
    return lax.dot_general(left, right, (((1,), (1,)), ((), ())), preferred_element_type=F32)


def tn(left, right):
    return lax.dot_general(left, right, (((0,), (0,)), ((), ())), preferred_element_type=F32)


def pool_matrix(coarse, factor, value):
    shape = (coarse, coarse * factor)
    row = lax.broadcasted_iota(jnp.int32, shape, 0)
    low = row * factor
    col = lax.broadcasted_iota(jnp.int32, shape, 1)
    return jnp.where((col >= low) & (col < low + factor), value, 0.0).astype(BF16)


def pool_both(half, quarter):
    parts = [pool_matrix(BLOCK // 2, 2, half), pool_matrix(BLOCK // 4, 4, quarter)]
    return jnp.concatenate(parts, axis=0)


def spread_matrix(coarse, factor, value):
    shape = (coarse * factor, coarse)
    low = lax.broadcasted_iota(jnp.int32, shape, 1) * factor
    row = lax.broadcasted_iota(jnp.int32, shape, 0)
    return jnp.where((row >= low) & (row < low + factor), value, 0.0).astype(BF16)


def share_rows(me, step, width):
    return pl.ds(pl.multiple_of(((me + step) & (MP - 1)) * width, width), width)


SMALL = pl.CostEstimate(flops=10**6, bytes_accessed=10**4, transcendentals=0)
LARGE = pl.CostEstimate(flops=4 * 10**9, bytes_accessed=10**4, transcendentals=0)
RELAY = pl.CostEstimate(flops=10**9, bytes_accessed=10**4, transcendentals=0)
SCALAR = pl.BlockSpec(memory_space=pltpu.SMEM)
RESIDENT = pl.BlockSpec(memory_space=pltpu.VMEM)


def held(shape, dtype):
    return jax.ShapeDtypeStruct(shape, dtype)


def run(kernel, name, limit_mib, scalars, inputs, outputs, scratch=(), cost=SMALL):
    return pl.pallas_call(
        kernel,
        in_specs=[SCALAR] * len(scalars) + [RESIDENT] * len(inputs),
        out_specs=[RESIDENT] * len(outputs),
        out_shape=outputs,
        scratch_shapes=list(scratch),
        compiler_params=pltpu.CompilerParams(vmem_limit_bytes=limit_mib * 2**20),
        cost_estimate=cost,
        name=name,
    )(*scalars, *inputs)


def block_rows(block):
    return slice(block * BLOCK, (block + 1) * BLOCK)


ALL_ROWS = 7 * BLOCK
LEVEL_BLOCK = (0, 4, 6)


def share_edges(place, edges, to_core, to_other):
    core = place[1]
    to_core[...] = edges[1 - core]
    to_other[...] = edges[core]


def halo_rows(halo, left, index):
    place, from_core, from_other = halo
    near, away = from_core[index], from_other[index]
    return jnp.where(place[1] == 0, away if left else near, near if left else away)


def as_row(column):
    return jnp.broadcast_to(column, (column.shape[0], LANES)).T[0:1, :]


def as_column(row):
    return jnp.broadcast_to(row, (LANES, row.shape[1])).T[:, 0:1]


def project_kernel(
    place, t1a_any, t1b_any, t2a_any, t2b_any, t3a_any, t3b_any,
    t0_hbm, wq_hbm, wk_hbm, wv_hbm,
    inverse, q, kv, to_core, to_other, normed_hbm, w_hbm,
    t0, t1, t2, t3, w, normed, edges, in_sems, out_sems,
):
    me = place[0]
    width = t0.shape[1]
    low, high = pl.ds(0, 2 * BLOCK), pl.ds(2 * BLOCK, 2 * BLOCK)
    moves = [
        (t0_hbm, t0),
        (t1a_any, t1.at[low]),
        (t2a_any, t2.at[low]),
        (t3a_any, t3.at[low]),
        (t1b_any, t1.at[high]),
        (t2b_any, t2.at[high]),
        (t3b_any, t3.at[high]),
    ]
    for n, source in enumerate((wq_hbm, wk_hbm, wv_hbm)):
        for r in range(MP):
            target = w.at[pl.ds(r * width, width), pl.ds(n * width, width)]
            moves.append((source.at[share_rows(me, r, width), :], target))
    loads = [
        pltpu.make_async_copy(source, target, in_sems.at[n])
        for n, (source, target) in enumerate(moves)
    ]
    for load in loads:
        load.start()
    pools = pool_both(0.5, 0.25)
    inverse[4:8, :] = jnp.zeros((4, BLOCK), F32)
    stores = []

    def normalise(step):
        if step in (0, 2):
            for load in loads[0:4] if step == 0 else loads[4:7]:
                load.wait()
        rows = block_rows(step)
        shares = [share[rows, :].astype(F32) for share in (t0, t1, t2, t3)]
        squares = shares[0] * shares[0]
        for share in shares[1:]:
            squares = squares + share * share
        total = jnp.sum(squares, axis=1, keepdims=True)
        inv = lax.rsqrt(total / (MP * width) + EPSILON)
        inverse[step : step + 1, :] = as_row(inv)
        parts = [(share * inv).astype(BF16) for share in shares]
        for r, part in enumerate(parts):
            normed[rows, r * width : (r + 1) * width] = part
        store = pltpu.make_async_copy(normed.at[rows], normed_hbm.at[rows], out_sems.at[step])
        store.start()
        stores.append(store)
        return jnp.concatenate(parts, axis=1)

    def spread(step, whole):
        if step == 0:
            for load in loads[7:]:
                load.wait()
            store = pltpu.make_async_copy(w, w_hbm, out_sems.at[4])
            store.start()
            stores.append(store)
        rows = block_rows(step)
        fine = [nn(whole, w[:, n * width : (n + 1) * width]).astype(BF16) for n in range(3)]
        coarse = [nn(pools, x).astype(BF16) for x in fine]
        mid = [x[0:128] for x in coarse]
        low = [x[128:192] for x in coarse]
        mid_rows = slice(1024 + step * 128, 1024 + (step + 1) * 128)
        low_rows = slice(1536 + step * 64, 1536 + (step + 1) * 64)
        q[rows, :] = fine[0]
        q[mid_rows, :] = mid[0]
        q[low_rows, :] = low[0]
        edge_mid = slice(256 + (step % 2) * 128, 384 + (step % 2) * 128)
        edge_low = slice(512 + step * 64, 576 + step * 64)
        for n in range(2):
            kv[n, rows, :] = fine[1 + n]
            kv[n, mid_rows, :] = mid[1 + n]
            kv[n, low_rows, :] = low[1 + n]
            edges[0, n, edge_low, :] = low[1 + n]
            edges[1, n, edge_low, :] = low[1 + n]
            side = 0 if step < 2 else 1
            edges[side, n, edge_mid, :] = mid[1 + n]
            if step in (0, 3):
                edges[side, n, 0:BLOCK, :] = fine[1 + n]

    parts = normalise(0)
    for step in range(4):
        following = normalise(step + 1) if step < 3 else None
        spread(step, parts)
        parts = following
    share_edges(place, edges, to_core, to_other)
    for store in stores:
        store.wait()


def project(place, shares, wq, wk, wv):
    rows, width = shares[0].shape
    out = jax.ShapeDtypeStruct
    edge = out((2, 3 * BLOCK, width), BF16)
    anywhere = pl.BlockSpec(memory_space=pl.ANY)
    share = pltpu.VMEM((rows, width), BF16)
    fixed = [
        pltpu.with_memory_space_constraint(value, pltpu.HBM)
        for value in (*shares[1:], shares[0], wq, wk, wv)
    ]
    return pl.pallas_call(
        project_kernel,
        in_specs=[SCALAR] + [anywhere] * 10,
        out_specs=[RESIDENT] * 5 + [anywhere] * 2,
        out_shape=[
            out((8, width), F32),
            out((ALL_ROWS, width), BF16),
            out((2, ALL_ROWS, width), BF16),
            edge,
            edge,
            pltpu.HBM((rows, MP * width), BF16),
            pltpu.HBM((MP * width, 3 * width), BF16),
        ],
        scratch_shapes=[share] * 4
        + [
            pltpu.VMEM((MP * width, 3 * width), BF16),
            pltpu.VMEM((rows, MP * width), BF16),
            pltpu.VMEM((2, *edge.shape), BF16),
            pltpu.SemaphoreType.DMA((19,)),
            pltpu.SemaphoreType.DMA((5,)),
        ],
        compiler_params=pltpu.CompilerParams(vmem_limit_bytes=20 * 2**20),
        cost_estimate=SMALL,
        name="project",
    )(place, *fixed)


def cotangent_kernel(place, g0, g1, g2, g3, w_out, d_att, w_turned):
    me = place[0]
    width = g0.shape[1]
    pools = pool_both(1.0, 1.0)
    for r in range(MP):
        w_turned[block_rows(r), :] = w_out[:, share_rows(me, r, width)].T
    for step in range(4):
        rows = block_rows(step)
        shares = jnp.concatenate([share[rows, :] for share in (g0, g1, g2, g3)], axis=1)
        fine = nn(shares, w_turned[...]).astype(BF16)
        d_att[rows, :] = fine
        coarse = nn(pools, fine).astype(BF16)
        d_att[1024 + step * 128 : 1024 + (step + 1) * 128, :] = coarse[0:128]
        d_att[1536 + step * 64 : 1536 + (step + 1) * 64, :] = coarse[128:192]


def cotangent(place, shares, w_out):
    rows, width = shares[0].shape
    outputs = [held((ALL_ROWS, width), BF16)]
    scratch = [pltpu.VMEM((MP * width, width), BF16)]
    return run(cotangent_kernel, "cotangent", 10, [place], [*shares, w_out], outputs, scratch)[0]


EDGE_UNITS = ((0, 0), (0, 3), (1, 0), (1, 1), (2, 0))
INNER_UNITS = ((0, 1), (0, 2))


def unit_keys(level, block):
    last = EXT_BLOCKS[level] - 1
    offsets = (0, 1, 2) if level == 0 else (0, 2)
    keys = []
    for offset in offsets:
        at = block + offset
        keys.append((at, 0 if at == 0 else 1 if at == last else None))
    return keys


def ext_rows(kv, halo, n, level, at, lanes):
    if at in (0, EXT_BLOCKS[level] - 1):
        return halo_rows(halo, at == 0, (n, block_rows(level), lanes))
    return kv[n, block_rows(LEVEL_BLOCK[level] + at - 1), lanes]


def head_part(lane, head, rows):
    mine = (lane >= head * HD) & (lane < (head + 1) * HD)
    return jnp.where(mine, rows, 0.0).astype(BF16)


def unit_scores(keys, key_rows, query, bias_ref):
    scores = []
    for (_, bias), rows in zip(keys, key_rows):
        s = nt(rows, query)
        scores.append(s if bias is None else s + bias_ref[bias])
    return scores


def add_spread(target, block, factor, rows):
    if factor == 1:
        target[block_rows(block), :] = target[block_rows(block), :] + rows
        return
    for s in range(factor):
        spread = pl.ds(block * factor * BLOCK + s, BLOCK, factor)
        target[spread, :] = target[spread, :] + rows


def each_pair(width, body):
    def step(pair, _):
        body(pair, pl.ds(pl.multiple_of(pair * PAIR, PAIR), PAIR))
        return 0

    lax.fori_loop(0, width // PAIR, step, 0)


def head_part(lane, head, rows):
    mine = (lane >= head * HD) & (lane < (head + 1) * HD)
    return jnp.where(mine, rows, 0.0).astype(BF16)


def unit_scores(keys, key_rows, query, bias_ref):
    scores = []
    for (_, bias), rows in zip(keys, key_rows):
        s = nt(rows, query)
        scores.append(s if bias is None else s + bias_ref[bias])
    return scores


def add_spread(target, block, factor, rows):
    if factor == 1:
        target[block_rows(block), :] = target[block_rows(block), :] + rows
        return
    for s in range(factor):
        spread = pl.ds(block * factor * BLOCK + s, BLOCK, factor)
        target[spread, :] = target[spread, :] + rows


def forward_units(pair, lanes, units, bias_ref, q, kv, halo, stats, vt, out_f):
    lane = lax.broadcasted_iota(jnp.int32, (BLOCK, PAIR), 1)
    done = set()
    for level, block in units:
        for at, _ in unit_keys(level, block):
            if (level, at) not in done:
                done.add((level, at))
                rows = ext_rows(kv, halo, 1, level, at, lanes)
                vt[FIRST_EXT[level] + at] = rows.T

    def begin(u, head):
        level, block = units[u]
        keys = unit_keys(level, block)
        key_rows = [ext_rows(kv, halo, 0, level, at, lanes) for at, _ in keys]
        q_rows = q[block_rows(LEVEL_BLOCK[level] + block), lanes] * HD ** (-0.5)
        return unit_scores(keys, key_rows, head_part(lane, head, q_rows), bias_ref)

    def finish(u, head, scores):
        level, block = units[u]
        top = scores[0].max(axis=0, keepdims=True)
        for s in scores[1:]:
            top = jnp.maximum(top, s.max(axis=0, keepdims=True))
        exps = [jnp.exp(s - top) for s in scores]
        total = exps[0].sum(axis=0, keepdims=True)
        for e in exps[1:]:
            total = total + e.sum(axis=0, keepdims=True)
        scale = 1.0 / total
        row = 4 * u + 2 * head
        stats[pair, row : row + 1, :] = top
        stats[pair, row + 1 : row + 2, :] = scale
        return [(e * scale).astype(BF16) for e in exps]

    outs = []

    def give(u, head, weights):
        level, block = units[u]
        part = slice(head * HD, (head + 1) * HD)
        o_t = None
        for (at, _), w in zip(unit_keys(level, block), weights):
            o = nn(vt[FIRST_EXT[level] + at, part, :], w)
            o_t = o if o_t is None else o_t + o
        outs.append(o_t)
        if head == 1:
            add_spread(out_f, block, 2**level, jnp.concatenate(outs, axis=0).T)
            outs.clear()

    items = [(u, head) for u in range(len(units)) for head in range(2)]
    scores, last = begin(*items[0]), None
    for n, item in enumerate(items):
        following = begin(*items[n + 1]) if n + 1 < len(items) else None
        if last is not None:
            give(*items[n - 1], last)
        last = finish(*item, scores)
        scores = following
    give(*items[-1], last)


def forward_inner_kernel(bias_ref, q, kv, out, stats, vt, out_f):
    def one(pair, lanes):
        out_f[...] = jnp.zeros_like(out_f)
        forward_units(pair, lanes, INNER_UNITS, bias_ref, q, kv, None, stats, vt, out_f)
        out[:, lanes] = out_f[BLOCK : 3 * BLOCK, :]

    each_pair(q.shape[1], one)


def forward_edge_kernel(
    place, bias_ref, q, kv, from_other, from_core, inner, attended, stats, vt, out_f
):
    halo = (place, from_core, from_other)

    def one(pair, lanes):
        out_f[0:BLOCK, :] = jnp.zeros((BLOCK, PAIR), F32)
        out_f[BLOCK : 3 * BLOCK, :] = inner[:, lanes]
        out_f[3 * BLOCK :, :] = jnp.zeros((BLOCK, PAIR), F32)
        forward_units(
            pair, lanes, EDGE_UNITS, bias_ref, q, kv, halo, stats, vt, out_f
        )
        attended[:, lanes] = out_f[...].astype(BF16)

    each_pair(q.shape[1], one)


def backward_units(
    pair, lanes, units, bias_ref, q, kv, halo, grads, stats, kt, dq_f, keep
):
    lane = lax.broadcasted_iota(jnp.int32, (BLOCK, PAIR), 1)
    done = set()
    for level, block in units:
        for at, _ in unit_keys(level, block):
            if (level, at) not in done:
                done.add((level, at))
                rows = ext_rows(kv, halo, 0, level, at, lanes)
                kt[FIRST_EXT[level] + at] = rows.T

    def begin(u, head):
        level, block = units[u]
        keys = unit_keys(level, block)
        key_rows = [ext_rows(kv, halo, 0, level, at, lanes) for at, _ in keys]
        value_rows = [ext_rows(kv, halo, 1, level, at, lanes) for at, _ in keys]
        at = block_rows(LEVEL_BLOCK[level] + block)
        qm = head_part(lane, head, q[at, lanes] * HD ** (-0.5))
        am = head_part(lane, head, grads[at, lanes])
        scores = unit_scores(keys, key_rows, qm, bias_ref)
        return qm, am, scores, [nt(rows, am) for rows in value_rows]

    def finish(u, head, qm, am, scores, d_weights):
        level, block = units[u]
        row = 4 * u + 2 * head
        top, scale = stats[pair, row : row + 1, :], stats[pair, row + 1 : row + 2, :]
        probs = [jnp.exp(s - top) * scale for s in scores]
        dots = None
        for p, dw in zip(probs, d_weights):
            d = (p * dw).sum(axis=0, keepdims=True)
            dots = d if dots is None else dots + d
        weights = [p.astype(BF16) for p in probs]
        d_scores = [(p * (dw - dots)).astype(BF16) for p, dw in zip(probs, d_weights)]
        return qm, am, weights, d_scores

    first = []

    def give(u, head, qm, am, weights, d_scores):
        level, block = units[u]
        keys = unit_keys(level, block)
        part = slice(head * HD, (head + 1) * HD)
        d_values = [nn(w, am) for w in weights]
        d_keys = [nn(ds, qm) for ds in d_scores]
        dq_t = None
        for (at, _), ds in zip(keys, d_scores):
            g = nn(kt[FIRST_EXT[level] + at, part, :], ds)
            dq_t = g if dq_t is None else dq_t + g
        if head == 0:
            first.append((dq_t, d_keys, d_values))
            return
        dq_first, k_first, v_first = first.pop()
        for n, (at, _) in enumerate(keys):
            keep(0, level, at, k_first[n] + d_keys[n])
            keep(1, level, at, v_first[n] + d_values[n])
        dq = jnp.concatenate([dq_first, dq_t], axis=0).T * (HD ** (-0.5) / 2**level)
        add_spread(dq_f, block, 2**level, dq)

    items = [(u, head) for u in range(len(units)) for head in range(2)]
    ready, last = begin(*items[0]), None
    for n, item in enumerate(items):
        following = begin(*items[n + 1]) if n + 1 < len(items) else None
        if last is not None:
            give(*items[n - 1], *last)
        last = finish(*item, *ready)
        ready = following
    give(*items[-1], *last)


def edge_kernel(
    place, bias_ref, stats, q, kv, from_other, from_core, grads,
    dq_f, d_kv, to_core, to_other, kt, ext, dq_s, sums, edges,
):
    halo = (place, from_core, from_other)

    def one(pair, lanes):
        dq_s[...] = jnp.zeros_like(dq_s)
        seen = set()

        def keep(n, level, at, rows):
            slot = FIRST_EXT[level] + at
            if (n, slot) in seen:
                ext[n, slot] = ext[n, slot] + rows
            else:
                seen.add((n, slot))
                ext[n, slot] = rows

        backward_units(
            pair, lanes, EDGE_UNITS, bias_ref, q, kv, halo, grads, stats, kt, dq_s, keep,
        )
        dq_f[:, lanes] = dq_s[...]
        for n in range(2):
            for level in range(LEVELS):
                first, last = FIRST_EXT[level], FIRST_EXT[level] + EXT_BLOCKS[level] - 1
                edges[0, n, block_rows(level), lanes] = ext[n, first].astype(BF16)
                edges[1, n, block_rows(level), lanes] = ext[n, last].astype(BF16)
            for b in range(4):
                sums[block_rows(b), :] = ext[n, 1 + b]
            for b in range(2):
                add_spread(sums, b, 2, ext[n, FIRST_EXT[1] + 1 + b] * 0.5)
            d_kv[n, :, lanes] = sums[...]

    each_pair(q.shape[1], one)
    share_edges(place, edges, to_core, to_other)


def inner_units_kernel(bias_ref, stats, q, kv, grads, dq_in, d_kv_in, d_query, d_kv, kt, dq_s):
    def one(pair, lanes):
        dq_s[...] = dq_in[:, lanes]
        d_kv[:, :, lanes] = d_kv_in[:, :, lanes]

        def keep(n, level, at, rows):
            where = block_rows(at - 1)
            d_kv[n, where, lanes] = d_kv[n, where, lanes] + rows

        backward_units(
            pair, lanes, INNER_UNITS, bias_ref, q, kv, None, grads, stats, kt, dq_s, keep
        )
        d_query[:, lanes] = dq_s[...].astype(BF16)

    each_pair(q.shape[1], one)


def turned(count):
    return pltpu.VMEM((count, PAIR, BLOCK), BF16)


def forward_inner(bias, q, kv):
    width = q.shape[1]
    outputs = [held((2 * BLOCK, width), F32), held((width // PAIR, 8, BLOCK), F32)]
    scratch = [turned(EXT_BLOCKS[0]), pltpu.VMEM((4 * BLOCK, PAIR), F32)]
    return run(forward_inner_kernel, "forward_inner", 12, [bias], [q, kv], outputs, scratch, LARGE)


def forward_edge(place, bias, q, kv, halo, inner):
    width = q.shape[1]
    inputs = [q, kv, *halo[::-1], inner]
    outputs = [held((4 * BLOCK, width), BF16), held((width // PAIR, 24, BLOCK), F32)]
    scratch = [turned(EXT_TOTAL), pltpu.VMEM((4 * BLOCK, PAIR), F32)]
    return run(forward_edge_kernel, "forward_edge", 12, [place, bias], inputs, outputs, scratch)


def edge_backward(place, bias, stats, q, kv, halo, d_att):
    rows, width = 4 * BLOCK, q.shape[1]
    edge = held((2, 3 * BLOCK, width), BF16)
    inputs = [stats, q, kv, *halo[::-1], d_att]
    outputs = [held((rows, width), F32), held((2, rows, width), F32), edge, edge]
    scratch = [
        turned(EXT_TOTAL),
        pltpu.VMEM((2, EXT_TOTAL, BLOCK, PAIR), F32),
        pltpu.VMEM((rows, PAIR), F32),
        pltpu.VMEM((rows, PAIR), F32),
        pltpu.VMEM((2, *edge.shape), BF16),
    ]
    return run(edge_kernel, "edge_backward", 20, [place, bias], inputs, outputs, scratch)


def inner_backward(bias, stats, q, kv, d_att, dq_f, d_kv):
    rows, width = 4 * BLOCK, q.shape[1]
    inputs = [stats, q, kv, d_att, dq_f, d_kv]
    outputs = [held((rows, width), BF16), held((2, rows, width), F32)]
    scratch = [turned(EXT_BLOCKS[0]), pltpu.VMEM((rows, PAIR), F32)]
    return run(inner_units_kernel, "inner_backward", 12, [bias], inputs, outputs, scratch)


def term_outputs(rows, width):
    return [held((rows, width), BF16)] * MP


def store_terms(step, terms, own, keep_right, keep_left, right, left):
    own[block_rows(step), :] = terms[0]
    low, high = block_rows(step % 2), block_rows(2 + step % 2)
    if step < 2:
        keep_right[low, :] = terms[1]
        right[high, :] = terms[2]
        left[low, :] = terms[3]
    else:
        right[low, :] = terms[1]
        left[high, :] = terms[2]
        keep_left[low, :] = terms[3]


def out_terms_kernel(place, attended, w_out, *outs):
    me = place[0]
    width = attended.shape[1]
    for step in range(4):
        rows = attended[block_rows(step), :]
        for r, out in enumerate(outs):
            term = nn(rows, w_out[:, share_rows(me, r, width)])
            out[block_rows(step), :] = term.astype(BF16)


def out_terms(place, attended, w_out):
    outputs = term_outputs(*attended.shape)
    return run(out_terms_kernel, "out_terms", 8, [place], [attended, w_out], outputs)


def input_terms_kernel(
    place, d_query, d_kv, from_other, from_core, normed, w, d_proj,
    dots, own, keep_right, keep_left, right, left, dot_rows, w_turned,
):
    halo = (place, from_core, from_other)
    width = d_query.shape[1]
    half = spread_matrix(BLOCK // 2, 2, 0.5)
    quarter = spread_matrix(BLOCK // 4, 4, 0.25)
    dot_rows[12:16, :] = jnp.zeros((4, BLOCK), F32)
    for r in range(MP):
        for n in range(3):
            at = slice(r * width, (r + 1) * width)
            w_turned[block_rows(n), at] = w[at, n * width : (n + 1) * width].T
    for step in range(4):
        rows = block_rows(step)
        grads = [d_query[rows, :]]
        mid_rows = slice(256 + (step % 2) * 128, 384 + (step % 2) * 128)
        low_rows = slice(512 + step * 64, 576 + step * 64)
        first = step < 2
        for n in range(2):
            total = d_kv[n, rows, :]
            if step in (0, 3):
                fine = halo_rows(halo, first, (n, slice(0, BLOCK), slice(None)))
                total = total + fine.astype(F32)
            total = total + nn(half, halo_rows(halo, first, (n, mid_rows, slice(None))))
            total = total + nn(quarter, from_core[n, low_rows, :])
            total = total + nn(quarter, from_other[n, low_rows, :])
            grads.append(total.astype(BF16))
        for n, grad in enumerate(grads[1:]):
            d_proj[rows, n * width : (n + 1) * width] = grad
        dot = None
        every = jnp.concatenate(grads, axis=1)
        terms = []
        for r in range(MP):
            term = nn(every, w_turned[:, r * width : (r + 1) * width]).astype(BF16)
            terms.append(term)
            part = term.astype(F32) * normed[rows, r * width : (r + 1) * width].astype(F32)
            dot = part if dot is None else dot + part
        store_terms(step, terms, own, keep_right, keep_left, right, left)
        dot = as_row(jnp.sum(dot, axis=1, keepdims=True))
        first = dot.astype(BF16).astype(F32)
        second = (dot - first).astype(BF16).astype(F32)
        for n, piece in enumerate((first, second, dot - first - second)):
            dot_rows[4 * n + step : 4 * n + step + 1, :] = piece
    pieces = dot_rows[...].astype(BF16)
    dots[...] = pieces
    right[4 * BLOCK :, :] = pieces
    left[4 * BLOCK :, :] = pieces


def input_terms(place, d_query, d_kv, halo, normed, w):
    rows, width = d_query.shape
    inputs = [d_query, d_kv, *halo[::-1], normed, w]
    outputs = [held((rows, 2 * width), BF16), held((DOT_ROWS, width), BF16)]
    lengths = [rows, rows // 2, rows // 2, rows + DOT_ROWS, rows + DOT_ROWS]
    outputs += [held((n, width), BF16) for n in lengths]
    scratch = [pltpu.VMEM((DOT_ROWS, width), F32), pltpu.VMEM((3 * width, MP * width), BF16)]
    return run(input_terms_kernel, "input_terms", 18, [place], inputs, outputs, scratch)


def sum_terms(own, received, at):
    total = own[at, :].astype(F32)
    for term in received:
        total = total + term[at, :].astype(F32)
    return total


def finish_out_kernel(own, one, two, three, result):
    for b in range(4):
        at = block_rows(b)
        result[at, :] = sum_terms(own, (one, two, three), at).astype(BF16)


def finish_out(own, received):
    outputs = [held(own.shape, BF16)]
    return run(finish_out_kernel, "finish_out", 8, [], [own, *received], outputs)[0]


def relay_kernel(keep_right, keep_left, l1, r1, onward_right, onward_left):
    half = keep_right.shape[0]
    passed = l1[half : 2 * half, :].astype(F32)
    onward_right[0:half, :] = (keep_right[...].astype(F32) + passed).astype(BF16)
    passed = r1[half : 2 * half, :].astype(F32)
    onward_left[...] = (keep_left[...].astype(F32) + passed).astype(BF16)
    if onward_right.shape[0] > half:
        onward_right[half:, :] = l1[2 * half :, :]


def relay(keep_right, keep_left, l1, r1):
    half, width = keep_right.shape
    outputs = [held((half + DOT_ROWS, width), BF16), held((half, width), BF16)]
    return run(relay_kernel, "relay", 4, [], [keep_right, keep_left, l1, r1], outputs, (), RELAY)


def finish_grad_kernel(own, l1, r1, l2, r2, tokens, inverse, dots, result):
    rows, width = own.shape
    half = r2.shape[0]
    pieces = dots[...].astype(F32)
    for message, first in ((l1, rows), (r1, rows), (l2, half)):
        pieces = pieces + message[first : first + DOT_ROWS, :].astype(F32)
    means = (pieces[0:4] + pieces[4:8] + pieces[8:12]) / (MP * width)
    for b in range(rows // BLOCK):
        at, near = block_rows(b), block_rows(b % 2)
        mean = as_column(means[b : b + 1, :])
        inv = as_column(inverse[b : b + 1, :])
        total = own[at, :].astype(F32)
        for part in (r1, l2) if b < 2 else (l1, r2):
            total = total + part[near, :].astype(F32)
        result[at, :] = inv * (total - tokens[at, :].astype(F32) * inv * mean)


def finish_grad(own, l1, r1, l2, r2, tokens, inverse, dots):
    inputs = [own, l1, r1, l2, r2, tokens, inverse, dots]
    outputs = [held(own.shape, F32)]
    return run(finish_grad_kernel, "finish_grad", 8, [], inputs, outputs)[0]


def early_kernel(g0, g1, g2, g3, attended, normed, d_query, outer, inner):
    width = g0.shape[1]
    rows = attended[...]
    for r, share in enumerate((g0, g1, g2, g3)):
        at = slice(r * width, (r + 1) * width)
        outer[at, :] = tn(share[...], rows).astype(BF16)
        inner[at, :] = tn(normed[:, at], d_query[...]).astype(BF16)


def early_terms(shares, attended, normed, d_query):
    width = attended.shape[1]
    inputs = [*shares, attended, normed, d_query]
    outputs = [held((MP * width, width), BF16)] * 2
    return run(early_kernel, "early_terms", 14, [], inputs, outputs, (), LARGE)


def inner_kernel(place, normed, d_proj, inner, outer, mine, other_low, other_high, rows_held):
    core = place[1]
    width = outer.shape[1]
    for block in range(MP):
        at = block_rows(block)
        rows_held[at, 0:width] = inner[at, :]
        rows_held[at, width : 3 * width] = tn(normed[:, at], d_proj[...]).astype(BF16)
        rows_held[at, 3 * width :] = outer[at, :]
        for n in range(width // 64):
            out = slice((4 * block + n) * 32, (4 * block + n + 1) * 32)
            first = block * width + n * 64
            mine[out, :] = rows_held[pl.ds(pl.multiple_of(first + core * 32, 32), 32), :]
            other, start = (other_low, 0) if block < 2 else (other_high, 256)
            other[out.start - start : out.stop - start, :] = rows_held[pl.ds(pl.multiple_of(first + 32 - core * 32, 32), 32), :]


def inner_terms(place, normed, d_proj, inner, outer):
    total = normed.shape[1]
    width = outer.shape[1]
    outputs = [held((n, 4 * width), BF16) for n in (total // 2, total // 4, total // 4)]
    scratch = [pltpu.VMEM((total, 4 * width), BF16)]
    return run(inner_kernel, "inner_terms", 16, [place], [normed, d_proj, inner, outer], outputs, scratch)


def pair_sum_kernel(place, mine, got_low, got_high, *outs):
    z, core, x, y = place[0], place[1], place[2], place[3]
    for d, out in enumerate(outs):
        for n in range(4):
            chunk = jnp.where(core == 0, 4 * n + ((x + d) & 3), 4 * ((y + d - z + 4) & 3) + n)
            rows = pl.ds(pl.multiple_of(chunk * 32, 32), 32)
            half = pl.ds(pl.multiple_of((chunk & 7) * 32, 32), 32)
            got = jnp.where(chunk < 8, got_low[half, :], got_high[half, :])
            total = mine[rows, :].astype(F32) + got.astype(F32)
            out[32 * n : 32 * (n + 1), :] = total.astype(BF16)


def row_sum_kernel(place, a, b, c, d, *refs):
    *outs, total = refs
    z, core, x, y = place[0], place[1], place[2], place[3]
    first = jnp.where(core == 0, y - z + 4, x)
    total[...] = (
        a[...].astype(F32) + b[...].astype(F32) + c[...].astype(F32) + d[...].astype(F32)
    ).astype(BF16)
    for n, out in enumerate(outs):
        out[...] = total[pl.ds(pl.multiple_of(((first + n) & 3) * 32, 32), 32), :]


def last_sum_kernel(a, b, c, d, gq, gk, gv, go):
    width = gq.shape[1]
    total = a[...].astype(F32) + b[...].astype(F32) + c[...].astype(F32) + d[...].astype(F32)
    gq[...] = total[:, 0:width]
    gk[...] = total[:, width : 2 * width]
    gv[...] = total[:, 2 * width : 3 * width]
    go[...] = total[:, 3 * width :]


def sum_over_core(place, mine, *others):
    got = [lax.ppermute(other, "seq", [(i, i ^ 1) for i in range(32)]) for other in others]
    parts = [held((128, mine.shape[1]), BF16)] * 4
    return run(pair_sum_kernel, "pair_sum", 6, [place], [mine, *got], parts)


def sum_over_seq(place, parts, *first):
    cols = parts[0].shape[1]

    def sent(value, stage, d):
        pairs = []
        for i in range(32):
            core, x, y = i % 2, (i // 2) % 4, i // 8
            if stage == core:
                x = (x + d) % 4
            else:
                y = (y + d) % 4
            pairs.append((i, (y * 4 + x) * 2 + core))
        return lax.ppermute(value, "seq", pairs)

    parts = [parts[0]] + [sent(parts[d], 0, d) for d in (1, 2, 3)]
    parts = tied(parts, *first)
    rows = [held((32, cols), BF16)] * 4
    scratch = [pltpu.VMEM((128, cols), BF16)]
    rows = run(row_sum_kernel, "row_sum", 4, [place], parts, rows, scratch)
    rows = [rows[0]] + [sent(rows[d], 1, d) for d in (1, 2, 3)]
    outputs = [held((32, cols // 4), F32)] * 4
    return run(last_sum_kernel, "last_sum", 4, [], rows, outputs)


def to_next(value):
    return lax.ppermute(value, "mp", [(i, (i + 1) % MP) for i in range(MP)])


def to_previous(value):
    return lax.ppermute(value, "mp", [((i + 1) % MP, i) for i in range(MP)])


def gather_shares(share):
    half = share.shape[0] // 2
    low, high = share[:half], share[half:]
    after_low, before_high = to_previous(low), to_next(high)
    after_high, before_low = to_previous(high), to_next(low)
    far_low, far_high = to_previous(after_low), to_next(before_high)
    return [share, after_low, after_high, far_low, far_high, before_low, before_high]


def turned_by(value, step):
    return lax.ppermute(value, "mp", [(i, (i + step) % MP) for i in range(MP)])


def sum_over_mp(terms):
    return [turned_by(term, step) for step, term in zip((1, 2, 3), terms)]


def exchange(to_core, to_other):
    count = lax.axis_size("seq")
    pairs = []
    for i in range(1, count - 1, 2):
        pairs += [(i, i + 1), (i + 1, i)]
    from_other = lax.ppermute(to_other, "seq", pairs)
    from_core = lax.ppermute(to_core, "seq", [(i, i ^ 1) for i in range(count)])
    return from_core, from_other


def tied(values, *others):
    flat, tree = jax.tree.flatten(values)
    flat = lax.optimization_barrier((*flat, *others))[: len(flat)]
    return jax.tree.unflatten(tree, flat)


def per_device(tokens, w_query, w_key, w_value, w_out, grad_out):
    count = lax.axis_size("seq")
    index = lax.axis_index("seq")
    me = jnp.stack([lax.axis_index("mp"), index & 1, (index >> 1) & 3, index >> 3])
    me = me.astype(jnp.int32)
    bias = jnp.stack(
        [
            jnp.where(index == 0, NEGATIVE, 0.0).astype(F32),
            jnp.where(index == count - 1, NEGATIVE, 0.0).astype(F32),
        ]
    )
    token_shares = gather_shares(tokens)
    near_grad = tied(grad_out, *(token_shares[n] for n in (1, 2, 5, 6)))
    far_grad = tied(grad_out, *token_shares)
    far = turned_by(far_grad, 2)
    grad_shares = [grad_out, to_previous(near_grad), far, to_next(near_grad)]
    inverse, q, kv, to_core, to_other, normed, w = project(
        me, token_shares, w_query, w_key, w_value
    )
    halo = exchange(to_core, to_other)
    near_q = tied(q, grad_shares[1], grad_shares[3])
    inner_out, inner_stats = forward_inner(bias, near_q, kv)
    attended, stats = forward_edge(me, bias, q, kv, halo, inner_out)
    out_own, *terms = out_terms(me, attended, w_out)
    out_received = sum_over_mp(terms)
    grad_shares = tied(grad_shares, out_own)
    d_att = cotangent(me, grad_shares, w_out)
    dq_f, d_kv, to_core, to_other = edge_backward(me, bias, stats, q, kv, halo, d_att)
    halo = exchange(to_core, to_other)
    d_query, d_kv = inner_backward(bias, inner_stats, q, kv, d_att, dq_f, d_kv)
    attended = tied(attended, *out_received)
    outer, inner = early_terms(grad_shares, attended, normed, d_query)
    d_query = tied(d_query, outer)
    d_proj, dots, own, keep_right, keep_left, right, left = input_terms(
        me, d_query, d_kv, halo, normed, w
    )
    attn_out = finish_out(out_own, out_received)
    mine, *others = inner_terms(me, normed, d_proj, inner, outer)
    core_sums = sum_over_core(me, mine, *others)
    l1, r1 = to_next(right), to_previous(left)
    onward_right, onward_left = relay(keep_right, keep_left, l1, r1)
    l2, r2 = to_next(onward_right), to_previous(onward_left)
    grad_tokens = finish_grad(own, l1, r1, l2, r2, tokens, inverse, dots)
    *weight_grads, grad_w_out = sum_over_seq(me, core_sums, onward_right)
    return (attn_out, grad_tokens, *weight_grads, grad_w_out.T)


def solution(mesh):
    return jax.shard_map(
        per_device,
        mesh=mesh,
        in_specs=(
            P("seq", "mp"),
            P(None, "mp"),
            P(None, "mp"),
            P(None, "mp"),
            P("mp", None),
            P("seq", "mp"),
        ),
        out_specs=(
            P("seq", "mp"),
            P("seq", "mp"),
            P("seq", "mp"),
            P("seq", "mp"),
            P("seq", "mp"),
            P("mp", "seq"),
        ),
        check_vma=False,
    )
```

```python
import jax
import jax.numpy as jnp
from jax import lax
from jax.experimental import pallas as pl
from jax.experimental.pallas import tpu as pltpu
from jax.sharding import PartitionSpec as P

HD = 64
BLOCK = 256
LEVELS = 3
PAIR = 2 * HD
MP = 4
LANES = 128
DOT_ROWS = 16

EPSILON = 1e-06
NEGATIVE = -1e30

F32 = jnp.float32
BF16 = jnp.bfloat16

FIRST_EXT = (0, 6, 10)
EXT_BLOCKS = (6, 4, 3)
EXT_TOTAL = 13


def nn(left, right):
    return lax.dot_general(left, right, (((1,), (0,)), ((), ())), preferred_element_type=F32)


def nt(left, right):
    return lax.dot_general(left, right, (((1,), (1,)), ((), ())), preferred_element_type=F32)


def tn(left, right):
    return lax.dot_general(left, right, (((0,), (0,)), ((), ())), preferred_element_type=F32)


def pool_matrix(coarse, factor, value):
    shape = (coarse, coarse * factor)
    row = lax.broadcasted_iota(jnp.int32, shape, 0)
    low = row * factor
    col = lax.broadcasted_iota(jnp.int32, shape, 1)
    return jnp.where((col >= low) & (col < low + factor), value, 0.0).astype(BF16)


def pool_both(half, quarter):
    parts = [pool_matrix(BLOCK // 2, 2, half), pool_matrix(BLOCK // 4, 4, quarter)]
    return jnp.concatenate(parts, axis=0)


def spread_matrix(coarse, factor, value):
    shape = (coarse * factor, coarse)
    low = lax.broadcasted_iota(jnp.int32, shape, 1) * factor
    row = lax.broadcasted_iota(jnp.int32, shape, 0)
    return jnp.where((row >= low) & (row < low + factor), value, 0.0).astype(BF16)


def share_rows(me, step, width):
    return pl.ds(pl.multiple_of(((me + step) & (MP - 1)) * width, width), width)


SMALL = pl.CostEstimate(flops=10**6, bytes_accessed=10**4, transcendentals=0)
LARGE = pl.CostEstimate(flops=4 * 10**9, bytes_accessed=10**4, transcendentals=0)
MIDDLE = pl.CostEstimate(flops=25 * 10**8, bytes_accessed=10**4, transcendentals=0)
RELAY = pl.CostEstimate(flops=10**9, bytes_accessed=10**4, transcendentals=0)
SCALAR = pl.BlockSpec(memory_space=pltpu.SMEM)
RESIDENT = pl.BlockSpec(memory_space=pltpu.VMEM)


def held(shape, dtype):
    return jax.ShapeDtypeStruct(shape, dtype)


def run(kernel, name, limit_mib, scalars, inputs, outputs, scratch=(), cost=SMALL):
    return pl.pallas_call(
        kernel,
        in_specs=[SCALAR] * len(scalars) + [RESIDENT] * len(inputs),
        out_specs=[RESIDENT] * len(outputs),
        out_shape=outputs,
        scratch_shapes=list(scratch),
        compiler_params=pltpu.CompilerParams(vmem_limit_bytes=limit_mib * 2**20),
        cost_estimate=cost,
        name=name,
    )(*scalars, *inputs)


def block_rows(block):
    return slice(block * BLOCK, (block + 1) * BLOCK)


ALL_ROWS = 7 * BLOCK
EDGE_ROWS = 256 + 128 + 192
LEVEL_BLOCK = (0, 4, 6)


def share_edges(place, edges, to_core, to_other):
    core = place[1]
    to_core[...] = edges[1 - core]
    to_other[...] = edges[core]


def halo_rows(halo, left, index):
    place, from_core, from_other = halo
    near, away = from_core[index], from_other[index]
    return jnp.where(place[1] == 0, away if left else near, near if left else away)


def as_row(column):
    return jnp.broadcast_to(column, (column.shape[0], LANES)).T[0:1, :]


def as_column(row):
    return jnp.broadcast_to(row, (LANES, row.shape[1])).T[:, 0:1]


def project_kernel(
    place, t1a_any, t1b_any, t2a_any, t2b_any, t3a_any, t3b_any,
    t0_hbm, wq_hbm, wk_hbm, wv_hbm,
    inverse, q, kv, to_core, to_other, normed_hbm, w_hbm,
    t0, t1, t2, t3, w, normed, edges, in_sems, out_sems,
):
    me = place[0]
    width = t0.shape[1]
    low, high = pl.ds(0, 2 * BLOCK), pl.ds(2 * BLOCK, 2 * BLOCK)
    moves = [
        (t0_hbm, t0),
        (t1a_any, t1.at[low]),
        (t2a_any, t2.at[low]),
        (t3a_any, t3.at[low]),
        (t1b_any, t1.at[high]),
        (t2b_any, t2.at[high]),
        (t3b_any, t3.at[high]),
    ]
    for n, source in enumerate((wq_hbm, wk_hbm, wv_hbm)):
        for r in range(MP):
            target = w.at[pl.ds(r * width, width), pl.ds(n * width, width)]
            moves.append((source.at[share_rows(me, r, width), :], target))
    loads = [
        pltpu.make_async_copy(source, target, in_sems.at[n])
        for n, (source, target) in enumerate(moves)
    ]
    for load in loads:
        load.start()
    pools = pool_both(0.5, 0.25)
    inverse[4:8, :] = jnp.zeros((4, BLOCK), F32)
    stores = []

    def normalise(step):
        if step in (0, 2):
            for load in loads[0:4] if step == 0 else loads[4:7]:
                load.wait()
        rows = block_rows(step)
        shares = [share[rows, :].astype(F32) for share in (t0, t1, t2, t3)]
        squares = shares[0] * shares[0]
        for share in shares[1:]:
            squares = squares + share * share
        total = jnp.sum(squares, axis=1, keepdims=True)
        inv = lax.rsqrt(total / (MP * width) + EPSILON)
        inverse[step : step + 1, :] = as_row(inv)
        parts = [(share * inv).astype(BF16) for share in shares]
        for r, part in enumerate(parts):
            normed[rows, r * width : (r + 1) * width] = part
        store = pltpu.make_async_copy(normed.at[rows], normed_hbm.at[rows], out_sems.at[step])
        store.start()
        stores.append(store)
        return jnp.concatenate(parts, axis=1)

    def spread(step, whole):
        if step == 0:
            for load in loads[7:]:
                load.wait()
            store = pltpu.make_async_copy(w, w_hbm, out_sems.at[4])
            store.start()
            stores.append(store)
        rows = block_rows(step)
        fine = [nn(whole, w[:, n * width : (n + 1) * width]).astype(BF16) for n in range(3)]
        coarse = [nn(pools, x).astype(BF16) for x in fine]
        mid = [x[0:128] for x in coarse]
        low = [x[128:192] for x in coarse]
        mid_rows = slice(1024 + step * 128, 1024 + (step + 1) * 128)
        low_rows = slice(1536 + step * 64, 1536 + (step + 1) * 64)
        q[rows, :] = fine[0]
        q[mid_rows, :] = mid[0]
        q[low_rows, :] = low[0]
        for n in range(2):
            kv[n, rows, :] = fine[1 + n]
            kv[n, mid_rows, :] = mid[1 + n]
            kv[n, low_rows, :] = low[1 + n]
            if step in (0, 3):
                edges[step // 3, n, 0:BLOCK, :] = fine[1 + n]
            if step in (1, 2):
                edges[step - 1, n, 256:384, :] = mid[1 + n]
            if step > 0:
                edges[0, n, 320 + step * 64 : 384 + step * 64, :] = low[1 + n]
            if step < 3:
                edges[1, n, 384 + step * 64 : 448 + step * 64, :] = low[1 + n]

    parts = normalise(0)
    for step in range(4):
        following = normalise(step + 1) if step < 3 else None
        spread(step, parts)
        parts = following
    share_edges(place, edges, to_core, to_other)
    for store in stores:
        store.wait()


def project(place, shares, wq, wk, wv):
    rows, width = shares[0].shape
    out = jax.ShapeDtypeStruct
    edge = out((2, EDGE_ROWS, width), BF16)
    anywhere = pl.BlockSpec(memory_space=pl.ANY)
    share = pltpu.VMEM((rows, width), BF16)
    fixed = [
        pltpu.with_memory_space_constraint(value, pltpu.HBM)
        for value in (*shares[1:], shares[0], wq, wk, wv)
    ]
    return pl.pallas_call(
        project_kernel,
        in_specs=[SCALAR] + [anywhere] * 10,
        out_specs=[RESIDENT] * 5 + [anywhere] * 2,
        out_shape=[
            out((8, width), F32),
            out((ALL_ROWS, width), BF16),
            out((2, ALL_ROWS, width), BF16),
            edge,
            edge,
            pltpu.HBM((rows, MP * width), BF16),
            pltpu.HBM((MP * width, 3 * width), BF16),
        ],
        scratch_shapes=[share] * 4
        + [
            pltpu.VMEM((MP * width, 3 * width), BF16),
            pltpu.VMEM((rows, MP * width), BF16),
            pltpu.VMEM((2, *edge.shape), BF16),
            pltpu.SemaphoreType.DMA((19,)),
            pltpu.SemaphoreType.DMA((5,)),
        ],
        compiler_params=pltpu.CompilerParams(vmem_limit_bytes=20 * 2**20),
        cost_estimate=SMALL,
        name="project",
    )(place, *fixed)


def cotangent_kernel(place, g0, g1, g2, g3, w_out, d_att, w_turned):
    me = place[0]
    width = g0.shape[1]
    pools = pool_both(1.0, 1.0)
    for r in range(MP):
        w_turned[block_rows(r), :] = w_out[:, share_rows(me, r, width)].T
    for step in range(4):
        rows = block_rows(step)
        shares = jnp.concatenate([share[rows, :] for share in (g0, g1, g2, g3)], axis=1)
        fine = nn(shares, w_turned[...]).astype(BF16)
        d_att[rows, :] = fine
        coarse = nn(pools, fine).astype(BF16)
        d_att[1024 + step * 128 : 1024 + (step + 1) * 128, :] = coarse[0:128]
        d_att[1536 + step * 64 : 1536 + (step + 1) * 64, :] = coarse[128:192]


def cotangent(place, shares, w_out):
    rows, width = shares[0].shape
    outputs = [held((ALL_ROWS, width), BF16)]
    scratch = [pltpu.VMEM((MP * width, width), BF16)]
    return run(cotangent_kernel, "cotangent", 10, [place], [*shares, w_out], outputs, scratch)[0]


EDGE_UNITS = ((0, 0), (0, 3), (1, 0), (1, 1), (2, 0))
INNER_UNITS = ((0, 1), (0, 2))


def unit_keys(level, block):
    last = EXT_BLOCKS[level] - 1
    offsets = (0, 1, 2) if level == 0 else (0, 2)
    keys = []
    for offset in offsets:
        at = block + offset
        keys.append((at, 0 if at == 0 else 1 if at == last else None))
    return keys


def ext_rows(kv, halo, n, level, at, lanes):
    if at in (0, EXT_BLOCKS[level] - 1):
        return halo[0 if at == 0 else 1][n, block_rows(level), lanes]
    return kv[n, block_rows(LEVEL_BLOCK[level] + at - 1), lanes]


def head_part(lane, head, rows):
    mine = (lane >= head * HD) & (lane < (head + 1) * HD)
    return jnp.where(mine, rows, 0.0).astype(BF16)


def unit_scores(keys, key_rows, query, bias_ref):
    scores = []
    for (_, bias), rows in zip(keys, key_rows):
        s = nt(rows, query)
        scores.append(s if bias is None else s + bias_ref[bias])
    return scores


def add_spread(target, block, factor, rows):
    if factor == 1:
        target[block_rows(block), :] = target[block_rows(block), :] + rows
        return
    for s in range(factor):
        spread = pl.ds(block * factor * BLOCK + s, BLOCK, factor)
        target[spread, :] = target[spread, :] + rows


def each_pair(width, body):
    def step(pair, _):
        body(pair, pl.ds(pl.multiple_of(pair * PAIR, PAIR), PAIR))
        return 0

    lax.fori_loop(0, width // PAIR, step, 0)


def head_part(lane, head, rows):
    mine = (lane >= head * HD) & (lane < (head + 1) * HD)
    return jnp.where(mine, rows, 0.0).astype(BF16)


def unit_scores(keys, key_rows, query, bias_ref):
    scores = []
    for (_, bias), rows in zip(keys, key_rows):
        s = nt(rows, query)
        scores.append(s if bias is None else s + bias_ref[bias])
    return scores


def add_spread(target, block, factor, rows):
    if factor == 1:
        target[block_rows(block), :] = target[block_rows(block), :] + rows
        return
    for s in range(factor):
        spread = pl.ds(block * factor * BLOCK + s, BLOCK, factor)
        target[spread, :] = target[spread, :] + rows


def forward_units(pair, lanes, units, bias_ref, q, kv, halo, stats, vt, out_f):
    lane = lax.broadcasted_iota(jnp.int32, (BLOCK, PAIR), 1)
    done = set()
    for level, block in units:
        for at, _ in unit_keys(level, block):
            if (level, at) not in done:
                done.add((level, at))
                rows = ext_rows(kv, halo, 1, level, at, lanes)
                vt[FIRST_EXT[level] + at] = rows.T

    def begin(u, head):
        level, block = units[u]
        keys = unit_keys(level, block)
        key_rows = [ext_rows(kv, halo, 0, level, at, lanes) for at, _ in keys]
        q_rows = q[block_rows(LEVEL_BLOCK[level] + block), lanes] * HD ** (-0.5)
        return unit_scores(keys, key_rows, head_part(lane, head, q_rows), bias_ref)

    def finish(u, head, scores):
        level, block = units[u]
        top = scores[0].max(axis=0, keepdims=True)
        for s in scores[1:]:
            top = jnp.maximum(top, s.max(axis=0, keepdims=True))
        exps = [jnp.exp(s - top) for s in scores]
        total = exps[0].sum(axis=0, keepdims=True)
        for e in exps[1:]:
            total = total + e.sum(axis=0, keepdims=True)
        scale = 1.0 / total
        row = 4 * u + 2 * head
        stats[pair, row : row + 1, :] = top
        stats[pair, row + 1 : row + 2, :] = scale
        return [(e * scale).astype(BF16) for e in exps]

    outs = []

    def give(u, head, weights):
        level, block = units[u]
        part = slice(head * HD, (head + 1) * HD)
        o_t = None
        for (at, _), w in zip(unit_keys(level, block), weights):
            o = nn(vt[FIRST_EXT[level] + at, part, :], w)
            o_t = o if o_t is None else o_t + o
        outs.append(o_t)
        if head == 1:
            add_spread(out_f, block, 2**level, jnp.concatenate(outs, axis=0).T)
            outs.clear()

    items = [(u, head) for u in range(len(units)) for head in range(2)]
    scores, last = begin(*items[0]), None
    for n, item in enumerate(items):
        following = begin(*items[n + 1]) if n + 1 < len(items) else None
        if last is not None:
            give(*items[n - 1], last)
        last = finish(*item, scores)
        scores = following
    give(*items[-1], last)


def forward_inner_kernel(bias_ref, q, kv, out, stats, vt, out_f):
    def one(pair, lanes):
        out_f[...] = jnp.zeros_like(out_f)
        forward_units(pair, lanes, INNER_UNITS, bias_ref, q, kv, None, stats, vt, out_f)
        out[:, lanes] = out_f[BLOCK : 3 * BLOCK, :]

    each_pair(q.shape[1], one)


def forward_edge_kernel(
    place, bias_ref, q, kv, from_other, from_core, inner,
    attended, stats, left, right, vt, out_f,
):
    received = (place, from_core, from_other)
    pools = pool_both(0.5, 0.25)
    every = slice(None)
    for n in range(2):
        for out, is_left in ((left, True), (right, False)):
            fine = halo_rows(received, is_left, (n, slice(0, 256), every))
            mid = halo_rows(received, is_left, (n, slice(256, 384), every))
            low = halo_rows(received, is_left, (n, slice(384, 576), every))
            coarse = nn(pools, fine).astype(BF16)
            out[n, 0:256, :] = fine
            if is_left:
                out[n, 256:384, :], out[n, 384:512, :] = mid, coarse[0:128]
                out[n, 512:704, :], out[n, 704:768, :] = low, coarse[128:192]
            else:
                out[n, 256:384, :], out[n, 384:512, :] = coarse[0:128], mid
                out[n, 512:576, :], out[n, 576:768, :] = coarse[128:192], low
    halo = (left, right)

    def one(pair, lanes):
        out_f[0:BLOCK, :] = jnp.zeros((BLOCK, PAIR), F32)
        out_f[BLOCK : 3 * BLOCK, :] = inner[:, lanes]
        out_f[3 * BLOCK :, :] = jnp.zeros((BLOCK, PAIR), F32)
        forward_units(
            pair, lanes, EDGE_UNITS, bias_ref, q, kv, halo, stats, vt, out_f
        )
        attended[:, lanes] = out_f[...].astype(BF16)

    each_pair(q.shape[1], one)


def backward_units(
    pair, lanes, units, bias_ref, q, kv, halo, grads, stats, kt, dq_f, keep
):
    lane = lax.broadcasted_iota(jnp.int32, (BLOCK, PAIR), 1)
    done = set()
    for level, block in units:
        for at, _ in unit_keys(level, block):
            if (level, at) not in done:
                done.add((level, at))
                rows = ext_rows(kv, halo, 0, level, at, lanes)
                kt[FIRST_EXT[level] + at] = rows.T

    def begin(u, head):
        level, block = units[u]
        keys = unit_keys(level, block)
        key_rows = [ext_rows(kv, halo, 0, level, at, lanes) for at, _ in keys]
        value_rows = [ext_rows(kv, halo, 1, level, at, lanes) for at, _ in keys]
        at = block_rows(LEVEL_BLOCK[level] + block)
        qm = head_part(lane, head, q[at, lanes] * HD ** (-0.5))
        am = head_part(lane, head, grads[at, lanes])
        scores = unit_scores(keys, key_rows, qm, bias_ref)
        return qm, am, scores, [nt(rows, am) for rows in value_rows]

    def finish(u, head, qm, am, scores, d_weights):
        level, block = units[u]
        row = 4 * u + 2 * head
        top, scale = stats[pair, row : row + 1, :], stats[pair, row + 1 : row + 2, :]
        probs = [jnp.exp(s - top) * scale for s in scores]
        dots = None
        for p, dw in zip(probs, d_weights):
            d = (p * dw).sum(axis=0, keepdims=True)
            dots = d if dots is None else dots + d
        weights = [p.astype(BF16) for p in probs]
        d_scores = [(p * (dw - dots)).astype(BF16) for p, dw in zip(probs, d_weights)]
        return qm, am, weights, d_scores

    first = []

    def give(u, head, qm, am, weights, d_scores):
        level, block = units[u]
        keys = unit_keys(level, block)
        part = slice(head * HD, (head + 1) * HD)
        d_values = [nn(w, am) for w in weights]
        d_keys = [nn(ds, qm) for ds in d_scores]
        dq_t = None
        for (at, _), ds in zip(keys, d_scores):
            g = nn(kt[FIRST_EXT[level] + at, part, :], ds)
            dq_t = g if dq_t is None else dq_t + g
        if head == 0:
            first.append((dq_t, d_keys, d_values))
            return
        dq_first, k_first, v_first = first.pop()
        for n, (at, _) in enumerate(keys):
            keep(0, level, at, k_first[n] + d_keys[n])
            keep(1, level, at, v_first[n] + d_values[n])
        dq = jnp.concatenate([dq_first, dq_t], axis=0).T * (HD ** (-0.5) / 2**level)
        add_spread(dq_f, block, 2**level, dq)

    items = [(u, head) for u in range(len(units)) for head in range(2)]
    ready, last = begin(*items[0]), None
    for n, item in enumerate(items):
        following = begin(*items[n + 1]) if n + 1 < len(items) else None
        if last is not None:
            give(*items[n - 1], *last)
        last = finish(*item, *ready)
        ready = following
    give(*items[-1], *last)


def edge_kernel(
    place, bias_ref, stats, q, kv, left, right, grads,
    dq_f, d_kv, to_core, to_other, kt, ext, dq_s, sums, edges,
):
    halo = (left, right)

    def add_rows(factor, rows):
        for s in range(factor):
            spread = pl.ds(s, rows.shape[0], factor)
            sums[spread, :] = sums[spread, :] + rows * (1.0 / factor)

    def one(pair, lanes):
        dq_s[...] = jnp.zeros_like(dq_s)
        seen = set()

        def keep(n, level, at, rows):
            slot = FIRST_EXT[level] + at
            if (n, slot) in seen:
                ext[n, slot] = ext[n, slot] + rows
            else:
                seen.add((n, slot))
                ext[n, slot] = rows

        backward_units(
            pair, lanes, EDGE_UNITS, bias_ref, q, kv, halo, grads, stats, kt, dq_s, keep,
        )
        dq_f[:, lanes] = dq_s[...]
        for n in range(2):
            for side in range(2):
                fine, mid, low = (
                    ext[n, FIRST_EXT[level] + side * (EXT_BLOCKS[level] - 1)]
                    for level in range(LEVELS)
                )
                if side == 0:
                    (mid, mid_near), (low, low_near) = (mid[0:128], mid[128:]), (low[0:192], low[192:])
                else:
                    (mid_near, mid), (low_near, low) = (mid[0:128], mid[128:]), (low[0:64], low[64:])
                sums[0:BLOCK, :] = fine
                add_rows(2, mid_near)
                add_rows(4, low_near)
                edges[side, n, 0:256, lanes] = sums[0:BLOCK, :].astype(BF16)
                edges[side, n, 256:384, lanes] = mid.astype(BF16)
                edges[side, n, 384:576, lanes] = low.astype(BF16)
            for b in range(4):
                sums[block_rows(b), :] = ext[n, 1 + b]
            for b in range(2):
                add_spread(sums, b, 2, ext[n, FIRST_EXT[1] + 1 + b] * 0.5)
            d_kv[n, :, lanes] = sums[...]

    each_pair(q.shape[1], one)
    share_edges(place, edges, to_core, to_other)


def inner_units_kernel(bias_ref, stats, q, kv, grads, dq_in, d_kv_in, d_query, d_kv, kt, dq_s):
    def one(pair, lanes):
        dq_s[...] = dq_in[:, lanes]
        d_kv[:, :, lanes] = d_kv_in[:, :, lanes]

        def keep(n, level, at, rows):
            where = block_rows(at - 1)
            d_kv[n, where, lanes] = d_kv[n, where, lanes] + rows

        backward_units(
            pair, lanes, INNER_UNITS, bias_ref, q, kv, None, grads, stats, kt, dq_s, keep
        )
        d_query[:, lanes] = dq_s[...].astype(BF16)

    each_pair(q.shape[1], one)


def turned(count):
    return pltpu.VMEM((count, PAIR, BLOCK), BF16)


def forward_inner(bias, q, kv):
    width = q.shape[1]
    outputs = [held((2 * BLOCK, width), F32), held((width // PAIR, 8, BLOCK), F32)]
    scratch = [turned(EXT_BLOCKS[0]), pltpu.VMEM((4 * BLOCK, PAIR), F32)]
    return run(forward_inner_kernel, "forward_inner", 12, [bias], [q, kv], outputs, scratch, MIDDLE)


def forward_edge(place, bias, q, kv, halo, inner):
    width = q.shape[1]
    inputs = [q, kv, *halo[::-1], inner]
    outputs = [held((4 * BLOCK, width), BF16), held((width // PAIR, 24, BLOCK), F32)]
    outputs += [held((2, 3 * BLOCK, width), BF16)] * 2
    scratch = [turned(EXT_TOTAL), pltpu.VMEM((4 * BLOCK, PAIR), F32)]
    return run(forward_edge_kernel, "forward_edge", 12, [place, bias], inputs, outputs, scratch)


def edge_backward(place, bias, stats, q, kv, halo, d_att):
    rows, width = 4 * BLOCK, q.shape[1]
    edge = held((2, EDGE_ROWS, width), BF16)
    inputs = [stats, q, kv, *halo, d_att]
    outputs = [held((rows, width), F32), held((2, rows, width), F32), edge, edge]
    scratch = [
        turned(EXT_TOTAL),
        pltpu.VMEM((2, EXT_TOTAL, BLOCK, PAIR), F32),
        pltpu.VMEM((rows, PAIR), F32),
        pltpu.VMEM((rows, PAIR), F32),
        pltpu.VMEM((2, *edge.shape), BF16),
    ]
    return run(edge_kernel, "edge_backward", 20, [place, bias], inputs, outputs, scratch)


def inner_backward(bias, stats, q, kv, d_att, dq_f, d_kv):
    rows, width = 4 * BLOCK, q.shape[1]
    inputs = [stats, q, kv, d_att, dq_f, d_kv]
    outputs = [held((rows, width), BF16), held((2, rows, width), F32)]
    scratch = [turned(EXT_BLOCKS[0]), pltpu.VMEM((rows, PAIR), F32)]
    return run(inner_units_kernel, "inner_backward", 12, [bias], inputs, outputs, scratch)


def term_outputs(rows, width):
    return [held((rows, width), BF16)] * MP


def store_terms(step, terms, own, keep_right, keep_left, right, left):
    own[block_rows(step), :] = terms[0]
    low, high = block_rows(step % 2), block_rows(2 + step % 2)
    if step < 2:
        keep_right[low, :] = terms[1]
        right[high, :] = terms[2]
        left[low, :] = terms[3]
    else:
        right[low, :] = terms[1]
        left[high, :] = terms[2]
        keep_left[low, :] = terms[3]


def out_terms_kernel(place, attended, w_out, *outs):
    me = place[0]
    width = attended.shape[1]
    for step in range(4):
        rows = attended[block_rows(step), :]
        for r, out in enumerate(outs):
            term = nn(rows, w_out[:, share_rows(me, r, width)])
            out[block_rows(step), :] = term.astype(BF16)


def out_terms(place, attended, w_out):
    outputs = term_outputs(*attended.shape)
    return run(out_terms_kernel, "out_terms", 8, [place], [attended, w_out], outputs)


def input_terms_kernel(
    place, d_query, d_kv, from_other, from_core, normed, w, d_proj,
    dots, own, keep_right, keep_left, right, left, dot_rows, w_turned,
):
    halo = (place, from_core, from_other)
    width = d_query.shape[1]
    half = spread_matrix(BLOCK // 2, 2, 0.5)
    quarter = spread_matrix(BLOCK // 4, 4, 0.25)
    dot_rows[12:16, :] = jnp.zeros((4, BLOCK), F32)
    for r in range(MP):
        for n in range(3):
            at = slice(r * width, (r + 1) * width)
            w_turned[block_rows(n), at] = w[at, n * width : (n + 1) * width].T
    for step in range(4):
        rows = block_rows(step)
        grads = [d_query[rows, :]]
        every = slice(None)
        for n in range(2):
            total = d_kv[n, rows, :]
            if step in (0, 3):
                total = total + halo_rows(halo, step == 0, (n, slice(0, 256), every)).astype(F32)
            else:
                total = total + nn(half, halo_rows(halo, step == 1, (n, slice(256, 384), every)))
            if step > 0:
                low = slice(320 + step * 64, 384 + step * 64)
                total = total + nn(quarter, halo_rows(halo, True, (n, low, every)))
            if step < 3:
                low = slice(384 + step * 64, 448 + step * 64)
                total = total + nn(quarter, halo_rows(halo, False, (n, low, every)))
            grads.append(total.astype(BF16))
        for n, grad in enumerate(grads[1:]):
            d_proj[rows, n * width : (n + 1) * width] = grad
        dot = None
        every = jnp.concatenate(grads, axis=1)
        terms = []
        for r in range(MP):
            term = nn(every, w_turned[:, r * width : (r + 1) * width]).astype(BF16)
            terms.append(term)
            part = term.astype(F32) * normed[rows, r * width : (r + 1) * width].astype(F32)
            dot = part if dot is None else dot + part
        store_terms(step, terms, own, keep_right, keep_left, right, left)
        dot = as_row(jnp.sum(dot, axis=1, keepdims=True))
        first = dot.astype(BF16).astype(F32)
        second = (dot - first).astype(BF16).astype(F32)
        for n, piece in enumerate((first, second, dot - first - second)):
            dot_rows[4 * n + step : 4 * n + step + 1, :] = piece
    pieces = dot_rows[...].astype(BF16)
    dots[...] = pieces
    right[4 * BLOCK :, :] = pieces
    left[4 * BLOCK :, :] = pieces


def input_terms(place, d_query, d_kv, halo, normed, w):
    rows, width = d_query.shape
    inputs = [d_query, d_kv, *halo[::-1], normed, w]
    outputs = [held((rows, 2 * width), BF16), held((DOT_ROWS, width), BF16)]
    lengths = [rows, rows // 2, rows // 2, rows + DOT_ROWS, rows + DOT_ROWS]
    outputs += [held((n, width), BF16) for n in lengths]
    scratch = [pltpu.VMEM((DOT_ROWS, width), F32), pltpu.VMEM((3 * width, MP * width), BF16)]
    return run(input_terms_kernel, "input_terms", 18, [place], inputs, outputs, scratch)


def sum_terms(own, received, at):
    total = own[at, :].astype(F32)
    for term in received:
        total = total + term[at, :].astype(F32)
    return total


def finish_out_kernel(own, one, two, three, result):
    for b in range(4):
        at = block_rows(b)
        result[at, :] = sum_terms(own, (one, two, three), at).astype(BF16)


def finish_out(own, received):
    outputs = [held(own.shape, BF16)]
    return run(finish_out_kernel, "finish_out", 8, [], [own, *received], outputs)[0]


def relay_kernel(keep_right, keep_left, l1, r1, onward_right, onward_left):
    half = keep_right.shape[0]
    passed = l1[half : 2 * half, :].astype(F32)
    onward_right[0:half, :] = (keep_right[...].astype(F32) + passed).astype(BF16)
    passed = r1[half : 2 * half, :].astype(F32)
    onward_left[...] = (keep_left[...].astype(F32) + passed).astype(BF16)
    if onward_right.shape[0] > half:
        onward_right[half:, :] = l1[2 * half :, :]


def relay(keep_right, keep_left, l1, r1):
    half, width = keep_right.shape
    outputs = [held((half + DOT_ROWS, width), BF16), held((half, width), BF16)]
    return run(relay_kernel, "relay", 4, [], [keep_right, keep_left, l1, r1], outputs, (), RELAY)


def finish_grad_kernel(own, l1, r1, l2, r2, tokens, inverse, dots, result):
    rows, width = own.shape
    half = r2.shape[0]
    pieces = dots[...].astype(F32)
    for message, first in ((l1, rows), (r1, rows), (l2, half)):
        pieces = pieces + message[first : first + DOT_ROWS, :].astype(F32)
    means = (pieces[0:4] + pieces[4:8] + pieces[8:12]) / (MP * width)
    for b in range(rows // BLOCK):
        at, near = block_rows(b), block_rows(b % 2)
        mean = as_column(means[b : b + 1, :])
        inv = as_column(inverse[b : b + 1, :])
        total = own[at, :].astype(F32)
        for part in (r1, l2) if b < 2 else (l1, r2):
            total = total + part[near, :].astype(F32)
        result[at, :] = inv * (total - tokens[at, :].astype(F32) * inv * mean)


def finish_grad(own, l1, r1, l2, r2, tokens, inverse, dots):
    inputs = [own, l1, r1, l2, r2, tokens, inverse, dots]
    outputs = [held(own.shape, F32)]
    return run(finish_grad_kernel, "finish_grad", 8, [], inputs, outputs)[0]


def early_kernel(g0, g1, g2, g3, attended, normed, d_query, outer, inner):
    width = g0.shape[1]
    rows = attended[...]
    for r, share in enumerate((g0, g1, g2, g3)):
        at = slice(r * width, (r + 1) * width)
        outer[at, :] = tn(share[...], rows).astype(BF16)
        inner[at, :] = tn(normed[:, at], d_query[...]).astype(BF16)


def early_terms(shares, attended, normed, d_query):
    width = attended.shape[1]
    inputs = [*shares, attended, normed, d_query]
    outputs = [held((MP * width, width), BF16)] * 2
    return run(early_kernel, "early_terms", 14, [], inputs, outputs, (), LARGE)


def inner_kernel(place, normed, d_proj, inner, outer, mine, other_low, other_high, rows_held):
    core = place[1]
    width = outer.shape[1]
    for block in range(MP):
        at = block_rows(block)
        rows_held[at, 0:width] = inner[at, :]
        rows_held[at, width : 3 * width] = tn(normed[:, at], d_proj[...]).astype(BF16)
        rows_held[at, 3 * width :] = outer[at, :]
        for n in range(width // 64):
            out = slice((4 * block + n) * 32, (4 * block + n + 1) * 32)
            first = block * width + n * 64
            mine[out, :] = rows_held[pl.ds(pl.multiple_of(first + core * 32, 32), 32), :]
            other, start = (other_low, 0) if block < 2 else (other_high, 256)
            other[out.start - start : out.stop - start, :] = rows_held[pl.ds(pl.multiple_of(first + 32 - core * 32, 32), 32), :]


def inner_terms(place, normed, d_proj, inner, outer):
    total = normed.shape[1]
    width = outer.shape[1]
    outputs = [held((n, 4 * width), BF16) for n in (total // 2, total // 4, total // 4)]
    scratch = [pltpu.VMEM((total, 4 * width), BF16)]
    return run(inner_kernel, "inner_terms", 16, [place], [normed, d_proj, inner, outer], outputs, scratch)


def pair_sum_kernel(place, mine, got_low, got_high, *outs):
    z, core, x, y = place[0], place[1], place[2], place[3]
    for d, out in enumerate(outs):
        for n in range(4):
            chunk = jnp.where(core == 0, 4 * n + ((x + d) & 3), 4 * ((y + d - z + 4) & 3) + n)
            rows = pl.ds(pl.multiple_of(chunk * 32, 32), 32)
            half = pl.ds(pl.multiple_of((chunk & 7) * 32, 32), 32)
            got = jnp.where(chunk < 8, got_low[half, :], got_high[half, :])
            total = mine[rows, :].astype(F32) + got.astype(F32)
            out[32 * n : 32 * (n + 1), :] = total.astype(BF16)


def row_sum_kernel(place, a, b, c, d, *refs):
    *outs, total = refs
    z, core, x, y = place[0], place[1], place[2], place[3]
    first = jnp.where(core == 0, y - z + 4, x)
    total[...] = (
        a[...].astype(F32) + b[...].astype(F32) + c[...].astype(F32) + d[...].astype(F32)
    ).astype(BF16)
    for n, out in enumerate(outs):
        out[...] = total[pl.ds(pl.multiple_of(((first + n) & 3) * 32, 32), 32), :]


def last_sum_kernel(a, b, c, d, gq, gk, gv, go):
    width = gq.shape[1]
    total = a[...].astype(F32) + b[...].astype(F32) + c[...].astype(F32) + d[...].astype(F32)
    gq[...] = total[:, 0:width]
    gk[...] = total[:, width : 2 * width]
    gv[...] = total[:, 2 * width : 3 * width]
    go[...] = total[:, 3 * width :]


def sum_over_core(place, mine, *others):
    got = [lax.ppermute(other, "seq", [(i, i ^ 1) for i in range(32)]) for other in others]
    parts = [held((128, mine.shape[1]), BF16)] * 4
    return run(pair_sum_kernel, "pair_sum", 6, [place], [mine, *got], parts)


def sum_over_seq(place, parts, *first):
    cols = parts[0].shape[1]

    def sent(value, stage, d):
        pairs = []
        for i in range(32):
            core, x, y = i % 2, (i // 2) % 4, i // 8
            if stage == core:
                x = (x + d) % 4
            else:
                y = (y + d) % 4
            pairs.append((i, (y * 4 + x) * 2 + core))
        return lax.ppermute(value, "seq", pairs)

    parts = [parts[0]] + [sent(parts[d], 0, d) for d in (1, 2, 3)]
    parts = tied(parts, *first)
    rows = [held((32, cols), BF16)] * 4
    scratch = [pltpu.VMEM((128, cols), BF16)]
    rows = run(row_sum_kernel, "row_sum", 4, [place], parts, rows, scratch)
    rows = [rows[0]] + [sent(rows[d], 1, d) for d in (1, 2, 3)]
    outputs = [held((32, cols // 4), F32)] * 4
    return run(last_sum_kernel, "last_sum", 4, [], rows, outputs)


def to_next(value):
    return lax.ppermute(value, "mp", [(i, (i + 1) % MP) for i in range(MP)])


def to_previous(value):
    return lax.ppermute(value, "mp", [((i + 1) % MP, i) for i in range(MP)])


def gather_shares(share):
    half = share.shape[0] // 2
    low, high = share[:half], share[half:]
    after_low, before_high = to_previous(low), to_next(high)
    after_high, before_low = to_previous(high), to_next(low)
    far_low, far_high = to_previous(after_low), to_next(before_high)
    return [share, after_low, after_high, far_low, far_high, before_low, before_high]


def turned_by(value, step):
    return lax.ppermute(value, "mp", [(i, (i + step) % MP) for i in range(MP)])


def sum_over_mp(terms):
    return [turned_by(term, step) for step, term in zip((1, 2, 3), terms)]


def exchange(to_core, to_other):
    count = lax.axis_size("seq")
    pairs = []
    for i in range(1, count - 1, 2):
        pairs += [(i, i + 1), (i + 1, i)]
    from_other = lax.ppermute(to_other, "seq", pairs)
    from_core = lax.ppermute(to_core, "seq", [(i, i ^ 1) for i in range(count)])
    return from_core, from_other


def tied(values, *others):
    flat, tree = jax.tree.flatten(values)
    flat = lax.optimization_barrier((*flat, *others))[: len(flat)]
    return jax.tree.unflatten(tree, flat)


def per_device(tokens, w_query, w_key, w_value, w_out, grad_out):
    count = lax.axis_size("seq")
    index = lax.axis_index("seq")
    me = jnp.stack([lax.axis_index("mp"), index & 1, (index >> 1) & 3, index >> 3])
    me = me.astype(jnp.int32)
    bias = jnp.stack(
        [
            jnp.where(index == 0, NEGATIVE, 0.0).astype(F32),
            jnp.where(index == count - 1, NEGATIVE, 0.0).astype(F32),
        ]
    )
    token_shares = gather_shares(tokens)
    near_grad = tied(grad_out, *(token_shares[n] for n in (1, 2, 5, 6)))
    far_grad = tied(grad_out, *token_shares)
    far = turned_by(far_grad, 2)
    grad_shares = [grad_out, to_previous(near_grad), far, to_next(near_grad)]
    inverse, q, kv, to_core, to_other, normed, w = project(
        me, token_shares, w_query, w_key, w_value
    )
    halo = exchange(to_core, to_other)
    near_q = tied(q, grad_shares[1], grad_shares[3])
    inner_out, inner_stats = forward_inner(bias, near_q, kv)
    attended, stats, *halo = forward_edge(me, bias, q, kv, halo, inner_out)
    out_own, *terms = out_terms(me, attended, w_out)
    out_received = sum_over_mp(terms)
    grad_shares = tied(grad_shares, out_own)
    d_att = cotangent(me, grad_shares, w_out)
    dq_f, d_kv, to_core, to_other = edge_backward(me, bias, stats, q, kv, halo, d_att)
    halo = exchange(to_core, to_other)
    d_query, d_kv = inner_backward(bias, inner_stats, q, kv, d_att, dq_f, d_kv)
    attended = tied(attended, *out_received)
    outer, inner = early_terms(grad_shares, attended, normed, d_query)
    d_query = tied(d_query, outer)
    d_proj, dots, own, keep_right, keep_left, right, left = input_terms(
        me, d_query, d_kv, halo, normed, w
    )
    attn_out = finish_out(out_own, out_received)
    mine, *others = inner_terms(me, normed, d_proj, inner, outer)
    core_sums = sum_over_core(me, mine, *others)
    l1, r1 = to_next(right), to_previous(left)
    onward_right, onward_left = relay(keep_right, keep_left, l1, r1)
    l2, r2 = to_next(onward_right), to_previous(onward_left)
    grad_tokens = finish_grad(own, l1, r1, l2, r2, tokens, inverse, dots)
    *weight_grads, grad_w_out = sum_over_seq(me, core_sums, onward_right)
    return (attn_out, grad_tokens, *weight_grads, grad_w_out.T)


def solution(mesh):
    return jax.shard_map(
        per_device,
        mesh=mesh,
        in_specs=(
            P("seq", "mp"),
            P(None, "mp"),
            P(None, "mp"),
            P(None, "mp"),
            P("mp", None),
            P("seq", "mp"),
        ),
        out_specs=(
            P("seq", "mp"),
            P("seq", "mp"),
            P("seq", "mp"),
            P("seq", "mp"),
            P("seq", "mp"),
            P("mp", "seq"),
        ),
        check_vma=False,
    )
```

```python
import jax
import jax.numpy as jnp
from jax import lax
from jax.experimental import pallas as pl
from jax.experimental.pallas import tpu as pltpu
from jax.sharding import PartitionSpec as P

HD = 64
BLOCK = 256
LEVELS = 3
PAIR = 2 * HD
MP = 4
LANES = 128
DOT_ROWS = 16

EPSILON = 1e-06
NEGATIVE = -1e30

F32 = jnp.float32
BF16 = jnp.bfloat16

FIRST_EXT = (0, 6, 10)
EXT_BLOCKS = (6, 4, 3)
EXT_TOTAL = 13


def nn(left, right):
    return lax.dot_general(left, right, (((1,), (0,)), ((), ())), preferred_element_type=F32)


def nt(left, right):
    return lax.dot_general(left, right, (((1,), (1,)), ((), ())), preferred_element_type=F32)


def tn(left, right):
    return lax.dot_general(left, right, (((0,), (0,)), ((), ())), preferred_element_type=F32)


def pool_matrix(coarse, factor, value):
    shape = (coarse, coarse * factor)
    row = lax.broadcasted_iota(jnp.int32, shape, 0)
    low = row * factor
    col = lax.broadcasted_iota(jnp.int32, shape, 1)
    return jnp.where((col >= low) & (col < low + factor), value, 0.0).astype(BF16)


def pool_both(half, quarter):
    parts = [pool_matrix(BLOCK // 2, 2, half), pool_matrix(BLOCK // 4, 4, quarter)]
    return jnp.concatenate(parts, axis=0)


def spread_matrix(coarse, factor, value):
    shape = (coarse * factor, coarse)
    low = lax.broadcasted_iota(jnp.int32, shape, 1) * factor
    row = lax.broadcasted_iota(jnp.int32, shape, 0)
    return jnp.where((row >= low) & (row < low + factor), value, 0.0).astype(BF16)


def share_rows(me, step, width):
    return pl.ds(pl.multiple_of(((me + step) & (MP - 1)) * width, width), width)


SMALL = pl.CostEstimate(flops=10**6, bytes_accessed=10**4, transcendentals=0)
LARGE = pl.CostEstimate(flops=4 * 10**9, bytes_accessed=10**4, transcendentals=0)
MIDDLE = pl.CostEstimate(flops=25 * 10**8, bytes_accessed=10**4, transcendentals=0)
RELAY = pl.CostEstimate(flops=10**9, bytes_accessed=10**4, transcendentals=0)
SCALAR = pl.BlockSpec(memory_space=pltpu.SMEM)
RESIDENT = pl.BlockSpec(memory_space=pltpu.VMEM)


def held(shape, dtype):
    return jax.ShapeDtypeStruct(shape, dtype)


def run(kernel, name, limit_mib, scalars, inputs, outputs, scratch=(), cost=SMALL):
    return pl.pallas_call(
        kernel,
        in_specs=[SCALAR] * len(scalars) + [RESIDENT] * len(inputs),
        out_specs=[RESIDENT] * len(outputs),
        out_shape=outputs,
        scratch_shapes=list(scratch),
        compiler_params=pltpu.CompilerParams(vmem_limit_bytes=limit_mib * 2**20),
        cost_estimate=cost,
        name=name,
    )(*scalars, *inputs)


def block_rows(block):
    return slice(block * BLOCK, (block + 1) * BLOCK)


ALL_ROWS = 7 * BLOCK
EDGE_ROWS = 256 + 128 + 192
LEVEL_BLOCK = (0, 4, 6)


def share_edges(place, edges, to_core, to_other):
    core = place[1]
    to_core[...] = edges[1 - core]
    to_other[...] = edges[core]


def halo_rows(halo, left, index):
    place, from_core, from_other = halo
    near, away = from_core[index], from_other[index]
    return jnp.where(place[1] == 0, away if left else near, near if left else away)


def as_row(column):
    return jnp.broadcast_to(column, (column.shape[0], LANES)).T[0:1, :]


def as_column(row):
    return jnp.broadcast_to(row, (LANES, row.shape[1])).T[:, 0:1]


def project_kernel(
    place, t1a_any, t1b_any, t2a_any, t2b_any, t3a_any, t3b_any,
    t0_hbm, wq_hbm, wk_hbm, wv_hbm,
    inverse, q, kv, to_core, to_other, normed_hbm, w_hbm,
    t0, t1, t2, t3, w, normed, edges, in_sems, out_sems,
):
    me = place[0]
    width = t0.shape[1]
    low, high = pl.ds(0, 2 * BLOCK), pl.ds(2 * BLOCK, 2 * BLOCK)
    moves = [
        (t0_hbm, t0),
        (t1a_any, t1.at[low]),
        (t2a_any, t2.at[low]),
        (t3a_any, t3.at[low]),
        (t1b_any, t1.at[high]),
        (t2b_any, t2.at[high]),
        (t3b_any, t3.at[high]),
    ]
    for n, source in enumerate((wq_hbm, wk_hbm, wv_hbm)):
        for r in range(MP):
            target = w.at[pl.ds(r * width, width), pl.ds(n * width, width)]
            moves.append((source.at[share_rows(me, r, width), :], target))
    loads = [
        pltpu.make_async_copy(source, target, in_sems.at[n])
        for n, (source, target) in enumerate(moves)
    ]
    for load in loads:
        load.start()
    pools = pool_both(0.5, 0.25)
    inverse[4:8, :] = jnp.zeros((4, BLOCK), F32)
    stores = []

    def normalise(step):
        if step in (0, 2):
            for load in loads[0:4] if step == 0 else loads[4:7]:
                load.wait()
        rows = block_rows(step)
        shares = [share[rows, :].astype(F32) for share in (t0, t1, t2, t3)]
        squares = shares[0] * shares[0]
        for share in shares[1:]:
            squares = squares + share * share
        total = jnp.sum(squares, axis=1, keepdims=True)
        inv = lax.rsqrt(total / (MP * width) + EPSILON)
        inverse[step : step + 1, :] = as_row(inv)
        parts = [(share * inv).astype(BF16) for share in shares]
        for r, part in enumerate(parts):
            normed[rows, r * width : (r + 1) * width] = part
        store = pltpu.make_async_copy(normed.at[rows], normed_hbm.at[rows], out_sems.at[step])
        store.start()
        stores.append(store)
        return jnp.concatenate(parts, axis=1)

    def spread(step, whole):
        if step == 0:
            for load in loads[7:]:
                load.wait()
            store = pltpu.make_async_copy(w, w_hbm, out_sems.at[4])
            store.start()
            stores.append(store)
        rows = block_rows(step)
        fine = [nn(whole, w[:, n * width : (n + 1) * width]).astype(BF16) for n in range(3)]
        coarse = [nn(pools, x).astype(BF16) for x in fine]
        mid = [x[0:128] for x in coarse]
        low = [x[128:192] for x in coarse]
        mid_rows = slice(1024 + step * 128, 1024 + (step + 1) * 128)
        low_rows = slice(1536 + step * 64, 1536 + (step + 1) * 64)
        q[rows, :] = fine[0]
        q[mid_rows, :] = mid[0]
        q[low_rows, :] = low[0]
        for n in range(2):
            kv[n, rows, :] = fine[1 + n]
            kv[n, mid_rows, :] = mid[1 + n]
            kv[n, low_rows, :] = low[1 + n]
            if step in (0, 3):
                edges[step // 3, n, 0:BLOCK, :] = fine[1 + n]
            if step in (1, 2):
                edges[step - 1, n, 256:384, :] = mid[1 + n]
            if step > 0:
                edges[0, n, 320 + step * 64 : 384 + step * 64, :] = low[1 + n]
            if step < 3:
                edges[1, n, 384 + step * 64 : 448 + step * 64, :] = low[1 + n]

    parts = normalise(0)
    for step in range(4):
        following = normalise(step + 1) if step < 3 else None
        spread(step, parts)
        parts = following
    share_edges(place, edges, to_core, to_other)
    for store in stores:
        store.wait()


def project(place, shares, wq, wk, wv):
    rows, width = shares[0].shape
    out = jax.ShapeDtypeStruct
    edge = out((2, EDGE_ROWS, width), BF16)
    anywhere = pl.BlockSpec(memory_space=pl.ANY)
    share = pltpu.VMEM((rows, width), BF16)
    fixed = [
        pltpu.with_memory_space_constraint(value, pltpu.HBM)
        for value in (*shares[1:], shares[0], wq, wk, wv)
    ]
    return pl.pallas_call(
        project_kernel,
        in_specs=[SCALAR] + [anywhere] * 10,
        out_specs=[RESIDENT] * 5 + [anywhere] * 2,
        out_shape=[
            out((8, width), F32),
            out((ALL_ROWS, width), BF16),
            out((2, ALL_ROWS, width), BF16),
            edge,
            edge,
            pltpu.HBM((rows, MP * width), BF16),
            pltpu.HBM((MP * width, 3 * width), BF16),
        ],
        scratch_shapes=[share] * 4
        + [
            pltpu.VMEM((MP * width, 3 * width), BF16),
            pltpu.VMEM((rows, MP * width), BF16),
            pltpu.VMEM((2, *edge.shape), BF16),
            pltpu.SemaphoreType.DMA((19,)),
            pltpu.SemaphoreType.DMA((5,)),
        ],
        compiler_params=pltpu.CompilerParams(vmem_limit_bytes=20 * 2**20),
        cost_estimate=SMALL,
        name="project",
    )(place, *fixed)


def near_kernel(place, g0, g1, g3, w_out, total, w_turned):
    me = place[0]
    width = g0.shape[1]
    for n, r in enumerate((0, 1, 3)):
        w_turned[block_rows(n), :] = w_out[:, share_rows(me, r, width)].T
    for step in range(4):
        rows = block_rows(step)
        shares = jnp.concatenate([share[rows, :] for share in (g0, g1, g3)], axis=1)
        total[rows, :] = nn(shares, w_turned[...])


def near_cotangent(place, shares, w_out):
    rows, width = shares[0].shape
    inputs = [*shares, w_out]
    scratch = [pltpu.VMEM((3 * width, width), BF16)]
    outputs = [held((rows, width), F32)]
    return run(near_kernel, "near_cotangent", 10, [place], inputs, outputs, scratch)[0]


def cotangent_kernel(place, near, g2, w_out, d_att, w_turned):
    width = g2.shape[1]
    pools = pool_both(1.0, 1.0)
    w_turned[...] = w_out[:, share_rows(place[0], 2, width)].T
    for step in range(4):
        rows = block_rows(step)
        fine = (near[rows, :] + nn(g2[rows, :], w_turned[...])).astype(BF16)
        d_att[rows, :] = fine
        coarse = nn(pools, fine).astype(BF16)
        d_att[1024 + step * 128 : 1024 + (step + 1) * 128, :] = coarse[0:128]
        d_att[1536 + step * 64 : 1536 + (step + 1) * 64, :] = coarse[128:192]


def cotangent(place, near, far, w_out):
    width = far.shape[1]
    scratch = [pltpu.VMEM((width, width), BF16)]
    outputs = [held((ALL_ROWS, width), BF16)]
    return run(cotangent_kernel, "cotangent", 10, [place], [near, far, w_out], outputs, scratch)[0]


EDGE_UNITS = ((0, 0), (0, 3), (1, 0), (1, 1), (2, 0))
INNER_UNITS = ((0, 1), (0, 2))


def unit_keys(level, block):
    last = EXT_BLOCKS[level] - 1
    offsets = (0, 1, 2) if level == 0 else (0, 2)
    keys = []
    for offset in offsets:
        at = block + offset
        keys.append((at, 0 if at == 0 else 1 if at == last else None))
    return keys


def ext_rows(kv, halo, n, level, at, lanes):
    if at in (0, EXT_BLOCKS[level] - 1):
        return halo[0 if at == 0 else 1][n, block_rows(level), lanes]
    return kv[n, block_rows(LEVEL_BLOCK[level] + at - 1), lanes]


def head_part(lane, head, rows):
    mine = (lane >= head * HD) & (lane < (head + 1) * HD)
    return jnp.where(mine, rows, 0.0).astype(BF16)


def unit_scores(keys, key_rows, query, bias_ref):
    scores = []
    for (_, bias), rows in zip(keys, key_rows):
        s = nt(rows, query)
        scores.append(s if bias is None else s + bias_ref[bias])
    return scores


def add_spread(target, block, factor, rows):
    if factor == 1:
        target[block_rows(block), :] = target[block_rows(block), :] + rows
        return
    for s in range(factor):
        spread = pl.ds(block * factor * BLOCK + s, BLOCK, factor)
        target[spread, :] = target[spread, :] + rows


def each_pair(width, body):
    def step(pair, _):
        body(pair, pl.ds(pl.multiple_of(pair * PAIR, PAIR), PAIR))
        return 0

    lax.fori_loop(0, width // PAIR, step, 0)


def head_part(lane, head, rows):
    mine = (lane >= head * HD) & (lane < (head + 1) * HD)
    return jnp.where(mine, rows, 0.0).astype(BF16)


def unit_scores(keys, key_rows, query, bias_ref):
    scores = []
    for (_, bias), rows in zip(keys, key_rows):
        s = nt(rows, query)
        scores.append(s if bias is None else s + bias_ref[bias])
    return scores


def add_spread(target, block, factor, rows):
    if factor == 1:
        target[block_rows(block), :] = target[block_rows(block), :] + rows
        return
    for s in range(factor):
        spread = pl.ds(block * factor * BLOCK + s, BLOCK, factor)
        target[spread, :] = target[spread, :] + rows


def forward_units(pair, lanes, units, bias_ref, q, kv, halo, stats, vt, out_f):
    lane = lax.broadcasted_iota(jnp.int32, (BLOCK, PAIR), 1)
    done = set()
    for level, block in units:
        for at, _ in unit_keys(level, block):
            if (level, at) not in done:
                done.add((level, at))
                rows = ext_rows(kv, halo, 1, level, at, lanes)
                vt[FIRST_EXT[level] + at] = rows.T

    def begin(u, head):
        level, block = units[u]
        keys = unit_keys(level, block)
        key_rows = [ext_rows(kv, halo, 0, level, at, lanes) for at, _ in keys]
        q_rows = q[block_rows(LEVEL_BLOCK[level] + block), lanes] * HD ** (-0.5)
        return unit_scores(keys, key_rows, head_part(lane, head, q_rows), bias_ref)

    def finish(u, head, scores):
        level, block = units[u]
        top = scores[0].max(axis=0, keepdims=True)
        for s in scores[1:]:
            top = jnp.maximum(top, s.max(axis=0, keepdims=True))
        exps = [jnp.exp(s - top) for s in scores]
        total = exps[0].sum(axis=0, keepdims=True)
        for e in exps[1:]:
            total = total + e.sum(axis=0, keepdims=True)
        scale = 1.0 / total
        row = 4 * u + 2 * head
        stats[pair, row : row + 1, :] = top
        stats[pair, row + 1 : row + 2, :] = scale
        return [(e * scale).astype(BF16) for e in exps]

    outs = []

    def give(u, head, weights):
        level, block = units[u]
        part = slice(head * HD, (head + 1) * HD)
        o_t = None
        for (at, _), w in zip(unit_keys(level, block), weights):
            o = nn(vt[FIRST_EXT[level] + at, part, :], w)
            o_t = o if o_t is None else o_t + o
        outs.append(o_t)
        if head == 1:
            add_spread(out_f, block, 2**level, jnp.concatenate(outs, axis=0).T)
            outs.clear()

    items = [(u, head) for u in range(len(units)) for head in range(2)]
    scores, last = begin(*items[0]), None
    for n, item in enumerate(items):
        following = begin(*items[n + 1]) if n + 1 < len(items) else None
        if last is not None:
            give(*items[n - 1], last)
        last = finish(*item, scores)
        scores = following
    give(*items[-1], last)


def forward_inner_kernel(bias_ref, q, kv, out, stats, vt, out_f):
    def one(pair, lanes):
        out_f[...] = jnp.zeros_like(out_f)
        forward_units(pair, lanes, INNER_UNITS, bias_ref, q, kv, None, stats, vt, out_f)
        out[:, lanes] = out_f[BLOCK : 3 * BLOCK, :]

    each_pair(q.shape[1], one)


def forward_edge_kernel(
    place, bias_ref, q, kv, from_other, from_core, inner,
    attended, stats, left, right, vt, out_f,
):
    received = (place, from_core, from_other)
    pools = pool_both(0.5, 0.25)
    every = slice(None)
    for n in range(2):
        for out, is_left in ((left, True), (right, False)):
            fine = halo_rows(received, is_left, (n, slice(0, 256), every))
            mid = halo_rows(received, is_left, (n, slice(256, 384), every))
            low = halo_rows(received, is_left, (n, slice(384, 576), every))
            coarse = nn(pools, fine).astype(BF16)
            out[n, 0:256, :] = fine
            if is_left:
                out[n, 256:384, :], out[n, 384:512, :] = mid, coarse[0:128]
                out[n, 512:704, :], out[n, 704:768, :] = low, coarse[128:192]
            else:
                out[n, 256:384, :], out[n, 384:512, :] = coarse[0:128], mid
                out[n, 512:576, :], out[n, 576:768, :] = coarse[128:192], low
    halo = (left, right)

    def one(pair, lanes):
        out_f[0:BLOCK, :] = jnp.zeros((BLOCK, PAIR), F32)
        out_f[BLOCK : 3 * BLOCK, :] = inner[:, lanes]
        out_f[3 * BLOCK :, :] = jnp.zeros((BLOCK, PAIR), F32)
        forward_units(
            pair, lanes, EDGE_UNITS, bias_ref, q, kv, halo, stats, vt, out_f
        )
        attended[:, lanes] = out_f[...].astype(BF16)

    each_pair(q.shape[1], one)


def backward_units(
    pair, lanes, units, bias_ref, q, kv, halo, grads, stats, kt, dq_f, keep
):
    lane = lax.broadcasted_iota(jnp.int32, (BLOCK, PAIR), 1)
    done = set()
    for level, block in units:
        for at, _ in unit_keys(level, block):
            if (level, at) not in done:
                done.add((level, at))
                rows = ext_rows(kv, halo, 0, level, at, lanes)
                kt[FIRST_EXT[level] + at] = rows.T

    def begin(u, head):
        level, block = units[u]
        keys = unit_keys(level, block)
        key_rows = [ext_rows(kv, halo, 0, level, at, lanes) for at, _ in keys]
        value_rows = [ext_rows(kv, halo, 1, level, at, lanes) for at, _ in keys]
        at = block_rows(LEVEL_BLOCK[level] + block)
        qm = head_part(lane, head, q[at, lanes] * HD ** (-0.5))
        am = head_part(lane, head, grads[at, lanes])
        scores = unit_scores(keys, key_rows, qm, bias_ref)
        return qm, am, scores, [nt(rows, am) for rows in value_rows]

    def finish(u, head, qm, am, scores, d_weights):
        level, block = units[u]
        row = 4 * u + 2 * head
        top, scale = stats[pair, row : row + 1, :], stats[pair, row + 1 : row + 2, :]
        probs = [jnp.exp(s - top) * scale for s in scores]
        dots = None
        for p, dw in zip(probs, d_weights):
            d = (p * dw).sum(axis=0, keepdims=True)
            dots = d if dots is None else dots + d
        weights = [p.astype(BF16) for p in probs]
        d_scores = [(p * (dw - dots)).astype(BF16) for p, dw in zip(probs, d_weights)]
        return qm, am, weights, d_scores

    first = []

    def give(u, head, qm, am, weights, d_scores):
        level, block = units[u]
        keys = unit_keys(level, block)
        part = slice(head * HD, (head + 1) * HD)
        d_values = [nn(w, am) for w in weights]
        d_keys = [nn(ds, qm) for ds in d_scores]
        dq_t = None
        for (at, _), ds in zip(keys, d_scores):
            g = nn(kt[FIRST_EXT[level] + at, part, :], ds)
            dq_t = g if dq_t is None else dq_t + g
        if head == 0:
            first.append((dq_t, d_keys, d_values))
            return
        dq_first, k_first, v_first = first.pop()
        for n, (at, _) in enumerate(keys):
            keep(0, level, at, k_first[n] + d_keys[n])
            keep(1, level, at, v_first[n] + d_values[n])
        dq = jnp.concatenate([dq_first, dq_t], axis=0).T * (HD ** (-0.5) / 2**level)
        add_spread(dq_f, block, 2**level, dq)

    items = [(u, head) for u in range(len(units)) for head in range(2)]
    ready, last = begin(*items[0]), None
    for n, item in enumerate(items):
        following = begin(*items[n + 1]) if n + 1 < len(items) else None
        if last is not None:
            give(*items[n - 1], *last)
        last = finish(*item, *ready)
        ready = following
    give(*items[-1], *last)


def edge_kernel(
    place, bias_ref, stats, q, kv, left, right, grads,
    dq_f, d_kv, to_core, to_other, kt, ext, dq_s, sums, edges,
):
    halo = (left, right)

    def add_rows(factor, rows):
        for s in range(factor):
            spread = pl.ds(s, rows.shape[0], factor)
            sums[spread, :] = sums[spread, :] + rows * (1.0 / factor)

    def one(pair, lanes):
        dq_s[...] = jnp.zeros_like(dq_s)
        seen = set()

        def keep(n, level, at, rows):
            slot = FIRST_EXT[level] + at
            if (n, slot) in seen:
                ext[n, slot] = ext[n, slot] + rows
            else:
                seen.add((n, slot))
                ext[n, slot] = rows

        backward_units(
            pair, lanes, EDGE_UNITS, bias_ref, q, kv, halo, grads, stats, kt, dq_s, keep,
        )
        dq_f[:, lanes] = dq_s[...]
        for n in range(2):
            for side in range(2):
                fine, mid, low = (
                    ext[n, FIRST_EXT[level] + side * (EXT_BLOCKS[level] - 1)]
                    for level in range(LEVELS)
                )
                if side == 0:
                    (mid, mid_near), (low, low_near) = (mid[0:128], mid[128:]), (low[0:192], low[192:])
                else:
                    (mid_near, mid), (low_near, low) = (mid[0:128], mid[128:]), (low[0:64], low[64:])
                sums[0:BLOCK, :] = fine
                add_rows(2, mid_near)
                add_rows(4, low_near)
                edges[side, n, 0:256, lanes] = sums[0:BLOCK, :].astype(BF16)
                edges[side, n, 256:384, lanes] = mid.astype(BF16)
                edges[side, n, 384:576, lanes] = low.astype(BF16)
            for b in range(4):
                sums[block_rows(b), :] = ext[n, 1 + b]
            for b in range(2):
                add_spread(sums, b, 2, ext[n, FIRST_EXT[1] + 1 + b] * 0.5)
            d_kv[n, :, lanes] = sums[...]

    each_pair(q.shape[1], one)
    share_edges(place, edges, to_core, to_other)


def inner_units_kernel(bias_ref, stats, q, kv, grads, dq_in, d_kv_in, d_query, d_kv, kt, dq_s):
    def one(pair, lanes):
        dq_s[...] = dq_in[:, lanes]
        d_kv[:, :, lanes] = d_kv_in[:, :, lanes]

        def keep(n, level, at, rows):
            where = block_rows(at - 1)
            d_kv[n, where, lanes] = d_kv[n, where, lanes] + rows

        backward_units(
            pair, lanes, INNER_UNITS, bias_ref, q, kv, None, grads, stats, kt, dq_s, keep
        )
        d_query[:, lanes] = dq_s[...].astype(BF16)

    each_pair(q.shape[1], one)


def turned(count):
    return pltpu.VMEM((count, PAIR, BLOCK), BF16)


def forward_inner(bias, q, kv):
    width = q.shape[1]
    outputs = [held((2 * BLOCK, width), F32), held((width // PAIR, 8, BLOCK), F32)]
    scratch = [turned(EXT_BLOCKS[0]), pltpu.VMEM((4 * BLOCK, PAIR), F32)]
    return run(forward_inner_kernel, "forward_inner", 12, [bias], [q, kv], outputs, scratch, MIDDLE)


def forward_edge(place, bias, q, kv, halo, inner):
    width = q.shape[1]
    inputs = [q, kv, *halo[::-1], inner]
    outputs = [held((4 * BLOCK, width), BF16), held((width // PAIR, 24, BLOCK), F32)]
    outputs += [held((2, 3 * BLOCK, width), BF16)] * 2
    scratch = [turned(EXT_TOTAL), pltpu.VMEM((4 * BLOCK, PAIR), F32)]
    return run(forward_edge_kernel, "forward_edge", 12, [place, bias], inputs, outputs, scratch)


def edge_backward(place, bias, stats, q, kv, halo, d_att):
    rows, width = 4 * BLOCK, q.shape[1]
    edge = held((2, EDGE_ROWS, width), BF16)
    inputs = [stats, q, kv, *halo, d_att]
    outputs = [held((rows, width), F32), held((2, rows, width), F32), edge, edge]
    scratch = [
        turned(EXT_TOTAL),
        pltpu.VMEM((2, EXT_TOTAL, BLOCK, PAIR), F32),
        pltpu.VMEM((rows, PAIR), F32),
        pltpu.VMEM((rows, PAIR), F32),
        pltpu.VMEM((2, *edge.shape), BF16),
    ]
    return run(edge_kernel, "edge_backward", 20, [place, bias], inputs, outputs, scratch)


def inner_backward(bias, stats, q, kv, d_att, dq_f, d_kv):
    rows, width = 4 * BLOCK, q.shape[1]
    inputs = [stats, q, kv, d_att, dq_f, d_kv]
    outputs = [held((rows, width), BF16), held((2, rows, width), F32)]
    scratch = [turned(EXT_BLOCKS[0]), pltpu.VMEM((rows, PAIR), F32)]
    return run(inner_units_kernel, "inner_backward", 12, [bias], inputs, outputs, scratch)


def term_outputs(rows, width):
    return [held((rows, width), BF16)] * MP


def store_terms(step, terms, own, keep_right, keep_left, right, left):
    own[block_rows(step), :] = terms[0]
    low, high = block_rows(step % 2), block_rows(2 + step % 2)
    if step < 2:
        keep_right[low, :] = terms[1]
        right[high, :] = terms[2]
        left[low, :] = terms[3]
    else:
        right[low, :] = terms[1]
        left[high, :] = terms[2]
        keep_left[low, :] = terms[3]


def out_terms_kernel(place, attended, w_out, *outs):
    me = place[0]
    width = attended.shape[1]
    for step in range(4):
        rows = attended[block_rows(step), :]
        for r, out in enumerate(outs):
            term = nn(rows, w_out[:, share_rows(me, r, width)])
            out[block_rows(step), :] = term.astype(BF16)


def out_terms(place, attended, w_out):
    outputs = term_outputs(*attended.shape)
    return run(out_terms_kernel, "out_terms", 8, [place], [attended, w_out], outputs)


def input_terms_kernel(
    place, d_query, d_kv, from_other, from_core, normed, w, d_proj,
    dots, own, keep_right, keep_left, right, left, dot_rows, w_turned,
):
    halo = (place, from_core, from_other)
    width = d_query.shape[1]
    half = spread_matrix(BLOCK // 2, 2, 0.5)
    quarter = spread_matrix(BLOCK // 4, 4, 0.25)
    dot_rows[12:16, :] = jnp.zeros((4, BLOCK), F32)
    for r in range(MP):
        for n in range(3):
            at = slice(r * width, (r + 1) * width)
            w_turned[block_rows(n), at] = w[at, n * width : (n + 1) * width].T
    for step in range(4):
        rows = block_rows(step)
        grads = [d_query[rows, :]]
        every = slice(None)
        for n in range(2):
            total = d_kv[n, rows, :]
            if step in (0, 3):
                total = total + halo_rows(halo, step == 0, (n, slice(0, 256), every)).astype(F32)
            else:
                total = total + nn(half, halo_rows(halo, step == 1, (n, slice(256, 384), every)))
            if step > 0:
                low = slice(320 + step * 64, 384 + step * 64)
                total = total + nn(quarter, halo_rows(halo, True, (n, low, every)))
            if step < 3:
                low = slice(384 + step * 64, 448 + step * 64)
                total = total + nn(quarter, halo_rows(halo, False, (n, low, every)))
            grads.append(total.astype(BF16))
        for n, grad in enumerate(grads[1:]):
            d_proj[rows, n * width : (n + 1) * width] = grad
        dot = None
        every = jnp.concatenate(grads, axis=1)
        terms = []
        for r in range(MP):
            term = nn(every, w_turned[:, r * width : (r + 1) * width]).astype(BF16)
            terms.append(term)
            part = term.astype(F32) * normed[rows, r * width : (r + 1) * width].astype(F32)
            dot = part if dot is None else dot + part
        store_terms(step, terms, own, keep_right, keep_left, right, left)
        dot = as_row(jnp.sum(dot, axis=1, keepdims=True))
        first = dot.astype(BF16).astype(F32)
        second = (dot - first).astype(BF16).astype(F32)
        for n, piece in enumerate((first, second, dot - first - second)):
            dot_rows[4 * n + step : 4 * n + step + 1, :] = piece
    pieces = dot_rows[...].astype(BF16)
    dots[...] = pieces
    right[4 * BLOCK :, :] = pieces
    left[4 * BLOCK :, :] = pieces


def input_terms(place, d_query, d_kv, halo, normed, w):
    rows, width = d_query.shape
    inputs = [d_query, d_kv, *halo[::-1], normed, w]
    outputs = [held((rows, 2 * width), BF16), held((DOT_ROWS, width), BF16)]
    lengths = [rows, rows // 2, rows // 2, rows + DOT_ROWS, rows + DOT_ROWS]
    outputs += [held((n, width), BF16) for n in lengths]
    scratch = [pltpu.VMEM((DOT_ROWS, width), F32), pltpu.VMEM((3 * width, MP * width), BF16)]
    return run(input_terms_kernel, "input_terms", 18, [place], inputs, outputs, scratch)


def sum_terms(own, received, at):
    total = own[at, :].astype(F32)
    for term in received:
        total = total + term[at, :].astype(F32)
    return total


def finish_out_kernel(own, one, two, three, result):
    for b in range(4):
        at = block_rows(b)
        result[at, :] = sum_terms(own, (one, two, three), at).astype(BF16)


def finish_out(own, received):
    outputs = [held(own.shape, BF16)]
    return run(finish_out_kernel, "finish_out", 8, [], [own, *received], outputs)[0]


def relay_kernel(keep_right, keep_left, l1, r1, onward_right, onward_left):
    half = keep_right.shape[0]
    passed = l1[half : 2 * half, :].astype(F32)
    onward_right[0:half, :] = (keep_right[...].astype(F32) + passed).astype(BF16)
    passed = r1[half : 2 * half, :].astype(F32)
    onward_left[...] = (keep_left[...].astype(F32) + passed).astype(BF16)
    if onward_right.shape[0] > half:
        onward_right[half:, :] = l1[2 * half :, :]


def relay(keep_right, keep_left, l1, r1):
    half, width = keep_right.shape
    outputs = [held((half + DOT_ROWS, width), BF16), held((half, width), BF16)]
    return run(relay_kernel, "relay", 4, [], [keep_right, keep_left, l1, r1], outputs, (), RELAY)


def finish_grad_kernel(own, l1, r1, l2, r2, tokens, inverse, dots, result):
    rows, width = own.shape
    half = r2.shape[0]
    pieces = dots[...].astype(F32)
    for message, first in ((l1, rows), (r1, rows), (l2, half)):
        pieces = pieces + message[first : first + DOT_ROWS, :].astype(F32)
    means = (pieces[0:4] + pieces[4:8] + pieces[8:12]) / (MP * width)
    for b in range(rows // BLOCK):
        at, near = block_rows(b), block_rows(b % 2)
        mean = as_column(means[b : b + 1, :])
        inv = as_column(inverse[b : b + 1, :])
        total = own[at, :].astype(F32)
        for part in (r1, l2) if b < 2 else (l1, r2):
            total = total + part[near, :].astype(F32)
        result[at, :] = inv * (total - tokens[at, :].astype(F32) * inv * mean)


def finish_grad(own, l1, r1, l2, r2, tokens, inverse, dots):
    inputs = [own, l1, r1, l2, r2, tokens, inverse, dots]
    outputs = [held(own.shape, F32)]
    return run(finish_grad_kernel, "finish_grad", 8, [], inputs, outputs)[0]


def early_kernel(g0, g1, g2, g3, attended, normed, d_query, outer, inner):
    width = g0.shape[1]
    rows = attended[...]
    for r, share in enumerate((g0, g1, g2, g3)):
        at = slice(r * width, (r + 1) * width)
        outer[at, :] = tn(share[...], rows).astype(BF16)
        inner[at, :] = tn(normed[:, at], d_query[...]).astype(BF16)


def early_terms(shares, attended, normed, d_query):
    width = attended.shape[1]
    inputs = [*shares, attended, normed, d_query]
    outputs = [held((MP * width, width), BF16)] * 2
    return run(early_kernel, "early_terms", 14, [], inputs, outputs, (), LARGE)


def inner_kernel(place, normed, d_proj, inner, outer, mine, other_low, other_high, rows_held):
    core = place[1]
    width = outer.shape[1]
    for block in range(MP):
        at = block_rows(block)
        rows_held[at, 0:width] = inner[at, :]
        rows_held[at, width : 3 * width] = tn(normed[:, at], d_proj[...]).astype(BF16)
        rows_held[at, 3 * width :] = outer[at, :]
        for n in range(width // 64):
            out = slice((4 * block + n) * 32, (4 * block + n + 1) * 32)
            first = block * width + n * 64
            mine[out, :] = rows_held[pl.ds(pl.multiple_of(first + core * 32, 32), 32), :]
            other, start = (other_low, 0) if block < 2 else (other_high, 256)
            other[out.start - start : out.stop - start, :] = rows_held[pl.ds(pl.multiple_of(first + 32 - core * 32, 32), 32), :]


def inner_terms(place, normed, d_proj, inner, outer):
    total = normed.shape[1]
    width = outer.shape[1]
    outputs = [held((n, 4 * width), BF16) for n in (total // 2, total // 4, total // 4)]
    scratch = [pltpu.VMEM((total, 4 * width), BF16)]
    return run(inner_kernel, "inner_terms", 16, [place], [normed, d_proj, inner, outer], outputs, scratch)


def pair_sum_kernel(place, mine, got_low, got_high, *outs):
    z, core, x, y = place[0], place[1], place[2], place[3]
    for d, out in enumerate(outs):
        for n in range(4):
            chunk = jnp.where(core == 0, 4 * n + ((x + d) & 3), 4 * ((y + d - z + 4) & 3) + n)
            rows = pl.ds(pl.multiple_of(chunk * 32, 32), 32)
            half = pl.ds(pl.multiple_of((chunk & 7) * 32, 32), 32)
            got = jnp.where(chunk < 8, got_low[half, :], got_high[half, :])
            total = mine[rows, :].astype(F32) + got.astype(F32)
            out[32 * n : 32 * (n + 1), :] = total.astype(BF16)


def row_sum_kernel(place, a, b, c, d, *refs):
    *outs, total = refs
    z, core, x, y = place[0], place[1], place[2], place[3]
    first = jnp.where(core == 0, y - z + 4, x)
    total[...] = (
        a[...].astype(F32) + b[...].astype(F32) + c[...].astype(F32) + d[...].astype(F32)
    ).astype(BF16)
    for n, out in enumerate(outs):
        out[...] = total[pl.ds(pl.multiple_of(((first + n) & 3) * 32, 32), 32), :]


def last_sum_kernel(a, b, c, d, gq, gk, gv, go):
    width = gq.shape[1]
    total = a[...].astype(F32) + b[...].astype(F32) + c[...].astype(F32) + d[...].astype(F32)
    gq[...] = total[:, 0:width]
    gk[...] = total[:, width : 2 * width]
    gv[...] = total[:, 2 * width : 3 * width]
    go[...] = total[:, 3 * width :]


def sum_over_core(place, mine, *others):
    got = [lax.ppermute(other, "seq", [(i, i ^ 1) for i in range(32)]) for other in others]
    parts = [held((128, mine.shape[1]), BF16)] * 4
    return run(pair_sum_kernel, "pair_sum", 6, [place], [mine, *got], parts)


def sum_over_seq(place, parts, *first):
    cols = parts[0].shape[1]

    def sent(value, stage, d):
        pairs = []
        for i in range(32):
            core, x, y = i % 2, (i // 2) % 4, i // 8
            if stage == core:
                x = (x + d) % 4
            else:
                y = (y + d) % 4
            pairs.append((i, (y * 4 + x) * 2 + core))
        return lax.ppermute(value, "seq", pairs)

    parts = [parts[0]] + [sent(parts[d], 0, d) for d in (1, 2, 3)]
    parts = tied(parts, *first)
    rows = [held((32, cols), BF16)] * 4
    scratch = [pltpu.VMEM((128, cols), BF16)]
    rows = run(row_sum_kernel, "row_sum", 4, [place], parts, rows, scratch)
    rows = [rows[0]] + [sent(rows[d], 1, d) for d in (1, 2, 3)]
    outputs = [held((32, cols // 4), F32)] * 4
    return run(last_sum_kernel, "last_sum", 4, [], rows, outputs)


def to_next(value):
    return lax.ppermute(value, "mp", [(i, (i + 1) % MP) for i in range(MP)])


def to_previous(value):
    return lax.ppermute(value, "mp", [((i + 1) % MP, i) for i in range(MP)])


def gather_shares(share):
    half = share.shape[0] // 2
    low, high = share[:half], share[half:]
    after_low, before_high = to_previous(low), to_next(high)
    after_high, before_low = to_previous(high), to_next(low)
    far_low, far_high = to_previous(after_low), to_next(before_high)
    return [share, after_low, after_high, far_low, far_high, before_low, before_high]


def turned_by(value, step):
    return lax.ppermute(value, "mp", [(i, (i + step) % MP) for i in range(MP)])


def sum_over_mp(terms):
    return [turned_by(term, step) for step, term in zip((1, 2, 3), terms)]


def exchange(to_core, to_other):
    count = lax.axis_size("seq")
    pairs = []
    for i in range(1, count - 1, 2):
        pairs += [(i, i + 1), (i + 1, i)]
    from_other = lax.ppermute(to_other, "seq", pairs)
    from_core = lax.ppermute(to_core, "seq", [(i, i ^ 1) for i in range(count)])
    return from_core, from_other


def tied(values, *others):
    flat, tree = jax.tree.flatten(values)
    flat = lax.optimization_barrier((*flat, *others))[: len(flat)]
    return jax.tree.unflatten(tree, flat)


def per_device(tokens, w_query, w_key, w_value, w_out, grad_out):
    count = lax.axis_size("seq")
    index = lax.axis_index("seq")
    me = jnp.stack([lax.axis_index("mp"), index & 1, (index >> 1) & 3, index >> 3])
    me = me.astype(jnp.int32)
    bias = jnp.stack(
        [
            jnp.where(index == 0, NEGATIVE, 0.0).astype(F32),
            jnp.where(index == count - 1, NEGATIVE, 0.0).astype(F32),
        ]
    )
    token_shares = gather_shares(tokens)
    near_grad = tied(grad_out, *(token_shares[n] for n in (1, 2, 5, 6)))
    far_grad = tied(grad_out, *token_shares)
    far = turned_by(far_grad, 2)
    grad_shares = [grad_out, to_previous(near_grad), far, to_next(near_grad)]
    inverse, q, kv, to_core, to_other, normed, w = project(
        me, token_shares, w_query, w_key, w_value
    )
    halo = exchange(to_core, to_other)
    near_q = tied(q, grad_shares[1], grad_shares[3])
    inner_out, inner_stats = forward_inner(bias, near_q, kv)
    near = near_cotangent(me, tied([grad_shares[n] for n in (0, 1, 3)], inner_out), w_out)
    inner_out = tied(inner_out, near)
    attended, stats, *halo = forward_edge(me, bias, q, kv, halo, inner_out)
    out_own, *terms = out_terms(me, attended, w_out)
    out_received = sum_over_mp(terms)
    grad_shares = tied(grad_shares, out_own)
    d_att = cotangent(me, near, grad_shares[2], w_out)
    dq_f, d_kv, to_core, to_other = edge_backward(me, bias, stats, q, kv, halo, d_att)
    halo = exchange(to_core, to_other)
    d_query, d_kv = inner_backward(bias, inner_stats, q, kv, d_att, dq_f, d_kv)
    attended = tied(attended, *out_received)
    outer, inner = early_terms(grad_shares, attended, normed, d_query)
    d_query = tied(d_query, outer)
    d_proj, dots, own, keep_right, keep_left, right, left = input_terms(
        me, d_query, d_kv, halo, normed, w
    )
    attn_out = finish_out(out_own, out_received)
    mine, *others = inner_terms(me, normed, d_proj, inner, outer)
    core_sums = sum_over_core(me, mine, *others)
    l1, r1 = to_next(right), to_previous(left)
    onward_right, onward_left = relay(keep_right, keep_left, l1, r1)
    l2, r2 = to_next(onward_right), to_previous(onward_left)
    grad_tokens = finish_grad(own, l1, r1, l2, r2, tokens, inverse, dots)
    *weight_grads, grad_w_out = sum_over_seq(me, core_sums, onward_right, attn_out)
    return (attn_out, grad_tokens, *weight_grads, grad_w_out.T)


def solution(mesh):
    return jax.shard_map(
        per_device,
        mesh=mesh,
        in_specs=(
            P("seq", "mp"),
            P(None, "mp"),
            P(None, "mp"),
            P(None, "mp"),
            P("mp", None),
            P("seq", "mp"),
        ),
        out_specs=(
            P("seq", "mp"),
            P("seq", "mp"),
            P("seq", "mp"),
            P("seq", "mp"),
            P("seq", "mp"),
            P("mp", "seq"),
        ),
        check_vma=False,
    )
```

```python
import jax
import jax.numpy as jnp
from jax import lax
from jax.experimental import pallas as pl
from jax.experimental.pallas import tpu as pltpu
from jax.sharding import PartitionSpec as P

HD = 64
BLOCK = 256
LEVELS = 3
PAIR = 2 * HD
MP = 4
LANES = 128
DOT_ROWS = 16

EPSILON = 1e-06
NEGATIVE = -1e30

F32 = jnp.float32
BF16 = jnp.bfloat16

FIRST_EXT = (0, 6, 10)
EXT_BLOCKS = (6, 4, 3)
EXT_TOTAL = 13


def nn(left, right):
    return lax.dot_general(left, right, (((1,), (0,)), ((), ())), preferred_element_type=F32)


def nt(left, right):
    return lax.dot_general(left, right, (((1,), (1,)), ((), ())), preferred_element_type=F32)


def tn(left, right):
    return lax.dot_general(left, right, (((0,), (0,)), ((), ())), preferred_element_type=F32)


def pool_matrix(coarse, factor, value):
    shape = (coarse, coarse * factor)
    row = lax.broadcasted_iota(jnp.int32, shape, 0)
    low = row * factor
    col = lax.broadcasted_iota(jnp.int32, shape, 1)
    return jnp.where((col >= low) & (col < low + factor), value, 0.0).astype(BF16)


def pool_both(half, quarter):
    parts = [pool_matrix(BLOCK // 2, 2, half), pool_matrix(BLOCK // 4, 4, quarter)]
    return jnp.concatenate(parts, axis=0)


def spread_matrix(coarse, factor, value):
    shape = (coarse * factor, coarse)
    low = lax.broadcasted_iota(jnp.int32, shape, 1) * factor
    row = lax.broadcasted_iota(jnp.int32, shape, 0)
    return jnp.where((row >= low) & (row < low + factor), value, 0.0).astype(BF16)


def share_rows(me, step, width):
    return pl.ds(pl.multiple_of(((me + step) & (MP - 1)) * width, width), width)


SMALL = pl.CostEstimate(flops=10**6, bytes_accessed=10**4, transcendentals=0)
LARGE = pl.CostEstimate(flops=4 * 10**9, bytes_accessed=10**4, transcendentals=0)
MIDDLE = pl.CostEstimate(flops=25 * 10**8, bytes_accessed=10**4, transcendentals=0)
RELAY = pl.CostEstimate(flops=10**9, bytes_accessed=10**4, transcendentals=0)
SCALAR = pl.BlockSpec(memory_space=pltpu.SMEM)
RESIDENT = pl.BlockSpec(memory_space=pltpu.VMEM)


def held(shape, dtype):
    return jax.ShapeDtypeStruct(shape, dtype)


def run(kernel, name, limit_mib, scalars, inputs, outputs, scratch=(), cost=SMALL):
    return pl.pallas_call(
        kernel,
        in_specs=[SCALAR] * len(scalars) + [RESIDENT] * len(inputs),
        out_specs=[RESIDENT] * len(outputs),
        out_shape=outputs,
        scratch_shapes=list(scratch),
        compiler_params=pltpu.CompilerParams(vmem_limit_bytes=limit_mib * 2**20),
        cost_estimate=cost,
        name=name,
    )(*scalars, *inputs)


def block_rows(block):
    return slice(block * BLOCK, (block + 1) * BLOCK)


ALL_ROWS = 7 * BLOCK
EDGE_ROWS = 256 + 128 + 192
LEVEL_BLOCK = (0, 4, 6)


def share_edges(place, edges, to_core, to_other):
    core = place[1]
    to_core[...] = edges[1 - core]
    to_other[...] = edges[core]


def halo_rows(halo, left, index):
    place, from_core, from_other = halo
    near, away = from_core[index], from_other[index]
    return jnp.where(place[1] == 0, away if left else near, near if left else away)


def as_row(column):
    return jnp.broadcast_to(column, (column.shape[0], LANES)).T[0:1, :]


def as_column(row):
    return jnp.broadcast_to(row, (LANES, row.shape[1])).T[:, 0:1]


def project_kernel(
    place, t1a_any, t1b_any, t2a_any, t2b_any, t3a_any, t3b_any,
    t0_hbm, wq_hbm, wk_hbm, wv_hbm,
    inverse, q, kv, to_core, to_other, normed_hbm, w_hbm,
    t0, t1, t2, t3, w, normed, edges, in_sems, out_sems,
):
    me = place[0]
    width = t0.shape[1]
    low, high = pl.ds(0, 2 * BLOCK), pl.ds(2 * BLOCK, 2 * BLOCK)
    moves = [
        (t0_hbm, t0),
        (t1a_any, t1.at[low]),
        (t2a_any, t2.at[low]),
        (t3a_any, t3.at[low]),
        (t1b_any, t1.at[high]),
        (t2b_any, t2.at[high]),
        (t3b_any, t3.at[high]),
    ]
    for n, source in enumerate((wq_hbm, wk_hbm, wv_hbm)):
        for r in range(MP):
            target = w.at[pl.ds(r * width, width), pl.ds(n * width, width)]
            moves.append((source.at[share_rows(me, r, width), :], target))
    loads = [
        pltpu.make_async_copy(source, target, in_sems.at[n])
        for n, (source, target) in enumerate(moves)
    ]
    for load in loads:
        load.start()
    pools = pool_both(0.5, 0.25)
    inverse[4:8, :] = jnp.zeros((4, BLOCK), F32)
    stores = []

    def normalise(step):
        if step in (0, 2):
            for load in loads[0:4] if step == 0 else loads[4:7]:
                load.wait()
        rows = block_rows(step)
        shares = [share[rows, :].astype(F32) for share in (t0, t1, t2, t3)]
        squares = shares[0] * shares[0]
        for share in shares[1:]:
            squares = squares + share * share
        total = jnp.sum(squares, axis=1, keepdims=True)
        inv = lax.rsqrt(total / (MP * width) + EPSILON)
        inverse[step : step + 1, :] = as_row(inv)
        parts = [(share * inv).astype(BF16) for share in shares]
        for r, part in enumerate(parts):
            normed[rows, r * width : (r + 1) * width] = part
        store = pltpu.make_async_copy(normed.at[rows], normed_hbm.at[rows], out_sems.at[step])
        store.start()
        stores.append(store)
        return jnp.concatenate(parts, axis=1)

    def spread(step, whole):
        if step == 0:
            for load in loads[7:]:
                load.wait()
            store = pltpu.make_async_copy(w, w_hbm, out_sems.at[4])
            store.start()
            stores.append(store)
        rows = block_rows(step)
        fine = [nn(whole, w[:, n * width : (n + 1) * width]).astype(BF16) for n in range(3)]
        coarse = [nn(pools, x).astype(BF16) for x in fine]
        mid = [x[0:128] for x in coarse]
        low = [x[128:192] for x in coarse]
        mid_rows = slice(1024 + step * 128, 1024 + (step + 1) * 128)
        low_rows = slice(1536 + step * 64, 1536 + (step + 1) * 64)
        q[rows, :] = fine[0]
        q[mid_rows, :] = mid[0]
        q[low_rows, :] = low[0]
        for n in range(2):
            kv[n, rows, :] = fine[1 + n]
            kv[n, mid_rows, :] = mid[1 + n]
            kv[n, low_rows, :] = low[1 + n]
            if step in (0, 3):
                edges[step // 3, n, 0:BLOCK, :] = fine[1 + n]
            if step in (1, 2):
                edges[step - 1, n, 256:384, :] = mid[1 + n]
            if step > 0:
                edges[0, n, 320 + step * 64 : 384 + step * 64, :] = low[1 + n]
            if step < 3:
                edges[1, n, 384 + step * 64 : 448 + step * 64, :] = low[1 + n]

    parts = normalise(0)
    for step in range(4):
        following = normalise(step + 1) if step < 3 else None
        spread(step, parts)
        parts = following
    share_edges(place, edges, to_core, to_other)
    for store in stores:
        store.wait()


def project(place, shares, wq, wk, wv):
    rows, width = shares[0].shape
    out = jax.ShapeDtypeStruct
    edge = out((2, EDGE_ROWS, width), BF16)
    anywhere = pl.BlockSpec(memory_space=pl.ANY)
    share = pltpu.VMEM((rows, width), BF16)
    fixed = [
        pltpu.with_memory_space_constraint(value, pltpu.HBM)
        for value in (*shares[1:], shares[0], wq, wk, wv)
    ]
    return pl.pallas_call(
        project_kernel,
        in_specs=[SCALAR] + [anywhere] * 10,
        out_specs=[RESIDENT] * 5 + [anywhere] * 2,
        out_shape=[
            out((8, width), F32),
            out((ALL_ROWS, width), BF16),
            out((2, ALL_ROWS, width), BF16),
            edge,
            edge,
            pltpu.HBM((rows, MP * width), BF16),
            pltpu.HBM((MP * width, 3 * width), BF16),
        ],
        scratch_shapes=[share] * 4
        + [
            pltpu.VMEM((MP * width, 3 * width), BF16),
            pltpu.VMEM((rows, MP * width), BF16),
            pltpu.VMEM((2, *edge.shape), BF16),
            pltpu.SemaphoreType.DMA((19,)),
            pltpu.SemaphoreType.DMA((5,)),
        ],
        compiler_params=pltpu.CompilerParams(vmem_limit_bytes=20 * 2**20),
        cost_estimate=SMALL,
        name="project",
    )(place, *fixed)


def near_kernel(place, g0, g1, g3, w_out, total, w_turned):
    me = place[0]
    width = g0.shape[1]
    for n, r in enumerate((0, 1, 3)):
        w_turned[block_rows(n), :] = w_out[:, share_rows(me, r, width)].T
    for step in range(4):
        rows = block_rows(step)
        shares = jnp.concatenate([share[rows, :] for share in (g0, g1, g3)], axis=1)
        total[rows, :] = nn(shares, w_turned[...])


def near_cotangent(place, shares, w_out):
    rows, width = shares[0].shape
    inputs = [*shares, w_out]
    scratch = [pltpu.VMEM((3 * width, width), BF16)]
    outputs = [held((rows, width), F32)]
    return run(near_kernel, "near_cotangent", 10, [place], inputs, outputs, scratch)[0]


def cotangent_kernel(place, near, g2, w_out, d_att, w_turned):
    width = g2.shape[1]
    pools = pool_both(1.0, 1.0)
    w_turned[...] = w_out[:, share_rows(place[0], 2, width)].T
    for step in range(4):
        rows = block_rows(step)
        fine = (near[rows, :] + nn(g2[rows, :], w_turned[...])).astype(BF16)
        d_att[rows, :] = fine
        coarse = nn(pools, fine).astype(BF16)
        d_att[1024 + step * 128 : 1024 + (step + 1) * 128, :] = coarse[0:128]
        d_att[1536 + step * 64 : 1536 + (step + 1) * 64, :] = coarse[128:192]


def cotangent(place, near, far, w_out):
    width = far.shape[1]
    scratch = [pltpu.VMEM((width, width), BF16)]
    outputs = [held((ALL_ROWS, width), BF16)]
    return run(cotangent_kernel, "cotangent", 10, [place], [near, far, w_out], outputs, scratch)[0]


EDGE_UNITS = ((0, 0), (0, 3), (1, 0), (1, 1), (2, 0))
INNER_UNITS = ((0, 1), (0, 2))


def unit_keys(level, block):
    last = EXT_BLOCKS[level] - 1
    offsets = (0, 1, 2) if level == 0 else (0, 2)
    keys = []
    for offset in offsets:
        at = block + offset
        keys.append((at, 0 if at == 0 else 1 if at == last else None))
    return keys


def ext_rows(kv, halo, n, level, at, lanes):
    if at in (0, EXT_BLOCKS[level] - 1):
        return halo[0 if at == 0 else 1][n, block_rows(level), lanes]
    return kv[n, block_rows(LEVEL_BLOCK[level] + at - 1), lanes]


def head_part(lane, head, rows):
    mine = (lane >= head * HD) & (lane < (head + 1) * HD)
    return jnp.where(mine, rows, 0.0).astype(BF16)


def unit_scores(keys, key_rows, query, bias_ref):
    scores = []
    for (_, bias), rows in zip(keys, key_rows):
        s = nt(rows, query)
        scores.append(s if bias is None else s + bias_ref[bias])
    return scores


def add_spread(target, block, factor, rows):
    if factor == 1:
        target[block_rows(block), :] = target[block_rows(block), :] + rows
        return
    for s in range(factor):
        spread = pl.ds(block * factor * BLOCK + s, BLOCK, factor)
        target[spread, :] = target[spread, :] + rows


def each_pair(width, body):
    def step(pair, _):
        body(pair, pl.ds(pl.multiple_of(pair * PAIR, PAIR), PAIR))
        return 0

    lax.fori_loop(0, width // PAIR, step, 0)


def head_part(lane, head, rows):
    mine = (lane >= head * HD) & (lane < (head + 1) * HD)
    return jnp.where(mine, rows, 0.0).astype(BF16)


def unit_scores(keys, key_rows, query, bias_ref):
    scores = []
    for (_, bias), rows in zip(keys, key_rows):
        s = nt(rows, query)
        scores.append(s if bias is None else s + bias_ref[bias])
    return scores


def add_spread(target, block, factor, rows):
    if factor == 1:
        target[block_rows(block), :] = target[block_rows(block), :] + rows
        return
    for s in range(factor):
        spread = pl.ds(block * factor * BLOCK + s, BLOCK, factor)
        target[spread, :] = target[spread, :] + rows


def forward_units(pair, lanes, units, bias_ref, q, kv, halo, stats, vt, out_f):
    lane = lax.broadcasted_iota(jnp.int32, (BLOCK, PAIR), 1)
    done = set()
    for level, block in units:
        for at, _ in unit_keys(level, block):
            if (level, at) not in done:
                done.add((level, at))
                rows = ext_rows(kv, halo, 1, level, at, lanes)
                vt[FIRST_EXT[level] + at] = rows.T

    def begin(u, head):
        level, block = units[u]
        keys = unit_keys(level, block)
        key_rows = [ext_rows(kv, halo, 0, level, at, lanes) for at, _ in keys]
        q_rows = q[block_rows(LEVEL_BLOCK[level] + block), lanes] * HD ** (-0.5)
        return unit_scores(keys, key_rows, head_part(lane, head, q_rows), bias_ref)

    def finish(u, head, scores):
        level, block = units[u]
        top = scores[0].max(axis=0, keepdims=True)
        for s in scores[1:]:
            top = jnp.maximum(top, s.max(axis=0, keepdims=True))
        exps = [jnp.exp(s - top) for s in scores]
        total = exps[0].sum(axis=0, keepdims=True)
        for e in exps[1:]:
            total = total + e.sum(axis=0, keepdims=True)
        scale = 1.0 / total
        row = 4 * u + 2 * head
        stats[pair, row : row + 1, :] = top
        stats[pair, row + 1 : row + 2, :] = scale
        return [(e * scale).astype(BF16) for e in exps]

    outs = []

    def give(u, head, weights):
        level, block = units[u]
        part = slice(head * HD, (head + 1) * HD)
        o_t = None
        for (at, _), w in zip(unit_keys(level, block), weights):
            o = nn(vt[FIRST_EXT[level] + at, part, :], w)
            o_t = o if o_t is None else o_t + o
        outs.append(o_t)
        if head == 1:
            add_spread(out_f, block, 2**level, jnp.concatenate(outs, axis=0).T)
            outs.clear()

    items = [(u, head) for u in range(len(units)) for head in range(2)]
    scores, last = begin(*items[0]), None
    for n, item in enumerate(items):
        following = begin(*items[n + 1]) if n + 1 < len(items) else None
        if last is not None:
            give(*items[n - 1], last)
        last = finish(*item, scores)
        scores = following
    give(*items[-1], last)


def forward_inner_kernel(bias_ref, q, kv, out, stats, vt, out_f):
    def one(pair, lanes):
        out_f[...] = jnp.zeros_like(out_f)
        forward_units(pair, lanes, INNER_UNITS, bias_ref, q, kv, None, stats, vt, out_f)
        out[:, lanes] = out_f[BLOCK : 3 * BLOCK, :]

    each_pair(q.shape[1], one)


def forward_edge_kernel(
    place, bias_ref, q, kv, from_other, from_core, inner,
    attended, stats, left, right, vt, out_f,
):
    received = (place, from_core, from_other)
    pools = pool_both(0.5, 0.25)
    every = slice(None)
    for n in range(2):
        for out, is_left in ((left, True), (right, False)):
            fine = halo_rows(received, is_left, (n, slice(0, 256), every))
            mid = halo_rows(received, is_left, (n, slice(256, 384), every))
            low = halo_rows(received, is_left, (n, slice(384, 576), every))
            coarse = nn(pools, fine).astype(BF16)
            out[n, 0:256, :] = fine
            if is_left:
                out[n, 256:384, :], out[n, 384:512, :] = mid, coarse[0:128]
                out[n, 512:704, :], out[n, 704:768, :] = low, coarse[128:192]
            else:
                out[n, 256:384, :], out[n, 384:512, :] = coarse[0:128], mid
                out[n, 512:576, :], out[n, 576:768, :] = coarse[128:192], low
    halo = (left, right)

    def one(pair, lanes):
        out_f[0:BLOCK, :] = jnp.zeros((BLOCK, PAIR), F32)
        out_f[BLOCK : 3 * BLOCK, :] = inner[:, lanes]
        out_f[3 * BLOCK :, :] = jnp.zeros((BLOCK, PAIR), F32)
        forward_units(
            pair, lanes, EDGE_UNITS, bias_ref, q, kv, halo, stats, vt, out_f
        )
        attended[:, lanes] = out_f[...].astype(BF16)

    each_pair(q.shape[1], one)


def backward_units(
    pair, lanes, units, bias_ref, q, kv, halo, grads, stats, kt, dq_f, keep
):
    lane = lax.broadcasted_iota(jnp.int32, (BLOCK, PAIR), 1)
    done = set()
    for level, block in units:
        for at, _ in unit_keys(level, block):
            if (level, at) not in done:
                done.add((level, at))
                rows = ext_rows(kv, halo, 0, level, at, lanes)
                kt[FIRST_EXT[level] + at] = rows.T

    def begin(u, head):
        level, block = units[u]
        keys = unit_keys(level, block)
        key_rows = [ext_rows(kv, halo, 0, level, at, lanes) for at, _ in keys]
        value_rows = [ext_rows(kv, halo, 1, level, at, lanes) for at, _ in keys]
        at = block_rows(LEVEL_BLOCK[level] + block)
        qm = head_part(lane, head, q[at, lanes] * HD ** (-0.5))
        am = head_part(lane, head, grads[at, lanes])
        scores = unit_scores(keys, key_rows, qm, bias_ref)
        return qm, am, scores, [nt(rows, am) for rows in value_rows]

    def finish(u, head, qm, am, scores, d_weights):
        level, block = units[u]
        row = 4 * u + 2 * head
        top, scale = stats[pair, row : row + 1, :], stats[pair, row + 1 : row + 2, :]
        probs = [jnp.exp(s - top) * scale for s in scores]
        dots = None
        for p, dw in zip(probs, d_weights):
            d = (p * dw).sum(axis=0, keepdims=True)
            dots = d if dots is None else dots + d
        weights = [p.astype(BF16) for p in probs]
        d_scores = [(p * (dw - dots)).astype(BF16) for p, dw in zip(probs, d_weights)]
        return qm, am, weights, d_scores

    first = []

    def give(u, head, qm, am, weights, d_scores):
        level, block = units[u]
        keys = unit_keys(level, block)
        part = slice(head * HD, (head + 1) * HD)
        d_values = [nn(w, am) for w in weights]
        d_keys = [nn(ds, qm) for ds in d_scores]
        dq_t = None
        for (at, _), ds in zip(keys, d_scores):
            g = nn(kt[FIRST_EXT[level] + at, part, :], ds)
            dq_t = g if dq_t is None else dq_t + g
        if head == 0:
            first.append((dq_t, d_keys, d_values))
            return
        dq_first, k_first, v_first = first.pop()
        for n, (at, _) in enumerate(keys):
            keep(0, level, at, k_first[n] + d_keys[n])
            keep(1, level, at, v_first[n] + d_values[n])
        dq = jnp.concatenate([dq_first, dq_t], axis=0).T * (HD ** (-0.5) / 2**level)
        add_spread(dq_f, block, 2**level, dq)

    items = [(u, head) for u in range(len(units)) for head in range(2)]
    ready, last = begin(*items[0]), None
    for n, item in enumerate(items):
        following = begin(*items[n + 1]) if n + 1 < len(items) else None
        if last is not None:
            give(*items[n - 1], *last)
        last = finish(*item, *ready)
        ready = following
    give(*items[-1], *last)


def edge_kernel(
    place, bias_ref, stats, q, kv, left, right, grads,
    dq_f, d_kv, to_core, to_other, kt, ext, dq_s, sums, edges,
):
    halo = (left, right)

    def add_rows(factor, rows):
        for s in range(factor):
            spread = pl.ds(s, rows.shape[0], factor)
            sums[spread, :] = sums[spread, :] + rows * (1.0 / factor)

    def one(pair, lanes):
        dq_s[...] = jnp.zeros_like(dq_s)
        seen = set()

        def keep(n, level, at, rows):
            slot = FIRST_EXT[level] + at
            if (n, slot) in seen:
                ext[n, slot] = ext[n, slot] + rows
            else:
                seen.add((n, slot))
                ext[n, slot] = rows

        backward_units(
            pair, lanes, EDGE_UNITS, bias_ref, q, kv, halo, grads, stats, kt, dq_s, keep,
        )
        dq_f[:, lanes] = dq_s[...]
        for n in range(2):
            for side in range(2):
                fine, mid, low = (
                    ext[n, FIRST_EXT[level] + side * (EXT_BLOCKS[level] - 1)]
                    for level in range(LEVELS)
                )
                if side == 0:
                    (mid, mid_near), (low, low_near) = (mid[0:128], mid[128:]), (low[0:192], low[192:])
                else:
                    (mid_near, mid), (low_near, low) = (mid[0:128], mid[128:]), (low[0:64], low[64:])
                sums[0:BLOCK, :] = fine
                add_rows(2, mid_near)
                add_rows(4, low_near)
                edges[side, n, 0:256, lanes] = sums[0:BLOCK, :].astype(BF16)
                edges[side, n, 256:384, lanes] = mid.astype(BF16)
                edges[side, n, 384:576, lanes] = low.astype(BF16)
            for b in range(4):
                sums[block_rows(b), :] = ext[n, 1 + b]
            for b in range(2):
                add_spread(sums, b, 2, ext[n, FIRST_EXT[1] + 1 + b] * 0.5)
            d_kv[n, :, lanes] = sums[...]

    each_pair(q.shape[1], one)
    share_edges(place, edges, to_core, to_other)


def inner_units_kernel(bias_ref, stats, q, kv, grads, dq_in, d_kv_in, d_query, d_kv, kt, dq_s):
    def one(pair, lanes):
        dq_s[...] = dq_in[:, lanes]
        d_kv[:, :, lanes] = d_kv_in[:, :, lanes]

        def keep(n, level, at, rows):
            where = block_rows(at - 1)
            d_kv[n, where, lanes] = d_kv[n, where, lanes] + rows

        backward_units(
            pair, lanes, INNER_UNITS, bias_ref, q, kv, None, grads, stats, kt, dq_s, keep
        )
        d_query[:, lanes] = dq_s[...].astype(BF16)

    each_pair(q.shape[1], one)


def turned(count):
    return pltpu.VMEM((count, PAIR, BLOCK), BF16)


def forward_inner(bias, q, kv):
    width = q.shape[1]
    outputs = [held((2 * BLOCK, width), F32), held((width // PAIR, 8, BLOCK), F32)]
    scratch = [turned(EXT_BLOCKS[0]), pltpu.VMEM((4 * BLOCK, PAIR), F32)]
    return run(forward_inner_kernel, "forward_inner", 12, [bias], [q, kv], outputs, scratch, MIDDLE)


def forward_edge(place, bias, q, kv, halo, inner):
    width = q.shape[1]
    inputs = [q, kv, *halo[::-1], inner]
    outputs = [held((4 * BLOCK, width), BF16), held((width // PAIR, 24, BLOCK), F32)]
    outputs += [held((2, 3 * BLOCK, width), BF16)] * 2
    scratch = [turned(EXT_TOTAL), pltpu.VMEM((4 * BLOCK, PAIR), F32)]
    return run(forward_edge_kernel, "forward_edge", 12, [place, bias], inputs, outputs, scratch)


def edge_backward(place, bias, stats, q, kv, halo, d_att):
    rows, width = 4 * BLOCK, q.shape[1]
    edge = held((2, EDGE_ROWS, width), BF16)
    inputs = [stats, q, kv, *halo, d_att]
    outputs = [held((rows, width), F32), held((2, rows, width), F32), edge, edge]
    scratch = [
        turned(EXT_TOTAL),
        pltpu.VMEM((2, EXT_TOTAL, BLOCK, PAIR), F32),
        pltpu.VMEM((rows, PAIR), F32),
        pltpu.VMEM((rows, PAIR), F32),
        pltpu.VMEM((2, *edge.shape), BF16),
    ]
    return run(edge_kernel, "edge_backward", 20, [place, bias], inputs, outputs, scratch)


def inner_backward(bias, stats, q, kv, d_att, dq_f, d_kv):
    rows, width = 4 * BLOCK, q.shape[1]
    inputs = [stats, q, kv, d_att, dq_f, d_kv]
    outputs = [held((rows, width), BF16), held((2, rows, width), F32)]
    scratch = [turned(EXT_BLOCKS[0]), pltpu.VMEM((rows, PAIR), F32)]
    return run(inner_units_kernel, "inner_backward", 12, [bias], inputs, outputs, scratch)


def term_outputs(rows, width):
    return [held((rows, width), BF16)] * MP


def store_terms(step, terms, own, keep_right, keep_left, right, left):
    own[block_rows(step), :] = terms[0]
    low, high = block_rows(step % 2), block_rows(2 + step % 2)
    if step < 2:
        keep_right[low, :] = terms[1]
        right[high, :] = terms[2]
        left[low, :] = terms[3]
    else:
        right[low, :] = terms[1]
        left[high, :] = terms[2]
        keep_left[low, :] = terms[3]


def out_terms_kernel(place, attended, w_out, *outs):
    me = place[0]
    width = attended.shape[1]
    for step in range(4):
        rows = attended[block_rows(step), :]
        for r, out in enumerate(outs):
            term = nn(rows, w_out[:, share_rows(me, r, width)])
            out[block_rows(step), :] = term.astype(BF16)


def out_terms(place, attended, w_out):
    outputs = term_outputs(*attended.shape)
    return run(out_terms_kernel, "out_terms", 8, [place], [attended, w_out], outputs)


def input_terms_kernel(
    place, d_query, d_kv, from_other, from_core, normed, w_turned, d_proj,
    dots, own, keep_right, keep_left, right, left, dot_rows,
):
    halo = (place, from_core, from_other)
    width = d_query.shape[1]
    half = spread_matrix(BLOCK // 2, 2, 0.5)
    quarter = spread_matrix(BLOCK // 4, 4, 0.25)
    dot_rows[12:16, :] = jnp.zeros((4, BLOCK), F32)
    for step in range(4):
        rows = block_rows(step)
        grads = [d_query[rows, :]]
        every = slice(None)
        for n in range(2):
            total = d_kv[n, rows, :]
            if step in (0, 3):
                total = total + halo_rows(halo, step == 0, (n, slice(0, 256), every)).astype(F32)
            else:
                total = total + nn(half, halo_rows(halo, step == 1, (n, slice(256, 384), every)))
            if step > 0:
                low = slice(320 + step * 64, 384 + step * 64)
                total = total + nn(quarter, halo_rows(halo, True, (n, low, every)))
            if step < 3:
                low = slice(384 + step * 64, 448 + step * 64)
                total = total + nn(quarter, halo_rows(halo, False, (n, low, every)))
            grads.append(total.astype(BF16))
        for n, grad in enumerate(grads[1:]):
            d_proj[rows, n * width : (n + 1) * width] = grad
        dot = None
        every = jnp.concatenate(grads, axis=1)
        terms = []
        for r in range(MP):
            term = nn(every, w_turned[:, r * width : (r + 1) * width]).astype(BF16)
            terms.append(term)
            part = term.astype(F32) * normed[rows, r * width : (r + 1) * width].astype(F32)
            dot = part if dot is None else dot + part
        store_terms(step, terms, own, keep_right, keep_left, right, left)
        dot = as_row(jnp.sum(dot, axis=1, keepdims=True))
        first = dot.astype(BF16).astype(F32)
        second = (dot - first).astype(BF16).astype(F32)
        for n, piece in enumerate((first, second, dot - first - second)):
            dot_rows[4 * n + step : 4 * n + step + 1, :] = piece
    pieces = dot_rows[...].astype(BF16)
    dots[...] = pieces
    right[4 * BLOCK :, :] = pieces
    left[4 * BLOCK :, :] = pieces


def input_terms(place, d_query, d_kv, halo, normed, w):
    rows, width = d_query.shape
    inputs = [d_query, d_kv, *halo[::-1], normed, w]
    outputs = [held((rows, 2 * width), BF16), held((DOT_ROWS, width), BF16)]
    lengths = [rows, rows // 2, rows // 2, rows + DOT_ROWS, rows + DOT_ROWS]
    outputs += [held((n, width), BF16) for n in lengths]
    scratch = [pltpu.VMEM((DOT_ROWS, width), F32)]
    return run(input_terms_kernel, "input_terms", 18, [place], inputs, outputs, scratch)


def sum_terms(own, received, at):
    total = own[at, :].astype(F32)
    for term in received:
        total = total + term[at, :].astype(F32)
    return total


def finish_out_kernel(own, one, two, three, result):
    for b in range(4):
        at = block_rows(b)
        result[at, :] = sum_terms(own, (one, two, three), at).astype(BF16)


def finish_out(own, received):
    outputs = [held(own.shape, BF16)]
    return run(finish_out_kernel, "finish_out", 8, [], [own, *received], outputs)[0]


def relay_kernel(keep_right, keep_left, l1, r1, onward_right, onward_left):
    half = keep_right.shape[0]
    passed = l1[half : 2 * half, :].astype(F32)
    onward_right[0:half, :] = (keep_right[...].astype(F32) + passed).astype(BF16)
    passed = r1[half : 2 * half, :].astype(F32)
    onward_left[...] = (keep_left[...].astype(F32) + passed).astype(BF16)
    if onward_right.shape[0] > half:
        onward_right[half:, :] = l1[2 * half :, :]


def relay(keep_right, keep_left, l1, r1):
    half, width = keep_right.shape
    outputs = [held((half + DOT_ROWS, width), BF16), held((half, width), BF16)]
    return run(relay_kernel, "relay", 4, [], [keep_right, keep_left, l1, r1], outputs, (), RELAY)


def finish_grad_kernel(own, l1, r1, l2, r2, tokens, inverse, dots, result):
    rows, width = own.shape
    half = r2.shape[0]
    pieces = dots[...].astype(F32)
    for message, first in ((l1, rows), (r1, rows), (l2, half)):
        pieces = pieces + message[first : first + DOT_ROWS, :].astype(F32)
    means = (pieces[0:4] + pieces[4:8] + pieces[8:12]) / (MP * width)
    for b in range(rows // BLOCK):
        at, near = block_rows(b), block_rows(b % 2)
        mean = as_column(means[b : b + 1, :])
        inv = as_column(inverse[b : b + 1, :])
        total = own[at, :].astype(F32)
        for part in (r1, l2) if b < 2 else (l1, r2):
            total = total + part[near, :].astype(F32)
        result[at, :] = inv * (total - tokens[at, :].astype(F32) * inv * mean)


def finish_grad(own, l1, r1, l2, r2, tokens, inverse, dots):
    inputs = [own, l1, r1, l2, r2, tokens, inverse, dots]
    outputs = [held(own.shape, F32)]
    return run(finish_grad_kernel, "finish_grad", 8, [], inputs, outputs)[0]


def early_kernel(g0, g1, g2, g3, attended, normed, d_query, w, outer, inner, w_turned):
    width = g0.shape[1]
    rows = attended[...]
    for r, share in enumerate((g0, g1, g2, g3)):
        at = slice(r * width, (r + 1) * width)
        outer[at, :] = tn(share[...], rows).astype(BF16)
        inner[at, :] = tn(normed[:, at], d_query[...]).astype(BF16)
        for n in range(3):
            w_turned[block_rows(n), at] = w[at, n * width : (n + 1) * width].T


def early_terms(shares, attended, normed, d_query, w):
    width = attended.shape[1]
    inputs = [*shares, attended, normed, d_query, w]
    outputs = [held((MP * width, width), BF16)] * 2 + [held((3 * width, MP * width), BF16)]
    return run(early_kernel, "early_terms", 14, [], inputs, outputs, (), LARGE)


def inner_kernel(place, normed, d_proj, inner, outer, mine, other, rows_held):
    core = place[1]
    width = outer.shape[1]
    for block in range(MP):
        at = block_rows(block)
        rows_held[at, 0:width] = inner[at, :]
        rows_held[at, width : 3 * width] = tn(normed[:, at], d_proj[...]).astype(BF16)
        rows_held[at, 3 * width :] = outer[at, :]
        for n in range(width // 64):
            out = slice((4 * block + n) * 32, (4 * block + n + 1) * 32)
            first = block * width + n * 64
            mine[out, :] = rows_held[pl.ds(pl.multiple_of(first + core * 32, 32), 32), :]
            other[out, :] = rows_held[pl.ds(pl.multiple_of(first + 32 - core * 32, 32), 32), :]


def inner_terms(place, normed, d_proj, inner, outer):
    total = normed.shape[1]
    width = outer.shape[1]
    outputs = [held((total // 2, 4 * width), BF16)] * 2
    scratch = [pltpu.VMEM((total, 4 * width), BF16)]
    return run(inner_kernel, "inner_terms", 16, [place], [normed, d_proj, inner, outer], outputs, scratch)


def pair_sum_kernel(place, mine, got, *outs):
    z, core, x, y = place[0], place[1], place[2], place[3]
    for d, out in enumerate(outs):
        for n in range(4):
            chunk = jnp.where(core == 0, 4 * n + ((x + d) & 3), 4 * ((y + d - z + 4) & 3) + n)
            rows = pl.ds(pl.multiple_of(chunk * 32, 32), 32)
            total = mine[rows, :].astype(F32) + got[rows, :].astype(F32)
            out[32 * n : 32 * (n + 1), :] = total.astype(BF16)


def row_sum_kernel(place, a, b, c, d, *refs):
    *outs, total = refs
    z, core, x, y = place[0], place[1], place[2], place[3]
    first = jnp.where(core == 0, y - z + 4, x)
    total[...] = (
        a[...].astype(F32) + b[...].astype(F32) + c[...].astype(F32) + d[...].astype(F32)
    ).astype(BF16)
    for n, out in enumerate(outs):
        out[...] = total[pl.ds(pl.multiple_of(((first + n) & 3) * 32, 32), 32), :]


def last_sum_kernel(a, b, c, d, gq, gk, gv, go):
    width = gq.shape[1]
    total = a[...].astype(F32) + b[...].astype(F32) + c[...].astype(F32) + d[...].astype(F32)
    gq[...] = total[:, 0:width]
    gk[...] = total[:, width : 2 * width]
    gv[...] = total[:, 2 * width : 3 * width]
    go[...] = total[:, 3 * width :]


def sum_over_core(place, mine, *others):
    got = [lax.ppermute(other, "seq", [(i, i ^ 1) for i in range(32)]) for other in others]
    parts = [held((128, mine.shape[1]), BF16)] * 4
    return run(pair_sum_kernel, "pair_sum", 6, [place], [mine, *got], parts)


def sum_over_seq(place, parts, *first):
    cols = parts[0].shape[1]

    def sent(value, stage, d):
        pairs = []
        for i in range(32):
            core, x, y = i % 2, (i // 2) % 4, i // 8
            if stage == core:
                x = (x + d) % 4
            else:
                y = (y + d) % 4
            pairs.append((i, (y * 4 + x) * 2 + core))
        return lax.ppermute(value, "seq", pairs)

    parts = [parts[0]] + [sent(parts[d], 0, d) for d in (1, 2, 3)]
    parts = tied(parts, *first)
    rows = [held((32, cols), BF16)] * 4
    scratch = [pltpu.VMEM((128, cols), BF16)]
    rows = run(row_sum_kernel, "row_sum", 4, [place], parts, rows, scratch)
    rows = [rows[0]] + [sent(rows[d], 1, d) for d in (1, 2, 3)]
    outputs = [held((32, cols // 4), F32)] * 4
    return run(last_sum_kernel, "last_sum", 4, [], rows, outputs)


def to_next(value):
    return lax.ppermute(value, "mp", [(i, (i + 1) % MP) for i in range(MP)])


def to_previous(value):
    return lax.ppermute(value, "mp", [((i + 1) % MP, i) for i in range(MP)])


def gather_shares(share):
    half = share.shape[0] // 2
    low, high = share[:half], share[half:]
    after_low, before_high = to_previous(low), to_next(high)
    after_high, before_low = to_previous(high), to_next(low)
    far_low, far_high = to_previous(after_low), to_next(before_high)
    return [share, after_low, after_high, far_low, far_high, before_low, before_high]


def turned_by(value, step):
    return lax.ppermute(value, "mp", [(i, (i + step) % MP) for i in range(MP)])


def sum_over_mp(terms):
    return [turned_by(term, step) for step, term in zip((1, 2, 3), terms)]


def exchange(to_core, to_other):
    count = lax.axis_size("seq")
    pairs = []
    for i in range(1, count - 1, 2):
        pairs += [(i, i + 1), (i + 1, i)]
    from_other = lax.ppermute(to_other, "seq", pairs)
    from_core = lax.ppermute(to_core, "seq", [(i, i ^ 1) for i in range(count)])
    return from_core, from_other


def tied(values, *others):
    flat, tree = jax.tree.flatten(values)
    flat = lax.optimization_barrier((*flat, *others))[: len(flat)]
    return jax.tree.unflatten(tree, flat)


def per_device(tokens, w_query, w_key, w_value, w_out, grad_out):
    count = lax.axis_size("seq")
    index = lax.axis_index("seq")
    me = jnp.stack([lax.axis_index("mp"), index & 1, (index >> 1) & 3, index >> 3])
    me = me.astype(jnp.int32)
    bias = jnp.stack(
        [
            jnp.where(index == 0, NEGATIVE, 0.0).astype(F32),
            jnp.where(index == count - 1, NEGATIVE, 0.0).astype(F32),
        ]
    )
    token_shares = gather_shares(tokens)
    near_grad = tied(grad_out, *(token_shares[n] for n in (1, 2, 5, 6)))
    far_grad = tied(grad_out, *token_shares)
    far = turned_by(far_grad, 2)
    grad_shares = [grad_out, to_previous(near_grad), far, to_next(near_grad)]
    inverse, q, kv, to_core, to_other, normed, w = project(
        me, token_shares, w_query, w_key, w_value
    )
    halo = exchange(to_core, to_other)
    near_q = tied(q, grad_shares[1], grad_shares[3])
    inner_out, inner_stats = forward_inner(bias, near_q, kv)
    near = near_cotangent(me, tied([grad_shares[n] for n in (0, 1, 3)], inner_out), w_out)
    inner_out = tied(inner_out, near)
    attended, stats, *halo = forward_edge(me, bias, q, kv, halo, inner_out)
    out_own, *terms = out_terms(me, attended, w_out)
    out_received = sum_over_mp(terms)
    grad_shares = tied(grad_shares, out_own)
    d_att = cotangent(me, near, grad_shares[2], w_out)
    dq_f, d_kv, to_core, to_other = edge_backward(me, bias, stats, q, kv, halo, d_att)
    halo = exchange(to_core, to_other)
    d_query, d_kv = inner_backward(bias, inner_stats, q, kv, d_att, dq_f, d_kv)
    attended = tied(attended, *out_received)
    outer, inner, w = early_terms(grad_shares, attended, normed, d_query, w)
    d_query = tied(d_query, outer)
    d_proj, dots, own, keep_right, keep_left, right, left = input_terms(
        me, d_query, d_kv, halo, normed, w
    )
    attn_out = finish_out(out_own, out_received)
    mine, *others = inner_terms(me, normed, d_proj, inner, outer)
    core_sums = sum_over_core(me, mine, *others)
    l1, r1 = to_next(right), to_previous(left)
    onward_right, onward_left = relay(keep_right, keep_left, l1, r1)
    l2, r2 = to_next(onward_right), to_previous(onward_left)
    grad_tokens = finish_grad(own, l1, r1, l2, r2, tokens, inverse, dots)
    *weight_grads, grad_w_out = sum_over_seq(me, core_sums, onward_right, attn_out)
    return (attn_out, grad_tokens, *weight_grads, grad_w_out.T)


def solution(mesh):
    return jax.shard_map(
        per_device,
        mesh=mesh,
        in_specs=(
            P("seq", "mp"),
            P(None, "mp"),
            P(None, "mp"),
            P(None, "mp"),
            P("mp", None),
            P("seq", "mp"),
        ),
        out_specs=(
            P("seq", "mp"),
            P("seq", "mp"),
            P("seq", "mp"),
            P("seq", "mp"),
            P("seq", "mp"),
            P("mp", "seq"),
        ),
        check_vma=False,
    )
```

```python
import jax
import jax.numpy as jnp
from jax import lax
from jax.experimental import pallas as pl
from jax.experimental.pallas import tpu as pltpu
from jax.sharding import PartitionSpec as P

HD = 64
BLOCK = 256
LEVELS = 3
PAIR = 2 * HD
MP = 4
LANES = 128
DOT_ROWS = 16

EPSILON = 1e-06
NEGATIVE = -1e30

F32 = jnp.float32
BF16 = jnp.bfloat16

FIRST_EXT = (0, 6, 10)
EXT_BLOCKS = (6, 4, 3)
EXT_TOTAL = 13


def nn(left, right):
    return lax.dot_general(left, right, (((1,), (0,)), ((), ())), preferred_element_type=F32)


def nt(left, right):
    return lax.dot_general(left, right, (((1,), (1,)), ((), ())), preferred_element_type=F32)


def tn(left, right):
    return lax.dot_general(left, right, (((0,), (0,)), ((), ())), preferred_element_type=F32)


def pool_matrix(coarse, factor, value):
    shape = (coarse, coarse * factor)
    row = lax.broadcasted_iota(jnp.int32, shape, 0)
    low = row * factor
    col = lax.broadcasted_iota(jnp.int32, shape, 1)
    return jnp.where((col >= low) & (col < low + factor), value, 0.0).astype(BF16)


def pool_both(half, quarter):
    parts = [pool_matrix(BLOCK // 2, 2, half), pool_matrix(BLOCK // 4, 4, quarter)]
    return jnp.concatenate(parts, axis=0)


def spread_matrix(coarse, factor, value):
    shape = (coarse * factor, coarse)
    low = lax.broadcasted_iota(jnp.int32, shape, 1) * factor
    row = lax.broadcasted_iota(jnp.int32, shape, 0)
    return jnp.where((row >= low) & (row < low + factor), value, 0.0).astype(BF16)


def share_rows(me, step, width):
    return pl.ds(pl.multiple_of(((me + step) & (MP - 1)) * width, width), width)


SMALL = pl.CostEstimate(flops=10**6, bytes_accessed=10**4, transcendentals=0)
LARGE = pl.CostEstimate(flops=4 * 10**9, bytes_accessed=10**4, transcendentals=0)
MIDDLE = pl.CostEstimate(flops=25 * 10**8, bytes_accessed=10**4, transcendentals=0)
RELAY = pl.CostEstimate(flops=10**9, bytes_accessed=10**4, transcendentals=0)
SCALAR = pl.BlockSpec(memory_space=pltpu.SMEM)
RESIDENT = pl.BlockSpec(memory_space=pltpu.VMEM)


def held(shape, dtype):
    return jax.ShapeDtypeStruct(shape, dtype)


def run(kernel, name, limit_mib, scalars, inputs, outputs, scratch=(), cost=SMALL):
    return pl.pallas_call(
        kernel,
        in_specs=[SCALAR] * len(scalars) + [RESIDENT] * len(inputs),
        out_specs=[RESIDENT] * len(outputs),
        out_shape=outputs,
        scratch_shapes=list(scratch),
        compiler_params=pltpu.CompilerParams(vmem_limit_bytes=limit_mib * 2**20),
        cost_estimate=cost,
        name=name,
    )(*scalars, *inputs)


def block_rows(block):
    return slice(block * BLOCK, (block + 1) * BLOCK)


ALL_ROWS = 7 * BLOCK
EDGE_ROWS = 256 + 128 + 192
LEVEL_BLOCK = (0, 4, 6)


def share_edges(place, edges, to_core, to_other):
    core = place[1]
    to_core[...] = edges[1 - core]
    to_other[...] = edges[core]


def halo_rows(halo, left, index):
    place, from_core, from_other = halo
    near, away = from_core[index], from_other[index]
    return jnp.where(place[1] == 0, away if left else near, near if left else away)


def as_row(column):
    return jnp.broadcast_to(column, (column.shape[0], LANES)).T[0:1, :]


def as_column(row):
    return jnp.broadcast_to(row, (LANES, row.shape[1])).T[:, 0:1]


def project_kernel(
    place, t1a_any, t1b_any, t2a_any, t2b_any, t3a_any, t3b_any,
    t0_hbm, wq_hbm, wk_hbm, wv_hbm,
    inverse, q, kv, to_core, to_other, normed_hbm, w_hbm,
    t0, t1, t2, t3, w, normed, edges, in_sems, out_sems,
):
    me = place[0]
    width = t0.shape[1]
    low, high = pl.ds(0, 2 * BLOCK), pl.ds(2 * BLOCK, 2 * BLOCK)
    moves = [
        (t0_hbm, t0),
        (t1a_any, t1.at[low]),
        (t2a_any, t2.at[low]),
        (t3a_any, t3.at[low]),
        (t1b_any, t1.at[high]),
        (t2b_any, t2.at[high]),
        (t3b_any, t3.at[high]),
    ]
    for n, source in enumerate((wq_hbm, wk_hbm, wv_hbm)):
        for r in range(MP):
            target = w.at[pl.ds(r * width, width), pl.ds(n * width, width)]
            moves.append((source.at[share_rows(me, r, width), :], target))
    loads = [
        pltpu.make_async_copy(source, target, in_sems.at[n])
        for n, (source, target) in enumerate(moves)
    ]
    for load in loads:
        load.start()
    pools = pool_both(0.5, 0.25)
    inverse[4:8, :] = jnp.zeros((4, BLOCK), F32)
    stores = []

    def normalise(step):
        if step in (0, 2):
            for load in loads[0:4] if step == 0 else loads[4:7]:
                load.wait()
        rows = block_rows(step)
        shares = [share[rows, :].astype(F32) for share in (t0, t1, t2, t3)]
        squares = shares[0] * shares[0]
        for share in shares[1:]:
            squares = squares + share * share
        total = jnp.sum(squares, axis=1, keepdims=True)
        inv = lax.rsqrt(total / (MP * width) + EPSILON)
        inverse[step : step + 1, :] = as_row(inv)
        parts = [(share * inv).astype(BF16) for share in shares]
        for r, part in enumerate(parts):
            normed[rows, r * width : (r + 1) * width] = part
        store = pltpu.make_async_copy(normed.at[rows], normed_hbm.at[rows], out_sems.at[step])
        store.start()
        stores.append(store)
        return jnp.concatenate(parts, axis=1)

    def spread(step, whole):
        if step == 0:
            for load in loads[7:]:
                load.wait()
            store = pltpu.make_async_copy(w, w_hbm, out_sems.at[4])
            store.start()
            stores.append(store)
        rows = block_rows(step)
        fine = [nn(whole, w[:, n * width : (n + 1) * width]).astype(BF16) for n in range(3)]
        coarse = [nn(pools, x).astype(BF16) for x in fine]
        mid = [x[0:128] for x in coarse]
        low = [x[128:192] for x in coarse]
        mid_rows = slice(1024 + step * 128, 1024 + (step + 1) * 128)
        low_rows = slice(1536 + step * 64, 1536 + (step + 1) * 64)
        q[rows, :] = fine[0]
        q[mid_rows, :] = mid[0]
        q[low_rows, :] = low[0]
        for n in range(2):
            kv[n, rows, :] = fine[1 + n]
            kv[n, mid_rows, :] = mid[1 + n]
            kv[n, low_rows, :] = low[1 + n]
            if step in (0, 3):
                edges[step // 3, n, 0:BLOCK, :] = fine[1 + n]
            if step in (1, 2):
                edges[step - 1, n, 256:384, :] = mid[1 + n]
            if step > 0:
                edges[0, n, 320 + step * 64 : 384 + step * 64, :] = low[1 + n]
            if step < 3:
                edges[1, n, 384 + step * 64 : 448 + step * 64, :] = low[1 + n]

    parts = normalise(0)
    for step in range(4):
        following = normalise(step + 1) if step < 3 else None
        spread(step, parts)
        parts = following
    share_edges(place, edges, to_core, to_other)
    for store in stores:
        store.wait()


def project(place, shares, wq, wk, wv):
    rows, width = shares[0].shape
    out = jax.ShapeDtypeStruct
    edge = out((2, EDGE_ROWS, width), BF16)
    anywhere = pl.BlockSpec(memory_space=pl.ANY)
    share = pltpu.VMEM((rows, width), BF16)
    fixed = [
        pltpu.with_memory_space_constraint(value, pltpu.HBM)
        for value in (*shares[1:], shares[0], wq, wk, wv)
    ]
    return pl.pallas_call(
        project_kernel,
        in_specs=[SCALAR] + [anywhere] * 10,
        out_specs=[RESIDENT] * 5 + [anywhere] * 2,
        out_shape=[
            out((8, width), F32),
            out((ALL_ROWS, width), BF16),
            out((2, ALL_ROWS, width), BF16),
            edge,
            edge,
            pltpu.HBM((rows, MP * width), BF16),
            pltpu.HBM((MP * width, 3 * width), BF16),
        ],
        scratch_shapes=[share] * 4
        + [
            pltpu.VMEM((MP * width, 3 * width), BF16),
            pltpu.VMEM((rows, MP * width), BF16),
            pltpu.VMEM((2, *edge.shape), BF16),
            pltpu.SemaphoreType.DMA((19,)),
            pltpu.SemaphoreType.DMA((5,)),
        ],
        compiler_params=pltpu.CompilerParams(vmem_limit_bytes=20 * 2**20),
        cost_estimate=SMALL,
        name="project",
    )(place, *fixed)


def near_kernel(place, g0, g1, g3, w_out, total, w_turned):
    me = place[0]
    width = g0.shape[1]
    for n, r in enumerate((0, 1, 3)):
        w_turned[block_rows(n), :] = w_out[:, share_rows(me, r, width)].T
    for step in range(4):
        rows = block_rows(step)
        shares = jnp.concatenate([share[rows, :] for share in (g0, g1, g3)], axis=1)
        total[rows, :] = nn(shares, w_turned[...])


def near_cotangent(place, shares, w_out):
    rows, width = shares[0].shape
    inputs = [*shares, w_out]
    scratch = [pltpu.VMEM((3 * width, width), BF16)]
    outputs = [held((rows, width), F32)]
    return run(near_kernel, "near_cotangent", 10, [place], inputs, outputs, scratch)[0]


def cotangent_kernel(place, near, g2, w_out, d_att, w_turned):
    width = g2.shape[1]
    pools = pool_both(1.0, 1.0)
    w_turned[...] = w_out[:, share_rows(place[0], 2, width)].T
    for step in range(4):
        rows = block_rows(step)
        fine = (near[rows, :] + nn(g2[rows, :], w_turned[...])).astype(BF16)
        d_att[rows, :] = fine
        coarse = nn(pools, fine).astype(BF16)
        d_att[1024 + step * 128 : 1024 + (step + 1) * 128, :] = coarse[0:128]
        d_att[1536 + step * 64 : 1536 + (step + 1) * 64, :] = coarse[128:192]


def cotangent(place, near, far, w_out):
    width = far.shape[1]
    scratch = [pltpu.VMEM((width, width), BF16)]
    outputs = [held((ALL_ROWS, width), BF16)]
    return run(cotangent_kernel, "cotangent", 10, [place], [near, far, w_out], outputs, scratch)[0]


EDGE_UNITS = ((0, 0), (0, 3), (1, 0), (1, 1), (2, 0))
INNER_UNITS = ((0, 1), (0, 2))


def unit_keys(level, block):
    last = EXT_BLOCKS[level] - 1
    offsets = (0, 1, 2) if level == 0 else (0, 2)
    keys = []
    for offset in offsets:
        at = block + offset
        keys.append((at, 0 if at == 0 else 1 if at == last else None))
    return keys


def ext_rows(kv, halo, n, level, at, lanes):
    if at in (0, EXT_BLOCKS[level] - 1):
        return halo[0 if at == 0 else 1][n, block_rows(level), lanes]
    return kv[n, block_rows(LEVEL_BLOCK[level] + at - 1), lanes]


def head_part(lane, head, rows):
    mine = (lane >= head * HD) & (lane < (head + 1) * HD)
    return jnp.where(mine, rows, 0.0).astype(BF16)


def unit_scores(keys, key_rows, query, bias_ref):
    scores = []
    for (_, bias), rows in zip(keys, key_rows):
        s = nt(rows, query)
        scores.append(s if bias is None else s + bias_ref[bias])
    return scores


def add_spread(target, block, factor, rows):
    if factor == 1:
        target[block_rows(block), :] = target[block_rows(block), :] + rows
        return
    for s in range(factor):
        spread = pl.ds(block * factor * BLOCK + s, BLOCK, factor)
        target[spread, :] = target[spread, :] + rows


def each_pair(width, body):
    def step(pair, _):
        body(pair, pl.ds(pl.multiple_of(pair * PAIR, PAIR), PAIR))
        return 0

    lax.fori_loop(0, width // PAIR, step, 0)


def head_part(lane, head, rows):
    mine = (lane >= head * HD) & (lane < (head + 1) * HD)
    return jnp.where(mine, rows, 0.0).astype(BF16)


def unit_scores(keys, key_rows, query, bias_ref):
    scores = []
    for (_, bias), rows in zip(keys, key_rows):
        s = nt(rows, query)
        scores.append(s if bias is None else s + bias_ref[bias])
    return scores


def add_spread(target, block, factor, rows):
    if factor == 1:
        target[block_rows(block), :] = target[block_rows(block), :] + rows
        return
    for s in range(factor):
        spread = pl.ds(block * factor * BLOCK + s, BLOCK, factor)
        target[spread, :] = target[spread, :] + rows


def forward_units(pair, lanes, units, bias_ref, q, kv, halo, stats, vt, out_f):
    lane = lax.broadcasted_iota(jnp.int32, (BLOCK, PAIR), 1)
    done = set()
    for level, block in units:
        for at, _ in unit_keys(level, block):
            if (level, at) not in done:
                done.add((level, at))
                rows = ext_rows(kv, halo, 1, level, at, lanes)
                vt[FIRST_EXT[level] + at] = rows.T

    def begin(u, head):
        level, block = units[u]
        keys = unit_keys(level, block)
        key_rows = [ext_rows(kv, halo, 0, level, at, lanes) for at, _ in keys]
        q_rows = q[block_rows(LEVEL_BLOCK[level] + block), lanes] * HD ** (-0.5)
        return unit_scores(keys, key_rows, head_part(lane, head, q_rows), bias_ref)

    def finish(u, head, scores):
        level, block = units[u]
        top = scores[0].max(axis=0, keepdims=True)
        for s in scores[1:]:
            top = jnp.maximum(top, s.max(axis=0, keepdims=True))
        exps = [jnp.exp(s - top) for s in scores]
        total = exps[0].sum(axis=0, keepdims=True)
        for e in exps[1:]:
            total = total + e.sum(axis=0, keepdims=True)
        scale = 1.0 / total
        row = 4 * u + 2 * head
        stats[pair, row : row + 1, :] = top
        stats[pair, row + 1 : row + 2, :] = scale
        return [(e * scale).astype(BF16) for e in exps]

    outs = []

    def give(u, head, weights):
        level, block = units[u]
        part = slice(head * HD, (head + 1) * HD)
        o_t = None
        for (at, _), w in zip(unit_keys(level, block), weights):
            o = nn(vt[FIRST_EXT[level] + at, part, :], w)
            o_t = o if o_t is None else o_t + o
        outs.append(o_t)
        if head == 1:
            add_spread(out_f, block, 2**level, jnp.concatenate(outs, axis=0).T)
            outs.clear()

    items = [(u, head) for u in range(len(units)) for head in range(2)]
    scores, last = begin(*items[0]), None
    for n, item in enumerate(items):
        following = begin(*items[n + 1]) if n + 1 < len(items) else None
        if last is not None:
            give(*items[n - 1], last)
        last = finish(*item, scores)
        scores = following
    give(*items[-1], last)


def forward_inner_kernel(bias_ref, q, kv, out, stats, vt, out_f):
    def one(pair, lanes):
        out_f[...] = jnp.zeros_like(out_f)
        forward_units(pair, lanes, INNER_UNITS, bias_ref, q, kv, None, stats, vt, out_f)
        out[:, lanes] = out_f[BLOCK : 3 * BLOCK, :]

    each_pair(q.shape[1], one)


def forward_edge_kernel(
    place, bias_ref, q, kv, from_other, from_core, inner,
    attended, stats, left, right, vt, out_f,
):
    received = (place, from_core, from_other)
    pools = pool_both(0.5, 0.25)
    every = slice(None)
    for n in range(2):
        for out, is_left in ((left, True), (right, False)):
            fine = halo_rows(received, is_left, (n, slice(0, 256), every))
            mid = halo_rows(received, is_left, (n, slice(256, 384), every))
            low = halo_rows(received, is_left, (n, slice(384, 576), every))
            coarse = nn(pools, fine).astype(BF16)
            out[n, 0:256, :] = fine
            if is_left:
                out[n, 256:384, :], out[n, 384:512, :] = mid, coarse[0:128]
                out[n, 512:704, :], out[n, 704:768, :] = low, coarse[128:192]
            else:
                out[n, 256:384, :], out[n, 384:512, :] = coarse[0:128], mid
                out[n, 512:576, :], out[n, 576:768, :] = coarse[128:192], low
    halo = (left, right)

    def one(pair, lanes):
        out_f[0:BLOCK, :] = jnp.zeros((BLOCK, PAIR), F32)
        out_f[BLOCK : 3 * BLOCK, :] = inner[:, lanes]
        out_f[3 * BLOCK :, :] = jnp.zeros((BLOCK, PAIR), F32)
        forward_units(
            pair, lanes, EDGE_UNITS, bias_ref, q, kv, halo, stats, vt, out_f
        )
        attended[:, lanes] = out_f[...].astype(BF16)

    each_pair(q.shape[1], one)


def backward_units(
    pair, lanes, units, bias_ref, q, kv, halo, grads, stats, kt, dq_f, keep
):
    lane = lax.broadcasted_iota(jnp.int32, (BLOCK, PAIR), 1)
    done = set()
    for level, block in units:
        for at, _ in unit_keys(level, block):
            if (level, at) not in done:
                done.add((level, at))
                rows = ext_rows(kv, halo, 0, level, at, lanes)
                kt[FIRST_EXT[level] + at] = rows.T

    def begin(u, head):
        level, block = units[u]
        keys = unit_keys(level, block)
        key_rows = [ext_rows(kv, halo, 0, level, at, lanes) for at, _ in keys]
        value_rows = [ext_rows(kv, halo, 1, level, at, lanes) for at, _ in keys]
        at = block_rows(LEVEL_BLOCK[level] + block)
        qm = head_part(lane, head, q[at, lanes] * HD ** (-0.5))
        am = head_part(lane, head, grads[at, lanes])
        scores = unit_scores(keys, key_rows, qm, bias_ref)
        return qm, am, scores, [nt(rows, am) for rows in value_rows]

    def finish(u, head, qm, am, scores, d_weights):
        level, block = units[u]
        row = 4 * u + 2 * head
        top, scale = stats[pair, row : row + 1, :], stats[pair, row + 1 : row + 2, :]
        probs = [jnp.exp(s - top) * scale for s in scores]
        dots = None
        for p, dw in zip(probs, d_weights):
            d = (p * dw).sum(axis=0, keepdims=True)
            dots = d if dots is None else dots + d
        weights = [p.astype(BF16) for p in probs]
        d_scores = [(p * (dw - dots)).astype(BF16) for p, dw in zip(probs, d_weights)]
        return qm, am, weights, d_scores

    first = []

    def give(u, head, qm, am, weights, d_scores):
        level, block = units[u]
        keys = unit_keys(level, block)
        part = slice(head * HD, (head + 1) * HD)
        d_values = [nn(w, am) for w in weights]
        d_keys = [nn(ds, qm) for ds in d_scores]
        dq_t = None
        for (at, _), ds in zip(keys, d_scores):
            g = nn(kt[FIRST_EXT[level] + at, part, :], ds)
            dq_t = g if dq_t is None else dq_t + g
        if head == 0:
            first.append((dq_t, d_keys, d_values))
            return
        dq_first, k_first, v_first = first.pop()
        for n, (at, _) in enumerate(keys):
            keep(0, level, at, k_first[n] + d_keys[n])
            keep(1, level, at, v_first[n] + d_values[n])
        dq = jnp.concatenate([dq_first, dq_t], axis=0).T * (HD ** (-0.5) / 2**level)
        add_spread(dq_f, block, 2**level, dq)

    items = [(u, head) for u in range(len(units)) for head in range(2)]
    ready, last = begin(*items[0]), None
    for n, item in enumerate(items):
        following = begin(*items[n + 1]) if n + 1 < len(items) else None
        if last is not None:
            give(*items[n - 1], *last)
        last = finish(*item, *ready)
        ready = following
    give(*items[-1], *last)


def edge_kernel(
    place, bias_ref, stats, q, kv, left, right, grads,
    dq_f, d_kv, to_core, to_other, kt, ext, dq_s, sums, edges,
):
    halo = (left, right)

    def add_rows(factor, rows):
        for s in range(factor):
            spread = pl.ds(s, rows.shape[0], factor)
            sums[spread, :] = sums[spread, :] + rows * (1.0 / factor)

    def one(pair, lanes):
        dq_s[...] = jnp.zeros_like(dq_s)
        seen = set()

        def keep(n, level, at, rows):
            slot = FIRST_EXT[level] + at
            if (n, slot) in seen:
                ext[n, slot] = ext[n, slot] + rows
            else:
                seen.add((n, slot))
                ext[n, slot] = rows

        backward_units(
            pair, lanes, EDGE_UNITS, bias_ref, q, kv, halo, grads, stats, kt, dq_s, keep,
        )
        dq_f[:, lanes] = dq_s[...]
        for n in range(2):
            for side in range(2):
                fine, mid, low = (
                    ext[n, FIRST_EXT[level] + side * (EXT_BLOCKS[level] - 1)]
                    for level in range(LEVELS)
                )
                if side == 0:
                    (mid, mid_near), (low, low_near) = (mid[0:128], mid[128:]), (low[0:192], low[192:])
                else:
                    (mid_near, mid), (low_near, low) = (mid[0:128], mid[128:]), (low[0:64], low[64:])
                sums[0:BLOCK, :] = fine
                add_rows(2, mid_near)
                add_rows(4, low_near)
                edges[side, n, 0:256, lanes] = sums[0:BLOCK, :].astype(BF16)
                edges[side, n, 256:384, lanes] = mid.astype(BF16)
                edges[side, n, 384:576, lanes] = low.astype(BF16)
            for b in range(4):
                sums[block_rows(b), :] = ext[n, 1 + b]
            for b in range(2):
                add_spread(sums, b, 2, ext[n, FIRST_EXT[1] + 1 + b] * 0.5)
            d_kv[n, :, lanes] = sums[...]

    each_pair(q.shape[1], one)
    share_edges(place, edges, to_core, to_other)


def inner_units_kernel(bias_ref, stats, q, kv, grads, dq_in, d_kv_in, d_query, d_kv, kt, dq_s):
    def one(pair, lanes):
        dq_s[...] = dq_in[:, lanes]
        d_kv[:, :, lanes] = d_kv_in[:, :, lanes]

        def keep(n, level, at, rows):
            where = block_rows(at - 1)
            d_kv[n, where, lanes] = d_kv[n, where, lanes] + rows

        backward_units(
            pair, lanes, INNER_UNITS, bias_ref, q, kv, None, grads, stats, kt, dq_s, keep
        )
        d_query[:, lanes] = dq_s[...].astype(BF16)

    each_pair(q.shape[1], one)


def turned(count):
    return pltpu.VMEM((count, PAIR, BLOCK), BF16)


def forward_inner(bias, q, kv):
    width = q.shape[1]
    outputs = [held((2 * BLOCK, width), F32), held((width // PAIR, 8, BLOCK), F32)]
    scratch = [turned(EXT_BLOCKS[0]), pltpu.VMEM((4 * BLOCK, PAIR), F32)]
    return run(forward_inner_kernel, "forward_inner", 12, [bias], [q, kv], outputs, scratch, MIDDLE)


def forward_edge(place, bias, q, kv, halo, inner):
    width = q.shape[1]
    inputs = [q, kv, *halo[::-1], inner]
    outputs = [held((4 * BLOCK, width), BF16), held((width // PAIR, 24, BLOCK), F32)]
    outputs += [held((2, 3 * BLOCK, width), BF16)] * 2
    scratch = [turned(EXT_TOTAL), pltpu.VMEM((4 * BLOCK, PAIR), F32)]
    return run(forward_edge_kernel, "forward_edge", 12, [place, bias], inputs, outputs, scratch)


def edge_backward(place, bias, stats, q, kv, halo, d_att):
    rows, width = 4 * BLOCK, q.shape[1]
    edge = held((2, EDGE_ROWS, width), BF16)
    inputs = [stats, q, kv, *halo, d_att]
    outputs = [held((rows, width), F32), held((2, rows, width), F32), edge, edge]
    scratch = [
        turned(EXT_TOTAL),
        pltpu.VMEM((2, EXT_TOTAL, BLOCK, PAIR), F32),
        pltpu.VMEM((rows, PAIR), F32),
        pltpu.VMEM((rows, PAIR), F32),
        pltpu.VMEM((2, *edge.shape), BF16),
    ]
    return run(edge_kernel, "edge_backward", 20, [place, bias], inputs, outputs, scratch)


def inner_backward(bias, stats, q, kv, d_att, dq_f, d_kv):
    rows, width = 4 * BLOCK, q.shape[1]
    inputs = [stats, q, kv, d_att, dq_f, d_kv]
    outputs = [held((rows, width), BF16), held((2, rows, width), F32)]
    scratch = [turned(EXT_BLOCKS[0]), pltpu.VMEM((rows, PAIR), F32)]
    return run(inner_units_kernel, "inner_backward", 12, [bias], inputs, outputs, scratch)


def term_outputs(rows, width):
    return [held((rows, width), BF16)] * MP


def store_terms(step, terms, own, keep_right, keep_left, right, left):
    own[block_rows(step), :] = terms[0]
    low, high = block_rows(step % 2), block_rows(2 + step % 2)
    if step < 2:
        keep_right[low, :] = terms[1]
        right[high, :] = terms[2]
        left[low, :] = terms[3]
    else:
        right[low, :] = terms[1]
        left[high, :] = terms[2]
        keep_left[low, :] = terms[3]


def out_terms_kernel(place, attended, w_out, *outs):
    me = place[0]
    width = attended.shape[1]
    for step in range(4):
        rows = attended[block_rows(step), :]
        for r, out in enumerate(outs):
            term = nn(rows, w_out[:, share_rows(me, r, width)])
            out[block_rows(step), :] = term.astype(BF16)


def out_terms(place, attended, w_out):
    outputs = term_outputs(*attended.shape)
    return run(out_terms_kernel, "out_terms", 8, [place], [attended, w_out], outputs)


def by_partner(place, sent, to_a, to_b):
    odd = place[0] & 1
    to_a[...] = sent[odd]
    to_b[...] = sent[1 - odd]


def from_side(place, from_a, from_b, before, rows):
    odd = place[0] & 1
    one, other = from_a[rows, :], from_b[rows, :]
    return jnp.where(odd == 1, one, other) if before else jnp.where(odd == 1, other, one)


def input_terms_kernel(
    place, d_query, d_kv, from_other, from_core, normed, w, d_proj,
    dots, own, keep_right, keep_left, to_a, to_b, dot_rows, w_turned, sent,
):
    halo = (place, from_core, from_other)
    width = d_query.shape[1]
    half = spread_matrix(BLOCK // 2, 2, 0.5)
    quarter = spread_matrix(BLOCK // 4, 4, 0.25)
    dot_rows[12:16, :] = jnp.zeros((4, BLOCK), F32)
    for r in range(MP):
        for n in range(3):
            at = slice(r * width, (r + 1) * width)
            w_turned[block_rows(n), at] = w[at, n * width : (n + 1) * width].T
    for step in range(4):
        rows = block_rows(step)
        grads = [d_query[rows, :]]
        every = slice(None)
        for n in range(2):
            total = d_kv[n, rows, :]
            if step in (0, 3):
                total = total + halo_rows(halo, step == 0, (n, slice(0, 256), every)).astype(F32)
            else:
                total = total + nn(half, halo_rows(halo, step == 1, (n, slice(256, 384), every)))
            if step > 0:
                low = slice(320 + step * 64, 384 + step * 64)
                total = total + nn(quarter, halo_rows(halo, True, (n, low, every)))
            if step < 3:
                low = slice(384 + step * 64, 448 + step * 64)
                total = total + nn(quarter, halo_rows(halo, False, (n, low, every)))
            grads.append(total.astype(BF16))
        for n, grad in enumerate(grads[1:]):
            d_proj[rows, n * width : (n + 1) * width] = grad
        dot = None
        every = jnp.concatenate(grads, axis=1)
        terms = []
        for r in range(MP):
            term = nn(every, w_turned[:, r * width : (r + 1) * width]).astype(BF16)
            terms.append(term)
            part = term.astype(F32) * normed[rows, r * width : (r + 1) * width].astype(F32)
            dot = part if dot is None else dot + part
        store_terms(step, terms, own, keep_right, keep_left, sent.at[0], sent.at[1])
        dot = as_row(jnp.sum(dot, axis=1, keepdims=True))
        first = dot.astype(BF16).astype(F32)
        second = (dot - first).astype(BF16).astype(F32)
        for n, piece in enumerate((first, second, dot - first - second)):
            dot_rows[4 * n + step : 4 * n + step + 1, :] = piece
    pieces = dot_rows[...].astype(BF16)
    dots[...] = pieces
    for side in range(2):
        sent[side, 4 * BLOCK :, :] = pieces
    by_partner(place, sent, to_a, to_b)


def input_terms(place, d_query, d_kv, halo, normed, w):
    rows, width = d_query.shape
    inputs = [d_query, d_kv, *halo[::-1], normed, w]
    outputs = [held((rows, 2 * width), BF16), held((DOT_ROWS, width), BF16)]
    lengths = [rows, rows // 2, rows // 2, rows + DOT_ROWS, rows + DOT_ROWS]
    outputs += [held((n, width), BF16) for n in lengths]
    scratch = [pltpu.VMEM((DOT_ROWS, width), F32), pltpu.VMEM((3 * width, MP * width), BF16)]
    scratch += [pltpu.VMEM((2, rows + DOT_ROWS, width), BF16)]
    return run(input_terms_kernel, "input_terms", 18, [place], inputs, outputs, scratch)


def sum_terms(own, received, at):
    total = own[at, :].astype(F32)
    for term in received:
        total = total + term[at, :].astype(F32)
    return total


def finish_out_kernel(own, one, two, three, result):
    for b in range(4):
        at = block_rows(b)
        result[at, :] = sum_terms(own, (one, two, three), at).astype(BF16)


def finish_out(own, received):
    outputs = [held(own.shape, BF16)]
    return run(finish_out_kernel, "finish_out", 8, [], [own, *received], outputs)[0]


def relay_kernel(place, keep_right, keep_left, from_a, from_b, to_a, to_b, sent):
    half = keep_right.shape[0]
    terms, dots = slice(half, 2 * half), slice(2 * half, 2 * half + DOT_ROWS)
    for side, keep in enumerate((keep_right, keep_left)):
        passed = from_side(place, from_a, from_b, side == 0, terms).astype(F32)
        sent[side, 0:half, :] = (keep[...].astype(F32) + passed).astype(BF16)
        sent[side, half:, :] = from_side(place, from_a, from_b, side == 0, dots)
    by_partner(place, sent, to_a, to_b)


def relay(place, keep_right, keep_left, from_a, from_b):
    half, width = keep_right.shape
    outputs = [held((half + DOT_ROWS, width), BF16)] * 2
    scratch = [pltpu.VMEM((2, half + DOT_ROWS, width), BF16)]
    inputs = [keep_right, keep_left, from_a, from_b]
    return run(relay_kernel, "relay", 6, [place], inputs, outputs, scratch, RELAY)


def finish_grad_kernel(place, own, a1, b1, a2, b2, tokens, inverse, dots, result):
    rows, width = own.shape
    half = rows // 2
    whole, part = slice(rows, rows + DOT_ROWS), slice(half, half + DOT_ROWS)
    pieces = dots[...].astype(F32) + a1[whole, :].astype(F32) + b1[whole, :].astype(F32)
    pieces = pieces + from_side(place, a2, b2, True, part).astype(F32)
    means = (pieces[0:4] + pieces[4:8] + pieces[8:12]) / (MP * width)
    for b in range(rows // BLOCK):
        at, near = block_rows(b), block_rows(b % 2)
        mean = as_column(means[b : b + 1, :])
        inv = as_column(inverse[b : b + 1, :])
        total = own[at, :].astype(F32)
        total = total + from_side(place, a1, b1, b >= 2, near).astype(F32)
        total = total + from_side(place, a2, b2, b < 2, near).astype(F32)
        result[at, :] = inv * (total - tokens[at, :].astype(F32) * inv * mean)


def finish_grad(place, own, a1, b1, a2, b2, tokens, inverse, dots):
    inputs = [own, a1, b1, a2, b2, tokens, inverse, dots]
    outputs = [held(own.shape, F32)]
    return run(finish_grad_kernel, "finish_grad", 8, [place], inputs, outputs)[0]


def early_kernel(g0, g1, g2, g3, attended, normed, d_query, outer, inner):
    width = g0.shape[1]
    rows = attended[...]
    for r, share in enumerate((g0, g1, g2, g3)):
        at = slice(r * width, (r + 1) * width)
        outer[at, :] = tn(share[...], rows).astype(BF16)
        inner[at, :] = tn(normed[:, at], d_query[...]).astype(BF16)


def early_terms(shares, attended, normed, d_query):
    width = attended.shape[1]
    inputs = [*shares, attended, normed, d_query]
    outputs = [held((MP * width, width), BF16)] * 2
    return run(early_kernel, "early_terms", 14, [], inputs, outputs, (), LARGE)


def inner_kernel(place, normed, d_proj, inner, outer, mine, other_low, other_high, rows_held):
    core = place[1]
    width = outer.shape[1]
    for block in range(MP):
        at = block_rows(block)
        rows_held[at, 0:width] = inner[at, :]
        rows_held[at, width : 3 * width] = tn(normed[:, at], d_proj[...]).astype(BF16)
        rows_held[at, 3 * width :] = outer[at, :]
        for n in range(width // 64):
            out = slice((4 * block + n) * 32, (4 * block + n + 1) * 32)
            first = block * width + n * 64
            mine[out, :] = rows_held[pl.ds(pl.multiple_of(first + core * 32, 32), 32), :]
            other, start = (other_low, 0) if block < 2 else (other_high, 256)
            other[out.start - start : out.stop - start, :] = rows_held[pl.ds(pl.multiple_of(first + 32 - core * 32, 32), 32), :]


def inner_terms(place, normed, d_proj, inner, outer):
    total = normed.shape[1]
    width = outer.shape[1]
    outputs = [held((n, 4 * width), BF16) for n in (total // 2, total // 4, total // 4)]
    scratch = [pltpu.VMEM((total, 4 * width), BF16)]
    return run(inner_kernel, "inner_terms", 16, [place], [normed, d_proj, inner, outer], outputs, scratch)


def pair_sum_kernel(place, mine, got_low, got_high, *outs):
    z, core, x, y = place[0], place[1], place[2], place[3]
    for d, out in enumerate(outs):
        for n in range(4):
            chunk = jnp.where(core == 0, 4 * n + ((x + d) & 3), 4 * ((y + d - z + 4) & 3) + n)
            rows = pl.ds(pl.multiple_of(chunk * 32, 32), 32)
            half = pl.ds(pl.multiple_of((chunk & 7) * 32, 32), 32)
            got = jnp.where(chunk < 8, got_low[half, :], got_high[half, :])
            total = mine[rows, :].astype(F32) + got.astype(F32)
            out[32 * n : 32 * (n + 1), :] = total.astype(BF16)


def row_sum_kernel(place, a, b, c, d, *refs):
    *outs, total = refs
    z, core, x, y = place[0], place[1], place[2], place[3]
    first = jnp.where(core == 0, y - z + 4, x)
    total[...] = (
        a[...].astype(F32) + b[...].astype(F32) + c[...].astype(F32) + d[...].astype(F32)
    ).astype(BF16)
    for n, out in enumerate(outs):
        out[...] = total[pl.ds(pl.multiple_of(((first + n) & 3) * 32, 32), 32), :]


def last_sum_kernel(a, b, c, d, gq, gk, gv, go):
    width = gq.shape[1]
    total = a[...].astype(F32) + b[...].astype(F32) + c[...].astype(F32) + d[...].astype(F32)
    gq[...] = total[:, 0:width]
    gk[...] = total[:, width : 2 * width]
    gv[...] = total[:, 2 * width : 3 * width]
    go[...] = total[:, 3 * width :]


def sum_over_core(place, mine, *others):
    got = [lax.ppermute(other, "seq", [(i, i ^ 1) for i in range(32)]) for other in others]
    parts = [held((128, mine.shape[1]), BF16)] * 4
    return run(pair_sum_kernel, "pair_sum", 6, [place], [mine, *got], parts)


def sum_over_seq(place, parts, *first):
    cols = parts[0].shape[1]

    def sent(value, stage, d):
        pairs = []
        for i in range(32):
            core, x, y = i % 2, (i // 2) % 4, i // 8
            if stage == core:
                x = (x + d) % 4
            else:
                y = (y + d) % 4
            pairs.append((i, (y * 4 + x) * 2 + core))
        return lax.ppermute(value, "seq", pairs)

    parts = [parts[0]] + [sent(parts[d], 0, d) for d in (1, 2, 3)]
    parts = tied(parts, *first)
    rows = [held((32, cols), BF16)] * 4
    scratch = [pltpu.VMEM((128, cols), BF16)]
    rows = run(row_sum_kernel, "row_sum", 4, [place], parts, rows, scratch)
    rows = [rows[0]] + [sent(rows[d], 1, d) for d in (1, 2, 3)]
    outputs = [held((32, cols // 4), F32)] * 4
    return run(last_sum_kernel, "last_sum", 4, [], rows, outputs)


def to_next(value):
    return lax.ppermute(value, "mp", [(i, (i + 1) % MP) for i in range(MP)])


def to_previous(value):
    return lax.ppermute(value, "mp", [((i + 1) % MP, i) for i in range(MP)])


def swap_a(value):
    return lax.ppermute(value, "mp", [(0, 1), (1, 0), (2, 3), (3, 2)])


def swap_b(value):
    return lax.ppermute(value, "mp", [(1, 2), (2, 1), (3, 0), (0, 3)])


def gather_shares(share):
    half = share.shape[0] // 2
    low, high = share[:half], share[half:]
    after_low, before_high = to_previous(low), to_next(high)
    after_high, before_low = to_previous(high), to_next(low)
    far_low, far_high = to_previous(after_low), to_next(before_high)
    return [share, after_low, after_high, far_low, far_high, before_low, before_high]


def turned_by(value, step):
    return lax.ppermute(value, "mp", [(i, (i + step) % MP) for i in range(MP)])


def sum_over_mp(terms):
    return [turned_by(term, step) for step, term in zip((1, 2, 3), terms)]


def exchange(to_core, to_other):
    count = lax.axis_size("seq")
    pairs = []
    for i in range(1, count - 1, 2):
        pairs += [(i, i + 1), (i + 1, i)]
    from_other = lax.ppermute(to_other, "seq", pairs)
    from_core = lax.ppermute(to_core, "seq", [(i, i ^ 1) for i in range(count)])
    return from_core, from_other


def tied(values, *others):
    flat, tree = jax.tree.flatten(values)
    flat = lax.optimization_barrier((*flat, *others))[: len(flat)]
    return jax.tree.unflatten(tree, flat)


def per_device(tokens, w_query, w_key, w_value, w_out, grad_out):
    count = lax.axis_size("seq")
    index = lax.axis_index("seq")
    me = jnp.stack([lax.axis_index("mp"), index & 1, (index >> 1) & 3, index >> 3])
    me = me.astype(jnp.int32)
    bias = jnp.stack(
        [
            jnp.where(index == 0, NEGATIVE, 0.0).astype(F32),
            jnp.where(index == count - 1, NEGATIVE, 0.0).astype(F32),
        ]
    )
    token_shares = gather_shares(tokens)
    near_grad = tied(grad_out, *(token_shares[n] for n in (1, 2, 5, 6)))
    far_grad = tied(grad_out, *token_shares)
    far = turned_by(far_grad, 2)
    grad_shares = [grad_out, to_previous(near_grad), far, to_next(near_grad)]
    inverse, q, kv, to_core, to_other, normed, w = project(
        me, token_shares, w_query, w_key, w_value
    )
    halo = exchange(to_core, to_other)
    near_q = tied(q, grad_shares[1], grad_shares[3])
    inner_out, inner_stats = forward_inner(bias, near_q, kv)
    near = near_cotangent(me, tied([grad_shares[n] for n in (0, 1, 3)], inner_out), w_out)
    inner_out = tied(inner_out, near)
    attended, stats, *halo = forward_edge(me, bias, q, kv, halo, inner_out)
    out_own, *terms = out_terms(me, attended, w_out)
    out_received = sum_over_mp(terms)
    grad_shares = tied(grad_shares, out_own)
    d_att = cotangent(me, near, grad_shares[2], w_out)
    dq_f, d_kv, to_core, to_other = edge_backward(me, bias, stats, q, kv, halo, d_att)
    halo = exchange(to_core, to_other)
    d_query, d_kv = inner_backward(bias, inner_stats, q, kv, d_att, dq_f, d_kv)
    attended = tied(attended, *out_received)
    outer, inner = early_terms(grad_shares, attended, normed, d_query)
    d_query = tied(d_query, outer)
    d_proj, dots, own, keep_right, keep_left, to_a, to_b = input_terms(
        me, d_query, d_kv, halo, normed, w
    )
    attn_out = finish_out(out_own, out_received)
    mine, *others = inner_terms(me, normed, d_proj, inner, outer)
    core_sums = sum_over_core(me, mine, *others)
    a1, b1 = swap_a(to_a), swap_b(to_b)
    to_a, to_b = relay(me, keep_right, keep_left, a1, b1)
    a2, b2 = swap_a(to_a), swap_b(to_b)
    grad_tokens = finish_grad(me, own, a1, b1, a2, b2, tokens, inverse, dots)
    *weight_grads, grad_w_out = sum_over_seq(me, core_sums, to_a, attn_out)
    return (attn_out, grad_tokens, *weight_grads, grad_w_out.T)


def solution(mesh):
    return jax.shard_map(
        per_device,
        mesh=mesh,
        in_specs=(
            P("seq", "mp"),
            P(None, "mp"),
            P(None, "mp"),
            P(None, "mp"),
            P("mp", None),
            P("seq", "mp"),
        ),
        out_specs=(
            P("seq", "mp"),
            P("seq", "mp"),
            P("seq", "mp"),
            P("seq", "mp"),
            P("seq", "mp"),
            P("mp", "seq"),
        ),
        check_vma=False,
    )
```

```python
import jax
import jax.numpy as jnp
from jax import lax
from jax.experimental import pallas as pl
from jax.experimental.pallas import tpu as pltpu
from jax.sharding import PartitionSpec as P

HD = 64
BLOCK = 256
LEVELS = 3
PAIR = 2 * HD
MP = 4
LANES = 128
DOT_ROWS = 16

EPSILON = 1e-06
NEGATIVE = -1e30

F32 = jnp.float32
BF16 = jnp.bfloat16

FIRST_EXT = (0, 6, 10)
EXT_BLOCKS = (6, 4, 3)
EXT_TOTAL = 13


def nn(left, right):
    return lax.dot_general(left, right, (((1,), (0,)), ((), ())), preferred_element_type=F32)


def nt(left, right):
    return lax.dot_general(left, right, (((1,), (1,)), ((), ())), preferred_element_type=F32)


def tn(left, right):
    return lax.dot_general(left, right, (((0,), (0,)), ((), ())), preferred_element_type=F32)


def pool_matrix(coarse, factor, value):
    shape = (coarse, coarse * factor)
    row = lax.broadcasted_iota(jnp.int32, shape, 0)
    low = row * factor
    col = lax.broadcasted_iota(jnp.int32, shape, 1)
    return jnp.where((col >= low) & (col < low + factor), value, 0.0).astype(BF16)


def pool_both(half, quarter):
    parts = [pool_matrix(BLOCK // 2, 2, half), pool_matrix(BLOCK // 4, 4, quarter)]
    return jnp.concatenate(parts, axis=0)


def spread_matrix(coarse, factor, value):
    shape = (coarse * factor, coarse)
    low = lax.broadcasted_iota(jnp.int32, shape, 1) * factor
    row = lax.broadcasted_iota(jnp.int32, shape, 0)
    return jnp.where((row >= low) & (row < low + factor), value, 0.0).astype(BF16)


def share_rows(me, step, width):
    return pl.ds(pl.multiple_of(((me + step) & (MP - 1)) * width, width), width)


SMALL = pl.CostEstimate(flops=10**6, bytes_accessed=10**4, transcendentals=0)
LARGE = pl.CostEstimate(flops=4 * 10**9, bytes_accessed=10**4, transcendentals=0)
MIDDLE = pl.CostEstimate(flops=25 * 10**8, bytes_accessed=10**4, transcendentals=0)
RELAY = pl.CostEstimate(flops=10**9, bytes_accessed=10**4, transcendentals=0)
SCALAR = pl.BlockSpec(memory_space=pltpu.SMEM)
RESIDENT = pl.BlockSpec(memory_space=pltpu.VMEM)


def held(shape, dtype):
    return jax.ShapeDtypeStruct(shape, dtype)


def run(kernel, name, limit_mib, scalars, inputs, outputs, scratch=(), cost=SMALL):
    return pl.pallas_call(
        kernel,
        in_specs=[SCALAR] * len(scalars) + [RESIDENT] * len(inputs),
        out_specs=[RESIDENT] * len(outputs),
        out_shape=outputs,
        scratch_shapes=list(scratch),
        compiler_params=pltpu.CompilerParams(vmem_limit_bytes=limit_mib * 2**20),
        cost_estimate=cost,
        name=name,
    )(*scalars, *inputs)


def block_rows(block):
    return slice(block * BLOCK, (block + 1) * BLOCK)


ALL_ROWS = 7 * BLOCK
EDGE_ROWS = 256 + 128 + 192
LEVEL_BLOCK = (0, 4, 6)


def share_edges(place, edges, to_core, to_other):
    core = place[1]
    to_core[...] = edges[1 - core]
    to_other[...] = edges[core]


def halo_rows(halo, left, index):
    place, from_core, from_other = halo
    near, away = from_core[index], from_other[index]
    return jnp.where(place[1] == 0, away if left else near, near if left else away)


def as_row(column):
    return jnp.broadcast_to(column, (column.shape[0], LANES)).T[0:1, :]


def as_column(row):
    return jnp.broadcast_to(row, (LANES, row.shape[1])).T[:, 0:1]


def project_kernel(
    place, t1a_any, t1b_any, t2a_any, t2b_any, t3a_any, t3b_any,
    t0_hbm, wq_hbm, wk_hbm, wv_hbm,
    inverse, q, kv, to_core, to_other, normed_hbm, w_hbm,
    t0, t1, t2, t3, w, normed, edges, in_sems, out_sems,
):
    me = place[0]
    width = t0.shape[1]
    low, high = pl.ds(0, 2 * BLOCK), pl.ds(2 * BLOCK, 2 * BLOCK)
    moves = [
        (t0_hbm, t0),
        (t1a_any, t1.at[low]),
        (t2a_any, t2.at[low]),
        (t3a_any, t3.at[low]),
        (t1b_any, t1.at[high]),
        (t2b_any, t2.at[high]),
        (t3b_any, t3.at[high]),
    ]
    for n, source in enumerate((wq_hbm, wk_hbm, wv_hbm)):
        for r in range(MP):
            target = w.at[pl.ds(r * width, width), pl.ds(n * width, width)]
            moves.append((source.at[share_rows(me, r, width), :], target))
    loads = [
        pltpu.make_async_copy(source, target, in_sems.at[n])
        for n, (source, target) in enumerate(moves)
    ]
    for load in loads:
        load.start()
    pools = pool_both(0.5, 0.25)
    inverse[4:8, :] = jnp.zeros((4, BLOCK), F32)
    stores = []

    def normalise(step):
        if step in (0, 2):
            for load in loads[0:4] if step == 0 else loads[4:7]:
                load.wait()
        rows = block_rows(step)
        shares = [share[rows, :].astype(F32) for share in (t0, t1, t2, t3)]
        squares = shares[0] * shares[0]
        for share in shares[1:]:
            squares = squares + share * share
        total = jnp.sum(squares, axis=1, keepdims=True)
        inv = lax.rsqrt(total / (MP * width) + EPSILON)
        inverse[step : step + 1, :] = as_row(inv)
        parts = [(share * inv).astype(BF16) for share in shares]
        for r, part in enumerate(parts):
            normed[rows, r * width : (r + 1) * width] = part
        store = pltpu.make_async_copy(normed.at[rows], normed_hbm.at[rows], out_sems.at[step])
        store.start()
        stores.append(store)
        return jnp.concatenate(parts, axis=1)

    def spread(step, whole):
        if step == 0:
            for load in loads[7:]:
                load.wait()
            store = pltpu.make_async_copy(w, w_hbm, out_sems.at[4])
            store.start()
            stores.append(store)
        rows = block_rows(step)
        fine = [nn(whole, w[:, n * width : (n + 1) * width]).astype(BF16) for n in range(3)]
        coarse = [nn(pools, x).astype(BF16) for x in fine]
        mid = [x[0:128] for x in coarse]
        low = [x[128:192] for x in coarse]
        mid_rows = slice(1024 + step * 128, 1024 + (step + 1) * 128)
        low_rows = slice(1536 + step * 64, 1536 + (step + 1) * 64)
        q[rows, :] = fine[0]
        q[mid_rows, :] = mid[0]
        q[low_rows, :] = low[0]
        for n in range(2):
            kv[n, rows, :] = fine[1 + n]
            kv[n, mid_rows, :] = mid[1 + n]
            kv[n, low_rows, :] = low[1 + n]
            if step in (0, 3):
                edges[step // 3, n, 0:BLOCK, :] = fine[1 + n]
            if step in (1, 2):
                edges[step - 1, n, 256:384, :] = mid[1 + n]
            if step > 0:
                edges[0, n, 320 + step * 64 : 384 + step * 64, :] = low[1 + n]
            if step < 3:
                edges[1, n, 384 + step * 64 : 448 + step * 64, :] = low[1 + n]

    parts = normalise(0)
    for step in range(4):
        following = normalise(step + 1) if step < 3 else None
        spread(step, parts)
        parts = following
    share_edges(place, edges, to_core, to_other)
    for store in stores:
        store.wait()


def project(place, shares, wq, wk, wv):
    rows, width = shares[0].shape
    out = jax.ShapeDtypeStruct
    edge = out((2, EDGE_ROWS, width), BF16)
    anywhere = pl.BlockSpec(memory_space=pl.ANY)
    share = pltpu.VMEM((rows, width), BF16)
    fixed = [
        pltpu.with_memory_space_constraint(value, pltpu.HBM)
        for value in (*shares[1:], shares[0], wq, wk, wv)
    ]
    return pl.pallas_call(
        project_kernel,
        in_specs=[SCALAR] + [anywhere] * 10,
        out_specs=[RESIDENT] * 5 + [anywhere] * 2,
        out_shape=[
            out((8, width), F32),
            out((ALL_ROWS, width), BF16),
            out((2, ALL_ROWS, width), BF16),
            edge,
            edge,
            pltpu.HBM((rows, MP * width), BF16),
            pltpu.HBM((MP * width, 3 * width), BF16),
        ],
        scratch_shapes=[share] * 4
        + [
            pltpu.VMEM((MP * width, 3 * width), BF16),
            pltpu.VMEM((rows, MP * width), BF16),
            pltpu.VMEM((2, *edge.shape), BF16),
            pltpu.SemaphoreType.DMA((19,)),
            pltpu.SemaphoreType.DMA((5,)),
        ],
        compiler_params=pltpu.CompilerParams(vmem_limit_bytes=20 * 2**20),
        cost_estimate=SMALL,
        name="project",
    )(place, *fixed)


def near_kernel(place, g0, g1, g3, w_out, total, w_turned):
    me = place[0]
    width = g0.shape[1]
    for n, r in enumerate((0, 1, 3)):
        w_turned[block_rows(n), :] = w_out[:, share_rows(me, r, width)].T
    for step in range(4):
        rows = block_rows(step)
        shares = jnp.concatenate([share[rows, :] for share in (g0, g1, g3)], axis=1)
        total[rows, :] = nn(shares, w_turned[...])


def near_cotangent(place, shares, w_out):
    rows, width = shares[0].shape
    inputs = [*shares, w_out]
    scratch = [pltpu.VMEM((3 * width, width), BF16)]
    outputs = [held((rows, width), F32)]
    return run(near_kernel, "near_cotangent", 10, [place], inputs, outputs, scratch)[0]


def cotangent_kernel(place, near, g2, w_out, d_att, w_turned):
    width = g2.shape[1]
    pools = pool_both(1.0, 1.0)
    w_turned[...] = w_out[:, share_rows(place[0], 2, width)].T
    for step in range(4):
        rows = block_rows(step)
        fine = (near[rows, :] + nn(g2[rows, :], w_turned[...])).astype(BF16)
        d_att[rows, :] = fine
        coarse = nn(pools, fine).astype(BF16)
        d_att[1024 + step * 128 : 1024 + (step + 1) * 128, :] = coarse[0:128]
        d_att[1536 + step * 64 : 1536 + (step + 1) * 64, :] = coarse[128:192]


def cotangent(place, near, far, w_out):
    width = far.shape[1]
    scratch = [pltpu.VMEM((width, width), BF16)]
    outputs = [held((ALL_ROWS, width), BF16)]
    return run(cotangent_kernel, "cotangent", 10, [place], [near, far, w_out], outputs, scratch)[0]


EDGE_UNITS = ((0, 0), (0, 3), (1, 0), (1, 1), (2, 0))
INNER_UNITS = ((0, 1), (0, 2))


def unit_keys(level, block):
    last = EXT_BLOCKS[level] - 1
    offsets = (0, 1, 2) if level == 0 else (0, 2)
    keys = []
    for offset in offsets:
        at = block + offset
        keys.append((at, 0 if at == 0 else 1 if at == last else None))
    return keys


def ext_rows(kv, halo, n, level, at, lanes):
    if at in (0, EXT_BLOCKS[level] - 1):
        return halo[0 if at == 0 else 1][n, block_rows(level), lanes]
    return kv[n, block_rows(LEVEL_BLOCK[level] + at - 1), lanes]


def head_part(lane, head, rows):
    mine = (lane >= head * HD) & (lane < (head + 1) * HD)
    return jnp.where(mine, rows, 0.0).astype(BF16)


def unit_scores(keys, key_rows, query, bias_ref):
    scores = []
    for (_, bias), rows in zip(keys, key_rows):
        s = nt(rows, query)
        scores.append(s if bias is None else s + bias_ref[bias])
    return scores


def add_spread(target, block, factor, rows):
    if factor == 1:
        target[block_rows(block), :] = target[block_rows(block), :] + rows
        return
    for s in range(factor):
        spread = pl.ds(block * factor * BLOCK + s, BLOCK, factor)
        target[spread, :] = target[spread, :] + rows


def each_pair(width, body):
    def step(pair, _):
        body(pair, pl.ds(pl.multiple_of(pair * PAIR, PAIR), PAIR))
        return 0

    lax.fori_loop(0, width // PAIR, step, 0)


def head_part(lane, head, rows):
    mine = (lane >= head * HD) & (lane < (head + 1) * HD)
    return jnp.where(mine, rows, 0.0).astype(BF16)


def unit_scores(keys, key_rows, query, bias_ref):
    scores = []
    for (_, bias), rows in zip(keys, key_rows):
        s = nt(rows, query)
        scores.append(s if bias is None else s + bias_ref[bias])
    return scores


def add_spread(target, block, factor, rows):
    if factor == 1:
        target[block_rows(block), :] = target[block_rows(block), :] + rows
        return
    for s in range(factor):
        spread = pl.ds(block * factor * BLOCK + s, BLOCK, factor)
        target[spread, :] = target[spread, :] + rows


def forward_units(pair, lanes, units, bias_ref, q, kv, halo, stats, vt, out_f):
    lane = lax.broadcasted_iota(jnp.int32, (BLOCK, PAIR), 1)
    done = set()
    for level, block in units:
        for at, _ in unit_keys(level, block):
            if (level, at) not in done:
                done.add((level, at))
                rows = ext_rows(kv, halo, 1, level, at, lanes)
                vt[FIRST_EXT[level] + at] = rows.T

    def begin(u, head):
        level, block = units[u]
        keys = unit_keys(level, block)
        key_rows = [ext_rows(kv, halo, 0, level, at, lanes) for at, _ in keys]
        q_rows = q[block_rows(LEVEL_BLOCK[level] + block), lanes] * HD ** (-0.5)
        return unit_scores(keys, key_rows, head_part(lane, head, q_rows), bias_ref)

    def finish(u, head, scores):
        level, block = units[u]
        top = scores[0].max(axis=0, keepdims=True)
        for s in scores[1:]:
            top = jnp.maximum(top, s.max(axis=0, keepdims=True))
        exps = [jnp.exp(s - top) for s in scores]
        total = exps[0].sum(axis=0, keepdims=True)
        for e in exps[1:]:
            total = total + e.sum(axis=0, keepdims=True)
        scale = 1.0 / total
        row = 4 * u + 2 * head
        stats[pair, row : row + 1, :] = top
        stats[pair, row + 1 : row + 2, :] = scale
        return [(e * scale).astype(BF16) for e in exps]

    outs = []

    def give(u, head, weights):
        level, block = units[u]
        part = slice(head * HD, (head + 1) * HD)
        o_t = None
        for (at, _), w in zip(unit_keys(level, block), weights):
            o = nn(vt[FIRST_EXT[level] + at, part, :], w)
            o_t = o if o_t is None else o_t + o
        outs.append(o_t)
        if head == 1:
            add_spread(out_f, block, 2**level, jnp.concatenate(outs, axis=0).T)
            outs.clear()

    items = [(u, head) for u in range(len(units)) for head in range(2)]
    scores, last = begin(*items[0]), None
    for n, item in enumerate(items):
        following = begin(*items[n + 1]) if n + 1 < len(items) else None
        if last is not None:
            give(*items[n - 1], last)
        last = finish(*item, scores)
        scores = following
    give(*items[-1], last)


def forward_inner_kernel(bias_ref, q, kv, out, stats, vt, out_f):
    def one(pair, lanes):
        out_f[...] = jnp.zeros_like(out_f)
        forward_units(pair, lanes, INNER_UNITS, bias_ref, q, kv, None, stats, vt, out_f)
        out[:, lanes] = out_f[BLOCK : 3 * BLOCK, :]

    each_pair(q.shape[1], one)


def forward_edge_kernel(
    place, bias_ref, q, kv, from_other, from_core, inner,
    attended, stats, left, right, vt, out_f,
):
    received = (place, from_core, from_other)
    pools = pool_both(0.5, 0.25)
    every = slice(None)
    for n in range(2):
        for out, is_left in ((left, True), (right, False)):
            fine = halo_rows(received, is_left, (n, slice(0, 256), every))
            mid = halo_rows(received, is_left, (n, slice(256, 384), every))
            low = halo_rows(received, is_left, (n, slice(384, 576), every))
            coarse = nn(pools, fine).astype(BF16)
            out[n, 0:256, :] = fine
            if is_left:
                out[n, 256:384, :], out[n, 384:512, :] = mid, coarse[0:128]
                out[n, 512:704, :], out[n, 704:768, :] = low, coarse[128:192]
            else:
                out[n, 256:384, :], out[n, 384:512, :] = coarse[0:128], mid
                out[n, 512:576, :], out[n, 576:768, :] = coarse[128:192], low
    halo = (left, right)

    def one(pair, lanes):
        out_f[0:BLOCK, :] = jnp.zeros((BLOCK, PAIR), F32)
        out_f[BLOCK : 3 * BLOCK, :] = inner[:, lanes]
        out_f[3 * BLOCK :, :] = jnp.zeros((BLOCK, PAIR), F32)
        forward_units(
            pair, lanes, EDGE_UNITS, bias_ref, q, kv, halo, stats, vt, out_f
        )
        attended[:, lanes] = out_f[...].astype(BF16)

    each_pair(q.shape[1], one)


def backward_units(
    pair, lanes, units, bias_ref, q, kv, halo, grads, stats, kt, dq_f, keep
):
    lane = lax.broadcasted_iota(jnp.int32, (BLOCK, PAIR), 1)
    done = set()
    for level, block in units:
        for at, _ in unit_keys(level, block):
            if (level, at) not in done:
                done.add((level, at))
                rows = ext_rows(kv, halo, 0, level, at, lanes)
                kt[FIRST_EXT[level] + at] = rows.T

    def begin(u, head):
        level, block = units[u]
        keys = unit_keys(level, block)
        key_rows = [ext_rows(kv, halo, 0, level, at, lanes) for at, _ in keys]
        value_rows = [ext_rows(kv, halo, 1, level, at, lanes) for at, _ in keys]
        at = block_rows(LEVEL_BLOCK[level] + block)
        qm = head_part(lane, head, q[at, lanes] * HD ** (-0.5))
        am = head_part(lane, head, grads[at, lanes])
        scores = unit_scores(keys, key_rows, qm, bias_ref)
        return qm, am, scores, [nt(rows, am) for rows in value_rows]

    def finish(u, head, qm, am, scores, d_weights):
        level, block = units[u]
        row = 4 * u + 2 * head
        top, scale = stats[pair, row : row + 1, :], stats[pair, row + 1 : row + 2, :]
        probs = [jnp.exp(s - top) * scale for s in scores]
        dots = None
        for p, dw in zip(probs, d_weights):
            d = (p * dw).sum(axis=0, keepdims=True)
            dots = d if dots is None else dots + d
        weights = [p.astype(BF16) for p in probs]
        d_scores = [(p * (dw - dots)).astype(BF16) for p, dw in zip(probs, d_weights)]
        return qm, am, weights, d_scores

    first = []

    def give(u, head, qm, am, weights, d_scores):
        level, block = units[u]
        keys = unit_keys(level, block)
        part = slice(head * HD, (head + 1) * HD)
        d_values = [nn(w, am) for w in weights]
        d_keys = [nn(ds, qm) for ds in d_scores]
        dq_t = None
        for (at, _), ds in zip(keys, d_scores):
            g = nn(kt[FIRST_EXT[level] + at, part, :], ds)
            dq_t = g if dq_t is None else dq_t + g
        if head == 0:
            first.append((dq_t, d_keys, d_values))
            return
        dq_first, k_first, v_first = first.pop()
        for n, (at, _) in enumerate(keys):
            keep(0, level, at, k_first[n] + d_keys[n])
            keep(1, level, at, v_first[n] + d_values[n])
        dq = jnp.concatenate([dq_first, dq_t], axis=0).T * (HD ** (-0.5) / 2**level)
        add_spread(dq_f, block, 2**level, dq)

    items = [(u, head) for u in range(len(units)) for head in range(2)]
    ready, last = begin(*items[0]), None
    for n, item in enumerate(items):
        following = begin(*items[n + 1]) if n + 1 < len(items) else None
        if last is not None:
            give(*items[n - 1], *last)
        last = finish(*item, *ready)
        ready = following
    give(*items[-1], *last)


def edge_kernel(
    place, bias_ref, stats, q, kv, left, right, grads,
    dq_f, d_kv, to_core, to_other, kt, ext, dq_s, sums, edges,
):
    halo = (left, right)

    def add_rows(factor, rows):
        for s in range(factor):
            spread = pl.ds(s, rows.shape[0], factor)
            sums[spread, :] = sums[spread, :] + rows * (1.0 / factor)

    def one(pair, lanes):
        dq_s[...] = jnp.zeros_like(dq_s)
        seen = set()

        def keep(n, level, at, rows):
            slot = FIRST_EXT[level] + at
            if (n, slot) in seen:
                ext[n, slot] = ext[n, slot] + rows
            else:
                seen.add((n, slot))
                ext[n, slot] = rows

        backward_units(
            pair, lanes, EDGE_UNITS, bias_ref, q, kv, halo, grads, stats, kt, dq_s, keep,
        )
        dq_f[:, lanes] = dq_s[...]
        for n in range(2):
            for side in range(2):
                fine, mid, low = (
                    ext[n, FIRST_EXT[level] + side * (EXT_BLOCKS[level] - 1)]
                    for level in range(LEVELS)
                )
                if side == 0:
                    (mid, mid_near), (low, low_near) = (mid[0:128], mid[128:]), (low[0:192], low[192:])
                else:
                    (mid_near, mid), (low_near, low) = (mid[0:128], mid[128:]), (low[0:64], low[64:])
                sums[0:BLOCK, :] = fine
                add_rows(2, mid_near)
                add_rows(4, low_near)
                edges[side, n, 0:256, lanes] = sums[0:BLOCK, :].astype(BF16)
                edges[side, n, 256:384, lanes] = mid.astype(BF16)
                edges[side, n, 384:576, lanes] = low.astype(BF16)
            for b in range(4):
                sums[block_rows(b), :] = ext[n, 1 + b]
            for b in range(2):
                add_spread(sums, b, 2, ext[n, FIRST_EXT[1] + 1 + b] * 0.5)
            d_kv[n, :, lanes] = sums[...]

    each_pair(q.shape[1], one)
    share_edges(place, edges, to_core, to_other)


def inner_units_kernel(bias_ref, stats, q, kv, grads, dq_in, d_kv_in, d_query, d_kv, kt, dq_s):
    def one(pair, lanes):
        dq_s[...] = dq_in[:, lanes]
        d_kv[:, :, lanes] = d_kv_in[:, :, lanes]

        def keep(n, level, at, rows):
            where = block_rows(at - 1)
            d_kv[n, where, lanes] = d_kv[n, where, lanes] + rows

        backward_units(
            pair, lanes, INNER_UNITS, bias_ref, q, kv, None, grads, stats, kt, dq_s, keep
        )
        d_query[:, lanes] = dq_s[...].astype(BF16)

    each_pair(q.shape[1], one)


def turned(count):
    return pltpu.VMEM((count, PAIR, BLOCK), BF16)


def forward_inner(bias, q, kv):
    width = q.shape[1]
    outputs = [held((2 * BLOCK, width), F32), held((width // PAIR, 8, BLOCK), F32)]
    scratch = [turned(EXT_BLOCKS[0]), pltpu.VMEM((4 * BLOCK, PAIR), F32)]
    return run(forward_inner_kernel, "forward_inner", 12, [bias], [q, kv], outputs, scratch, MIDDLE)


def forward_edge(place, bias, q, kv, halo, inner):
    width = q.shape[1]
    inputs = [q, kv, *halo[::-1], inner]
    outputs = [held((4 * BLOCK, width), BF16), held((width // PAIR, 24, BLOCK), F32)]
    outputs += [held((2, 3 * BLOCK, width), BF16)] * 2
    scratch = [turned(EXT_TOTAL), pltpu.VMEM((4 * BLOCK, PAIR), F32)]
    return run(forward_edge_kernel, "forward_edge", 12, [place, bias], inputs, outputs, scratch)


def edge_backward(place, bias, stats, q, kv, halo, d_att):
    rows, width = 4 * BLOCK, q.shape[1]
    edge = held((2, EDGE_ROWS, width), BF16)
    inputs = [stats, q, kv, *halo, d_att]
    outputs = [held((rows, width), F32), held((2, rows, width), F32), edge, edge]
    scratch = [
        turned(EXT_TOTAL),
        pltpu.VMEM((2, EXT_TOTAL, BLOCK, PAIR), F32),
        pltpu.VMEM((rows, PAIR), F32),
        pltpu.VMEM((rows, PAIR), F32),
        pltpu.VMEM((2, *edge.shape), BF16),
    ]
    return run(edge_kernel, "edge_backward", 20, [place, bias], inputs, outputs, scratch)


def inner_backward(bias, stats, q, kv, d_att, dq_f, d_kv):
    rows, width = 4 * BLOCK, q.shape[1]
    inputs = [stats, q, kv, d_att, dq_f, d_kv]
    outputs = [held((rows, width), BF16), held((2, rows, width), F32)]
    scratch = [turned(EXT_BLOCKS[0]), pltpu.VMEM((rows, PAIR), F32)]
    return run(inner_units_kernel, "inner_backward", 12, [bias], inputs, outputs, scratch)


def term_outputs(rows, width):
    return [held((rows, width), BF16)] * MP


def store_terms(step, terms, own, keep_right, keep_left, right, left):
    own[block_rows(step), :] = terms[0]
    low, high = block_rows(step % 2), block_rows(2 + step % 2)
    if step < 2:
        keep_right[low, :] = terms[1]
        right[high, :] = terms[2]
        left[low, :] = terms[3]
    else:
        right[low, :] = terms[1]
        left[high, :] = terms[2]
        keep_left[low, :] = terms[3]


def out_terms_kernel(place, attended, w_out, *outs):
    me = place[0]
    width = attended.shape[1]
    near = 1 + 2 * (me & 1)
    for step in range(4):
        rows = attended[block_rows(step), :]
        for r, out in zip((0, near, 2, 4 - near), outs):
            term = nn(rows, w_out[:, share_rows(me, r, width)])
            out[block_rows(step), :] = term.astype(BF16)


def out_terms(place, attended, w_out):
    outputs = term_outputs(*attended.shape)
    return run(out_terms_kernel, "out_terms", 8, [place], [attended, w_out], outputs)


def by_partner(place, sent, to_a, to_b):
    odd = place[0] & 1
    to_a[...] = sent[odd]
    to_b[...] = sent[1 - odd]


def from_side(place, from_a, from_b, before, rows):
    odd = place[0] & 1
    one, other = from_a[rows, :], from_b[rows, :]
    return jnp.where(odd == 1, one, other) if before else jnp.where(odd == 1, other, one)


def input_terms_kernel(
    place, d_query, d_kv, from_other, from_core, normed, w, d_proj,
    dots, own, keep_right, keep_left, to_a, to_b, dot_rows, w_turned, sent,
):
    halo = (place, from_core, from_other)
    width = d_query.shape[1]
    half = spread_matrix(BLOCK // 2, 2, 0.5)
    quarter = spread_matrix(BLOCK // 4, 4, 0.25)
    dot_rows[12:16, :] = jnp.zeros((4, BLOCK), F32)
    for r in range(MP):
        for n in range(3):
            at = slice(r * width, (r + 1) * width)
            w_turned[block_rows(n), at] = w[at, n * width : (n + 1) * width].T
    for step in range(4):
        rows = block_rows(step)
        grads = [d_query[rows, :]]
        every = slice(None)
        for n in range(2):
            total = d_kv[n, rows, :]
            if step in (0, 3):
                total = total + halo_rows(halo, step == 0, (n, slice(0, 256), every)).astype(F32)
            else:
                total = total + nn(half, halo_rows(halo, step == 1, (n, slice(256, 384), every)))
            if step > 0:
                low = slice(320 + step * 64, 384 + step * 64)
                total = total + nn(quarter, halo_rows(halo, True, (n, low, every)))
            if step < 3:
                low = slice(384 + step * 64, 448 + step * 64)
                total = total + nn(quarter, halo_rows(halo, False, (n, low, every)))
            grads.append(total.astype(BF16))
        for n, grad in enumerate(grads[1:]):
            d_proj[rows, n * width : (n + 1) * width] = grad
        dot = None
        every = jnp.concatenate(grads, axis=1)
        terms = []
        for r in range(MP):
            term = nn(every, w_turned[:, r * width : (r + 1) * width]).astype(BF16)
            terms.append(term)
            part = term.astype(F32) * normed[rows, r * width : (r + 1) * width].astype(F32)
            dot = part if dot is None else dot + part
        store_terms(step, terms, own, keep_right, keep_left, sent.at[0], sent.at[1])
        dot = as_row(jnp.sum(dot, axis=1, keepdims=True))
        first = dot.astype(BF16).astype(F32)
        second = (dot - first).astype(BF16).astype(F32)
        for n, piece in enumerate((first, second, dot - first - second)):
            dot_rows[4 * n + step : 4 * n + step + 1, :] = piece
    pieces = dot_rows[...].astype(BF16)
    dots[...] = pieces
    for side in range(2):
        sent[side, 4 * BLOCK :, :] = pieces
    by_partner(place, sent, to_a, to_b)


def input_terms(place, d_query, d_kv, halo, normed, w):
    rows, width = d_query.shape
    inputs = [d_query, d_kv, *halo[::-1], normed, w]
    outputs = [held((rows, 2 * width), BF16), held((DOT_ROWS, width), BF16)]
    lengths = [rows, rows // 2, rows // 2, rows + DOT_ROWS, rows + DOT_ROWS]
    outputs += [held((n, width), BF16) for n in lengths]
    scratch = [pltpu.VMEM((DOT_ROWS, width), F32), pltpu.VMEM((3 * width, MP * width), BF16)]
    scratch += [pltpu.VMEM((2, rows + DOT_ROWS, width), BF16)]
    return run(input_terms_kernel, "input_terms", 18, [place], inputs, outputs, scratch)


def sum_terms(own, received, at):
    total = own[at, :].astype(F32)
    for term in received:
        total = total + term[at, :].astype(F32)
    return total


def finish_out_kernel(own, one, two, three, result):
    for b in range(4):
        at = block_rows(b)
        result[at, :] = sum_terms(own, (one, two, three), at).astype(BF16)


def finish_out(own, received):
    outputs = [held(own.shape, BF16)]
    return run(finish_out_kernel, "finish_out", 8, [], [own, *received], outputs)[0]


def relay_kernel(place, keep_right, keep_left, from_a, from_b, to_a, to_b, sent):
    half = keep_right.shape[0]
    terms, dots = slice(half, 2 * half), slice(2 * half, 2 * half + DOT_ROWS)
    for side, keep in enumerate((keep_right, keep_left)):
        passed = from_side(place, from_a, from_b, side == 0, terms).astype(F32)
        sent[side, 0:half, :] = (keep[...].astype(F32) + passed).astype(BF16)
        sent[side, half:, :] = from_side(place, from_a, from_b, side == 0, dots)
    by_partner(place, sent, to_a, to_b)


def relay(place, keep_right, keep_left, from_a, from_b):
    half, width = keep_right.shape
    outputs = [held((half + DOT_ROWS, width), BF16)] * 2
    scratch = [pltpu.VMEM((2, half + DOT_ROWS, width), BF16)]
    inputs = [keep_right, keep_left, from_a, from_b]
    return run(relay_kernel, "relay", 6, [place], inputs, outputs, scratch, RELAY)


def finish_grad_kernel(place, own, a1, b1, a2, b2, tokens, inverse, dots, result):
    rows, width = own.shape
    half = rows // 2
    whole, part = slice(rows, rows + DOT_ROWS), slice(half, half + DOT_ROWS)
    pieces = dots[...].astype(F32) + a1[whole, :].astype(F32) + b1[whole, :].astype(F32)
    pieces = pieces + from_side(place, a2, b2, True, part).astype(F32)
    means = (pieces[0:4] + pieces[4:8] + pieces[8:12]) / (MP * width)
    for b in range(rows // BLOCK):
        at, near = block_rows(b), block_rows(b % 2)
        mean = as_column(means[b : b + 1, :])
        inv = as_column(inverse[b : b + 1, :])
        total = own[at, :].astype(F32)
        total = total + from_side(place, a1, b1, b >= 2, near).astype(F32)
        total = total + from_side(place, a2, b2, b < 2, near).astype(F32)
        result[at, :] = inv * (total - tokens[at, :].astype(F32) * inv * mean)


def finish_grad(place, own, a1, b1, a2, b2, tokens, inverse, dots):
    inputs = [own, a1, b1, a2, b2, tokens, inverse, dots]
    outputs = [held(own.shape, F32)]
    return run(finish_grad_kernel, "finish_grad", 8, [place], inputs, outputs)[0]


def early_kernel(g0, g1, g2, g3, attended, normed, d_query, outer, inner):
    width = g0.shape[1]
    rows = attended[...]
    for r, share in enumerate((g0, g1, g2, g3)):
        at = slice(r * width, (r + 1) * width)
        outer[at, :] = tn(share[...], rows).astype(BF16)
        inner[at, :] = tn(normed[:, at], d_query[...]).astype(BF16)


def early_terms(shares, attended, normed, d_query):
    width = attended.shape[1]
    inputs = [*shares, attended, normed, d_query]
    outputs = [held((MP * width, width), BF16)] * 2
    return run(early_kernel, "early_terms", 14, [], inputs, outputs, (), LARGE)


def inner_kernel(place, normed, d_proj, inner, outer, mine, other_low, other_high, rows_held):
    core = place[1]
    width = outer.shape[1]
    for block in range(MP):
        at = block_rows(block)
        rows_held[at, 0:width] = inner[at, :]
        rows_held[at, width : 3 * width] = tn(normed[:, at], d_proj[...]).astype(BF16)
        rows_held[at, 3 * width :] = outer[at, :]
        for n in range(width // 64):
            out = slice((4 * block + n) * 32, (4 * block + n + 1) * 32)
            first = block * width + n * 64
            mine[out, :] = rows_held[pl.ds(pl.multiple_of(first + core * 32, 32), 32), :]
            other, start = (other_low, 0) if block < 2 else (other_high, 256)
            other[out.start - start : out.stop - start, :] = rows_held[pl.ds(pl.multiple_of(first + 32 - core * 32, 32), 32), :]


def inner_terms(place, normed, d_proj, inner, outer):
    total = normed.shape[1]
    width = outer.shape[1]
    outputs = [held((n, 4 * width), BF16) for n in (total // 2, total // 4, total // 4)]
    scratch = [pltpu.VMEM((total, 4 * width), BF16)]
    return run(inner_kernel, "inner_terms", 16, [place], [normed, d_proj, inner, outer], outputs, scratch)


def pair_sum_kernel(place, mine, got_low, got_high, *outs):
    z, core, x, y = place[0], place[1], place[2], place[3]
    for d, out in enumerate(outs):
        for n in range(4):
            chunk = jnp.where(core == 0, 4 * n + ((x + d) & 3), 4 * ((y + d - z + 4) & 3) + n)
            rows = pl.ds(pl.multiple_of(chunk * 32, 32), 32)
            half = pl.ds(pl.multiple_of((chunk & 7) * 32, 32), 32)
            got = jnp.where(chunk < 8, got_low[half, :], got_high[half, :])
            total = mine[rows, :].astype(F32) + got.astype(F32)
            out[32 * n : 32 * (n + 1), :] = total.astype(BF16)


def row_sum_kernel(place, a, b, c, d, *refs):
    *outs, total = refs
    z, core, x, y = place[0], place[1], place[2], place[3]
    first = jnp.where(core == 0, y - z + 4, x)
    total[...] = (
        a[...].astype(F32) + b[...].astype(F32) + c[...].astype(F32) + d[...].astype(F32)
    ).astype(BF16)
    for n, out in enumerate(outs):
        out[...] = total[pl.ds(pl.multiple_of(((first + n) & 3) * 32, 32), 32), :]


def last_sum_kernel(a, b, c, d, gq, gk, gv, go):
    width = gq.shape[1]
    total = a[...].astype(F32) + b[...].astype(F32) + c[...].astype(F32) + d[...].astype(F32)
    gq[...] = total[:, 0:width]
    gk[...] = total[:, width : 2 * width]
    gv[...] = total[:, 2 * width : 3 * width]
    go[...] = total[:, 3 * width :]


def sum_over_core(place, mine, *others):
    got = [lax.ppermute(other, "seq", [(i, i ^ 1) for i in range(32)]) for other in others]
    parts = [held((128, mine.shape[1]), BF16)] * 4
    return run(pair_sum_kernel, "pair_sum", 6, [place], [mine, *got], parts)


def sum_over_seq(place, parts, *first):
    cols = parts[0].shape[1]

    def sent(value, stage, d):
        pairs = []
        for i in range(32):
            core, x, y = i % 2, (i // 2) % 4, i // 8
            if stage == core:
                x = (x + d) % 4
            else:
                y = (y + d) % 4
            pairs.append((i, (y * 4 + x) * 2 + core))
        return lax.ppermute(value, "seq", pairs)

    parts = [parts[0]] + [sent(parts[d], 0, d) for d in (1, 2, 3)]
    parts = tied(parts, *first)
    rows = [held((32, cols), BF16)] * 4
    scratch = [pltpu.VMEM((128, cols), BF16)]
    rows = run(row_sum_kernel, "row_sum", 4, [place], parts, rows, scratch)
    rows = [rows[0]] + [sent(rows[d], 1, d) for d in (1, 2, 3)]
    outputs = [held((32, cols // 4), F32)] * 4
    return run(last_sum_kernel, "last_sum", 4, [], rows, outputs)


def to_next(value):
    return lax.ppermute(value, "mp", [(i, (i + 1) % MP) for i in range(MP)])


def to_previous(value):
    return lax.ppermute(value, "mp", [((i + 1) % MP, i) for i in range(MP)])


def swap_a(value):
    return lax.ppermute(value, "mp", [(0, 1), (1, 0), (2, 3), (3, 2)])


def swap_b(value):
    return lax.ppermute(value, "mp", [(1, 2), (2, 1), (3, 0), (0, 3)])


def gather_shares(share):
    half = share.shape[0] // 2
    low, high = share[:half], share[half:]
    after_low, before_high = to_previous(low), to_next(high)
    after_high, before_low = to_previous(high), to_next(low)
    far_low, far_high = to_previous(after_low), to_next(before_high)
    return [share, after_low, after_high, far_low, far_high, before_low, before_high]


def turned_by(value, step):
    return lax.ppermute(value, "mp", [(i, (i + step) % MP) for i in range(MP)])


def sum_over_mp(terms):
    to_a, far, to_b = terms
    return [swap_a(to_a), turned_by(far, 2), swap_b(to_b)]


def exchange(to_core, to_other):
    count = lax.axis_size("seq")
    pairs = []
    for i in range(1, count - 1, 2):
        pairs += [(i, i + 1), (i + 1, i)]
    from_other = lax.ppermute(to_other, "seq", pairs)
    from_core = lax.ppermute(to_core, "seq", [(i, i ^ 1) for i in range(count)])
    return from_core, from_other


def tied(values, *others):
    flat, tree = jax.tree.flatten(values)
    flat = lax.optimization_barrier((*flat, *others))[: len(flat)]
    return jax.tree.unflatten(tree, flat)


def per_device(tokens, w_query, w_key, w_value, w_out, grad_out):
    count = lax.axis_size("seq")
    index = lax.axis_index("seq")
    me = jnp.stack([lax.axis_index("mp"), index & 1, (index >> 1) & 3, index >> 3])
    me = me.astype(jnp.int32)
    bias = jnp.stack(
        [
            jnp.where(index == 0, NEGATIVE, 0.0).astype(F32),
            jnp.where(index == count - 1, NEGATIVE, 0.0).astype(F32),
        ]
    )
    token_shares = gather_shares(tokens)
    near_grad = tied(grad_out, *(token_shares[n] for n in (1, 2, 5, 6)))
    far_grad = tied(grad_out, *token_shares)
    far = turned_by(far_grad, 2)
    grad_shares = [grad_out, to_previous(near_grad), far, to_next(near_grad)]
    inverse, q, kv, to_core, to_other, normed, w = project(
        me, token_shares, w_query, w_key, w_value
    )
    halo = exchange(to_core, to_other)
    near_q = tied(q, grad_shares[1], grad_shares[3])
    inner_out, inner_stats = forward_inner(bias, near_q, kv)
    near = near_cotangent(me, tied([grad_shares[n] for n in (0, 1, 3)], inner_out), w_out)
    inner_out = tied(inner_out, near)
    attended, stats, *halo = forward_edge(me, bias, q, kv, halo, inner_out)
    out_own, *terms = out_terms(me, attended, w_out)
    out_received = sum_over_mp(terms)
    grad_shares = tied(grad_shares, out_own)
    d_att = cotangent(me, near, grad_shares[2], w_out)
    dq_f, d_kv, to_core, to_other = edge_backward(me, bias, stats, q, kv, halo, d_att)
    halo = exchange(to_core, to_other)
    d_query, d_kv = inner_backward(bias, inner_stats, q, kv, d_att, dq_f, d_kv)
    attended = tied(attended, *out_received)
    outer, inner = early_terms(grad_shares, attended, normed, d_query)
    d_query = tied(d_query, outer)
    d_proj, dots, own, keep_right, keep_left, to_a, to_b = input_terms(
        me, d_query, d_kv, halo, normed, w
    )
    attn_out = finish_out(out_own, out_received)
    mine, *others = inner_terms(me, normed, d_proj, inner, outer)
    core_sums = sum_over_core(me, mine, *others)
    a1, b1 = swap_a(to_a), swap_b(to_b)
    to_a, to_b = relay(me, keep_right, keep_left, a1, b1)
    a2, b2 = swap_a(to_a), swap_b(to_b)
    grad_tokens = finish_grad(me, own, a1, b1, a2, b2, tokens, inverse, dots)
    *weight_grads, grad_w_out = sum_over_seq(me, core_sums, to_a, attn_out)
    return (attn_out, grad_tokens, *weight_grads, grad_w_out.T)


def solution(mesh):
    return jax.shard_map(
        per_device,
        mesh=mesh,
        in_specs=(
            P("seq", "mp"),
            P(None, "mp"),
            P(None, "mp"),
            P(None, "mp"),
            P("mp", None),
            P("seq", "mp"),
        ),
        out_specs=(
            P("seq", "mp"),
            P("seq", "mp"),
            P("seq", "mp"),
            P("seq", "mp"),
            P("seq", "mp"),
            P("mp", "seq"),
        ),
        check_vma=False,
    )
```
